32 devices in a mesh: dp: 4 (over y, x), expert: 8 (over z, core).
Axes of the slice: x: 2, y: 2, z: 4, core: 2. Of those that a mesh axis runs over, the one named last changes fastest.
Arguments:
- tokens: bfloat16 [31520, 512], P(('dp', 'expert')), may hold values from -6 to 6
- targets: bfloat16 [31520, 512], P(('dp', 'expert')), may hold values from -6 to 6
- valid_mask: int32 [31520], P(('dp', 'expert')), may hold values from 0 to 1
- routes: int32 [31520, 2], P(('dp', 'expert')), may hold values from 0 to 7, as said below
- slot_ids: int32 [31520, 2], P(('dp', 'expert')), may hold values from 0 to 312, as said below
- ln1_gain: bfloat16 [512], P(('dp', 'expert')), may hold values from 0.5 to 1.5
- qkv_weight: bfloat16 [512, 1536], P(('dp', 'expert')), may hold values from -0.25 to 0.25
- out_weight: bfloat16 [512, 512], P(('dp', 'expert')), may hold values from -0.5 to 0.5
- ln2_gain: bfloat16 [512], P(('dp', 'expert')), may hold values from 0.5 to 1.5
- router_weight: bfloat16 [512, 8], P(('dp', 'expert')), may hold values from -0.1875 to 0.1875
- expert_in: bfloat16 [8, 512, 2048], P('expert', 'dp'), may hold values from -0.25 to 0.25
- expert_out: bfloat16 [8, 2048, 512], P('expert', 'dp'), may hold values from -0.1875 to 0.1875
Outputs:
- block_out: bfloat16 [31520, 512], P(('dp', 'expert'))
- loss: float32 [], replicated
- tokens_grad: float32 [31520, 512], P(('dp', 'expert'))
- ln1_gain_grad: float32 [512], P(('dp', 'expert'))
- qkv_grad: float32 [512, 1536], P(('dp', 'expert'))
- out_grad: float32 [512, 512], P(('dp', 'expert'))
- ln2_gain_grad: float32 [512], P(('dp', 'expert'))
- router_grad: float32 [512, 8], P(('dp', 'expert'))
- expert_in_grad: float32 [8, 512, 2048], P('expert', 'dp')
- expert_out_grad: float32 [8, 2048, 512], P('expert', 'dp')
The draws below stay inside these ranges and needn't reach their ends.
Inputs may be any that keep to these rules, and one draw needn't show every extreme that they name: `routes`: the two experts of a token differ. `slot_ids`: within each block of 985 rows (one device's tokens) the kept pairs routed to one expert have distinct slots; 312 marks a dropped pair. In every draw one expert holds all 312 slots from every block.
All inputs are finite; a program needn't handle non-finite values.
Results may differ from the reference program's by a relative error of at most 0.009.
Values may be sent and summed in bfloat16 or wider, within the bound.
A program may use at most 192 MiB of HBM per device.

```python
import jax
import jax.numpy as jnp
from jax import lax

D = 512
HEADS = 8
HEAD_DIM = 64
H = 2048
IMG_LEN = 197
IMG_DEV = 5
TOK_DEV = 985
EXPERTS = 8
CAP = 312
TOKENS = 31520


def shuffle_block(block_key):
    return jax.random.permutation(block_key, 2 * TOK_DEV)


def route_plan(key):
    blocks = TOKENS // TOK_DEV
    subkeys = jax.random.split(key, 6)
    expert_weights = jax.random.permutation(subkeys[0], EXPERTS).astype(jnp.int32) + 1
    bounds = jnp.cumsum(expert_weights)
    weight_total = EXPERTS * (EXPERTS + 1) // 2
    first_draw = jax.random.randint(subkeys[1], (TOKENS,), 0, weight_total)
    first_choice = jnp.sum((first_draw[:, None] >= bounds[None, :]).astype(jnp.int32), axis=1)
    hot_expert = jax.random.randint(subkeys[2], (), 0, EXPERTS)
    local_rows = jnp.arange(TOKENS, dtype=jnp.int32) % TOK_DEV
    first_choice = jnp.where(local_rows < CAP, hot_expert, first_choice)
    second_draw = jax.random.randint(subkeys[3], (TOKENS,), 0, weight_total)
    second_choice = jnp.sum((second_draw[:, None] >= bounds[None, :]).astype(jnp.int32), axis=1)
    offsets = jax.random.randint(subkeys[4], (TOKENS,), 1, EXPERTS)
    second_choice = jnp.where(second_choice == first_choice, (first_choice + offsets) % EXPERTS, second_choice)
    route_pairs = jnp.stack([first_choice, second_choice], axis=1).astype(jnp.int32)
    by_block = route_pairs.reshape(blocks, 2 * TOK_DEV)
    priority = jax.vmap(shuffle_block)(jax.random.split(subkeys[5], blocks))
    sorted_routes = jnp.take_along_axis(by_block, priority, axis=1)
    onehot = (sorted_routes[:, :, None] == jnp.arange(EXPERTS, dtype=jnp.int32)[None, None, :]).astype(jnp.int32)
    rank_table = jnp.sum((jnp.cumsum(onehot, axis=1) - onehot) * onehot, axis=2)
    inverse = jnp.argsort(priority, axis=1)
    slot_rank = jnp.take_along_axis(rank_table, inverse, axis=1)
    slot_table = jnp.minimum(slot_rank, CAP).reshape(TOKENS, 2).astype(jnp.int32)
    return (route_pairs, slot_table)


def draw_routes(key, part):
    route_pairs, slot_table = route_plan(key)
    return route_pairs


def draw_slot_ids(key, part):
    route_pairs, slot_table = route_plan(key)
    return slot_table


def draw_valid_mask(key, part):
    key = jax.random.fold_in(key, 7)
    blocks = TOKENS // TOK_DEV
    owner_block = jnp.arange(TOKENS, dtype=jnp.int32) // TOK_DEV
    threshold = 30 + 60 * owner_block // max(blocks - 1, 1)
    dice_rolls = jax.random.randint(key, (TOKENS,), 0, 100)
    return (dice_rolls < threshold).astype(jnp.int32)


def spiked(array, stream_key, source, target, shards_of, factor):
    def block_of(position):
        return (jnp.arange(array.shape[position]) // (array.shape[position] // shards_of)).reshape((-1,) + (1,) * (array.ndim - 1 - position))

    one_side = jax.random.permutation(stream_key, shards_of)[block_of(target)]
    far = (block_of(target) + shards_of // 2) % shards_of
    return jnp.where((block_of(source) == one_side) | (block_of(source) == far), factor * array, array)


def shard_levels(key, shape, cuts, smallest, largest):
    factor_of = 1.0
    for position, blocks in cuts:
        heights = jax.random.uniform(jax.random.fold_in(jax.random.fold_in(key, 6), position), (blocks,), jnp.float32, smallest / len(cuts), largest / len(cuts))
        factor_of = factor_of * jnp.repeat(jnp.exp(heights), shape[position] // blocks).reshape((-1,) + (1,) * (len(shape) - 1 - position))
    return factor_of


def gaussian(key, extent, scale, limit, cuts=(), kind=jnp.bfloat16):
    factor_of = shard_levels(key, extent, cuts, -0.22, 0.18) if cuts else 1.0
    result = jax.random.normal(key, extent, jnp.float32) * scale * factor_of
    return jnp.minimum(jnp.maximum(result, -limit), limit).astype(kind)


def noise_with(stream_key, extent, deviation, bound, shards, heavy, held_as=jnp.bfloat16):
    result = deviation * jax.random.normal(stream_key, extent, jnp.float32)
    if shards:
        result = result * shard_levels(stream_key, extent, shards, -0.22, 0.18)
    return jnp.clip(spiked(result, jax.random.fold_in(stream_key, 3), *heavy), -bound, bound).astype(held_as)


def setup_inputs(seed: int = 0) -> dict:
    splits = jax.random.split(jax.random.key(seed), 13)
    tokens = noise_with(splits[0], (TOKENS, D), 1.0, 6.0, ((0, 32),), (0, 1, 32, 2.75))
    targets = gaussian(splits[1], (TOKENS, D), 1.0, 6.0, ((0, 32),))
    valid_mask = draw_valid_mask(jax.random.fold_in(splits[12], 71), 0)
    routes = draw_routes(jax.random.fold_in(splits[12], 71), 0)
    slot_ids = draw_slot_ids(jax.random.fold_in(splits[12], 71), 0)
    ln1_gain = jnp.clip(1.0 + 0.1 * jax.random.normal(splits[5], (D,), jnp.float32), 0.5, 1.5).astype(jnp.bfloat16)
    qkv_weight = gaussian(splits[6], (D, 3 * D), D ** -0.5, 0.25, ((0, 32),))
    out_weight = gaussian(splits[7], (D, D), (D // 4) ** -0.5, 0.5, ((0, 32),))
    ln2_gain = jnp.clip(1.0 + 0.1 * jax.random.normal(splits[8], (D,), jnp.float32), 0.5, 1.5).astype(jnp.bfloat16)
    router_weight = gaussian(splits[9], (D, EXPERTS), (2 * D) ** -0.5, 0.1875, ((0, 32),))
    expert_in = gaussian(splits[10], (EXPERTS, D, H), D ** -0.5, 0.25, ((0, 8), (1, 4)))
    expert_out = gaussian(splits[11], (EXPERTS, H, D), (H // 2) ** -0.5, 0.1875, ((0, 8), (1, 4)))
    return {"tokens": tokens, "targets": targets, "valid_mask": valid_mask, "routes": routes, "slot_ids": slot_ids, "ln1_gain": ln1_gain, "qkv_weight": qkv_weight, "out_weight": out_weight, "ln2_gain": ln2_gain, "router_weight": router_weight, "expert_in": expert_in, "expert_out": expert_out}


HIGH = lax.Precision.HIGHEST
EPS = 1e-06

@jax.custom_vjp
def low(v):
    return lax.optimization_barrier(v.astype(jnp.bfloat16)).astype(jnp.float32)

@jax.custom_vjp
def low_back(v):
    return v

def low_keep(v):
    return (low(v), None)

def low_pass(kept, grad):
    return (grad,)

def back_keep(v):
    return (v, None)

def back_low(kept, grad):
    return (low(grad),)
low.defvjp(low_keep, low_pass)
low_back.defvjp(back_keep, back_low)

def layer_norm(values, scale_gain):
    row_mean = lax.optimization_barrier(jnp.mean(values, axis=-1, keepdims=True))
    centered = values - row_mean
    variance = lax.optimization_barrier(jnp.mean(centered * centered, axis=-1, keepdims=True))
    return centered * lax.rsqrt(variance + EPS) * scale_gain

def attend_block(qkv_rows):
    pieces = qkv_rows.reshape(IMG_DEV, IMG_LEN, 3, HEADS, HEAD_DIM)
    queries = pieces[:, :, 0]
    key_rows = pieces[:, :, 1]
    values = pieces[:, :, 2]
    scores = jnp.einsum('ilhd,imhd->ihlm', queries, key_rows, precision=HIGH) * HEAD_DIM ** (-0.5)
    scores = low_back(scores)
    weights_low = low(jax.nn.softmax(scores, axis=-1))
    mixed_rows = jnp.einsum('ihlm,imhd->ilhd', weights_low, values, precision=HIGH)
    return low(low_back(mixed_rows.reshape(IMG_DEV * IMG_LEN, D)))

def expert_block(operands):
    rows_in, weight_in, weight_out = operands
    pre_act = low_back(jnp.dot(rows_in, weight_in, precision=HIGH))
    hidden = low(jax.nn.gelu(pre_act, approximate=False))
    return low(low_back(jnp.dot(hidden, weight_out, precision=HIGH)))

def forward(inputs_f, gain_one, qkv_weight, out_weight, gain_two, router_weight, expert_in, expert_out, targets_f, valid_f, routes, slot_ids):
    device_count = TOKENS // TOK_DEV
    act_one = low(layer_norm(inputs_f, gain_one))
    qkv_low = low(low_back(jnp.dot(act_one, qkv_weight, precision=HIGH)))
    mixed_low = lax.map(jax.checkpoint(attend_block), qkv_low.reshape(device_count, TOK_DEV, 3 * D)).reshape(TOKENS, D)
    residual = inputs_f + low_back(jnp.dot(mixed_low, out_weight, precision=HIGH))
    act_two = low(layer_norm(residual, gain_two))
    gate_probs = jax.nn.softmax(jnp.dot(act_two, router_weight, precision=HIGH), axis=-1)
    picked = jnp.take_along_axis(gate_probs, routes, axis=1)
    kept = slot_ids < CAP
    keep_f = kept.astype(jnp.float32)
    owner_block = (jnp.arange(TOKENS, dtype=jnp.int32) // TOK_DEV)[:, None]
    buffer_size = device_count * EXPERTS * CAP
    target_slot = jnp.where(kept, (owner_block * EXPERTS + routes) * CAP + slot_ids, buffer_size).astype(jnp.int32)
    outgoing = jnp.zeros((buffer_size, D), jnp.float32)
    outgoing = outgoing.at[target_slot[:, 0]].add(act_two, mode='drop')
    outgoing = outgoing.at[target_slot[:, 1]].add(act_two, mode='drop')
    outgoing = low_back(outgoing)
    per_expert = outgoing.reshape(device_count, EXPERTS, CAP, D).transpose(1, 0, 2, 3).reshape(EXPERTS, device_count * CAP, D)
    produced = lax.map(jax.checkpoint(expert_block), (per_expert, expert_in, expert_out))
    returned = produced.reshape(EXPERTS, device_count, CAP, D).transpose(1, 0, 2, 3).reshape(buffer_size, D)
    safe_slot = jnp.minimum(target_slot, buffer_size - 1)
    from_first = returned[safe_slot[:, 0]] * keep_f[:, 0:1]
    from_second = returned[safe_slot[:, 1]] * keep_f[:, 1:2]
    output = residual + picked[:, 0:1] * from_first + picked[:, 1:2] * from_second
    residue = output - targets_f
    loss_sum = jnp.sum(valid_f * lax.optimization_barrier(jnp.mean(residue * residue, axis=-1)))
    valid_count = jnp.sum(valid_f)
    loss_value = loss_sum / valid_count
    return (loss_value * (TOKENS * D / 2), (output, loss_value))

def reference(tokens, targets, valid_mask, routes, slot_ids, ln1_gain, qkv_weight, out_weight, ln2_gain, router_weight, expert_in, expert_out):
    targets_f = targets.astype(jnp.float32)
    valid_f = valid_mask.astype(jnp.float32)

    def objective(inputs_f, gain_one, qkv_f, out_f, gain_two, router_f, expert_in_f, expert_out_f):
        return forward(inputs_f, gain_one, qkv_f, out_f, gain_two, router_f, expert_in_f, expert_out_f, targets_f, valid_f, routes, slot_ids)
    scaled, back_fn, extras = jax.vjp(objective, tokens.astype(jnp.float32), ln1_gain.astype(jnp.float32), qkv_weight.astype(jnp.float32), out_weight.astype(jnp.float32), ln2_gain.astype(jnp.float32), router_weight.astype(jnp.float32), expert_in.astype(jnp.float32), expert_out.astype(jnp.float32), has_aux=True)
    gradients = back_fn(jnp.ones_like(scaled))
    output, loss_value = extras
    return (output.astype(jnp.bfloat16), loss_value, gradients[0], gradients[1], gradients[2], gradients[3], gradients[4], gradients[5], gradients[6], gradients[7])
```

```python
import jax
import jax.numpy as jnp
from jax import lax
from jax.experimental import pallas as pl
from jax.experimental.pallas import tpu as pltpu
from jax.sharding import PartitionSpec as P

HEADS = 8
IMG_DEV = 5


HIGH = lax.Precision.HIGHEST
EPS = 1e-06


def layer_norm(values, scale_gain):
    row_mean = jnp.mean(values, axis=-1, keepdims=True)
    centered = values - row_mean
    variance = jnp.mean(centered * centered, axis=-1, keepdims=True)
    inverse = lax.rsqrt(variance + EPS)
    normed = centered * inverse
    return (normed * scale_gain, normed, inverse)


def layer_norm_back(grad_in, normed, inverse, scale_gain):
    scaled = grad_in * scale_gain
    gain_grad = jnp.sum(grad_in * normed, axis=0)
    inner_term = (
        scaled
        - jnp.mean(scaled, axis=-1, keepdims=True)
        - normed * jnp.mean(scaled * normed, axis=-1, keepdims=True)
    )
    return (inverse * inner_term, gain_grad)


def contract_rows(left_side, right_side):
    return lax.dot_general(
        left_side, right_side, (((0,), (0,)), ((), ())), preferred_element_type=jnp.float32
    )


def contract_cols(left_side, right_side):
    return lax.dot_general(
        left_side, right_side, (((1,), (1,)), ((), ())), preferred_element_type=jnp.float32
    )


def exact_gelu(values):
    return jax.nn.gelu(values, approximate=False)


def split_heads(qkv_low, images, head_count):
    row_count, triple_width = qkv_low.shape
    head_dim = triple_width // (3 * head_count)
    pieces = qkv_low.reshape(images, row_count // images, 3, head_count, head_dim)
    return (pieces[:, :, 0], pieces[:, :, 1], pieces[:, :, 2], head_dim ** (-0.5))


def attention_forward(qkv_low, images, head_count):
    queries, key_rows, values, score_scale = split_heads(qkv_low, images, head_count)
    scores = (
        jnp.einsum("ilhd,imhd->ihlm", queries, key_rows, preferred_element_type=jnp.float32)
        * score_scale
    )
    row_max = jnp.max(scores, axis=-1, keepdims=True)
    exp_scores = jnp.exp(scores - row_max)
    row_sum = jnp.sum(exp_scores, axis=-1, keepdims=True)
    weights_low = (exp_scores / row_sum).astype(jnp.bfloat16)
    log_total = row_max + jnp.log(row_sum)
    mixed_rows = jnp.einsum(
        "ihlm,imhd->ilhd", weights_low, values, preferred_element_type=jnp.float32
    )
    return (mixed_rows.reshape(qkv_low.shape[0], -1).astype(jnp.bfloat16), log_total)


def attention_back(qkv_low, log_total, grad_mixed, images, head_count):
    queries, key_rows, values, score_scale = split_heads(qkv_low, images, head_count)
    scores = (
        jnp.einsum("ilhd,imhd->ihlm", queries, key_rows, preferred_element_type=jnp.float32)
        * score_scale
    )
    weights_full = jnp.exp(scores - log_total)
    weights_low = weights_full.astype(jnp.bfloat16)
    grad_heads = grad_mixed.reshape(queries.shape)
    grad_weights = jnp.einsum(
        "ilhd,imhd->ihlm", grad_heads, values, preferred_element_type=jnp.float32
    )
    grad_values = jnp.einsum(
        "ihlm,ilhd->imhd", weights_low, grad_heads, preferred_element_type=jnp.float32
    )
    grad_scores = weights_full * (
        grad_weights - jnp.sum(weights_full * grad_weights, axis=-1, keepdims=True)
    )
    grad_low = grad_scores.astype(jnp.bfloat16)
    grad_queries = (
        jnp.einsum("ihlm,imhd->ilhd", grad_low, key_rows, preferred_element_type=jnp.float32)
        * score_scale
    )
    grad_keys = (
        jnp.einsum("ihlm,ilhd->imhd", grad_low, queries, preferred_element_type=jnp.float32)
        * score_scale
    )
    stacked = jnp.stack([grad_queries, grad_keys, grad_values], axis=2)
    return stacked.reshape(qkv_low.shape).astype(jnp.bfloat16)


def expert_forward(rows_in, weight_in, weight_out, block_size):
    result = jnp.zeros((rows_in.shape[0], weight_out.shape[1]), jnp.float32)
    for offset in range(0, weight_in.shape[1], block_size):
        pre_act = jnp.dot(
            rows_in, weight_in[:, offset : offset + block_size], preferred_element_type=jnp.float32
        )
        hidden = exact_gelu(pre_act).astype(jnp.bfloat16)
        result = result + jnp.dot(
            hidden, weight_out[offset : offset + block_size], preferred_element_type=jnp.float32
        )
    return result


def expert_back(rows_in, weight_in, weight_out, grad_rows_out, block_size):
    grad_rows = jnp.zeros(rows_in.shape, jnp.float32)
    grads_first = []
    grads_second = []
    for offset in range(0, weight_in.shape[1], block_size):
        slice_in = weight_in[:, offset : offset + block_size]
        slice_out = weight_out[offset : offset + block_size]
        pre_act = jnp.dot(rows_in, slice_in, preferred_element_type=jnp.float32)
        hidden, gelu_back = jax.vjp(exact_gelu, pre_act)
        grads_second.append(contract_rows(hidden.astype(jnp.bfloat16), grad_rows_out))
        grad_hidden = contract_cols(grad_rows_out, slice_out)
        grad_pre = gelu_back(grad_hidden)[0].astype(jnp.bfloat16)
        grads_first.append(contract_rows(rows_in, grad_pre))
        grad_rows = grad_rows + contract_cols(grad_pre, slice_in)
    return (grad_rows, jnp.concatenate(grads_first, axis=1), jnp.concatenate(grads_second, axis=0))


def shards(
    tokens,
    targets,
    valid_mask,
    routes,
    slot_ids,
    ln1_gain,
    qkv_weight,
    out_weight,
    ln2_gain,
    router_weight,
    expert_in,
    expert_out,
):
    tok_rows, model_width = tokens.shape
    experts = lax.axis_size("expert")
    total_tokens = tok_rows * lax.axis_size("dp") * experts
    capacity = (5 * tok_rows // 2 // experts + 7) // 8 * 8
    dense_full = (
        lax.all_gather(ln1_gain, ("dp", "expert"), axis=0, tiled=True),
        lax.all_gather(qkv_weight, ("dp", "expert"), axis=0, tiled=True),
        lax.all_gather(out_weight, ("dp", "expert"), axis=0, tiled=True),
        lax.all_gather(ln2_gain, ("dp", "expert"), axis=0, tiled=True),
        lax.all_gather(router_weight, ("dp", "expert"), axis=0, tiled=True),
    )
    gain_one, qkv_full, out_full, gain_two, router_full = dense_full
    expert_full = (
        lax.all_gather(expert_in, "dp", axis=1, tiled=True),
        lax.all_gather(expert_out, "dp", axis=1, tiled=True),
    )
    weight_in = expert_full[0][0]
    weight_out = expert_full[1][0]
    valid_f = valid_mask.astype(jnp.float32)
    valid_count = lax.psum(jnp.sum(valid_f), ("dp", "expert"))
    inputs_f = tokens.astype(jnp.float32)
    gain_one_f = gain_one.astype(jnp.float32)
    gain_two_f = gain_two.astype(jnp.float32)
    norm_one, normed_one, inverse_one = layer_norm(inputs_f, gain_one_f)
    act_one = norm_one.astype(jnp.bfloat16)
    qkv_low = jnp.dot(act_one, qkv_full, preferred_element_type=jnp.float32).astype(jnp.bfloat16)
    mixed_low, log_total = attention_forward(qkv_low, IMG_DEV, HEADS)
    residual = inputs_f + jnp.dot(mixed_low, out_full, preferred_element_type=jnp.float32)
    norm_two, normed_two, inverse_two = layer_norm(residual, gain_two_f)
    act_two = norm_two.astype(jnp.bfloat16)
    gate_probs = jax.nn.softmax(
        jnp.dot(act_two, router_full, preferred_element_type=jnp.float32), axis=-1
    )
    expert_ids = lax.broadcasted_iota(jnp.int32, (1, experts), 1)
    first_pick = (routes[:, 0:1] == expert_ids).astype(jnp.float32)
    second_pick = (routes[:, 1:2] == expert_ids).astype(jnp.float32)
    gate_first = jnp.sum(gate_probs * first_pick, axis=-1, keepdims=True)
    gate_second = jnp.sum(gate_probs * second_pick, axis=-1, keepdims=True)
    target_slot = jnp.where(slot_ids < capacity, routes * capacity + slot_ids, -1)
    slot_columns = lax.broadcasted_iota(jnp.int32, (1, experts * capacity), 1)
    first_hot = (target_slot[:, 0:1] == slot_columns).astype(jnp.bfloat16)
    second_hot = (target_slot[:, 1:2] == slot_columns).astype(jnp.bfloat16)
    both_hot = first_hot + second_hot
    outgoing = contract_rows(both_hot, act_two).astype(jnp.bfloat16)
    arrived = lax.all_to_all(
        outgoing.reshape(experts, capacity, model_width),
        "expert",
        split_axis=0,
        concat_axis=0,
        tiled=True,
    ).reshape(-1, model_width)
    hidden_block = min(512, weight_in.shape[1])
    produced = expert_forward(arrived, weight_in, weight_out, hidden_block).astype(jnp.bfloat16)
    returned = lax.all_to_all(
        produced.reshape(experts, capacity, model_width),
        "expert",
        split_axis=0,
        concat_axis=0,
        tiled=True,
    ).reshape(-1, model_width)
    from_first = jnp.dot(first_hot, returned, preferred_element_type=jnp.float32)
    from_second = jnp.dot(second_hot, returned, preferred_element_type=jnp.float32)
    output = residual + gate_first * from_first + gate_second * from_second
    residue = output - targets.astype(jnp.float32)
    local_loss = jnp.sum(valid_f * jnp.mean(residue * residue, axis=-1))
    loss_sum = lax.psum(local_loss, ("dp", "expert"))
    loss_value = loss_sum / valid_count
    grad_out = total_tokens / valid_count * valid_f[:, None] * residue
    dense_back = (
        lax.all_gather(ln1_gain, ("dp", "expert"), axis=0, tiled=True),
        lax.all_gather(qkv_weight, ("dp", "expert"), axis=0, tiled=True),
        lax.all_gather(out_weight, ("dp", "expert"), axis=0, tiled=True),
        lax.all_gather(ln2_gain, ("dp", "expert"), axis=0, tiled=True),
        lax.all_gather(router_weight, ("dp", "expert"), axis=0, tiled=True),
    )
    expert_back_full = (
        lax.all_gather(expert_in, "dp", axis=1, tiled=True),
        lax.all_gather(expert_out, "dp", axis=1, tiled=True),
    )
    qkv_back = dense_back[1]
    out_back = dense_back[2]
    router_back = dense_back[4]
    weight_in_back = expert_back_full[0][0]
    weight_out_back = expert_back_full[1][0]
    slot_grads = (
        contract_rows(first_hot, (gate_first * grad_out).astype(jnp.bfloat16))
        + contract_rows(second_hot, (gate_second * grad_out).astype(jnp.bfloat16))
    ).astype(jnp.bfloat16)
    expert_grad_rows = lax.all_to_all(
        slot_grads.reshape(experts, capacity, model_width),
        "expert",
        split_axis=0,
        concat_axis=0,
        tiled=True,
    ).reshape(-1, model_width)
    grad_rows, grad_first_weight, grad_second_weight = expert_back(
        arrived, weight_in_back, weight_out_back, expert_grad_rows, hidden_block
    )
    grad_back = lax.all_to_all(
        grad_rows.astype(jnp.bfloat16).reshape(experts, capacity, model_width),
        "expert",
        split_axis=0,
        concat_axis=0,
        tiled=True,
    ).reshape(-1, model_width)
    grad_act_two = jnp.dot(both_hot, grad_back, preferred_element_type=jnp.float32)
    gate_grad = first_pick * jnp.sum(
        grad_out * from_first, axis=-1, keepdims=True
    ) + second_pick * jnp.sum(grad_out * from_second, axis=-1, keepdims=True)
    logit_grad = gate_probs * (gate_grad - jnp.sum(gate_probs * gate_grad, axis=-1, keepdims=True))
    router_f = router_back.astype(jnp.float32)
    grad_act_two = grad_act_two + lax.dot_general(
        logit_grad,
        router_f,
        (((1,), (1,)), ((), ())),
        precision=HIGH,
        preferred_element_type=jnp.float32,
    )
    router_grad = lax.dot_general(
        act_two.astype(jnp.float32),
        logit_grad,
        (((0,), (0,)), ((), ())),
        precision=HIGH,
        preferred_element_type=jnp.float32,
    )
    grad_norm_two, gain_two_grad = layer_norm_back(
        grad_act_two, normed_two, inverse_two, gain_two_f
    )
    grad_resid = grad_out + grad_norm_two
    branch_grad = grad_resid.astype(jnp.bfloat16)
    out_weight_grad = contract_rows(mixed_low, branch_grad)
    grad_mixed = contract_cols(branch_grad, out_back).astype(jnp.bfloat16)
    qkv_grad_low = attention_back(qkv_low, log_total, grad_mixed, IMG_DEV, HEADS)
    qkv_weight_grad = contract_rows(act_one, qkv_grad_low)
    grad_act_one = contract_cols(qkv_grad_low, qkv_back)
    grad_norm_one, gain_one_grad = layer_norm_back(
        grad_act_one, normed_one, inverse_one, gain_one_f
    )
    tokens_grad = grad_resid + grad_norm_one
    dense_grads = (
        lax.psum_scatter(gain_one_grad, ("dp", "expert"), scatter_dimension=0, tiled=True),
        lax.psum_scatter(qkv_weight_grad, ("dp", "expert"), scatter_dimension=0, tiled=True),
        lax.psum_scatter(out_weight_grad, ("dp", "expert"), scatter_dimension=0, tiled=True),
        lax.psum_scatter(gain_two_grad, ("dp", "expert"), scatter_dimension=0, tiled=True),
        lax.psum_scatter(router_grad, ("dp", "expert"), scatter_dimension=0, tiled=True),
    )
    expert_grads = (
        lax.psum_scatter(
            grad_first_weight[None].astype(jnp.bfloat16), "dp", scatter_dimension=1, tiled=True
        ).astype(jnp.float32),
        lax.psum_scatter(
            grad_second_weight[None].astype(jnp.bfloat16), "dp", scatter_dimension=1, tiled=True
        ).astype(jnp.float32),
    )
    first_result = expert_grads[0]
    second_result = expert_grads[1]
    return (
        output.astype(jnp.bfloat16),
        loss_value,
        tokens_grad,
        dense_grads[0],
        dense_grads[1],
        dense_grads[2],
        dense_grads[3],
        dense_grads[4],
        first_result,
        second_result,
    )


F32 = jnp.float32
BF16 = jnp.bfloat16
MB = 2**20


def round_up(value, unit):
    return (value + unit - 1) // unit * unit


def dot(left_side, right_side):
    return jnp.dot(left_side, right_side, preferred_element_type=F32)


def lane_ids(shape):
    return lax.broadcasted_iota(jnp.int32, shape, len(shape) - 1)


def row_ids(shape):
    return lax.broadcasted_iota(jnp.int32, shape, len(shape) - 2)


def normalize(values):
    centered = values - jnp.mean(values, axis=-1, keepdims=True)
    inverse = lax.rsqrt(jnp.mean(centered * centered, axis=-1, keepdims=True) + EPS)
    return centered * inverse, inverse


def gelu_pair(values):
    size = jnp.abs(values)
    inv = 1.0 / (1.0 + 0.2316419 * size)
    density = 0.3989422804014327 * jnp.exp(-0.5 * values * values)
    series = inv * (
        0.319381530
        + inv * (-0.356563782 + inv * (1.781477937 + inv * (-1.821255978 + inv * 1.330274429)))
    )
    tail = density * series
    cumulative = jnp.where(values >= 0, 1.0 - tail, tail)
    return values * cumulative, cumulative + values * density


def forward_kernel(
    real_rows,
    experts,
    tok_ref,
    wqkv_ref,
    wout_ref,
    gain_ref,
    router_ref,
    router_t_ref,
    cols_ref,
    rows_ref,
    qkv_ref,
    probs_ref,
    mixed_ref,
    resid_ref,
    act_ref,
    gates_ref,
    grow_ref,
):
    inputs = tok_ref[...].astype(F32)
    normed, _ = normalize(inputs)
    act_one = (normed * gain_ref[0:1, :]).astype(BF16)
    qkv = dot(act_one, wqkv_ref[...]).astype(BF16)
    qkv_ref[...] = qkv
    width = inputs.shape[1]
    rows = inputs.shape[0]
    low_half = lane_ids((1, 128)) < 64
    key_bias = jnp.where(lane_ids((1, rows)) < real_rows, 0.0, -1e30)
    parts = []
    for pair in range(width // 128):
        lanes = slice(128 * pair, 128 * (pair + 1))
        queries = qkv[:, lanes]
        key_rows = qkv[:, width + 128 * pair : width + 128 * (pair + 1)]
        values = qkv[:, 2 * width + 128 * pair : 2 * width + 128 * (pair + 1)]
        outs = []
        for side in range(2):
            mask = low_half if side == 0 else jnp.logical_not(low_half)
            masked = jnp.where(mask, queries, jnp.zeros_like(queries))
            scores = contract_cols(masked, key_rows) * 0.125 + key_bias
            exped = jnp.exp(scores - jnp.max(scores, axis=-1, keepdims=True))
            probs = (exped * (1.0 / jnp.sum(exped, axis=-1, keepdims=True))).astype(BF16)
            probs_ref[2 * pair + side] = probs
            outs.append(dot(probs, values))
        parts.append(jnp.where(low_half, outs[0], outs[1]).astype(BF16))
    mixed = jnp.concatenate(parts, axis=1)
    mixed_ref[...] = mixed
    resid = inputs + dot(mixed, wout_ref[...])
    resid_ref[...] = resid
    normed_two, _ = normalize(resid)
    act_two = (normed_two * gain_ref[1:2, :]).astype(BF16)
    act_ref[...] = act_two
    lanes = lane_ids((1, 128))
    logits = jnp.where(lanes < experts, dot(act_two, router_ref[...]), -1e30)
    exped = jnp.exp(logits - jnp.max(logits, axis=-1, keepdims=True))
    gates = exped / jnp.sum(exped, axis=-1, keepdims=True)
    cols = cols_ref[...]
    first = jnp.sum(jnp.where(lanes == cols[:, 2:3], gates, 0.0), axis=-1, keepdims=True)
    second = jnp.sum(jnp.where(lanes == cols[:, 3:4], gates, 0.0), axis=-1, keepdims=True)
    gates_ref[...] = jnp.where(lanes == experts, first, jnp.where(lanes == experts + 1, second, gates))
    logits_t = contract_cols(router_t_ref[...], act_two)[:experts]
    exped_t = jnp.exp(logits_t - jnp.max(logits_t, axis=0, keepdims=True))
    gates_t = exped_t / jnp.sum(exped_t, axis=0, keepdims=True)
    ids_t = row_ids(gates_t.shape)
    first_t = jnp.sum(jnp.where(ids_t == rows_ref[2:3, :], gates_t, 0.0), axis=0, keepdims=True)
    second_t = jnp.sum(jnp.where(ids_t == rows_ref[3:4, :], gates_t, 0.0), axis=0, keepdims=True)
    grow_ref[...] = jnp.where(row_ids((8, rows)) == 0, first_t, second_t)


def hot_rows(codes, start, count):
    slots = row_ids((count, codes.shape[1])) + start
    return (slots == codes[0:1, :]) | (slots == codes[1:2, :])


def expert_forward_kernel(
    cap, group, act_ref, codes_ref, win_ref, wout_ref, rows_out_ref, hidden_ref, slope_ref, out_ref
):
    which, half = pl.program_id(0), pl.program_id(1)
    blocks, images = act_ref.shape[0], act_ref.shape[1]
    hidden_width = win_ref.shape[1]
    pieces = []
    for block in range(blocks):
        start = (which * group + half * blocks + block) * cap
        total = None
        for image in range(images):
            hot = jnp.where(hot_rows(codes_ref[block, image], start, cap), 1.0, 0.0).astype(BF16)
            term = dot(hot, act_ref[block, image])
            total = term if total is None else total + term
        pieces.append(total.astype(BF16))
    rows_in = jnp.concatenate(pieces, axis=0)
    rows_out_ref[...] = rows_in.reshape(rows_out_ref.shape)
    step = 512
    result = None
    for offset in range(0, hidden_width, step):
        act, slope = gelu_pair(dot(rows_in, win_ref[:, offset : offset + step]))
        act = act.astype(BF16)
        hidden_ref[:, :, offset : offset + step] = act.reshape(blocks, cap, step)
        slope_ref[:, :, offset : offset + step] = slope.astype(BF16).reshape(blocks, cap, step)
        term = dot(act, wout_ref[offset : offset + step, :])
        result = term if result is None else result + term
    out_ref[...] = result.astype(BF16).reshape(out_ref.shape)


def hot_cols(codes, count):
    return lane_ids((codes.shape[0], count)) == codes


def combine_kernel(
    experts, scale_ref, resid_ref, back_ref, cols_ref, gates_ref, target_ref, valid_ref,
    out_ref, dout_ref, dlow_ref, dlogit_ref, loss_ref,
):
    count = back_ref.shape[0]
    cols = cols_ref[...]
    rows = cols.shape[0]
    hot = jnp.concatenate(
        [
            jnp.where(hot_cols(cols[:, 0:1], count), 1.0, 0.0).astype(BF16),
            jnp.where(hot_cols(cols[:, 1:2], count), 1.0, 0.0).astype(BF16),
        ],
        axis=0,
    )
    both = dot(hot, back_ref[...])
    from_first, from_second = both[:rows], both[rows:]
    gates = gates_ref[...]
    first, second = gates[:, experts : experts + 1], gates[:, experts + 1 : experts + 2]
    output = resid_ref[...] + first * from_first + second * from_second
    out_ref[...] = output.astype(BF16)
    residue = output - target_ref[...].astype(F32)
    valid = valid_ref[...]
    square = jnp.mean(residue * residue, axis=-1, keepdims=True) * valid[:, 0:1]

    @pl.when(pl.program_id(0) == 0)
    def _():
        loss_ref[...] = jnp.zeros_like(loss_ref)

    loss_ref[...] += jnp.sum(square)
    dout = (scale_ref[0, 0] * valid[:, 0:1]) * residue
    dout_ref[...] = dout
    dlow_ref[...] = dout.astype(BF16)
    lanes = lane_ids((1, 128))
    grad = jnp.where(
        lanes == cols[:, 2:3], jnp.sum(dout * from_first, axis=-1, keepdims=True), 0.0
    ) + jnp.where(lanes == cols[:, 3:4], jnp.sum(dout * from_second, axis=-1, keepdims=True), 0.0)
    real = jnp.where(lanes < experts, gates, 0.0)
    dlogit_ref[...] = real * (grad - jnp.sum(real * grad, axis=-1, keepdims=True))


def expert_back_kernel(
    cap, group, dlow_ref, codes_ref, grow_ref, rows_ref, hidden_ref, slope_ref, win_ref, wout_ref,
    back_ref, gin_ref, gout_ref, acc_in, acc_out,
):
    which, half = pl.program_id(0), pl.program_id(1)
    blocks, images = dlow_ref.shape[0], dlow_ref.shape[1]
    hidden_width = win_ref.shape[1]
    pieces = []
    for block in range(blocks):
        start = (which * group + half * blocks + block) * cap
        total = None
        slot_gate = None
        for image in range(images):
            codes = codes_ref[block, image]
            slots = row_ids((cap, codes.shape[1])) + start
            is_first = slots == codes[0:1, :]
            is_second = slots == codes[1:2, :]
            hot = jnp.where(is_first | is_second, 1.0, 0.0).astype(BF16)
            term = dot(hot, dlow_ref[block, image])
            gain = grow_ref[block, image]
            picked = jnp.where(is_first, gain[0:1, :], jnp.where(is_second, gain[1:2, :], 0.0))
            picked = jnp.sum(picked, axis=-1, keepdims=True)
            total = term if total is None else total + term
            slot_gate = picked if slot_gate is None else slot_gate + picked
        pieces.append((total * slot_gate).astype(BF16))
    grads = jnp.concatenate(pieces, axis=0)
    grads_t = grads.T
    rows_in_t = rows_ref[...].reshape(blocks * cap, -1).T
    step = 512
    result = None
    for offset in range(0, hidden_width, step):
        cut = slice(offset, offset + step)
        hidden = hidden_ref[:, :, cut].reshape(blocks * cap, step)
        slope = slope_ref[:, :, cut].reshape(blocks * cap, step).astype(F32)
        dpre = (contract_cols(grads, wout_ref[cut, :]) * slope).astype(BF16)
        gin = dot(rows_in_t, dpre)
        gout = dot(grads_t, hidden)
        term = contract_cols(dpre, win_ref[:, cut])
        result = term if result is None else result + term

        @pl.when(half == 0)
        def _():
            acc_in[:, cut] = gin
            acc_out[:, cut] = gout

        @pl.when(half == 1)
        def _():
            gin_ref[:, cut] = (acc_in[:, cut] + gin).astype(BF16)
            gout_ref[:, cut] = (acc_out[:, cut] + gout).astype(BF16)

    back_ref[...] = result.astype(BF16).reshape(back_ref.shape)


def back_kernel(
    tok_ref, wqkv_ref, wout_ref, gain_ref, router_t_ref, cols_ref, back_ref, dlogit_ref, resid_ref,
    dout_ref, qkv_ref, probs_ref, mixed_ref,
    tgrad_ref, gqkv_ref, gout_ref, gmisc_ref,
):
    count = back_ref.shape[0]
    cols = cols_ref[...]
    hot = jnp.where(hot_cols(cols[:, 0:1], count) | hot_cols(cols[:, 1:2], count), 1.0, 0.0)
    dlogits = dlogit_ref[...]
    dact = dot(hot.astype(BF16), back_ref[...])
    dlogits_high = dlogits.astype(BF16)
    dlogits_low = (dlogits - dlogits_high.astype(F32)).astype(BF16)
    dact = dact + dot(dlogits_high, router_t_ref[...]) + dot(dlogits_low, router_t_ref[...])

    resid = resid_ref[...]
    normed_two, inverse_two = normalize(resid)
    gain_two = gain_ref[1:2, :]
    act_two = (normed_two * gain_two).astype(BF16)
    grouter = contract_rows(dlogits_high, act_two) + contract_rows(dlogits_low, act_two)

    def norm_back(grad, normed, inverse, gain):
        scaled = grad * gain
        gain_grad = jnp.sum(grad * normed, axis=0, keepdims=True)
        inner = (
            scaled
            - jnp.mean(scaled, axis=-1, keepdims=True)
            - normed * jnp.mean(scaled * normed, axis=-1, keepdims=True)
        )
        return inverse * inner, gain_grad

    grad_two, ggain_two = norm_back(dact, normed_two, inverse_two, gain_two)
    dresid = dout_ref[...] + grad_two
    branch = dresid.astype(BF16)
    mixed = mixed_ref[...]
    gout = contract_rows(mixed, branch)
    dmixed = contract_cols(branch, wout_ref[...]).astype(BF16)
    qkv = qkv_ref[...]
    width = dmixed.shape[1]
    low_half = lane_ids((1, 128)) < 64
    dqs, dks, dvs = [], [], []
    for pair in range(width // 128):
        cut = slice(128 * pair, 128 * (pair + 1))
        queries = qkv[:, cut]
        key_rows = qkv[:, width + 128 * pair : width + 128 * (pair + 1)]
        values = qkv[:, 2 * width + 128 * pair : 2 * width + 128 * (pair + 1)]
        dmix = dmixed[:, cut]
        dq = []
        dk = dv = None
        for side in range(2):
            mask = low_half if side == 0 else jnp.logical_not(low_half)
            dmask = jnp.where(mask, dmix, jnp.zeros_like(dmix))
            qmask = jnp.where(mask, queries, jnp.zeros_like(queries))
            probs_low = probs_ref[2 * pair + side]
            probs = probs_low.astype(F32)
            dprobs = contract_cols(dmask, values)
            dscore = probs * (dprobs - jnp.sum(probs * dprobs, axis=-1, keepdims=True))
            dscore = dscore.astype(BF16)
            dq.append(dot(dscore, key_rows))
            dk_term = contract_rows(dscore, qmask)
            dv_term = contract_rows(probs_low, dmask)
            dk = dk_term if dk is None else dk + dk_term
            dv = dv_term if dv is None else dv + dv_term
        dqs.append((jnp.where(low_half, dq[0], dq[1]) * 0.125).astype(BF16))
        dks.append((dk * 0.125).astype(BF16))
        dvs.append(dv.astype(BF16))
    dqkv = jnp.concatenate(dqs + dks + dvs, axis=1)
    inputs = tok_ref[...].astype(F32)
    normed_one, inverse_one = normalize(inputs)
    gain_one = gain_ref[0:1, :]
    act_one = (normed_one * gain_one).astype(BF16)
    gqkv = contract_rows(act_one, dqkv)
    dact_one = contract_cols(dqkv, wqkv_ref[...])
    grad_one, ggain_one = norm_back(dact_one, normed_one, inverse_one, gain_one)
    tgrad_ref[...] = dresid + grad_one
    gmisc = jnp.concatenate(
        [
            grouter[:8],
            jnp.where(row_ids((8, width)) == 0, ggain_one, jnp.where(row_ids((8, width)) == 1, ggain_two, 0.0)),
        ],
        axis=0,
    )

    @pl.when(pl.program_id(0) == 0)
    def _():
        gqkv_ref[...] = gqkv
        gout_ref[...] = gout
        gmisc_ref[...] = gmisc

    @pl.when(pl.program_id(0) > 0)
    def _():
        gqkv_ref[...] += gqkv
        gout_ref[...] += gout
        gmisc_ref[...] += gmisc


def shape(dims, kind):
    return jax.ShapeDtypeStruct(dims, kind)


def whole(dims):
    return pl.BlockSpec(dims, lambda *_: (0,) * len(dims))


def per_image(*dims):
    return pl.BlockSpec((None,) + dims, lambda i: (i,) + (0,) * len(dims))


def params():
    return pltpu.CompilerParams(vmem_limit_bytes=56 * MB)


def fast_shards(
    tokens, targets, valid_mask, routes, slot_ids, ln1_gain, qkv_weight, out_weight, ln2_gain,
    router_weight, expert_in, expert_out,
):
    axes = ("dp", "expert")
    tok_rows, width = tokens.shape
    experts = lax.axis_size("expert")
    group = experts // 2
    dp = lax.axis_size("dp")
    total_tokens = tok_rows * dp * experts
    hidden_width = expert_in.shape[2]
    capacity = (5 * tok_rows // 2 // experts + 7) // 8 * 8
    cap = round_up(capacity, 16)
    images = IMG_DEV
    real_rows = tok_rows // images
    rows = round_up(real_rows, 16)
    me = lax.axis_index("expert")

    def pad_rows(array, value=0):
        array = array.reshape(images, real_rows, -1)
        return jnp.pad(array, ((0, 0), (0, rows - real_rows), (0, 0)), constant_values=value)

    valid_f = valid_mask.astype(F32)
    my_count = jnp.sum(valid_f)
    count_high = jnp.floor(my_count / 128.0)
    count_low = my_count - 128.0 * count_high
    shard = qkv_weight.shape[0]
    extra = jnp.concatenate(
        [
            router_weight,
            ln1_gain[:, None],
            ln2_gain[:, None],
            jnp.broadcast_to(count_high.astype(BF16), (shard, 1)),
            jnp.broadcast_to(count_low.astype(BF16), (shard, 1)),
            jnp.zeros((shard, 128 - experts - 4), BF16),
        ],
        axis=1,
    )
    dense = lax.all_gather(
        jnp.concatenate([qkv_weight, out_weight, extra], axis=1), axes, axis=0, tiled=True
    )
    qkv_full = dense[:, : 3 * width]
    out_full = dense[:, 3 * width : 4 * width]
    extra_full = dense[:, 4 * width :]
    router_full = jnp.where(lane_ids((1, 128)) < experts, extra_full, 0)
    extra_t = extra_full.T
    router_t = jnp.where(row_ids((128, 1)) < experts, extra_t, 0)
    gains = extra_t[experts : experts + 2].astype(F32)
    counts = extra_full[::shard].astype(F32)
    valid_count = jnp.sum(counts[:, experts + 2] * 128.0 + counts[:, experts + 3])
    scale = (total_tokens / valid_count).reshape(1, 1)

    far = [(i, i ^ group) for i in range(experts)]
    w_in = [expert_in[0]]
    w_out = [expert_out[0]]
    w_in.append(lax.ppermute(w_in[0], "expert", far))
    w_out.append(lax.ppermute(w_out[0], "expert", far))
    win_full = jnp.stack([lax.all_gather(w, "dp", axis=0, tiled=True) for w in w_in])
    wout_full = jnp.stack([lax.all_gather(w, "dp", axis=0, tiled=True) for w in w_out])

    def exchange(blocks):
        out = [blocks[0]]
        for k in range(1, group):
            out.append(lax.ppermute(blocks[k], "expert", [(i, i ^ k) for i in range(experts)]))
        return out

    code = jnp.where(slot_ids < capacity, (routes ^ me) * cap + slot_ids, -1)
    cols = pad_rows(jnp.concatenate([code, routes], axis=1), -1)
    row_codes = jnp.pad(cols.transpose(0, 2, 1), ((0, 0), (0, 4), (0, 0)))
    cols = jnp.pad(cols, ((0, 0), (0, 0), (0, 4)))
    tok_p = pad_rows(tokens)
    target_p = pad_rows(targets)
    valid_p = pad_rows(jnp.broadcast_to(valid_f[:, None], (tok_rows, 8)))

    gate_lanes = 128
    qkv_p, probs, mixed, resid, act_two, gates, grow = pl.pallas_call(
        lambda *refs: forward_kernel(real_rows, experts, *refs),
        grid=(images,),
        in_specs=[
            per_image(rows, width), whole((width, 3 * width)), whole((width, width)), whole((2, width)),
            whole((width, 128)), whole((128, width)), per_image(rows, 8), per_image(8, rows),
        ],
        out_specs=[
            per_image(rows, 3 * width), per_image(HEADS, rows, rows), per_image(rows, width),
            per_image(rows, width), per_image(rows, width), per_image(rows, gate_lanes), per_image(8, rows),
        ],
        out_shape=[
            shape((images, rows, 3 * width), BF16), shape((images, HEADS, rows, rows), BF16),
            shape((images, rows, width), BF16), shape((images, rows, width), F32),
            shape((images, rows, width), BF16), shape((images, rows, gate_lanes), F32),
            shape((images, 8, rows), F32),
        ],
        compiler_params=params(),
        cost_estimate=pl.CostEstimate(flops=int(5e9), bytes_accessed=int(2e7), transcendentals=0),
        name="attention_forward",
    )(tok_p, qkv_full, out_full, gains, router_full, router_t, cols, row_codes)

    act_all = jnp.stack(exchange([act_two] * group))
    code_all = jnp.stack(exchange([row_codes] * group))

    half_blocks = group // 2
    def by_half(*dims):
        return pl.BlockSpec((half_blocks,) + dims, lambda q, h: (h,) + (0,) * len(dims))
    def by_expert(*dims):
        return pl.BlockSpec((None,) + dims, lambda q, h: (q,) + (0,) * len(dims))
    def by_both(*dims):
        return pl.BlockSpec((None, half_blocks) + dims, lambda q, h: (q, h) + (0,) * len(dims))

    rows_in, hidden, slope, produced = pl.pallas_call(
        lambda *refs: expert_forward_kernel(cap, group, *refs),
        grid=(2, 2),
        in_specs=[
            by_half(images, rows, width), by_half(images, 8, rows), by_expert(width, hidden_width),
            by_expert(hidden_width, width),
        ],
        out_specs=[by_both(cap, width), by_both(cap, hidden_width), by_both(cap, hidden_width), by_both(cap, width)],
        out_shape=[
            shape((2, group, cap, width), BF16), shape((2, group, cap, hidden_width), BF16),
            shape((2, group, cap, hidden_width), BF16), shape((2, group, cap, width), BF16),
        ],
        compiler_params=params(),
        cost_estimate=pl.CostEstimate(flops=int(14e9), bytes_accessed=int(4e7), transcendentals=0),
        name="expert_forward",
    )(act_all, code_all, win_full, wout_full)

    def give_back(array):
        came = exchange([array[:, k] for k in range(group)])
        return jnp.stack(came, axis=1).reshape(2 * group * cap, width)

    returned = give_back(produced)
    block_out, dout, dlow, dlogits, loss_part = pl.pallas_call(
        lambda *refs: combine_kernel(experts, *refs),
        grid=(images,),
        in_specs=[
            pl.BlockSpec(memory_space=pltpu.SMEM), per_image(rows, width), whole((2 * group * cap, width)),
            per_image(rows, 8), per_image(rows, gate_lanes), per_image(rows, width), per_image(rows, 8),
        ],
        out_specs=[
            per_image(rows, width), per_image(rows, width), per_image(rows, width), per_image(rows, gate_lanes),
            whole((8, 128)),
        ],
        out_shape=[
            shape((images, rows, width), BF16), shape((images, rows, width), F32),
            shape((images, rows, width), BF16), shape((images, rows, gate_lanes), F32), shape((8, 128), F32),
        ],
        compiler_params=params(),
        cost_estimate=pl.CostEstimate(flops=int(5e9), bytes_accessed=int(1e7), transcendentals=0),
        name="combine_and_loss",
    )(scale, resid, returned, cols, gates, target_p, valid_p)

    dlow_all = jnp.stack(exchange([dlow] * group))
    grow_all = jnp.stack(exchange([grow] * group))
    drows, gin, gout_t = pl.pallas_call(
        lambda *refs: expert_back_kernel(cap, group, *refs),
        grid=(2, 2),
        in_specs=[
            by_half(images, rows, width), by_half(images, 8, rows), by_half(images, 8, rows),
            by_both(cap, width), by_both(cap, hidden_width), by_both(cap, hidden_width),
            by_expert(width, hidden_width), by_expert(hidden_width, width),
        ],
        out_specs=[by_both(cap, width), by_expert(width, hidden_width), by_expert(width, hidden_width)],
        out_shape=[
            shape((2, group, cap, width), BF16), shape((2, width, hidden_width), BF16),
            shape((2, width, hidden_width), BF16),
        ],
        scratch_shapes=[pltpu.VMEM((width, hidden_width), F32), pltpu.VMEM((width, hidden_width), F32)],
        compiler_params=params(),
        cost_estimate=pl.CostEstimate(flops=int(24e9), bytes_accessed=int(4e7), transcendentals=0),
        name="expert_backward",
    )(dlow_all, code_all, grow_all, rows_in, hidden, slope, win_full, wout_full)
    grad_back = give_back(drows)

    tgrad, gqkv, gout_w, gmisc = pl.pallas_call(
        back_kernel,
        grid=(images,),
        in_specs=[
            per_image(rows, width), whole((width, 3 * width)), whole((width, width)), whole((2, width)),
            whole((128, width)), per_image(rows, 8), whole((2 * group * cap, width)),
            per_image(rows, gate_lanes), per_image(rows, width), per_image(rows, width),
            per_image(rows, 3 * width), per_image(HEADS, rows, rows), per_image(rows, width),
        ],
        out_specs=[per_image(rows, width), whole((width, 3 * width)), whole((width, width)), whole((16, width))],
        out_shape=[
            shape((images, rows, width), F32), shape((width, 3 * width), F32), shape((width, width), F32),
            shape((16, width), F32),
        ],
        compiler_params=params(),
        cost_estimate=pl.CostEstimate(flops=int(10e9), bytes_accessed=int(3e7), transcendentals=0),
        name="attention_backward",
    )(tok_p, qkv_full, out_full, gains, router_t, cols, grad_back, dlogits, resid, dout, qkv_p, probs, mixed)

    gin_sums = [lax.psum_scatter(gin[q], "dp", scatter_dimension=0, tiled=True) for q in (1, 0)]
    gout_sums = [lax.psum_scatter(gout_t[q], "dp", scatter_dimension=1, tiled=True) for q in (1, 0)]
    gin_own = gin_sums[1].astype(F32) + lax.ppermute(gin_sums[0], "expert", far).astype(F32)
    gout_own = (gout_sums[1].astype(F32) + lax.ppermute(gout_sums[0], "expert", far).astype(F32)).T

    dense_grad = jnp.concatenate(
        [
            gqkv, gout_w, gmisc.T,
            jnp.broadcast_to(loss_part[0:1, 0:1] / 16.0, (width, 1)), jnp.zeros((width, 111), F32),
        ],
        axis=1,
    )
    mine = lax.psum_scatter(dense_grad, axes, scatter_dimension=0, tiled=True)
    misc = mine[:, 4 * width :]
    loss_value = jnp.sum(misc[:, 16]) * (16.0 / shard) / valid_count

    def unpad(array):
        return array[:, :real_rows].reshape(tok_rows, width)

    return (
        unpad(block_out),
        loss_value,
        unpad(tgrad),
        misc[:, 8],
        mine[:, : 3 * width],
        mine[:, 3 * width : 4 * width],
        misc[:, 9],
        misc[:, :experts],
        gin_own[None],
        gout_own[None],
    )


def solution(mesh):
    in_specs = (
        P(("dp", "expert"), None),
        P(("dp", "expert"), None),
        P(("dp", "expert")),
        P(("dp", "expert"), None),
        P(("dp", "expert"), None),
        P(("dp", "expert")),
        P(("dp", "expert"), None),
        P(("dp", "expert"), None),
        P(("dp", "expert")),
        P(("dp", "expert"), None),
        P("expert", "dp", None),
        P("expert", "dp", None),
    )
    out_specs = (
        P(("dp", "expert"), None),
        P(),
        P(("dp", "expert"), None),
        P(("dp", "expert")),
        P(("dp", "expert"), None),
        P(("dp", "expert"), None),
        P(("dp", "expert")),
        P(("dp", "expert"), None),
        P("expert", "dp", None),
        P("expert", "dp", None),
    )
    halves = mesh.shape["expert"] == 8 and mesh.shape["dp"] == 4
    body = fast_shards if halves else shards
    return jax.shard_map(body, mesh=mesh, in_specs=in_specs, out_specs=out_specs, check_vma=False)
```

```python
import jax
import jax.numpy as jnp
from jax import lax
from jax.experimental import pallas as pl
from jax.experimental.pallas import tpu as pltpu
from jax.sharding import PartitionSpec as P

HEADS = 8
IMG_DEV = 5


HIGH = lax.Precision.HIGHEST
EPS = 1e-06


def layer_norm(values, scale_gain):
    row_mean = jnp.mean(values, axis=-1, keepdims=True)
    centered = values - row_mean
    variance = jnp.mean(centered * centered, axis=-1, keepdims=True)
    inverse = lax.rsqrt(variance + EPS)
    normed = centered * inverse
    return (normed * scale_gain, normed, inverse)


def layer_norm_back(grad_in, normed, inverse, scale_gain):
    scaled = grad_in * scale_gain
    gain_grad = jnp.sum(grad_in * normed, axis=0)
    inner_term = (
        scaled
        - jnp.mean(scaled, axis=-1, keepdims=True)
        - normed * jnp.mean(scaled * normed, axis=-1, keepdims=True)
    )
    return (inverse * inner_term, gain_grad)


def contract_rows(left_side, right_side):
    return lax.dot_general(
        left_side, right_side, (((0,), (0,)), ((), ())), preferred_element_type=jnp.float32
    )


def contract_cols(left_side, right_side):
    return lax.dot_general(
        left_side, right_side, (((1,), (1,)), ((), ())), preferred_element_type=jnp.float32
    )


def exact_gelu(values):
    return jax.nn.gelu(values, approximate=False)


def split_heads(qkv_low, images, head_count):
    row_count, triple_width = qkv_low.shape
    head_dim = triple_width // (3 * head_count)
    pieces = qkv_low.reshape(images, row_count // images, 3, head_count, head_dim)
    return (pieces[:, :, 0], pieces[:, :, 1], pieces[:, :, 2], head_dim ** (-0.5))


def attention_forward(qkv_low, images, head_count):
    queries, key_rows, values, score_scale = split_heads(qkv_low, images, head_count)
    scores = (
        jnp.einsum("ilhd,imhd->ihlm", queries, key_rows, preferred_element_type=jnp.float32)
        * score_scale
    )
    row_max = jnp.max(scores, axis=-1, keepdims=True)
    exp_scores = jnp.exp(scores - row_max)
    row_sum = jnp.sum(exp_scores, axis=-1, keepdims=True)
    weights_low = (exp_scores / row_sum).astype(jnp.bfloat16)
    log_total = row_max + jnp.log(row_sum)
    mixed_rows = jnp.einsum(
        "ihlm,imhd->ilhd", weights_low, values, preferred_element_type=jnp.float32
    )
    return (mixed_rows.reshape(qkv_low.shape[0], -1).astype(jnp.bfloat16), log_total)


def attention_back(qkv_low, log_total, grad_mixed, images, head_count):
    queries, key_rows, values, score_scale = split_heads(qkv_low, images, head_count)
    scores = (
        jnp.einsum("ilhd,imhd->ihlm", queries, key_rows, preferred_element_type=jnp.float32)
        * score_scale
    )
    weights_full = jnp.exp(scores - log_total)
    weights_low = weights_full.astype(jnp.bfloat16)
    grad_heads = grad_mixed.reshape(queries.shape)
    grad_weights = jnp.einsum(
        "ilhd,imhd->ihlm", grad_heads, values, preferred_element_type=jnp.float32
    )
    grad_values = jnp.einsum(
        "ihlm,ilhd->imhd", weights_low, grad_heads, preferred_element_type=jnp.float32
    )
    grad_scores = weights_full * (
        grad_weights - jnp.sum(weights_full * grad_weights, axis=-1, keepdims=True)
    )
    grad_low = grad_scores.astype(jnp.bfloat16)
    grad_queries = (
        jnp.einsum("ihlm,imhd->ilhd", grad_low, key_rows, preferred_element_type=jnp.float32)
        * score_scale
    )
    grad_keys = (
        jnp.einsum("ihlm,ilhd->imhd", grad_low, queries, preferred_element_type=jnp.float32)
        * score_scale
    )
    stacked = jnp.stack([grad_queries, grad_keys, grad_values], axis=2)
    return stacked.reshape(qkv_low.shape).astype(jnp.bfloat16)


def expert_forward(rows_in, weight_in, weight_out, block_size):
    result = jnp.zeros((rows_in.shape[0], weight_out.shape[1]), jnp.float32)
    for offset in range(0, weight_in.shape[1], block_size):
        pre_act = jnp.dot(
            rows_in, weight_in[:, offset : offset + block_size], preferred_element_type=jnp.float32
        )
        hidden = exact_gelu(pre_act).astype(jnp.bfloat16)
        result = result + jnp.dot(
            hidden, weight_out[offset : offset + block_size], preferred_element_type=jnp.float32
        )
    return result


def expert_back(rows_in, weight_in, weight_out, grad_rows_out, block_size):
    grad_rows = jnp.zeros(rows_in.shape, jnp.float32)
    grads_first = []
    grads_second = []
    for offset in range(0, weight_in.shape[1], block_size):
        slice_in = weight_in[:, offset : offset + block_size]
        slice_out = weight_out[offset : offset + block_size]
        pre_act = jnp.dot(rows_in, slice_in, preferred_element_type=jnp.float32)
        hidden, gelu_back = jax.vjp(exact_gelu, pre_act)
        grads_second.append(contract_rows(hidden.astype(jnp.bfloat16), grad_rows_out))
        grad_hidden = contract_cols(grad_rows_out, slice_out)
        grad_pre = gelu_back(grad_hidden)[0].astype(jnp.bfloat16)
        grads_first.append(contract_rows(rows_in, grad_pre))
        grad_rows = grad_rows + contract_cols(grad_pre, slice_in)
    return (grad_rows, jnp.concatenate(grads_first, axis=1), jnp.concatenate(grads_second, axis=0))


def shards(
    tokens,
    targets,
    valid_mask,
    routes,
    slot_ids,
    ln1_gain,
    qkv_weight,
    out_weight,
    ln2_gain,
    router_weight,
    expert_in,
    expert_out,
):
    tok_rows, model_width = tokens.shape
    experts = lax.axis_size("expert")
    total_tokens = tok_rows * lax.axis_size("dp") * experts
    capacity = (5 * tok_rows // 2 // experts + 7) // 8 * 8
    dense_full = (
        lax.all_gather(ln1_gain, ("dp", "expert"), axis=0, tiled=True),
        lax.all_gather(qkv_weight, ("dp", "expert"), axis=0, tiled=True),
        lax.all_gather(out_weight, ("dp", "expert"), axis=0, tiled=True),
        lax.all_gather(ln2_gain, ("dp", "expert"), axis=0, tiled=True),
        lax.all_gather(router_weight, ("dp", "expert"), axis=0, tiled=True),
    )
    gain_one, qkv_full, out_full, gain_two, router_full = dense_full
    expert_full = (
        lax.all_gather(expert_in, "dp", axis=1, tiled=True),
        lax.all_gather(expert_out, "dp", axis=1, tiled=True),
    )
    weight_in = expert_full[0][0]
    weight_out = expert_full[1][0]
    valid_f = valid_mask.astype(jnp.float32)
    valid_count = lax.psum(jnp.sum(valid_f), ("dp", "expert"))
    inputs_f = tokens.astype(jnp.float32)
    gain_one_f = gain_one.astype(jnp.float32)
    gain_two_f = gain_two.astype(jnp.float32)
    norm_one, normed_one, inverse_one = layer_norm(inputs_f, gain_one_f)
    act_one = norm_one.astype(jnp.bfloat16)
    qkv_low = jnp.dot(act_one, qkv_full, preferred_element_type=jnp.float32).astype(jnp.bfloat16)
    mixed_low, log_total = attention_forward(qkv_low, IMG_DEV, HEADS)
    residual = inputs_f + jnp.dot(mixed_low, out_full, preferred_element_type=jnp.float32)
    norm_two, normed_two, inverse_two = layer_norm(residual, gain_two_f)
    act_two = norm_two.astype(jnp.bfloat16)
    gate_probs = jax.nn.softmax(
        jnp.dot(act_two, router_full, preferred_element_type=jnp.float32), axis=-1
    )
    expert_ids = lax.broadcasted_iota(jnp.int32, (1, experts), 1)
    first_pick = (routes[:, 0:1] == expert_ids).astype(jnp.float32)
    second_pick = (routes[:, 1:2] == expert_ids).astype(jnp.float32)
    gate_first = jnp.sum(gate_probs * first_pick, axis=-1, keepdims=True)
    gate_second = jnp.sum(gate_probs * second_pick, axis=-1, keepdims=True)
    target_slot = jnp.where(slot_ids < capacity, routes * capacity + slot_ids, -1)
    slot_columns = lax.broadcasted_iota(jnp.int32, (1, experts * capacity), 1)
    first_hot = (target_slot[:, 0:1] == slot_columns).astype(jnp.bfloat16)
    second_hot = (target_slot[:, 1:2] == slot_columns).astype(jnp.bfloat16)
    both_hot = first_hot + second_hot
    outgoing = contract_rows(both_hot, act_two).astype(jnp.bfloat16)
    arrived = lax.all_to_all(
        outgoing.reshape(experts, capacity, model_width),
        "expert",
        split_axis=0,
        concat_axis=0,
        tiled=True,
    ).reshape(-1, model_width)
    hidden_block = min(512, weight_in.shape[1])
    produced = expert_forward(arrived, weight_in, weight_out, hidden_block).astype(jnp.bfloat16)
    returned = lax.all_to_all(
        produced.reshape(experts, capacity, model_width),
        "expert",
        split_axis=0,
        concat_axis=0,
        tiled=True,
    ).reshape(-1, model_width)
    from_first = jnp.dot(first_hot, returned, preferred_element_type=jnp.float32)
    from_second = jnp.dot(second_hot, returned, preferred_element_type=jnp.float32)
    output = residual + gate_first * from_first + gate_second * from_second
    residue = output - targets.astype(jnp.float32)
    local_loss = jnp.sum(valid_f * jnp.mean(residue * residue, axis=-1))
    loss_sum = lax.psum(local_loss, ("dp", "expert"))
    loss_value = loss_sum / valid_count
    grad_out = total_tokens / valid_count * valid_f[:, None] * residue
    dense_back = (
        lax.all_gather(ln1_gain, ("dp", "expert"), axis=0, tiled=True),
        lax.all_gather(qkv_weight, ("dp", "expert"), axis=0, tiled=True),
        lax.all_gather(out_weight, ("dp", "expert"), axis=0, tiled=True),
        lax.all_gather(ln2_gain, ("dp", "expert"), axis=0, tiled=True),
        lax.all_gather(router_weight, ("dp", "expert"), axis=0, tiled=True),
    )
    expert_back_full = (
        lax.all_gather(expert_in, "dp", axis=1, tiled=True),
        lax.all_gather(expert_out, "dp", axis=1, tiled=True),
    )
    qkv_back = dense_back[1]
    out_back = dense_back[2]
    router_back = dense_back[4]
    weight_in_back = expert_back_full[0][0]
    weight_out_back = expert_back_full[1][0]
    slot_grads = (
        contract_rows(first_hot, (gate_first * grad_out).astype(jnp.bfloat16))
        + contract_rows(second_hot, (gate_second * grad_out).astype(jnp.bfloat16))
    ).astype(jnp.bfloat16)
    expert_grad_rows = lax.all_to_all(
        slot_grads.reshape(experts, capacity, model_width),
        "expert",
        split_axis=0,
        concat_axis=0,
        tiled=True,
    ).reshape(-1, model_width)
    grad_rows, grad_first_weight, grad_second_weight = expert_back(
        arrived, weight_in_back, weight_out_back, expert_grad_rows, hidden_block
    )
    grad_back = lax.all_to_all(
        grad_rows.astype(jnp.bfloat16).reshape(experts, capacity, model_width),
        "expert",
        split_axis=0,
        concat_axis=0,
        tiled=True,
    ).reshape(-1, model_width)
    grad_act_two = jnp.dot(both_hot, grad_back, preferred_element_type=jnp.float32)
    gate_grad = first_pick * jnp.sum(
        grad_out * from_first, axis=-1, keepdims=True
    ) + second_pick * jnp.sum(grad_out * from_second, axis=-1, keepdims=True)
    logit_grad = gate_probs * (gate_grad - jnp.sum(gate_probs * gate_grad, axis=-1, keepdims=True))
    router_f = router_back.astype(jnp.float32)
    grad_act_two = grad_act_two + lax.dot_general(
        logit_grad,
        router_f,
        (((1,), (1,)), ((), ())),
        precision=HIGH,
        preferred_element_type=jnp.float32,
    )
    router_grad = lax.dot_general(
        act_two.astype(jnp.float32),
        logit_grad,
        (((0,), (0,)), ((), ())),
        precision=HIGH,
        preferred_element_type=jnp.float32,
    )
    grad_norm_two, gain_two_grad = layer_norm_back(
        grad_act_two, normed_two, inverse_two, gain_two_f
    )
    grad_resid = grad_out + grad_norm_two
    branch_grad = grad_resid.astype(jnp.bfloat16)
    out_weight_grad = contract_rows(mixed_low, branch_grad)
    grad_mixed = contract_cols(branch_grad, out_back).astype(jnp.bfloat16)
    qkv_grad_low = attention_back(qkv_low, log_total, grad_mixed, IMG_DEV, HEADS)
    qkv_weight_grad = contract_rows(act_one, qkv_grad_low)
    grad_act_one = contract_cols(qkv_grad_low, qkv_back)
    grad_norm_one, gain_one_grad = layer_norm_back(
        grad_act_one, normed_one, inverse_one, gain_one_f
    )
    tokens_grad = grad_resid + grad_norm_one
    dense_grads = (
        lax.psum_scatter(gain_one_grad, ("dp", "expert"), scatter_dimension=0, tiled=True),
        lax.psum_scatter(qkv_weight_grad, ("dp", "expert"), scatter_dimension=0, tiled=True),
        lax.psum_scatter(out_weight_grad, ("dp", "expert"), scatter_dimension=0, tiled=True),
        lax.psum_scatter(gain_two_grad, ("dp", "expert"), scatter_dimension=0, tiled=True),
        lax.psum_scatter(router_grad, ("dp", "expert"), scatter_dimension=0, tiled=True),
    )
    expert_grads = (
        lax.psum_scatter(
            grad_first_weight[None].astype(jnp.bfloat16), "dp", scatter_dimension=1, tiled=True
        ).astype(jnp.float32),
        lax.psum_scatter(
            grad_second_weight[None].astype(jnp.bfloat16), "dp", scatter_dimension=1, tiled=True
        ).astype(jnp.float32),
    )
    first_result = expert_grads[0]
    second_result = expert_grads[1]
    return (
        output.astype(jnp.bfloat16),
        loss_value,
        tokens_grad,
        dense_grads[0],
        dense_grads[1],
        dense_grads[2],
        dense_grads[3],
        dense_grads[4],
        first_result,
        second_result,
    )


F32 = jnp.float32
BF16 = jnp.bfloat16
MB = 2**20


def round_up(value, unit):
    return (value + unit - 1) // unit * unit


def dot(left_side, right_side):
    return jnp.dot(left_side, right_side, preferred_element_type=F32)


def lane_ids(shape):
    return lax.broadcasted_iota(jnp.int32, shape, len(shape) - 1)


def row_ids(shape):
    return lax.broadcasted_iota(jnp.int32, shape, len(shape) - 2)


MESH = pl.DeviceIdType.MESH


def flip(index, bit):
    return index + bit * (1 - 2 * lax.rem(index // bit, 2))


def send(src, dst, sems, slot, device):
    return pltpu.make_async_remote_copy(
        src_ref=src, dst_ref=dst, send_sem=sems[0].at[slot], recv_sem=sems[1].at[slot],
        device_id=device, device_id_type=MESH,
    )


def greet(peers):
    barrier = pltpu.get_barrier_semaphore()
    for peer in peers:
        pl.semaphore_signal(barrier, inc=1, device_id=peer, device_id_type=MESH)
    pl.semaphore_wait(barrier, len(peers))


def place():
    dp_at, ex_at = lax.axis_index("dp"), lax.axis_index("expert")
    near = [None, flip(dp_at, 1), flip(dp_at, 2), flip(flip(dp_at, 1), 2)]
    return dp_at, ex_at, near


def sem_pairs(count):
    return [pltpu.SemaphoreType.DMA((count,)), pltpu.SemaphoreType.DMA((count,))]


def normalize(values):
    centered = values - jnp.mean(values, axis=-1, keepdims=True)
    inverse = lax.rsqrt(jnp.mean(centered * centered, axis=-1, keepdims=True) + EPS)
    return centered * inverse, inverse


def gelu_pair(values):
    size = jnp.abs(values)
    inv = 1.0 / (1.0 + 0.2316419 * size)
    density = 0.3989422804014327 * jnp.exp(-0.5 * values * values)
    series = inv * (
        0.319381530
        + inv * (-0.356563782 + inv * (1.781477937 + inv * (-1.821255978 + inv * 1.330274429)))
    )
    tail = density * series
    cumulative = jnp.where(values >= 0, 1.0 - tail, tail)
    return values * cumulative, cumulative + values * density


def forward_kernel(
    real_rows,
    experts,
    tok_ref,
    wqkv_ref,
    wout_ref,
    gain_ref,
    router_ref,
    router_t_ref,
    cols_ref,
    rows_ref,
    qkv_ref,
    probs_ref,
    mixed_ref,
    resid_ref,
    act_ref,
    gates_ref,
    grow_ref,
):
    inputs = tok_ref[...].astype(F32)
    normed, _ = normalize(inputs)
    act_one = (normed * gain_ref[0:1, :]).astype(BF16)
    qkv = dot(act_one, wqkv_ref[...]).astype(BF16)
    qkv_ref[...] = qkv
    width = inputs.shape[1]
    rows = inputs.shape[0]
    low_half = lane_ids((1, 128)) < 64
    key_bias = jnp.where(lane_ids((1, rows)) < real_rows, 0.0, -1e30)
    parts = []
    for pair in range(width // 128):
        lanes = slice(128 * pair, 128 * (pair + 1))
        queries = qkv[:, lanes]
        key_rows = qkv[:, width + 128 * pair : width + 128 * (pair + 1)]
        values = qkv[:, 2 * width + 128 * pair : 2 * width + 128 * (pair + 1)]
        outs = []
        for side in range(2):
            mask = low_half if side == 0 else jnp.logical_not(low_half)
            masked = jnp.where(mask, queries, jnp.zeros_like(queries))
            scores = contract_cols(masked, key_rows) * 0.125 + key_bias
            exped = jnp.exp(scores - jnp.max(scores, axis=-1, keepdims=True))
            probs = (exped * (1.0 / jnp.sum(exped, axis=-1, keepdims=True))).astype(BF16)
            probs_ref[2 * pair + side] = probs
            outs.append(dot(probs, values))
        parts.append(jnp.where(low_half, outs[0], outs[1]).astype(BF16))
    mixed = jnp.concatenate(parts, axis=1)
    mixed_ref[...] = mixed
    resid = inputs + dot(mixed, wout_ref[...])
    resid_ref[...] = resid
    normed_two, _ = normalize(resid)
    act_two = (normed_two * gain_ref[1:2, :]).astype(BF16)
    act_ref[...] = act_two
    lanes = lane_ids((1, 128))
    logits = jnp.where(lanes < experts, dot(act_two, router_ref[...]), -1e30)
    exped = jnp.exp(logits - jnp.max(logits, axis=-1, keepdims=True))
    gates = exped / jnp.sum(exped, axis=-1, keepdims=True)
    cols = cols_ref[...]
    first = jnp.sum(jnp.where(lanes == cols[:, 2:3], gates, 0.0), axis=-1, keepdims=True)
    second = jnp.sum(jnp.where(lanes == cols[:, 3:4], gates, 0.0), axis=-1, keepdims=True)
    gates_ref[...] = jnp.where(lanes == experts, first, jnp.where(lanes == experts + 1, second, gates))
    logits_t = contract_cols(router_t_ref[...], act_two)[:experts]
    exped_t = jnp.exp(logits_t - jnp.max(logits_t, axis=0, keepdims=True))
    gates_t = exped_t / jnp.sum(exped_t, axis=0, keepdims=True)
    ids_t = row_ids(gates_t.shape)
    first_t = jnp.sum(jnp.where(ids_t == rows_ref[2:3, :], gates_t, 0.0), axis=0, keepdims=True)
    second_t = jnp.sum(jnp.where(ids_t == rows_ref[3:4, :], gates_t, 0.0), axis=0, keepdims=True)
    grow_ref[...] = jnp.where(row_ids((8, rows)) == 0, first_t, second_t)


def hot_rows(codes, start, count):
    slots = row_ids((count, codes.shape[1])) + start
    return (slots == codes[0:1, :]) | (slots == codes[1:2, :])


def expert_forward_kernel(
    cap, group, act_ref, codes_ref, win_ref, wout_ref, rows_out_ref, hidden_ref, slope_ref, out_ref
):
    which, half = pl.program_id(0), pl.program_id(1)
    blocks, images = act_ref.shape[0], act_ref.shape[1]
    hidden_width = win_ref.shape[1]
    pieces = []
    for block in range(blocks):
        start = (which * group + half * blocks + block) * cap
        total = None
        for image in range(images):
            hot = jnp.where(hot_rows(codes_ref[block, image], start, cap), 1.0, 0.0).astype(BF16)
            term = dot(hot, act_ref[block, image])
            total = term if total is None else total + term
        pieces.append(total.astype(BF16))
    rows_in = jnp.concatenate(pieces, axis=0)
    rows_out_ref[...] = rows_in.reshape(rows_out_ref.shape)
    step = 512
    result = None
    for offset in range(0, hidden_width, step):
        act, slope = gelu_pair(dot(rows_in, win_ref[:, offset : offset + step]))
        act = act.astype(BF16)
        hidden_ref[:, :, offset : offset + step] = act.reshape(blocks, cap, step)
        slope_ref[:, :, offset : offset + step] = slope.astype(BF16).reshape(blocks, cap, step)
        term = dot(act, wout_ref[offset : offset + step, :])
        result = term if result is None else result + term
    out_ref[...] = result.astype(BF16).reshape(out_ref.shape)


def hot_cols(codes, count):
    return lane_ids((codes.shape[0], count)) == codes


def combine_kernel(
    experts, scale_ref, resid_ref, back_ref, cols_ref, gates_ref, target_ref, valid_ref,
    out_ref, dout_ref, dlow_ref, dlogit_ref, loss_ref,
):
    count = back_ref.shape[0]
    cols = cols_ref[...]
    rows = cols.shape[0]
    hot = jnp.concatenate(
        [
            jnp.where(hot_cols(cols[:, 0:1], count), 1.0, 0.0).astype(BF16),
            jnp.where(hot_cols(cols[:, 1:2], count), 1.0, 0.0).astype(BF16),
        ],
        axis=0,
    )
    both = dot(hot, back_ref[...])
    from_first, from_second = both[:rows], both[rows:]
    gates = gates_ref[...]
    first, second = gates[:, experts : experts + 1], gates[:, experts + 1 : experts + 2]
    output = resid_ref[...] + first * from_first + second * from_second
    out_ref[...] = output.astype(BF16)
    residue = output - target_ref[...].astype(F32)
    valid = valid_ref[...]
    square = jnp.mean(residue * residue, axis=-1, keepdims=True) * valid[:, 0:1]

    @pl.when(pl.program_id(0) == 0)
    def _():
        loss_ref[...] = jnp.zeros_like(loss_ref)

    loss_ref[...] += jnp.sum(square)
    dout = (scale_ref[0, 0] * valid[:, 0:1]) * residue
    dout_ref[...] = dout
    dlow_ref[...] = dout.astype(BF16)
    lanes = lane_ids((1, 128))
    grad = jnp.where(
        lanes == cols[:, 2:3], jnp.sum(dout * from_first, axis=-1, keepdims=True), 0.0
    ) + jnp.where(lanes == cols[:, 3:4], jnp.sum(dout * from_second, axis=-1, keepdims=True), 0.0)
    real = jnp.where(lanes < experts, gates, 0.0)
    dlogit_ref[...] = real * (grad - jnp.sum(real * grad, axis=-1, keepdims=True))


def expert_back_kernel(
    cap, group, dlow_ref, codes_ref, grow_ref, rows_ref, hidden_ref, slope_ref, win_ref, wout_ref,
    back_ref, gin_ref, gout_ref, acc_in, acc_out,
):
    which, half = pl.program_id(0), pl.program_id(1)
    blocks, images = dlow_ref.shape[0], dlow_ref.shape[1]
    hidden_width = win_ref.shape[1]
    pieces = []
    for block in range(blocks):
        start = (which * group + half * blocks + block) * cap
        total = None
        slot_gate = None
        for image in range(images):
            codes = codes_ref[block, image]
            slots = row_ids((cap, codes.shape[1])) + start
            is_first = slots == codes[0:1, :]
            is_second = slots == codes[1:2, :]
            hot = jnp.where(is_first | is_second, 1.0, 0.0).astype(BF16)
            term = dot(hot, dlow_ref[block, image])
            gain = grow_ref[block, image]
            picked = jnp.where(is_first, gain[0:1, :], jnp.where(is_second, gain[1:2, :], 0.0))
            picked = jnp.sum(picked, axis=-1, keepdims=True)
            total = term if total is None else total + term
            slot_gate = picked if slot_gate is None else slot_gate + picked
        pieces.append((total * slot_gate).astype(BF16))
    grads = jnp.concatenate(pieces, axis=0)
    grads_t = grads.T
    rows_in_t = rows_ref[...].reshape(blocks * cap, -1).T
    step = 512
    result = None
    for offset in range(0, hidden_width, step):
        cut = slice(offset, offset + step)
        hidden = hidden_ref[:, :, cut].reshape(blocks * cap, step)
        slope = slope_ref[:, :, cut].reshape(blocks * cap, step).astype(F32)
        dpre = (contract_cols(grads, wout_ref[cut, :]) * slope).astype(BF16)
        gin = dot(rows_in_t, dpre)
        gout = dot(grads_t, hidden)
        term = contract_cols(dpre, win_ref[:, cut])
        result = term if result is None else result + term

        @pl.when(half == 0)
        def _():
            acc_in[:, cut] = gin
            acc_out[:, cut] = gout

        @pl.when(half == 1)
        def _():
            gin_ref[:, cut] = (acc_in[:, cut] + gin).astype(BF16)
            gout_ref[offset // step] = (acc_out[:, cut] + gout).astype(BF16)

    back_ref[...] = result.astype(BF16).reshape(back_ref.shape)


def back_kernel(
    images, tok_ref, wqkv_ref, wout_ref, gain_ref, router_t_ref, cols_ref, back_ref, dlogit_ref, resid_ref,
    dout_ref, qkv_ref, probs_ref, mixed_ref, loss_ref, gin_ref, gex_ref,
    tgrad_ref, dense_ref, misc_ref, gin_out, gex_out,
    acc, acc_misc, part_in, part_ex, got_in, got_ex, sum_in, sum_ex, more_in, more_ex, far_in, far_ex, came_in, came_ex,
    low, mate, low_mate, plane, low_plane, line, misc_got, local_sem, w_send, w_recv, d_send, d_recv, m_send, m_recv,
):
    step_at = pl.program_id(0)
    dp_at, ex_at, near = place()
    core, floor = lax.rem(ex_at, 2), ex_at // 2
    wsem, dsem, msem = (w_send, w_recv), (d_send, d_recv), (m_send, m_recv)
    tensors = [
        (gin_ref, part_in, got_in, sum_in, more_in, far_in, came_in, gin_out, 1, 2),
        (gex_ref, part_ex, got_ex, sum_ex, more_ex, far_ex, came_ex, gex_out, 2, 1),
    ]

    def local_copies():
        copies = []
        for t, (grad, part, _, _, _, _, _, _, _, second) in enumerate(tensors):
            for q in range(2):
                for s in range(2):
                    owner = dp_at if s == 0 else near[second]
                    copies.append(
                        pltpu.make_async_copy(grad.at[q, owner], part.at[q, s], local_sem.at[4 * t + 2 * q + s])
                    )
        return copies

    def first_round(q):
        copies = []
        for t, (grad, _, got, _, _, _, _, _, first, _) in enumerate(tensors):
            for s in range(2):
                owner = near[first] if s == 0 else near[3]
                copies.append(
                    send(grad.at[q, owner], got.at[q, s], wsem, 8 * q + 4 * t + s, (near[first], ex_at))
                )
        return copies

    def second_round(q):
        return [
            send(passed.at[q], more.at[q], wsem, 8 * q + 4 * t + 2, (near[second], ex_at))
            for t, (_, _, _, passed, more, _, _, _, _, second) in enumerate(tensors)
        ]

    def far_round():
        return [
            send(far, came, wsem, 4 * t + 3, (dp_at, flip(ex_at, 4)))
            for t, (_, _, _, _, _, far, came, _, _, _) in enumerate(tensors)
        ]

    def add_first(q):
        for copy in first_round(q):
            copy.wait_recv()
        for _, part, got, passed, _, _, _, _, _, _ in tensors:
            passed[q] = (part[q, 1].astype(F32) + got[q, 1].astype(F32)).astype(BF16)
        for copy in second_round(q):
            copy.start()

    def total_of(tensor, q):
        _, part, got, _, more, _, _, _, _, _ = tensor
        return part[q, 0].astype(F32) + got[q, 0].astype(F32) + more[q].astype(F32)

    @pl.when(step_at == 0)
    def _():
        greet(
            [(near[k], ex_at) for k in (1, 2, 3)]
            + [(dp_at, flip(ex_at, bit)) for bit in (1, 2, 4)]
            + [(dp_at, flip(flip(ex_at, 2), 4))]
        )
        for copy in first_round(1) + first_round(0) + local_copies():
            copy.start()

    count = back_ref.shape[0]
    cols = cols_ref[...]
    hot = jnp.where(hot_cols(cols[:, 0:1], count) | hot_cols(cols[:, 1:2], count), 1.0, 0.0)
    dlogits = dlogit_ref[...]
    dact = dot(hot.astype(BF16), back_ref[...])
    dlogits_high = dlogits.astype(BF16)
    dlogits_low = (dlogits - dlogits_high.astype(F32)).astype(BF16)
    dact = dact + dot(dlogits_high, router_t_ref[...]) + dot(dlogits_low, router_t_ref[...])

    resid = resid_ref[...]
    normed_two, inverse_two = normalize(resid)
    gain_two = gain_ref[1:2, :]
    act_two = (normed_two * gain_two).astype(BF16)
    grouter = contract_rows(dlogits_high, act_two) + contract_rows(dlogits_low, act_two)

    def norm_back(grad, normed, inverse, gain):
        scaled = grad * gain
        gain_grad = jnp.sum(grad * normed, axis=0, keepdims=True)
        inner = (
            scaled
            - jnp.mean(scaled, axis=-1, keepdims=True)
            - normed * jnp.mean(scaled * normed, axis=-1, keepdims=True)
        )
        return inverse * inner, gain_grad

    grad_two, ggain_two = norm_back(dact, normed_two, inverse_two, gain_two)
    dresid = dout_ref[...] + grad_two
    branch = dresid.astype(BF16)
    mixed = mixed_ref[...]
    gout = contract_rows(mixed, branch)
    dmixed = contract_cols(branch, wout_ref[...]).astype(BF16)
    qkv = qkv_ref[...]
    width = dmixed.shape[1]
    low_half = lane_ids((1, 128)) < 64
    dqs, dks, dvs = [], [], []
    for pair in range(width // 128):
        cut = slice(128 * pair, 128 * (pair + 1))
        queries = qkv[:, cut]
        key_rows = qkv[:, width + 128 * pair : width + 128 * (pair + 1)]
        values = qkv[:, 2 * width + 128 * pair : 2 * width + 128 * (pair + 1)]
        dmix = dmixed[:, cut]
        dq = []
        dk = dv = None
        for side in range(2):
            mask = low_half if side == 0 else jnp.logical_not(low_half)
            dmask = jnp.where(mask, dmix, jnp.zeros_like(dmix))
            qmask = jnp.where(mask, queries, jnp.zeros_like(queries))
            probs_low = probs_ref[2 * pair + side]
            probs = probs_low.astype(F32)
            dprobs = contract_cols(dmask, values)
            dscore = probs * (dprobs - jnp.sum(probs * dprobs, axis=-1, keepdims=True))
            dscore = dscore.astype(BF16)
            dq.append(dot(dscore, key_rows))
            dk_term = contract_rows(dscore, qmask)
            dv_term = contract_rows(probs_low, dmask)
            dk = dk_term if dk is None else dk + dk_term
            dv = dv_term if dv is None else dv + dv_term
        dqs.append((jnp.where(low_half, dq[0], dq[1]) * 0.125).astype(BF16))
        dks.append((dk * 0.125).astype(BF16))
        dvs.append(dv.astype(BF16))
    dqkv = jnp.concatenate(dqs + dks + dvs, axis=1)
    inputs = tok_ref[...].astype(F32)
    normed_one, inverse_one = normalize(inputs)
    gain_one = gain_ref[0:1, :]
    act_one = (normed_one * gain_one).astype(BF16)
    gqkv = contract_rows(act_one, dqkv)
    dact_one = contract_cols(dqkv, wqkv_ref[...])
    grad_one, ggain_one = norm_back(dact_one, normed_one, inverse_one, gain_one)
    tgrad_ref[...] = dresid + grad_one
    ids = row_ids((8, width))
    gmisc = jnp.concatenate(
        [grouter[:8], jnp.where(ids == 0, ggain_one, jnp.where(ids == 1, ggain_two, 0.0))], axis=0
    )

    @pl.when(step_at == 0)
    def _():
        for copy in local_copies():
            copy.wait()
        acc[:, : 3 * width] = gqkv
        acc[:, 3 * width :] = gout
        loss_row = jnp.where(row_ids((8, 128)) == 2, loss_ref[...], 0.0)
        acc_misc[...] = gmisc + jnp.concatenate(
            [jnp.zeros((8, width), F32), jnp.concatenate([loss_row] * (width // 128), axis=1)], axis=0
        )

    @pl.when(step_at > 0)
    def _():
        acc[:, : 3 * width] += gqkv
        acc[:, 3 * width :] += gout
        acc_misc[...] += gmisc

    @pl.when(step_at == images - 2)
    def _():
        add_first(1)

    @pl.when(step_at == images - 1)
    def _():
        lines, shard = low.shape[1], low.shape[3]
        low[...] = acc[...].astype(BF16).reshape(low.shape)
        other = lax.rem(core + 1, 2)
        to_mate = send(low.at[:, :, other], mate, dsem, 0, (dp_at, flip(ex_at, 1)))
        to_mate.start()
        misc_peers = [
            (dp_at, flip(ex_at, 1)), (near[1], ex_at), (near[2], ex_at), (dp_at, flip(ex_at, 2)), (dp_at, flip(ex_at, 4)),
        ]
        misc = [send(acc_misc.at[...] if k == 0 else misc_got.at[5 + k - 1], misc_got.at[k], msem, k, misc_peers[k]) for k in range(5)]
        misc[0].start()
        add_first(0)

        for copy in second_round(1):
            copy.wait_recv()
        for tensor in tensors:
            tensor[5][...] = total_of(tensor, 1).astype(BF16)
        for copy in far_round():
            copy.start()

        def misc_step(k):
            misc[k].wait_recv()
            before = acc_misc[...] if k == 0 else misc_got[5 + k - 1]
            misc_got[5 + k] = before + misc_got[k]
            if k < 4:
                misc[k + 1].start()

        to_mate.wait_recv()
        low_mate[...] = (low[:, :, core].astype(F32) + mate[...].astype(F32)).astype(BF16)
        to_plane = [send(low_mate.at[near[k]], plane.at[k - 1], dsem, k, (near[k], ex_at)) for k in (1, 2, 3)]
        for copy in to_plane:
            copy.start()
        misc_step(0)
        misc_step(1)
        misc_step(2)
        for copy in to_plane:
            copy.wait_recv()
        summed = low_mate[dp_at].astype(F32)
        for k in range(3):
            summed = summed + plane[k].astype(F32)
        low_plane[...] = summed.astype(BF16)
        floors = [flip(floor, 1), flip(floor, 2), flip(flip(floor, 1), 2)]
        to_line = [
            send(low_plane.at[floors[k]], line.at[k], dsem, 4 + k, (dp_at, 2 * floors[k] + core)) for k in range(3)
        ]
        for copy in to_line:
            copy.start()
        misc_step(3)
        misc_step(4)
        misc_ref[...] = misc_got[9]
        for copy in to_line:
            copy.wait_recv()
        result = low_plane[floor].astype(F32)
        for k in range(3):
            result = result + line[k].astype(F32)
        dense_ref[...] = result

        for copy in second_round(0):
            copy.wait_recv()
        for copy in far_round():
            copy.wait_recv()
        for tensor in tensors:
            tensor[7][...] = total_of(tensor, 0) + tensor[6][...].astype(F32)
        for copy in [to_mate] + misc + to_plane + to_line + first_round(0) + first_round(1):
            copy.wait_send()
        for copy in second_round(0) + second_round(1) + far_round():
            copy.wait_send()


def shape(dims, kind):
    return jax.ShapeDtypeStruct(dims, kind)


def whole(dims):
    return pl.BlockSpec(dims, lambda *_: (0,) * len(dims))


def per_image(*dims):
    return pl.BlockSpec((None,) + dims, lambda i: (i,) + (0,) * len(dims))


def params():
    return pltpu.CompilerParams(vmem_limit_bytes=56 * MB)


def fast_shards(
    tokens, targets, valid_mask, routes, slot_ids, ln1_gain, qkv_weight, out_weight, ln2_gain,
    router_weight, expert_in, expert_out,
):
    axes = ("dp", "expert")
    tok_rows, width = tokens.shape
    experts = lax.axis_size("expert")
    group = experts // 2
    dp = lax.axis_size("dp")
    total_tokens = tok_rows * dp * experts
    hidden_width = expert_in.shape[2]
    capacity = (5 * tok_rows // 2 // experts + 7) // 8 * 8
    cap = round_up(capacity, 16)
    images = IMG_DEV
    real_rows = tok_rows // images
    rows = round_up(real_rows, 16)
    me = lax.axis_index("expert")

    def pad_rows(array, value=0):
        array = array.reshape(images, real_rows, -1)
        return jnp.pad(array, ((0, 0), (0, rows - real_rows), (0, 0)), constant_values=value)

    valid_f = valid_mask.astype(F32)
    my_count = jnp.sum(valid_f)
    count_high = jnp.floor(my_count / 128.0)
    count_low = my_count - 128.0 * count_high
    shard = qkv_weight.shape[0]
    extra = jnp.concatenate(
        [
            router_weight,
            ln1_gain[:, None],
            ln2_gain[:, None],
            jnp.broadcast_to(count_high.astype(BF16), (shard, 1)),
            jnp.broadcast_to(count_low.astype(BF16), (shard, 1)),
            jnp.zeros((shard, 128 - experts - 4), BF16),
        ],
        axis=1,
    )
    dense = lax.all_gather(
        jnp.concatenate([qkv_weight, out_weight, extra], axis=1), axes, axis=0, tiled=True
    )
    qkv_full = dense[:, : 3 * width]
    out_full = dense[:, 3 * width : 4 * width]
    extra_full = dense[:, 4 * width :]
    router_full = jnp.where(lane_ids((1, 128)) < experts, extra_full, 0)
    extra_t = extra_full.T
    router_t = jnp.where(row_ids((128, 1)) < experts, extra_t, 0)
    gains = extra_t[experts : experts + 2].astype(F32)
    counts = extra_full[::shard].astype(F32)
    valid_count = jnp.sum(counts[:, experts + 2] * 128.0 + counts[:, experts + 3])
    scale = (total_tokens / valid_count).reshape(1, 1)

    far = [(i, i ^ group) for i in range(experts)]
    w_in = [expert_in[0]]
    w_out = [expert_out[0]]
    w_in.append(lax.ppermute(w_in[0], "expert", far))
    w_out.append(lax.ppermute(w_out[0], "expert", far))
    win_full = jnp.stack([lax.all_gather(w, "dp", axis=0, tiled=True) for w in w_in])
    wout_full = jnp.stack([lax.all_gather(w, "dp", axis=0, tiled=True) for w in w_out])

    def exchange(blocks):
        out = [blocks[0]]
        for k in range(1, group):
            out.append(lax.ppermute(blocks[k], "expert", [(i, i ^ k) for i in range(experts)]))
        return out

    code = jnp.where(slot_ids < capacity, (routes ^ me) * cap + slot_ids, -1)
    cols = pad_rows(jnp.concatenate([code, routes], axis=1), -1)
    row_codes = jnp.pad(cols.transpose(0, 2, 1), ((0, 0), (0, 4), (0, 0)))
    cols = jnp.pad(cols, ((0, 0), (0, 0), (0, 4)))
    tok_p = pad_rows(tokens)
    target_p = pad_rows(targets)
    valid_p = pad_rows(jnp.broadcast_to(valid_f[:, None], (tok_rows, 8)))

    gate_lanes = 128
    qkv_p, probs, mixed, resid, act_two, gates, grow = pl.pallas_call(
        lambda *refs: forward_kernel(real_rows, experts, *refs),
        grid=(images,),
        in_specs=[
            per_image(rows, width), whole((width, 3 * width)), whole((width, width)), whole((2, width)),
            whole((width, 128)), whole((128, width)), per_image(rows, 8), per_image(8, rows),
        ],
        out_specs=[
            per_image(rows, 3 * width), per_image(HEADS, rows, rows), per_image(rows, width),
            per_image(rows, width), per_image(rows, width), per_image(rows, gate_lanes), per_image(8, rows),
        ],
        out_shape=[
            shape((images, rows, 3 * width), BF16), shape((images, HEADS, rows, rows), BF16),
            shape((images, rows, width), BF16), shape((images, rows, width), F32),
            shape((images, rows, width), BF16), shape((images, rows, gate_lanes), F32),
            shape((images, 8, rows), F32),
        ],
        compiler_params=params(),
        cost_estimate=pl.CostEstimate(flops=int(5e9), bytes_accessed=int(2e7), transcendentals=0),
        name="attention_forward",
    )(tok_p, qkv_full, out_full, gains, router_full, router_t, cols, row_codes)

    act_all = jnp.stack(exchange([act_two] * group))
    code_all = jnp.stack(exchange([row_codes] * group))

    half_blocks = group // 2
    def by_half(*dims):
        return pl.BlockSpec((half_blocks,) + dims, lambda q, h: (h,) + (0,) * len(dims))
    def by_expert(*dims):
        return pl.BlockSpec((None,) + dims, lambda q, h: (q,) + (0,) * len(dims))
    def by_both(*dims):
        return pl.BlockSpec((None, half_blocks) + dims, lambda q, h: (q, h) + (0,) * len(dims))

    rows_in, hidden, slope, produced = pl.pallas_call(
        lambda *refs: expert_forward_kernel(cap, group, *refs),
        grid=(2, 2),
        in_specs=[
            by_half(images, rows, width), by_half(images, 8, rows), by_expert(width, hidden_width),
            by_expert(hidden_width, width),
        ],
        out_specs=[by_both(cap, width), by_both(cap, hidden_width), by_both(cap, hidden_width), by_both(cap, width)],
        out_shape=[
            shape((2, group, cap, width), BF16), shape((2, group, cap, hidden_width), BF16),
            shape((2, group, cap, hidden_width), BF16), shape((2, group, cap, width), BF16),
        ],
        compiler_params=params(),
        cost_estimate=pl.CostEstimate(flops=int(14e9), bytes_accessed=int(4e7), transcendentals=0),
        name="expert_forward",
    )(act_all, code_all, win_full, wout_full)

    def give_back(array):
        came = exchange([array[:, k] for k in range(group)])
        return jnp.stack(came, axis=1).reshape(2 * group * cap, width)

    returned = give_back(produced)
    block_out, dout, dlow, dlogits, loss_part = pl.pallas_call(
        lambda *refs: combine_kernel(experts, *refs),
        grid=(images,),
        in_specs=[
            pl.BlockSpec(memory_space=pltpu.SMEM), per_image(rows, width), whole((2 * group * cap, width)),
            per_image(rows, 8), per_image(rows, gate_lanes), per_image(rows, width), per_image(rows, 8),
        ],
        out_specs=[
            per_image(rows, width), per_image(rows, width), per_image(rows, width), per_image(rows, gate_lanes),
            whole((8, 128)),
        ],
        out_shape=[
            shape((images, rows, width), BF16), shape((images, rows, width), F32),
            shape((images, rows, width), BF16), shape((images, rows, gate_lanes), F32), shape((8, 128), F32),
        ],
        compiler_params=params(),
        cost_estimate=pl.CostEstimate(flops=int(5e9), bytes_accessed=int(1e7), transcendentals=0),
        name="combine_and_loss",
    )(scale, resid, returned, cols, gates, target_p, valid_p)

    dlow_all = jnp.stack(exchange([dlow] * group))
    grow_all = jnp.stack(exchange([grow] * group))
    drows, gin, gout_t = pl.pallas_call(
        lambda *refs: expert_back_kernel(cap, group, *refs),
        grid=(2, 2),
        in_specs=[
            by_half(images, rows, width), by_half(images, 8, rows), by_half(images, 8, rows),
            by_both(cap, width), by_both(cap, hidden_width), by_both(cap, hidden_width),
            by_expert(width, hidden_width), by_expert(hidden_width, width),
        ],
        out_specs=[
            by_both(cap, width), by_expert(width, hidden_width), by_expert(dp, width, hidden_width // dp),
        ],
        out_shape=[
            shape((2, group, cap, width), BF16), shape((2, width, hidden_width), BF16),
            shape((2, dp, width, hidden_width // dp), BF16),
        ],
        scratch_shapes=[pltpu.VMEM((width, hidden_width), F32), pltpu.VMEM((width, hidden_width), F32)],
        compiler_params=params(),
        cost_estimate=pl.CostEstimate(flops=int(24e9), bytes_accessed=int(4e7), transcendentals=0),
        name="expert_backward",
    )(dlow_all, code_all, grow_all, rows_in, hidden, slope, win_full, wout_full)
    grad_back = give_back(drows)

    floors = experts // 2
    in_part, ex_part = (width // dp, hidden_width), (width, hidden_width // dp)
    any_space = pl.BlockSpec(memory_space=pl.ANY)

    def vmem(*dims):
        return pltpu.VMEM(dims, BF16)

    tgrad, dense_grad, misc, gin_own, gex_own = pl.pallas_call(
        lambda *refs: back_kernel(images, *refs),
        grid=(images,),
        in_specs=[
            per_image(rows, width), whole((width, 3 * width)), whole((width, width)), whole((2, width)),
            whole((128, width)), per_image(rows, 8), whole((2 * group * cap, width)),
            per_image(rows, gate_lanes), per_image(rows, width), per_image(rows, width),
            per_image(rows, 3 * width), per_image(HEADS, rows, rows), per_image(rows, width), whole((8, 128)),
            any_space, any_space,
        ],
        out_specs=[
            per_image(rows, width), whole((shard, 4 * width)), whole((16, width)), whole(in_part), whole(ex_part),
        ],
        out_shape=[
            shape((images, rows, width), F32), shape((shard, 4 * width), F32), shape((16, width), F32),
            shape(in_part, F32), shape(ex_part, F32),
        ],
        scratch_shapes=[
            pltpu.VMEM((width, 4 * width), F32), pltpu.VMEM((16, width), F32),
            vmem(2, 2, *in_part), vmem(2, 2, *ex_part), vmem(2, 2, *in_part), vmem(2, 2, *ex_part),
            vmem(2, *in_part), vmem(2, *ex_part), vmem(2, *in_part), vmem(2, *ex_part),
            vmem(*in_part), vmem(*ex_part), vmem(*in_part), vmem(*ex_part),
            vmem(dp, floors, 2, shard, 4 * width), vmem(dp, floors, shard, 4 * width), vmem(dp, floors, shard, 4 * width),
            vmem(3, floors, shard, 4 * width), vmem(floors, shard, 4 * width), vmem(3, shard, 4 * width),
            pltpu.VMEM((10, 16, width), F32), pltpu.SemaphoreType.DMA((8,)),
            *sem_pairs(16), *sem_pairs(8), *sem_pairs(5),
        ],
        compiler_params=pltpu.CompilerParams(
            vmem_limit_bytes=60 * MB, collective_id=1, has_side_effects=True
        ),
        cost_estimate=pl.CostEstimate(flops=int(10e9), bytes_accessed=int(3e7), transcendentals=0),
        name="attention_backward",
    )(
        tok_p, qkv_full, out_full, gains, router_t, cols, grad_back, dlogits, resid, dout, qkv_p, probs, mixed,
        loss_part, gin.reshape(2, dp, *in_part), gout_t,
    )
    flat = lax.axis_index("dp") * experts + me
    mine = lax.dynamic_slice_in_dim(misc, flat * shard, shard, axis=1)
    loss_value = misc[10, 0] / valid_count

    def unpad(array):
        return array[:, :real_rows].reshape(tok_rows, width)

    return (
        unpad(block_out),
        loss_value,
        unpad(tgrad),
        mine[8],
        dense_grad[:, : 3 * width],
        dense_grad[:, 3 * width :],
        mine[9],
        mine[:experts].T,
        gin_own[None],
        gex_own.T[None],
    )


def solution(mesh):
    in_specs = (
        P(("dp", "expert"), None),
        P(("dp", "expert"), None),
        P(("dp", "expert")),
        P(("dp", "expert"), None),
        P(("dp", "expert"), None),
        P(("dp", "expert")),
        P(("dp", "expert"), None),
        P(("dp", "expert"), None),
        P(("dp", "expert")),
        P(("dp", "expert"), None),
        P("expert", "dp", None),
        P("expert", "dp", None),
    )
    out_specs = (
        P(("dp", "expert"), None),
        P(),
        P(("dp", "expert"), None),
        P(("dp", "expert")),
        P(("dp", "expert"), None),
        P(("dp", "expert"), None),
        P(("dp", "expert")),
        P(("dp", "expert"), None),
        P("expert", "dp", None),
        P("expert", "dp", None),
    )
    halves = mesh.shape["expert"] == 8 and mesh.shape["dp"] == 4
    body = fast_shards if halves else shards
    return jax.shard_map(body, mesh=mesh, in_specs=in_specs, out_specs=out_specs, check_vma=False)
```

```python
import jax
import jax.numpy as jnp
from jax import lax
from jax.experimental import pallas as pl
from jax.experimental.pallas import tpu as pltpu
from jax.sharding import PartitionSpec as P

HEADS = 8
IMG_DEV = 5


HIGH = lax.Precision.HIGHEST
EPS = 1e-06


def layer_norm(values, scale_gain):
    row_mean = jnp.mean(values, axis=-1, keepdims=True)
    centered = values - row_mean
    variance = jnp.mean(centered * centered, axis=-1, keepdims=True)
    inverse = lax.rsqrt(variance + EPS)
    normed = centered * inverse
    return (normed * scale_gain, normed, inverse)


def layer_norm_back(grad_in, normed, inverse, scale_gain):
    scaled = grad_in * scale_gain
    gain_grad = jnp.sum(grad_in * normed, axis=0)
    inner_term = (
        scaled
        - jnp.mean(scaled, axis=-1, keepdims=True)
        - normed * jnp.mean(scaled * normed, axis=-1, keepdims=True)
    )
    return (inverse * inner_term, gain_grad)


def contract_rows(left_side, right_side):
    return lax.dot_general(
        left_side, right_side, (((0,), (0,)), ((), ())), preferred_element_type=jnp.float32
    )


def contract_cols(left_side, right_side):
    return lax.dot_general(
        left_side, right_side, (((1,), (1,)), ((), ())), preferred_element_type=jnp.float32
    )


def exact_gelu(values):
    return jax.nn.gelu(values, approximate=False)


def split_heads(qkv_low, images, head_count):
    row_count, triple_width = qkv_low.shape
    head_dim = triple_width // (3 * head_count)
    pieces = qkv_low.reshape(images, row_count // images, 3, head_count, head_dim)
    return (pieces[:, :, 0], pieces[:, :, 1], pieces[:, :, 2], head_dim ** (-0.5))


def attention_forward(qkv_low, images, head_count):
    queries, key_rows, values, score_scale = split_heads(qkv_low, images, head_count)
    scores = (
        jnp.einsum("ilhd,imhd->ihlm", queries, key_rows, preferred_element_type=jnp.float32)
        * score_scale
    )
    row_max = jnp.max(scores, axis=-1, keepdims=True)
    exp_scores = jnp.exp(scores - row_max)
    row_sum = jnp.sum(exp_scores, axis=-1, keepdims=True)
    weights_low = (exp_scores / row_sum).astype(jnp.bfloat16)
    log_total = row_max + jnp.log(row_sum)
    mixed_rows = jnp.einsum(
        "ihlm,imhd->ilhd", weights_low, values, preferred_element_type=jnp.float32
    )
    return (mixed_rows.reshape(qkv_low.shape[0], -1).astype(jnp.bfloat16), log_total)


def attention_back(qkv_low, log_total, grad_mixed, images, head_count):
    queries, key_rows, values, score_scale = split_heads(qkv_low, images, head_count)
    scores = (
        jnp.einsum("ilhd,imhd->ihlm", queries, key_rows, preferred_element_type=jnp.float32)
        * score_scale
    )
    weights_full = jnp.exp(scores - log_total)
    weights_low = weights_full.astype(jnp.bfloat16)
    grad_heads = grad_mixed.reshape(queries.shape)
    grad_weights = jnp.einsum(
        "ilhd,imhd->ihlm", grad_heads, values, preferred_element_type=jnp.float32
    )
    grad_values = jnp.einsum(
        "ihlm,ilhd->imhd", weights_low, grad_heads, preferred_element_type=jnp.float32
    )
    grad_scores = weights_full * (
        grad_weights - jnp.sum(weights_full * grad_weights, axis=-1, keepdims=True)
    )
    grad_low = grad_scores.astype(jnp.bfloat16)
    grad_queries = (
        jnp.einsum("ihlm,imhd->ilhd", grad_low, key_rows, preferred_element_type=jnp.float32)
        * score_scale
    )
    grad_keys = (
        jnp.einsum("ihlm,ilhd->imhd", grad_low, queries, preferred_element_type=jnp.float32)
        * score_scale
    )
    stacked = jnp.stack([grad_queries, grad_keys, grad_values], axis=2)
    return stacked.reshape(qkv_low.shape).astype(jnp.bfloat16)


def expert_forward(rows_in, weight_in, weight_out, block_size):
    result = jnp.zeros((rows_in.shape[0], weight_out.shape[1]), jnp.float32)
    for offset in range(0, weight_in.shape[1], block_size):
        pre_act = jnp.dot(
            rows_in, weight_in[:, offset : offset + block_size], preferred_element_type=jnp.float32
        )
        hidden = exact_gelu(pre_act).astype(jnp.bfloat16)
        result = result + jnp.dot(
            hidden, weight_out[offset : offset + block_size], preferred_element_type=jnp.float32
        )
    return result


def expert_back(rows_in, weight_in, weight_out, grad_rows_out, block_size):
    grad_rows = jnp.zeros(rows_in.shape, jnp.float32)
    grads_first = []
    grads_second = []
    for offset in range(0, weight_in.shape[1], block_size):
        slice_in = weight_in[:, offset : offset + block_size]
        slice_out = weight_out[offset : offset + block_size]
        pre_act = jnp.dot(rows_in, slice_in, preferred_element_type=jnp.float32)
        hidden, gelu_back = jax.vjp(exact_gelu, pre_act)
        grads_second.append(contract_rows(hidden.astype(jnp.bfloat16), grad_rows_out))
        grad_hidden = contract_cols(grad_rows_out, slice_out)
        grad_pre = gelu_back(grad_hidden)[0].astype(jnp.bfloat16)
        grads_first.append(contract_rows(rows_in, grad_pre))
        grad_rows = grad_rows + contract_cols(grad_pre, slice_in)
    return (grad_rows, jnp.concatenate(grads_first, axis=1), jnp.concatenate(grads_second, axis=0))


def shards(
    tokens,
    targets,
    valid_mask,
    routes,
    slot_ids,
    ln1_gain,
    qkv_weight,
    out_weight,
    ln2_gain,
    router_weight,
    expert_in,
    expert_out,
):
    tok_rows, model_width = tokens.shape
    experts = lax.axis_size("expert")
    total_tokens = tok_rows * lax.axis_size("dp") * experts
    capacity = (5 * tok_rows // 2 // experts + 7) // 8 * 8
    dense_full = (
        lax.all_gather(ln1_gain, ("dp", "expert"), axis=0, tiled=True),
        lax.all_gather(qkv_weight, ("dp", "expert"), axis=0, tiled=True),
        lax.all_gather(out_weight, ("dp", "expert"), axis=0, tiled=True),
        lax.all_gather(ln2_gain, ("dp", "expert"), axis=0, tiled=True),
        lax.all_gather(router_weight, ("dp", "expert"), axis=0, tiled=True),
    )
    gain_one, qkv_full, out_full, gain_two, router_full = dense_full
    expert_full = (
        lax.all_gather(expert_in, "dp", axis=1, tiled=True),
        lax.all_gather(expert_out, "dp", axis=1, tiled=True),
    )
    weight_in = expert_full[0][0]
    weight_out = expert_full[1][0]
    valid_f = valid_mask.astype(jnp.float32)
    valid_count = lax.psum(jnp.sum(valid_f), ("dp", "expert"))
    inputs_f = tokens.astype(jnp.float32)
    gain_one_f = gain_one.astype(jnp.float32)
    gain_two_f = gain_two.astype(jnp.float32)
    norm_one, normed_one, inverse_one = layer_norm(inputs_f, gain_one_f)
    act_one = norm_one.astype(jnp.bfloat16)
    qkv_low = jnp.dot(act_one, qkv_full, preferred_element_type=jnp.float32).astype(jnp.bfloat16)
    mixed_low, log_total = attention_forward(qkv_low, IMG_DEV, HEADS)
    residual = inputs_f + jnp.dot(mixed_low, out_full, preferred_element_type=jnp.float32)
    norm_two, normed_two, inverse_two = layer_norm(residual, gain_two_f)
    act_two = norm_two.astype(jnp.bfloat16)
    gate_probs = jax.nn.softmax(
        jnp.dot(act_two, router_full, preferred_element_type=jnp.float32), axis=-1
    )
    expert_ids = lax.broadcasted_iota(jnp.int32, (1, experts), 1)
    first_pick = (routes[:, 0:1] == expert_ids).astype(jnp.float32)
    second_pick = (routes[:, 1:2] == expert_ids).astype(jnp.float32)
    gate_first = jnp.sum(gate_probs * first_pick, axis=-1, keepdims=True)
    gate_second = jnp.sum(gate_probs * second_pick, axis=-1, keepdims=True)
    target_slot = jnp.where(slot_ids < capacity, routes * capacity + slot_ids, -1)
    slot_columns = lax.broadcasted_iota(jnp.int32, (1, experts * capacity), 1)
    first_hot = (target_slot[:, 0:1] == slot_columns).astype(jnp.bfloat16)
    second_hot = (target_slot[:, 1:2] == slot_columns).astype(jnp.bfloat16)
    both_hot = first_hot + second_hot
    outgoing = contract_rows(both_hot, act_two).astype(jnp.bfloat16)
    arrived = lax.all_to_all(
        outgoing.reshape(experts, capacity, model_width),
        "expert",
        split_axis=0,
        concat_axis=0,
        tiled=True,
    ).reshape(-1, model_width)
    hidden_block = min(512, weight_in.shape[1])
    produced = expert_forward(arrived, weight_in, weight_out, hidden_block).astype(jnp.bfloat16)
    returned = lax.all_to_all(
        produced.reshape(experts, capacity, model_width),
        "expert",
        split_axis=0,
        concat_axis=0,
        tiled=True,
    ).reshape(-1, model_width)
    from_first = jnp.dot(first_hot, returned, preferred_element_type=jnp.float32)
    from_second = jnp.dot(second_hot, returned, preferred_element_type=jnp.float32)
    output = residual + gate_first * from_first + gate_second * from_second
    residue = output - targets.astype(jnp.float32)
    local_loss = jnp.sum(valid_f * jnp.mean(residue * residue, axis=-1))
    loss_sum = lax.psum(local_loss, ("dp", "expert"))
    loss_value = loss_sum / valid_count
    grad_out = total_tokens / valid_count * valid_f[:, None] * residue
    dense_back = (
        lax.all_gather(ln1_gain, ("dp", "expert"), axis=0, tiled=True),
        lax.all_gather(qkv_weight, ("dp", "expert"), axis=0, tiled=True),
        lax.all_gather(out_weight, ("dp", "expert"), axis=0, tiled=True),
        lax.all_gather(ln2_gain, ("dp", "expert"), axis=0, tiled=True),
        lax.all_gather(router_weight, ("dp", "expert"), axis=0, tiled=True),
    )
    expert_back_full = (
        lax.all_gather(expert_in, "dp", axis=1, tiled=True),
        lax.all_gather(expert_out, "dp", axis=1, tiled=True),
    )
    qkv_back = dense_back[1]
    out_back = dense_back[2]
    router_back = dense_back[4]
    weight_in_back = expert_back_full[0][0]
    weight_out_back = expert_back_full[1][0]
    slot_grads = (
        contract_rows(first_hot, (gate_first * grad_out).astype(jnp.bfloat16))
        + contract_rows(second_hot, (gate_second * grad_out).astype(jnp.bfloat16))
    ).astype(jnp.bfloat16)
    expert_grad_rows = lax.all_to_all(
        slot_grads.reshape(experts, capacity, model_width),
        "expert",
        split_axis=0,
        concat_axis=0,
        tiled=True,
    ).reshape(-1, model_width)
    grad_rows, grad_first_weight, grad_second_weight = expert_back(
        arrived, weight_in_back, weight_out_back, expert_grad_rows, hidden_block
    )
    grad_back = lax.all_to_all(
        grad_rows.astype(jnp.bfloat16).reshape(experts, capacity, model_width),
        "expert",
        split_axis=0,
        concat_axis=0,
        tiled=True,
    ).reshape(-1, model_width)
    grad_act_two = jnp.dot(both_hot, grad_back, preferred_element_type=jnp.float32)
    gate_grad = first_pick * jnp.sum(
        grad_out * from_first, axis=-1, keepdims=True
    ) + second_pick * jnp.sum(grad_out * from_second, axis=-1, keepdims=True)
    logit_grad = gate_probs * (gate_grad - jnp.sum(gate_probs * gate_grad, axis=-1, keepdims=True))
    router_f = router_back.astype(jnp.float32)
    grad_act_two = grad_act_two + lax.dot_general(
        logit_grad,
        router_f,
        (((1,), (1,)), ((), ())),
        precision=HIGH,
        preferred_element_type=jnp.float32,
    )
    router_grad = lax.dot_general(
        act_two.astype(jnp.float32),
        logit_grad,
        (((0,), (0,)), ((), ())),
        precision=HIGH,
        preferred_element_type=jnp.float32,
    )
    grad_norm_two, gain_two_grad = layer_norm_back(
        grad_act_two, normed_two, inverse_two, gain_two_f
    )
    grad_resid = grad_out + grad_norm_two
    branch_grad = grad_resid.astype(jnp.bfloat16)
    out_weight_grad = contract_rows(mixed_low, branch_grad)
    grad_mixed = contract_cols(branch_grad, out_back).astype(jnp.bfloat16)
    qkv_grad_low = attention_back(qkv_low, log_total, grad_mixed, IMG_DEV, HEADS)
    qkv_weight_grad = contract_rows(act_one, qkv_grad_low)
    grad_act_one = contract_cols(qkv_grad_low, qkv_back)
    grad_norm_one, gain_one_grad = layer_norm_back(
        grad_act_one, normed_one, inverse_one, gain_one_f
    )
    tokens_grad = grad_resid + grad_norm_one
    dense_grads = (
        lax.psum_scatter(gain_one_grad, ("dp", "expert"), scatter_dimension=0, tiled=True),
        lax.psum_scatter(qkv_weight_grad, ("dp", "expert"), scatter_dimension=0, tiled=True),
        lax.psum_scatter(out_weight_grad, ("dp", "expert"), scatter_dimension=0, tiled=True),
        lax.psum_scatter(gain_two_grad, ("dp", "expert"), scatter_dimension=0, tiled=True),
        lax.psum_scatter(router_grad, ("dp", "expert"), scatter_dimension=0, tiled=True),
    )
    expert_grads = (
        lax.psum_scatter(
            grad_first_weight[None].astype(jnp.bfloat16), "dp", scatter_dimension=1, tiled=True
        ).astype(jnp.float32),
        lax.psum_scatter(
            grad_second_weight[None].astype(jnp.bfloat16), "dp", scatter_dimension=1, tiled=True
        ).astype(jnp.float32),
    )
    first_result = expert_grads[0]
    second_result = expert_grads[1]
    return (
        output.astype(jnp.bfloat16),
        loss_value,
        tokens_grad,
        dense_grads[0],
        dense_grads[1],
        dense_grads[2],
        dense_grads[3],
        dense_grads[4],
        first_result,
        second_result,
    )


F32 = jnp.float32
BF16 = jnp.bfloat16
MB = 2**20


def round_up(value, unit):
    return (value + unit - 1) // unit * unit


def dot(left_side, right_side):
    return jnp.dot(left_side, right_side, preferred_element_type=F32)


def lane_ids(shape):
    return lax.broadcasted_iota(jnp.int32, shape, len(shape) - 1)


def row_ids(shape):
    return lax.broadcasted_iota(jnp.int32, shape, len(shape) - 2)


MESH = pl.DeviceIdType.MESH


def flip(index, bit):
    return index + bit * (1 - 2 * lax.rem(index // bit, 2))


def send(src, dst, sems, slot, device):
    return pltpu.make_async_remote_copy(
        src_ref=src, dst_ref=dst, send_sem=sems[0].at[slot], recv_sem=sems[1].at[slot],
        device_id=device, device_id_type=MESH,
    )


def greet(peers):
    barrier = pltpu.get_barrier_semaphore()
    for peer in peers:
        pl.semaphore_signal(barrier, inc=1, device_id=peer, device_id_type=MESH)
    pl.semaphore_wait(barrier, len(peers))


def place():
    dp_at, ex_at = lax.axis_index("dp"), lax.axis_index("expert")
    near = [None, flip(dp_at, 1), flip(dp_at, 2), flip(flip(dp_at, 1), 2)]
    return dp_at, ex_at, near


def sem_pairs(count):
    return [pltpu.SemaphoreType.DMA((count,)), pltpu.SemaphoreType.DMA((count,))]


def normalize(values):
    centered = values - jnp.mean(values, axis=-1, keepdims=True)
    inverse = lax.rsqrt(jnp.mean(centered * centered, axis=-1, keepdims=True) + EPS)
    return centered * inverse, inverse


def gelu_pair(values):
    size = jnp.abs(values)
    inv = 1.0 / (1.0 + 0.2316419 * size)
    density = 0.3989422804014327 * jnp.exp(-0.5 * values * values)
    series = inv * (
        0.319381530
        + inv * (-0.356563782 + inv * (1.781477937 + inv * (-1.821255978 + inv * 1.330274429)))
    )
    tail = density * series
    cumulative = jnp.where(values >= 0, 1.0 - tail, tail)
    return values * cumulative, cumulative + values * density


def plane_gather(blocks, sems, base, dp_at, ex_at, near):
    half = blocks.shape[1] // 2
    first, second = pl.ds(0, half), pl.ds(half, half)
    own = [
        send(blocks.at[dp_at], blocks.at[dp_at], sems, base + k - 1, (near[k], ex_at)) for k in (1, 2)
    ]
    passed = [
        send(blocks.at[near[1], first], blocks.at[near[1], first], sems, base + 2, (near[2], ex_at)),
        send(blocks.at[near[2], second], blocks.at[near[2], second], sems, base + 3, (near[1], ex_at)),
    ]
    return own, passed


def group_copies(images, step, buf, dest, tsem, lsem, dp_at, ex_at):
    mate, across = flip(ex_at, 1), flip(ex_at, 2)
    keep = pltpu.make_async_copy(buf.at[step], dest.at[0, step], lsem.at[step])
    to_mate = send(buf.at[step], dest.at[1, step], tsem, step, (dp_at, mate))
    to_chip = send(buf.at[step], dest.at[2, step], tsem, images + step, (dp_at, across))
    onward = send(dest.at[2, step], dest.at[3, step], tsem, 2 * images + step, (dp_at, mate))
    return keep, to_mate, to_chip, onward


def forward_kernel(
    images, real_rows, experts, tok_ref, qkvw_ref, outw_ref, extra_ref, cols_ref, rows_ref, codes_ref, win_ref, wex_ref,
    qkv_ref, probs_ref, mixed_ref, resid_ref, gates_ref, dense_ref, ext_ref,
    act_all, code_all, grow_all, win_all, wex_all, far_in,
    dense, act_buf, grow_buf, d_send, d_recv, t_send, t_recv, r_send, r_recv, w_send, w_recv, local_sem,
):
    step_at = pl.program_id(0)
    dp_at, ex_at, near = place()
    core, floor = lax.rem(ex_at, 2), ex_at // 2
    dsem, tsem, rsem, wsem = (d_send, d_recv), (t_send, t_recv), (r_send, r_recv), (w_send, w_recv)
    group_peers = [(dp_at, flip(ex_at, 1)), (dp_at, flip(ex_at, 2)), (dp_at, flip(flip(ex_at, 1), 2))]
    floors = [floor, flip(floor, 1), flip(floor, 2), flip(flip(floor, 1), 2)]
    columns = [dp_at] + near[1:]

    codes_out = [send(codes_ref, code_all.at[k + 1], rsem, k, group_peers[k]) for k in range(3)]
    grow_out = [send(grow_buf, grow_all.at[k + 1], rsem, 3 + k, group_peers[k]) for k in range(3)]
    keeps = [
        pltpu.make_async_copy(codes_ref, code_all.at[0], local_sem.at[images]),
        pltpu.make_async_copy(win_ref, win_all.at[dp_at], local_sem.at[images + 1]),
        pltpu.make_async_copy(wex_ref, wex_all.at[dp_at], local_sem.at[images + 2]),
    ]
    keep_grow = pltpu.make_async_copy(grow_buf, grow_all.at[0], local_sem.at[images + 3])
    in_own, in_passed = plane_gather(win_all, wsem, 0, dp_at, ex_at, near)
    ex_own, ex_passed = plane_gather(wex_all, wsem, 4, dp_at, ex_at, near)
    to_far = send(win_ref, far_in, wsem, 8, (dp_at, flip(ex_at, 4)))
    along_line = [
        send(dense.at[dp_at, floor, core], dense.at[dp_at, floor, core], dsem, k - 1, (dp_at, 2 * floors[k] + core))
        for k in (1, 2, 3)
    ]
    in_plane = [
        [
            send(
                dense.at[dp_at, floors[k], core], dense.at[dp_at, floors[k], core], dsem, 3 + 3 * k + p - 1,
                (near[p], ex_at),
            )
            for p in (1, 2, 3)
        ]
        for k in range(4)
    ]
    to_mate = [
        send(dense.at[columns[p], :, core], dense.at[columns[p], :, core], dsem, 15 + p, group_peers[0])
        for p in range(4)
    ]

    @pl.when(step_at == 0)
    def _():
        for copy in keeps:
            copy.start()
        width = outw_ref.shape[1]
        dense[dp_at, floor, core, :, : 3 * width] = qkvw_ref[...]
        dense[dp_at, floor, core, :, 3 * width : 4 * width] = outw_ref[...]
        dense[dp_at, floor, core, :, 4 * width :] = extra_ref[...]
        greet(
            [(near[k], ex_at) for k in (1, 2, 3)]
            + group_peers
            + [(dp_at, flip(ex_at, 4)), (dp_at, flip(flip(ex_at, 2), 4))]
        )
        for copy in along_line + in_plane[0]:
            copy.start()
        for k in (1, 2, 3):
            along_line[k - 1].wait_recv()
            for copy in in_plane[k]:
                copy.start()
        to_mate[0].start()
        for copy in codes_out:
            copy.start()
        for p in (1, 2, 3):
            for k in range(4):
                in_plane[k][p - 1].wait_recv()
            to_mate[p].start()
        for copy in keeps:
            copy.wait()
        for copy in in_own + ex_own + [to_far]:
            copy.start()
        for copy in to_mate:
            copy.wait_recv()
        full = dense[...].reshape(dense_ref.shape)
        dense_ref[...] = full
        ext_ref[...] = full[:, 4 * width :].astype(F32).T

    inputs = tok_ref[...].astype(F32)
    normed, _ = normalize(inputs)
    width = inputs.shape[1]
    act_one = (normed * ext_ref[experts : experts + 1, :]).astype(BF16)
    qkv = dot(act_one, dense_ref[:, : 3 * width]).astype(BF16)
    qkv_ref[...] = qkv
    rows = inputs.shape[0]
    low_half = lane_ids((1, 128)) < 64
    key_bias = jnp.where(lane_ids((1, rows)) < real_rows, 0.0, -1e30)
    parts = []
    for pair in range(width // 128):
        lanes = slice(128 * pair, 128 * (pair + 1))
        queries = qkv[:, lanes]
        key_rows = qkv[:, width + 128 * pair : width + 128 * (pair + 1)]
        values = qkv[:, 2 * width + 128 * pair : 2 * width + 128 * (pair + 1)]
        outs = []
        for side in range(2):
            mask = low_half if side == 0 else jnp.logical_not(low_half)
            masked = jnp.where(mask, queries, jnp.zeros_like(queries))
            scores = contract_cols(masked, key_rows) * 0.125 + key_bias
            exped = jnp.exp(scores - jnp.max(scores, axis=-1, keepdims=True))
            probs = (exped * (1.0 / jnp.sum(exped, axis=-1, keepdims=True))).astype(BF16)
            probs_ref[2 * pair + side] = probs
            outs.append(dot(probs, values))
        parts.append(jnp.where(low_half, outs[0], outs[1]).astype(BF16))
    mixed = jnp.concatenate(parts, axis=1)
    mixed_ref[...] = mixed
    resid = inputs + dot(mixed, dense_ref[:, 3 * width : 4 * width])
    resid_ref[...] = resid
    normed_two, _ = normalize(resid)
    act_two = (normed_two * ext_ref[experts + 1 : experts + 2, :]).astype(BF16)
    act_buf[step_at] = act_two
    lanes = lane_ids((1, 128))
    logits = jnp.where(lanes < experts, dot(act_two, dense_ref[:, 4 * width :]), -1e30)
    exped = jnp.exp(logits - jnp.max(logits, axis=-1, keepdims=True))
    gates = exped / jnp.sum(exped, axis=-1, keepdims=True)
    cols = cols_ref[...]
    first = jnp.sum(jnp.where(lanes == cols[:, 2:3], gates, 0.0), axis=-1, keepdims=True)
    second = jnp.sum(jnp.where(lanes == cols[:, 3:4], gates, 0.0), axis=-1, keepdims=True)
    gates_ref[...] = jnp.where(lanes == experts, first, jnp.where(lanes == experts + 1, second, gates))
    logits_t = contract_cols(ext_ref[0:16, :].astype(BF16), act_two)[:experts]
    exped_t = jnp.exp(logits_t - jnp.max(logits_t, axis=0, keepdims=True))
    gates_t = exped_t / jnp.sum(exped_t, axis=0, keepdims=True)
    ids_t = row_ids(gates_t.shape)
    first_t = jnp.sum(jnp.where(ids_t == rows_ref[2:3, :], gates_t, 0.0), axis=0, keepdims=True)
    second_t = jnp.sum(jnp.where(ids_t == rows_ref[3:4, :], gates_t, 0.0), axis=0, keepdims=True)
    grow_buf[step_at] = jnp.where(row_ids((8, rows)) == 0, first_t, second_t)

    for step in range(images):
        keep, mate_copy, chip_copy, _ = group_copies(images, step, act_buf, act_all, tsem, local_sem, dp_at, ex_at)

        @pl.when(step_at == step)
        def _():
            keep.start()
            mate_copy.start()
            chip_copy.start()

    def pass_on(step):
        _, _, chip_copy, onward = group_copies(images, step, act_buf, act_all, tsem, local_sem, dp_at, ex_at)
        chip_copy.wait_recv()
        onward.start()

    for step in range(images - 2):

        @pl.when(step_at == step + 2)
        def _():
            pass_on(step)

    @pl.when(step_at == images - 2)
    def _():
        in_own[0].wait_recv()
        in_passed[0].start()
        in_own[1].wait_recv()
        in_passed[1].start()

    @pl.when(step_at == images - 1)
    def _():
        keep_grow.start()
        for copy in grow_out:
            copy.start()
        ex_own[0].wait_recv()
        ex_passed[0].start()
        ex_own[1].wait_recv()
        ex_passed[1].start()
        for step in (images - 2, images - 1):
            pass_on(step)
        for step in range(images):
            keep, mate_copy, chip_copy, onward = group_copies(
                images, step, act_buf, act_all, tsem, local_sem, dp_at, ex_at
            )
            keep.wait()
            mate_copy.wait()
            chip_copy.wait_send()
            onward.wait()
        keep_grow.wait()
        for copy in codes_out + grow_out + in_passed + ex_passed + [to_far]:
            copy.wait()
        for copy in along_line + to_mate + in_own + ex_own + [c for line in in_plane for c in line]:
            copy.wait_send()


def hot_rows(codes, start, count):
    slots = row_ids((count, codes.shape[1])) + start
    return (slots == codes[0:1, :]) | (slots == codes[1:2, :])


def return_copies(buf, back, q, half, sems, local, dp_at, ex_at):
    peers = [None, (dp_at, flip(ex_at, 1)), (dp_at, flip(ex_at, 2)), (dp_at, flip(flip(ex_at, 1), 2))]
    copies = []
    for k in (2 * half, 2 * half + 1):
        if k == 0:
            copies.append(pltpu.make_async_copy(buf.at[q, 0], back.at[q, 0], local.at[q]))
        else:
            copies.append(send(buf.at[q, k], back.at[q, k], sems, 4 * q + k, peers[k]))
    return copies


def expert_forward_kernel(
    cap, group, act_ref, codes_ref, win_own, wex_own, win_far, wex_mine,
    rows_out_ref, hidden_ref, slope_ref, back_ref, win_other, wex_other,
    win_buf, wex_buf, out_buf, y_send, y_recv, w_send, w_recv, local_sem,
):
    which, half_step = pl.program_id(0), pl.program_id(1)
    half = 1 - half_step
    dp_at, ex_at, near = place()
    ysem, wsem = (y_send, y_recv), (w_send, w_recv)
    keep_in = pltpu.make_async_copy(win_far, win_other.at[dp_at], local_sem.at[2])
    loads = [
        pltpu.make_async_copy(win_own, win_buf.at[0], local_sem.at[3]),
        pltpu.make_async_copy(wex_own, wex_buf.at[0], local_sem.at[4]),
        pltpu.make_async_copy(win_other, win_buf.at[1], local_sem.at[5]),
        pltpu.make_async_copy(wex_other, wex_buf.at[1], local_sem.at[6]),
    ]
    in_own, in_passed = plane_gather(win_other, wsem, 0, dp_at, ex_at, near)
    ex_own, ex_passed = plane_gather(wex_other, wsem, 4, dp_at, ex_at, near)
    to_far = send(wex_mine, wex_other.at[dp_at], wsem, 8, (dp_at, flip(ex_at, 4)))

    def at(q, step):
        return pl.when((which == q) & (half_step == step))

    @at(0, 0)
    def _():
        keep_in.start()
        loads[0].start()
        loads[1].start()
        greet(
            [(near[k], ex_at) for k in (1, 2)]
            + [(dp_at, flip(ex_at, 1)), (dp_at, flip(ex_at, 2)), (dp_at, flip(flip(ex_at, 1), 2)), (dp_at, flip(ex_at, 4))]
        )
        to_far.start()
        keep_in.wait()
        for copy in in_own:
            copy.start()
        loads[0].wait()
        loads[1].wait()

    @at(1, 0)
    def _():
        for copy in in_passed:
            copy.wait_recv()
        loads[2].start()
        loads[2].wait()

    blocks, images = act_ref.shape[0], act_ref.shape[1]
    parts, width, hidden_width = win_buf.shape[1], act_ref.shape[3], win_buf.shape[3]
    pieces = []
    for block in range(blocks):
        start = (which * group + half * blocks + block) * cap
        total = None
        for image in range(images):
            hot = jnp.where(hot_rows(codes_ref[block, image], start, cap), 1.0, 0.0).astype(BF16)
            term = dot(hot, act_ref[block, image])
            total = term if total is None else total + term
        pieces.append(total.astype(BF16))
    rows_in = jnp.concatenate(pieces, axis=0)
    rows_out_ref[...] = rows_in.reshape(rows_out_ref.shape)
    step = hidden_width // parts
    for part in range(parts):
        cut = slice(part * step, (part + 1) * step)
        act, slope = gelu_pair(dot(rows_in, win_buf[which, :, :, cut].reshape(width, step)))
        hidden_ref[:, :, cut] = act.astype(BF16).reshape(blocks, cap, step)
        slope_ref[:, :, cut] = slope.astype(BF16).reshape(blocks, cap, step)

    @at(1, 0)
    def _():
        for own, passed in zip(ex_own, ex_passed):
            own.wait_recv()
            passed.start()
        for copy in ex_passed:
            copy.wait_recv()
        loads[3].start()
        loads[3].wait()

    result = None
    for part in range(parts):
        cut = slice(part * step, (part + 1) * step)
        term = dot(hidden_ref[:, :, cut].reshape(blocks * cap, step), wex_buf[which, part])
        result = term if result is None else result + term
    out_buf[which, pl.ds(half * blocks, blocks)] = result.astype(BF16).reshape(blocks, cap, width)

    for q in range(2):
        for step_at in range(2):

            @at(q, step_at)
            def _():
                for copy in return_copies(out_buf, back_ref, q, 1 - step_at, ysem, local_sem, dp_at, ex_at):
                    copy.start()

    @at(0, 0)
    def _():
        in_own[0].wait_recv()
        in_passed[0].start()
        in_own[1].wait_recv()
        in_passed[1].start()

    @at(0, 1)
    def _():
        to_far.wait_recv()
        for copy in ex_own:
            copy.start()

    @at(1, 1)
    def _():
        for q in range(2):
            for step_at in range(2):
                for copy in return_copies(out_buf, back_ref, q, 1 - step_at, ysem, local_sem, dp_at, ex_at):
                    copy.wait()
        for copy in in_own + in_passed + ex_own + ex_passed + [to_far]:
            copy.wait_send()


def hot_cols(codes, count):
    return lane_ids((codes.shape[0], count)) == codes


def combine_kernel(
    images, total_tokens, shard, experts, ext_ref, resid_ref, back_ref, cols_ref, gates_ref, target_ref, valid_ref,
    out_ref, dout_ref, dlogit_ref, loss_ref, dlow_all,
    dlow_buf, t_send, t_recv, local_sem,
):
    step_at = pl.program_id(0)
    dp_at, ex_at, _ = place()
    tsem = (t_send, t_recv)

    @pl.when(step_at == 0)
    def _():
        greet([(dp_at, flip(ex_at, 1)), (dp_at, flip(ex_at, 2))])

    count = back_ref.shape[0]
    cols = cols_ref[...]
    rows = cols.shape[0]
    hot = jnp.concatenate(
        [
            jnp.where(hot_cols(cols[:, 0:1], count), 1.0, 0.0).astype(BF16),
            jnp.where(hot_cols(cols[:, 1:2], count), 1.0, 0.0).astype(BF16),
        ],
        axis=0,
    )
    both = dot(hot, back_ref[...])
    from_first, from_second = both[:rows], both[rows:]
    gates = gates_ref[...]
    first, second = gates[:, experts : experts + 1], gates[:, experts + 1 : experts + 2]
    output = resid_ref[...] + first * from_first + second * from_second
    out_ref[...] = output.astype(BF16)
    residue = output - target_ref[...].astype(F32)
    valid = valid_ref[...]
    square = jnp.mean(residue * residue, axis=-1, keepdims=True) * valid[:, 0:1]

    @pl.when(pl.program_id(0) == 0)
    def _():
        loss_ref[...] = jnp.zeros_like(loss_ref)

    counts = jnp.sum(ext_ref[experts + 2 : experts + 4, :], axis=-1, keepdims=True)
    count_all = (counts[0:1] * 128.0 + counts[1:2]) / shard
    loss_ref[...] += jnp.sum(square) / count_all
    dout = (total_tokens / count_all * valid[:, 0:1]) * residue
    dout_ref[...] = dout
    dlow_buf[step_at] = dout.astype(BF16)
    lanes = lane_ids((1, 128))
    grad = jnp.where(
        lanes == cols[:, 2:3], jnp.sum(dout * from_first, axis=-1, keepdims=True), 0.0
    ) + jnp.where(lanes == cols[:, 3:4], jnp.sum(dout * from_second, axis=-1, keepdims=True), 0.0)
    real = jnp.where(lanes < experts, gates, 0.0)
    dlogit_ref[...] = real * (grad - jnp.sum(real * grad, axis=-1, keepdims=True))

    def copies(step):
        return group_copies(images, step, dlow_buf, dlow_all, tsem, local_sem, dp_at, ex_at)

    for step in range(images):

        @pl.when(step_at == step)
        def _():
            for copy in copies(step)[:3]:
                copy.start()
            if step >= 2:
                copies(step - 2)[2].wait_recv()
                copies(step - 2)[3].start()

    @pl.when(step_at == images - 1)
    def _():
        for step in (images - 2, images - 1):
            copies(step)[2].wait_recv()
            copies(step)[3].start()
        for step in range(images):
            keep, to_mate, to_chip, onward = copies(step)
            keep.wait()
            to_mate.wait()
            to_chip.wait_send()
            onward.wait()


def expert_back_kernel(
    cap, group, dlow_ref, codes_ref, grow_ref, rows_ref, hidden_ref, slope_ref, win_own, wex_own, win_other, wex_other,
    back_ref, gin_ref, gex_ref, got_in, got_ex,
    win_buf, wex_buf, acc_in, acc_out, low_in, low_ex, out_buf, y_send, y_recv, w_send, w_recv, local_sem,
):
    which_step, half_step = pl.program_id(0), pl.program_id(1)
    which, half = 1 - which_step, 1 - half_step
    dp_at, ex_at, near = place()
    ysem, wsem = (y_send, y_recv), (w_send, w_recv)
    loads = [
        pltpu.make_async_copy(win_own, win_buf.at[0], local_sem.at[3]),
        pltpu.make_async_copy(wex_own, wex_buf.at[0], local_sem.at[4]),
        pltpu.make_async_copy(win_other, win_buf.at[1], local_sem.at[5]),
        pltpu.make_async_copy(wex_other, wex_buf.at[1], local_sem.at[6]),
    ]
    stores = [
        pltpu.make_async_copy(low_in.at[0], gin_ref.at[0], local_sem.at[7]),
        pltpu.make_async_copy(low_ex.at[0], gex_ref.at[0], local_sem.at[8]),
        pltpu.make_async_copy(low_in.at[1], gin_ref.at[1], local_sem.at[9]),
        pltpu.make_async_copy(low_ex.at[1], gex_ref.at[1], local_sem.at[10]),
    ]
    spread = []
    for t, (grad, got, first) in enumerate(((low_in, got_in, 1), (low_ex, got_ex, 2))):
        for s, owner in enumerate((near[first], near[3])):
            spread.append(send(grad.at[1, owner], got.at[s], wsem, 2 * t + s, (near[first], ex_at)))

    def at(q, step):
        return pl.when((which == q) & (half_step == step))

    @at(1, 0)
    def _():
        for copy in (loads[2], loads[3], loads[0], loads[1]):
            copy.start()
        greet(
            [(near[k], ex_at) for k in (1, 2)]
            + [(dp_at, flip(ex_at, 1)), (dp_at, flip(ex_at, 2)), (dp_at, flip(flip(ex_at, 1), 2))]
        )
        for copy in loads:
            copy.wait()

    blocks, images = dlow_ref.shape[0], dlow_ref.shape[1]
    parts, width, hidden_width = win_buf.shape[1], dlow_ref.shape[3], win_buf.shape[3]
    pieces = []
    for block in range(blocks):
        start = (which * group + half * blocks + block) * cap
        total = None
        slot_gate = None
        for image in range(images):
            codes = codes_ref[block, image]
            slots = row_ids((cap, codes.shape[1])) + start
            is_first = slots == codes[0:1, :]
            is_second = slots == codes[1:2, :]
            hot = jnp.where(is_first | is_second, 1.0, 0.0).astype(BF16)
            term = dot(hot, dlow_ref[block, image])
            gain = grow_ref[block, image]
            picked = jnp.where(is_first, gain[0:1, :], jnp.where(is_second, gain[1:2, :], 0.0))
            picked = jnp.sum(picked, axis=-1, keepdims=True)
            total = term if total is None else total + term
            slot_gate = picked if slot_gate is None else slot_gate + picked
        pieces.append((total * slot_gate).astype(BF16))
    grads = jnp.concatenate(pieces, axis=0)
    grads_t = grads.T
    rows_in_t = rows_ref[...].reshape(blocks * cap, -1).T
    step = hidden_width // parts
    result = None
    for offset in range(0, hidden_width, step):
        cut = slice(offset, offset + step)
        hidden = hidden_ref[:, :, cut].reshape(blocks * cap, step)
        slope = slope_ref[:, :, cut].reshape(blocks * cap, step).astype(F32)
        dpre = (contract_cols(grads, wex_buf[which, offset // step]) * slope).astype(BF16)
        gin = dot(rows_in_t, dpre)
        gout = dot(grads_t, hidden)
        term = contract_cols(dpre, win_buf[which, :, :, cut].reshape(width, step))
        result = term if result is None else result + term

        @pl.when(half_step == 0)
        def _():
            acc_in[:, cut] = gin
            acc_out[:, cut] = gout

        @pl.when(half_step == 1)
        def _():
            total_in = (acc_in[:, cut] + gin).astype(BF16)
            low_in[which, :, :, cut] = total_in.reshape(parts, width // parts, step)
            low_ex[which, offset // step] = (acc_out[:, cut] + gout).astype(BF16)

    out_buf[which, pl.ds(half * blocks, blocks)] = result.astype(BF16).reshape(blocks, cap, width)

    for q in range(2):
        for step_at in range(2):

            @at(q, step_at)
            def _():
                for copy in return_copies(out_buf, back_ref, q, 1 - step_at, ysem, local_sem, dp_at, ex_at):
                    copy.start()

    @at(1, 1)
    def _():
        for copy in spread + stores[2:]:
            copy.start()

    @at(0, 1)
    def _():
        for copy in stores[:2]:
            copy.start()
        for q in range(2):
            for step_at in range(2):
                for copy in return_copies(out_buf, back_ref, q, 1 - step_at, ysem, local_sem, dp_at, ex_at):
                    copy.wait()
        for copy in spread + stores:
            copy.wait()


def back_kernel(
    images, experts, tok_ref, dense_w, ext_ref, cols_ref, back_ref, dlogit_ref, resid_ref,
    dout_ref, qkv_ref, probs_ref, mixed_ref, loss_ref, gin_ref, gex_ref, got_in_ref, got_ex_ref,
    tgrad_ref, dense_ref, misc_ref, gin_out, gex_out,
    acc, acc_misc, part_in, part_ex, got_in, got_ex, sum_in, sum_ex, more_in, more_ex, far_in, far_ex, came_in, came_ex,
    low, mate, low_mate, plane, low_plane, line, misc_got, local_sem, w_send, w_recv, d_send, d_recv, m_send, m_recv,
):
    step_at = pl.program_id(0)
    dp_at, ex_at, near = place()
    core, floor = lax.rem(ex_at, 2), ex_at // 2
    wsem, dsem, msem = (w_send, w_recv), (d_send, d_recv), (m_send, m_recv)
    tensors = [
        (gin_ref, part_in, got_in, sum_in, more_in, far_in, came_in, gin_out, 1, 2),
        (gex_ref, part_ex, got_ex, sum_ex, more_ex, far_ex, came_ex, gex_out, 2, 1),
    ]

    def local_copies():
        copies = []
        for t, (grad, part, _, _, _, _, _, _, _, second) in enumerate(tensors):
            for q in range(2):
                for s in range(2):
                    owner = dp_at if s == 0 else near[second]
                    copies.append(
                        pltpu.make_async_copy(grad.at[q, owner], part.at[q, s], local_sem.at[4 * t + 2 * q + s])
                    )
        copies.append(pltpu.make_async_copy(got_in_ref, got_in.at[1], local_sem.at[8]))
        copies.append(pltpu.make_async_copy(got_ex_ref, got_ex.at[1], local_sem.at[9]))
        return copies

    def first_round(q):
        copies = []
        for t, (grad, _, got, _, _, _, _, _, first, _) in enumerate(tensors):
            for s in range(2):
                owner = near[first] if s == 0 else near[3]
                copies.append(
                    send(grad.at[q, owner], got.at[q, s], wsem, 8 * q + 4 * t + s, (near[first], ex_at))
                )
        return copies

    def second_round(q):
        return [
            send(passed.at[q], more.at[q], wsem, 8 * q + 4 * t + 2, (near[second], ex_at))
            for t, (_, _, _, passed, more, _, _, _, _, second) in enumerate(tensors)
        ]

    def far_round():
        return [
            send(far, came, wsem, 4 * t + 3, (dp_at, flip(ex_at, 4)))
            for t, (_, _, _, _, _, far, came, _, _, _) in enumerate(tensors)
        ]

    def add_first(q):
        for _, part, got, passed, _, _, _, _, _, _ in tensors:
            passed[q] = (part[q, 1].astype(F32) + got[q, 1].astype(F32)).astype(BF16)
        for copy in second_round(q):
            copy.start()

    def total_of(tensor, q):
        _, part, got, _, more, _, _, _, _, _ = tensor
        return part[q, 0].astype(F32) + got[q, 0].astype(F32) + more[q].astype(F32)

    @pl.when(step_at == 0)
    def _():
        for copy in local_copies():
            copy.start()
        greet(
            [(near[k], ex_at) for k in (1, 2, 3)]
            + [(dp_at, flip(ex_at, bit)) for bit in (1, 2, 4)]
            + [(dp_at, flip(flip(ex_at, 2), 4))]
        )
        for copy in local_copies():
            copy.wait()
        add_first(1)

    count = back_ref.shape[0]
    cols = cols_ref[...]
    hot = jnp.where(hot_cols(cols[:, 0:1], count) | hot_cols(cols[:, 1:2], count), 1.0, 0.0)
    dlogits = dlogit_ref[...]
    dact = dot(hot.astype(BF16), back_ref[...])
    dlogits_high = dlogits.astype(BF16)
    router_t = ext_ref[...].astype(BF16)
    dlogits_low = (dlogits - dlogits_high.astype(F32)).astype(BF16)
    dact = dact + dot(dlogits_high, router_t) + dot(dlogits_low, router_t)

    resid = resid_ref[...]
    normed_two, inverse_two = normalize(resid)
    gain_two = ext_ref[experts + 1 : experts + 2, :]
    act_two = (normed_two * gain_two).astype(BF16)
    grouter = contract_rows(dlogits_high, act_two) + contract_rows(dlogits_low, act_two)

    def norm_back(grad, normed, inverse, gain):
        scaled = grad * gain
        gain_grad = jnp.sum(grad * normed, axis=0, keepdims=True)
        inner = (
            scaled
            - jnp.mean(scaled, axis=-1, keepdims=True)
            - normed * jnp.mean(scaled * normed, axis=-1, keepdims=True)
        )
        return inverse * inner, gain_grad

    grad_two, ggain_two = norm_back(dact, normed_two, inverse_two, gain_two)
    dresid = dout_ref[...] + grad_two
    branch = dresid.astype(BF16)
    mixed = mixed_ref[...]
    gout = contract_rows(mixed, branch)
    width = branch.shape[1]
    dmixed = contract_cols(branch, dense_w[:, 3 * width : 4 * width]).astype(BF16)
    qkv = qkv_ref[...]
    low_half = lane_ids((1, 128)) < 64
    dqs, dks, dvs = [], [], []
    for pair in range(width // 128):
        cut = slice(128 * pair, 128 * (pair + 1))
        queries = qkv[:, cut]
        key_rows = qkv[:, width + 128 * pair : width + 128 * (pair + 1)]
        values = qkv[:, 2 * width + 128 * pair : 2 * width + 128 * (pair + 1)]
        dmix = dmixed[:, cut]
        dq = []
        dk = dv = None
        for side in range(2):
            mask = low_half if side == 0 else jnp.logical_not(low_half)
            dmask = jnp.where(mask, dmix, jnp.zeros_like(dmix))
            qmask = jnp.where(mask, queries, jnp.zeros_like(queries))
            probs_low = probs_ref[2 * pair + side]
            probs = probs_low.astype(F32)
            dprobs = contract_cols(dmask, values)
            dscore = probs * (dprobs - jnp.sum(probs * dprobs, axis=-1, keepdims=True))
            dscore = dscore.astype(BF16)
            dq.append(dot(dscore, key_rows))
            dk_term = contract_rows(dscore, qmask)
            dv_term = contract_rows(probs_low, dmask)
            dk = dk_term if dk is None else dk + dk_term
            dv = dv_term if dv is None else dv + dv_term
        dqs.append((jnp.where(low_half, dq[0], dq[1]) * 0.125).astype(BF16))
        dks.append((dk * 0.125).astype(BF16))
        dvs.append(dv.astype(BF16))
    dqkv = jnp.concatenate(dqs + dks + dvs, axis=1)
    inputs = tok_ref[...].astype(F32)
    normed_one, inverse_one = normalize(inputs)
    gain_one = ext_ref[experts : experts + 1, :]
    act_one = (normed_one * gain_one).astype(BF16)
    gqkv = contract_rows(act_one, dqkv)
    dact_one = contract_cols(dqkv, dense_w[:, : 3 * width])
    grad_one, ggain_one = norm_back(dact_one, normed_one, inverse_one, gain_one)
    tgrad_ref[...] = dresid + grad_one
    ids = row_ids((8, width))
    gmisc = jnp.concatenate(
        [grouter[:8], jnp.where(ids == 0, ggain_one, jnp.where(ids == 1, ggain_two, 0.0))], axis=0
    )

    @pl.when(step_at == 0)
    def _():
        acc[:, : 3 * width] = gqkv
        acc[:, 3 * width :] = gout
        loss_row = jnp.where(row_ids((8, 128)) == 2, loss_ref[...], 0.0)
        acc_misc[...] = gmisc + jnp.concatenate(
            [jnp.zeros((8, width), F32), jnp.concatenate([loss_row] * (width // 128), axis=1)], axis=0
        )

    @pl.when(step_at > 0)
    def _():
        acc[:, : 3 * width] += gqkv
        acc[:, 3 * width :] += gout
        acc_misc[...] += gmisc

    @pl.when(step_at == 1)
    def _():
        for copy in second_round(1):
            copy.wait_recv()
        for tensor in tensors:
            tensor[5][...] = total_of(tensor, 1).astype(BF16)
        for copy in far_round() + first_round(0):
            copy.start()

    @pl.when(step_at == images - 1)
    def _():
        lines, shard = low.shape[1], low.shape[3]
        low[...] = acc[...].astype(BF16).reshape(low.shape)
        other = lax.rem(core + 1, 2)
        to_mate = send(low.at[:, :, other], mate, dsem, 0, (dp_at, flip(ex_at, 1)))
        to_mate.start()
        misc_peers = [
            (dp_at, flip(ex_at, 1)), (near[1], ex_at), (near[2], ex_at), (dp_at, flip(ex_at, 2)), (dp_at, flip(ex_at, 4)),
        ]
        misc = [send(acc_misc.at[...] if k == 0 else misc_got.at[5 + k - 1], misc_got.at[k], msem, k, misc_peers[k]) for k in range(5)]
        misc[0].start()

        def misc_step(k):
            misc[k].wait_recv()
            before = acc_misc[...] if k == 0 else misc_got[5 + k - 1]
            misc_got[5 + k] = before + misc_got[k]
            if k < 4:
                misc[k + 1].start()

        for copy in first_round(0):
            copy.wait_recv()
        add_first(0)
        to_mate.wait_recv()
        low_mate[...] = (low[:, :, core].astype(F32) + mate[...].astype(F32)).astype(BF16)
        to_plane = [send(low_mate.at[near[k]], plane.at[k - 1], dsem, k, (near[k], ex_at)) for k in (1, 2, 3)]
        for copy in to_plane:
            copy.start()
        misc_step(0)
        misc_step(1)
        misc_step(2)
        for copy in to_plane:
            copy.wait_recv()
        summed = low_mate[dp_at].astype(F32)
        for k in range(3):
            summed = summed + plane[k].astype(F32)
        low_plane[...] = summed.astype(BF16)
        floors = [flip(floor, 1), flip(floor, 2), flip(flip(floor, 1), 2)]
        to_line = [
            send(low_plane.at[floors[k]], line.at[k], dsem, 4 + k, (dp_at, 2 * floors[k] + core)) for k in range(3)
        ]
        for copy in to_line:
            copy.start()
        misc_step(3)
        misc_step(4)
        misc_ref[...] = misc_got[9]
        for copy in to_line:
            copy.wait_recv()
        result = low_plane[floor].astype(F32)
        for k in range(3):
            result = result + line[k].astype(F32)
        dense_ref[...] = result

        for copy in second_round(0):
            copy.wait_recv()
        for copy in far_round():
            copy.wait_recv()
        for tensor in tensors:
            tensor[7][...] = total_of(tensor, 0) + tensor[6][...].astype(F32)
        for copy in [to_mate] + misc + to_plane + to_line + first_round(0):
            copy.wait_send()
        for copy in second_round(0) + second_round(1) + far_round():
            copy.wait_send()


def shape(dims, kind):
    return jax.ShapeDtypeStruct(dims, kind)


def whole(dims):
    return pl.BlockSpec(dims, lambda *_: (0,) * len(dims))


def per_image(*dims):
    return pl.BlockSpec((None,) + dims, lambda i: (i,) + (0,) * len(dims))


def params():
    return pltpu.CompilerParams(vmem_limit_bytes=56 * MB)


def fast_shards(
    tokens, targets, valid_mask, routes, slot_ids, ln1_gain, qkv_weight, out_weight, ln2_gain,
    router_weight, expert_in, expert_out,
):
    axes = ("dp", "expert")
    tok_rows, width = tokens.shape
    experts = lax.axis_size("expert")
    group = experts // 2
    dp = lax.axis_size("dp")
    total_tokens = tok_rows * dp * experts
    hidden_width = expert_in.shape[2]
    capacity = (5 * tok_rows // 2 // experts + 7) // 8 * 8
    cap = round_up(capacity, 16)
    images = IMG_DEV
    real_rows = tok_rows // images
    rows = round_up(real_rows, 16)
    me = lax.axis_index("expert")

    def pad_rows(array, value=0):
        array = array.reshape(images, real_rows, -1)
        return jnp.pad(array, ((0, 0), (0, rows - real_rows), (0, 0)), constant_values=value)

    valid_f = valid_mask.astype(F32)
    my_count = jnp.sum(valid_f)
    count_high = jnp.floor(my_count / 128.0)
    count_low = my_count - 128.0 * count_high
    shard = qkv_weight.shape[0]
    small = jnp.concatenate(
        [
            router_weight,
            ln1_gain[:, None],
            ln2_gain[:, None],
            jnp.broadcast_to(count_high.astype(BF16), (shard, 1)),
            jnp.broadcast_to(count_low.astype(BF16), (shard, 1)),
        ],
        axis=1,
    )
    extra = jnp.pad(small, ((0, 0), (0, 128 - experts - 4)))
    floors = experts // 2
    in_part, ex_part = (width // dp, hidden_width), (hidden_width // dp, width)
    any_space = pl.BlockSpec(memory_space=pl.ANY)

    code = jnp.where(slot_ids < capacity, (routes ^ me) * cap + slot_ids, -1)
    cols = pad_rows(jnp.concatenate([code, routes], axis=1), -1)
    row_codes = jnp.pad(cols.transpose(0, 2, 1), ((0, 0), (0, 4), (0, 0)))
    cols = jnp.pad(cols, ((0, 0), (0, 0), (0, 4)))
    tok_p = pad_rows(tokens)
    target_p = pad_rows(targets)
    valid_p = pad_rows(jnp.broadcast_to(valid_f[:, None], (tok_rows, 8)))

    gate_lanes = 128
    dense_lanes = 4 * width + 128
    (
        qkv_p, probs, mixed, resid, gates, dense_full, ext, act_all, code_all, grow_all, win_own, wex_own, win_far,
    ) = pl.pallas_call(
        lambda *refs: forward_kernel(images, real_rows, experts, *refs),
        grid=(images,),
        in_specs=[
            per_image(rows, width), whole((shard, 3 * width)), whole((shard, width)), whole((shard, 128)),
            per_image(rows, 8), per_image(8, rows), any_space, any_space, any_space,
        ],
        out_specs=[
            per_image(rows, 3 * width), per_image(HEADS, rows, rows), per_image(rows, width),
            per_image(rows, width), per_image(rows, gate_lanes), whole((width, dense_lanes)), whole((128, width)),
            *[any_space] * 6,
        ],
        out_shape=[
            shape((images, rows, 3 * width), BF16), shape((images, HEADS, rows, rows), BF16),
            shape((images, rows, width), BF16), shape((images, rows, width), F32),
            shape((images, rows, gate_lanes), F32), shape((width, dense_lanes), BF16), shape((128, width), F32),
            shape((group, images, rows, width), BF16), shape((group, images, 8, rows), jnp.int32),
            shape((group, images, 8, rows), F32), shape((dp, *in_part), BF16), shape((dp, *ex_part), BF16),
            shape(in_part, BF16),
        ],
        scratch_shapes=[
            pltpu.VMEM((dp, floors, 2, shard, dense_lanes), BF16), pltpu.VMEM((images, rows, width), BF16),
            pltpu.VMEM((images, 8, rows), F32),
            *sem_pairs(19), *sem_pairs(3 * images), *sem_pairs(6), *sem_pairs(9),
            pltpu.SemaphoreType.DMA((images + 4,)),
        ],
        compiler_params=pltpu.CompilerParams(
            vmem_limit_bytes=56 * MB, collective_id=2, has_side_effects=True
        ),
        cost_estimate=pl.CostEstimate(flops=int(5e9), bytes_accessed=int(2e7), transcendentals=0),
        name="attention_forward",
    )(tok_p, qkv_weight, out_weight, extra, cols, row_codes, row_codes, expert_in[0], expert_out[0])

    half_blocks = group // 2
    def by_half(*dims):
        return pl.BlockSpec((half_blocks,) + dims, lambda q, h: (1 - h,) + (0,) * len(dims))

    def by_both(*dims, last_first=False):
        if last_first:
            return pl.BlockSpec((None, half_blocks) + dims, lambda q, h: (1 - q, 1 - h) + (0,) * len(dims))
        return pl.BlockSpec((None, half_blocks) + dims, lambda q, h: (q, 1 - h) + (0,) * len(dims))

    rows_in, hidden, slope, returned, win_other, wex_other = pl.pallas_call(
        lambda *refs: expert_forward_kernel(cap, group, *refs),
        grid=(2, 2),
        in_specs=[by_half(images, rows, width), by_half(images, 8, rows), *[any_space] * 4],
        out_specs=[by_both(cap, width), by_both(cap, hidden_width), by_both(cap, hidden_width), *[any_space] * 3],
        out_shape=[
            shape((2, group, cap, width), BF16), shape((2, group, cap, hidden_width), BF16),
            shape((2, group, cap, hidden_width), BF16), shape((2, group, cap, width), BF16),
            shape((dp, *in_part), BF16), shape((dp, *ex_part), BF16),
        ],
        scratch_shapes=[
            pltpu.VMEM((2, dp, *in_part), BF16), pltpu.VMEM((2, dp, *ex_part), BF16),
            pltpu.VMEM((2, group, cap, width), BF16), *sem_pairs(8), *sem_pairs(9), pltpu.SemaphoreType.DMA((7,)),
        ],
        compiler_params=pltpu.CompilerParams(
            vmem_limit_bytes=58 * MB, collective_id=3, has_side_effects=True
        ),
        cost_estimate=pl.CostEstimate(flops=int(14e9), bytes_accessed=int(4e7), transcendentals=0),
        name="expert_forward",
    )(act_all, code_all, win_own, wex_own, win_far, expert_out[0])
    returned = returned.reshape(2 * group * cap, width)

    block_out, dout, dlogits, loss_part, dlow_all = pl.pallas_call(
        lambda *refs: combine_kernel(images, total_tokens, shard, experts, *refs),
        grid=(images,),
        in_specs=[
            pl.BlockSpec((16, width), lambda i: (0, 0)), per_image(rows, width), whole((2 * group * cap, width)),
            per_image(rows, 8), per_image(rows, gate_lanes), per_image(rows, width), per_image(rows, 8),
        ],
        out_specs=[
            per_image(rows, width), per_image(rows, width), per_image(rows, gate_lanes), whole((8, 128)), any_space,
        ],
        out_shape=[
            shape((images, rows, width), BF16), shape((images, rows, width), F32),
            shape((images, rows, gate_lanes), F32), shape((8, 128), F32), shape((group, images, rows, width), BF16),
        ],
        scratch_shapes=[
            pltpu.VMEM((images, rows, width), BF16), *sem_pairs(3 * images), pltpu.SemaphoreType.DMA((images,)),
        ],
        compiler_params=pltpu.CompilerParams(
            vmem_limit_bytes=56 * MB, collective_id=4, has_side_effects=True
        ),
        cost_estimate=pl.CostEstimate(flops=int(5e9), bytes_accessed=int(1e7), transcendentals=0),
        name="combine_and_loss",
    )(ext, resid, returned, cols, gates, target_p, valid_p)

    flip_part = (width, hidden_width // dp)
    drows, gin, gout_t, got_in, got_ex = pl.pallas_call(
        lambda *refs: expert_back_kernel(cap, group, *refs),
        grid=(2, 2),
        in_specs=[
            by_half(images, rows, width), by_half(images, 8, rows), by_half(images, 8, rows),
            by_both(cap, width, last_first=True), by_both(cap, hidden_width, last_first=True),
            by_both(cap, hidden_width, last_first=True), *[any_space] * 4,
        ],
        out_specs=[any_space] * 5,
        out_shape=[
            shape((2, group, cap, width), BF16), shape((2, dp, *in_part), BF16), shape((2, dp, *flip_part), BF16),
            shape((2, *in_part), BF16), shape((2, *flip_part), BF16),
        ],
        scratch_shapes=[
            pltpu.VMEM((2, dp, *in_part), BF16), pltpu.VMEM((2, dp, *ex_part), BF16),
            pltpu.VMEM((width, hidden_width), F32), pltpu.VMEM((width, hidden_width), F32),
            pltpu.VMEM((2, dp, *in_part), BF16), pltpu.VMEM((2, dp, *flip_part), BF16),
            pltpu.VMEM((2, group, cap, width), BF16), *sem_pairs(8), *sem_pairs(4), pltpu.SemaphoreType.DMA((11,)),
        ],
        compiler_params=pltpu.CompilerParams(
            vmem_limit_bytes=60 * MB, collective_id=5, has_side_effects=True
        ),
        cost_estimate=pl.CostEstimate(flops=int(24e9), bytes_accessed=int(4e7), transcendentals=0),
        name="expert_backward",
    )(dlow_all, code_all, grow_all, rows_in, hidden, slope, win_own, wex_own, win_other, wex_other)
    grad_back = drows.reshape(2 * group * cap, width)

    def vmem(*dims):
        return pltpu.VMEM(dims, BF16)

    tgrad, dense_grad, misc, gin_own, gex_own = pl.pallas_call(
        lambda *refs: back_kernel(images, experts, *refs),
        grid=(images,),
        in_specs=[
            per_image(rows, width), whole((width, dense_lanes)), whole((128, width)), per_image(rows, 8),
            whole((2 * group * cap, width)), per_image(rows, gate_lanes), per_image(rows, width), per_image(rows, width),
            per_image(rows, 3 * width), per_image(HEADS, rows, rows), per_image(rows, width), whole((8, 128)),
            *[any_space] * 4,
        ],
        out_specs=[
            per_image(rows, width), whole((shard, 4 * width)), whole((16, width)), whole(in_part), whole(flip_part),
        ],
        out_shape=[
            shape((images, rows, width), F32), shape((shard, 4 * width), F32), shape((16, width), F32),
            shape(in_part, F32), shape(flip_part, F32),
        ],
        scratch_shapes=[
            pltpu.VMEM((width, 4 * width), F32), pltpu.VMEM((16, width), F32),
            vmem(2, 2, *in_part), vmem(2, 2, *flip_part), vmem(2, 2, *in_part), vmem(2, 2, *flip_part),
            vmem(2, *in_part), vmem(2, *flip_part), vmem(2, *in_part), vmem(2, *flip_part),
            vmem(*in_part), vmem(*flip_part), vmem(*in_part), vmem(*flip_part),
            vmem(dp, floors, 2, shard, 4 * width), vmem(dp, floors, shard, 4 * width), vmem(dp, floors, shard, 4 * width),
            vmem(3, floors, shard, 4 * width), vmem(floors, shard, 4 * width), vmem(3, shard, 4 * width),
            pltpu.VMEM((10, 16, width), F32), pltpu.SemaphoreType.DMA((10,)),
            *sem_pairs(16), *sem_pairs(8), *sem_pairs(5),
        ],
        compiler_params=pltpu.CompilerParams(
            vmem_limit_bytes=60 * MB, collective_id=1, has_side_effects=True
        ),
        cost_estimate=pl.CostEstimate(flops=int(10e9), bytes_accessed=int(3e7), transcendentals=0),
        name="attention_backward",
    )(
        tok_p, dense_full, ext, cols, grad_back, dlogits, resid, dout, qkv_p, probs, mixed,
        loss_part, gin, gout_t, got_in, got_ex,
    )
    flat = lax.axis_index("dp") * experts + me
    mine = lax.dynamic_slice_in_dim(misc, flat * shard, shard, axis=1)
    loss_value = misc[10, 0]

    def unpad(array):
        return array[:, :real_rows].reshape(tok_rows, width)

    return (
        unpad(block_out),
        loss_value,
        unpad(tgrad),
        mine[8],
        dense_grad[:, : 3 * width],
        dense_grad[:, 3 * width :],
        mine[9],
        mine[:experts].T,
        gin_own[None],
        gex_own.T[None],
    )


def solution(mesh):
    in_specs = (
        P(("dp", "expert"), None),
        P(("dp", "expert"), None),
        P(("dp", "expert")),
        P(("dp", "expert"), None),
        P(("dp", "expert"), None),
        P(("dp", "expert")),
        P(("dp", "expert"), None),
        P(("dp", "expert"), None),
        P(("dp", "expert")),
        P(("dp", "expert"), None),
        P("expert", "dp", None),
        P("expert", "dp", None),
    )
    out_specs = (
        P(("dp", "expert"), None),
        P(),
        P(("dp", "expert"), None),
        P(("dp", "expert")),
        P(("dp", "expert"), None),
        P(("dp", "expert"), None),
        P(("dp", "expert")),
        P(("dp", "expert"), None),
        P("expert", "dp", None),
        P("expert", "dp", None),
    )
    halves = mesh.shape["expert"] == 8 and mesh.shape["dp"] == 4
    body = fast_shards if halves else shards
    return jax.shard_map(body, mesh=mesh, in_specs=in_specs, out_specs=out_specs, check_vma=False)
```

```python
import jax
import jax.numpy as jnp
from jax import lax
from jax.experimental import pallas as pl
from jax.experimental.pallas import tpu as pltpu
from jax.sharding import PartitionSpec as P

HEADS = 8
IMG_DEV = 5


HIGH = lax.Precision.HIGHEST
EPS = 1e-06


def layer_norm(values, scale_gain):
    row_mean = jnp.mean(values, axis=-1, keepdims=True)
    centered = values - row_mean
    variance = jnp.mean(centered * centered, axis=-1, keepdims=True)
    inverse = lax.rsqrt(variance + EPS)
    normed = centered * inverse
    return (normed * scale_gain, normed, inverse)


def layer_norm_back(grad_in, normed, inverse, scale_gain):
    scaled = grad_in * scale_gain
    gain_grad = jnp.sum(grad_in * normed, axis=0)
    inner_term = (
        scaled
        - jnp.mean(scaled, axis=-1, keepdims=True)
        - normed * jnp.mean(scaled * normed, axis=-1, keepdims=True)
    )
    return (inverse * inner_term, gain_grad)


def contract_rows(left_side, right_side):
    return lax.dot_general(
        left_side, right_side, (((0,), (0,)), ((), ())), preferred_element_type=jnp.float32
    )


def contract_cols(left_side, right_side):
    return lax.dot_general(
        left_side, right_side, (((1,), (1,)), ((), ())), preferred_element_type=jnp.float32
    )


def exact_gelu(values):
    return jax.nn.gelu(values, approximate=False)


def split_heads(qkv_low, images, head_count):
    row_count, triple_width = qkv_low.shape
    head_dim = triple_width // (3 * head_count)
    pieces = qkv_low.reshape(images, row_count // images, 3, head_count, head_dim)
    return (pieces[:, :, 0], pieces[:, :, 1], pieces[:, :, 2], head_dim ** (-0.5))


def attention_forward(qkv_low, images, head_count):
    queries, key_rows, values, score_scale = split_heads(qkv_low, images, head_count)
    scores = (
        jnp.einsum("ilhd,imhd->ihlm", queries, key_rows, preferred_element_type=jnp.float32)
        * score_scale
    )
    row_max = jnp.max(scores, axis=-1, keepdims=True)
    exp_scores = jnp.exp(scores - row_max)
    row_sum = jnp.sum(exp_scores, axis=-1, keepdims=True)
    weights_low = (exp_scores / row_sum).astype(jnp.bfloat16)
    log_total = row_max + jnp.log(row_sum)
    mixed_rows = jnp.einsum(
        "ihlm,imhd->ilhd", weights_low, values, preferred_element_type=jnp.float32
    )
    return (mixed_rows.reshape(qkv_low.shape[0], -1).astype(jnp.bfloat16), log_total)


def attention_back(qkv_low, log_total, grad_mixed, images, head_count):
    queries, key_rows, values, score_scale = split_heads(qkv_low, images, head_count)
    scores = (
        jnp.einsum("ilhd,imhd->ihlm", queries, key_rows, preferred_element_type=jnp.float32)
        * score_scale
    )
    weights_full = jnp.exp(scores - log_total)
    weights_low = weights_full.astype(jnp.bfloat16)
    grad_heads = grad_mixed.reshape(queries.shape)
    grad_weights = jnp.einsum(
        "ilhd,imhd->ihlm", grad_heads, values, preferred_element_type=jnp.float32
    )
    grad_values = jnp.einsum(
        "ihlm,ilhd->imhd", weights_low, grad_heads, preferred_element_type=jnp.float32
    )
    grad_scores = weights_full * (
        grad_weights - jnp.sum(weights_full * grad_weights, axis=-1, keepdims=True)
    )
    grad_low = grad_scores.astype(jnp.bfloat16)
    grad_queries = (
        jnp.einsum("ihlm,imhd->ilhd", grad_low, key_rows, preferred_element_type=jnp.float32)
        * score_scale
    )
    grad_keys = (
        jnp.einsum("ihlm,ilhd->imhd", grad_low, queries, preferred_element_type=jnp.float32)
        * score_scale
    )
    stacked = jnp.stack([grad_queries, grad_keys, grad_values], axis=2)
    return stacked.reshape(qkv_low.shape).astype(jnp.bfloat16)


def expert_forward(rows_in, weight_in, weight_out, block_size):
    result = jnp.zeros((rows_in.shape[0], weight_out.shape[1]), jnp.float32)
    for offset in range(0, weight_in.shape[1], block_size):
        pre_act = jnp.dot(
            rows_in, weight_in[:, offset : offset + block_size], preferred_element_type=jnp.float32
        )
        hidden = exact_gelu(pre_act).astype(jnp.bfloat16)
        result = result + jnp.dot(
            hidden, weight_out[offset : offset + block_size], preferred_element_type=jnp.float32
        )
    return result


def expert_back(rows_in, weight_in, weight_out, grad_rows_out, block_size):
    grad_rows = jnp.zeros(rows_in.shape, jnp.float32)
    grads_first = []
    grads_second = []
    for offset in range(0, weight_in.shape[1], block_size):
        slice_in = weight_in[:, offset : offset + block_size]
        slice_out = weight_out[offset : offset + block_size]
        pre_act = jnp.dot(rows_in, slice_in, preferred_element_type=jnp.float32)
        hidden, gelu_back = jax.vjp(exact_gelu, pre_act)
        grads_second.append(contract_rows(hidden.astype(jnp.bfloat16), grad_rows_out))
        grad_hidden = contract_cols(grad_rows_out, slice_out)
        grad_pre = gelu_back(grad_hidden)[0].astype(jnp.bfloat16)
        grads_first.append(contract_rows(rows_in, grad_pre))
        grad_rows = grad_rows + contract_cols(grad_pre, slice_in)
    return (grad_rows, jnp.concatenate(grads_first, axis=1), jnp.concatenate(grads_second, axis=0))


def shards(
    tokens,
    targets,
    valid_mask,
    routes,
    slot_ids,
    ln1_gain,
    qkv_weight,
    out_weight,
    ln2_gain,
    router_weight,
    expert_in,
    expert_out,
):
    tok_rows, model_width = tokens.shape
    experts = lax.axis_size("expert")
    total_tokens = tok_rows * lax.axis_size("dp") * experts
    capacity = (5 * tok_rows // 2 // experts + 7) // 8 * 8
    dense_full = (
        lax.all_gather(ln1_gain, ("dp", "expert"), axis=0, tiled=True),
        lax.all_gather(qkv_weight, ("dp", "expert"), axis=0, tiled=True),
        lax.all_gather(out_weight, ("dp", "expert"), axis=0, tiled=True),
        lax.all_gather(ln2_gain, ("dp", "expert"), axis=0, tiled=True),
        lax.all_gather(router_weight, ("dp", "expert"), axis=0, tiled=True),
    )
    gain_one, qkv_full, out_full, gain_two, router_full = dense_full
    expert_full = (
        lax.all_gather(expert_in, "dp", axis=1, tiled=True),
        lax.all_gather(expert_out, "dp", axis=1, tiled=True),
    )
    weight_in = expert_full[0][0]
    weight_out = expert_full[1][0]
    valid_f = valid_mask.astype(jnp.float32)
    valid_count = lax.psum(jnp.sum(valid_f), ("dp", "expert"))
    inputs_f = tokens.astype(jnp.float32)
    gain_one_f = gain_one.astype(jnp.float32)
    gain_two_f = gain_two.astype(jnp.float32)
    norm_one, normed_one, inverse_one = layer_norm(inputs_f, gain_one_f)
    act_one = norm_one.astype(jnp.bfloat16)
    qkv_low = jnp.dot(act_one, qkv_full, preferred_element_type=jnp.float32).astype(jnp.bfloat16)
    mixed_low, log_total = attention_forward(qkv_low, IMG_DEV, HEADS)
    residual = inputs_f + jnp.dot(mixed_low, out_full, preferred_element_type=jnp.float32)
    norm_two, normed_two, inverse_two = layer_norm(residual, gain_two_f)
    act_two = norm_two.astype(jnp.bfloat16)
    gate_probs = jax.nn.softmax(
        jnp.dot(act_two, router_full, preferred_element_type=jnp.float32), axis=-1
    )
    expert_ids = lax.broadcasted_iota(jnp.int32, (1, experts), 1)
    first_pick = (routes[:, 0:1] == expert_ids).astype(jnp.float32)
    second_pick = (routes[:, 1:2] == expert_ids).astype(jnp.float32)
    gate_first = jnp.sum(gate_probs * first_pick, axis=-1, keepdims=True)
    gate_second = jnp.sum(gate_probs * second_pick, axis=-1, keepdims=True)
    target_slot = jnp.where(slot_ids < capacity, routes * capacity + slot_ids, -1)
    slot_columns = lax.broadcasted_iota(jnp.int32, (1, experts * capacity), 1)
    first_hot = (target_slot[:, 0:1] == slot_columns).astype(jnp.bfloat16)
    second_hot = (target_slot[:, 1:2] == slot_columns).astype(jnp.bfloat16)
    both_hot = first_hot + second_hot
    outgoing = contract_rows(both_hot, act_two).astype(jnp.bfloat16)
    arrived = lax.all_to_all(
        outgoing.reshape(experts, capacity, model_width),
        "expert",
        split_axis=0,
        concat_axis=0,
        tiled=True,
    ).reshape(-1, model_width)
    hidden_block = min(512, weight_in.shape[1])
    produced = expert_forward(arrived, weight_in, weight_out, hidden_block).astype(jnp.bfloat16)
    returned = lax.all_to_all(
        produced.reshape(experts, capacity, model_width),
        "expert",
        split_axis=0,
        concat_axis=0,
        tiled=True,
    ).reshape(-1, model_width)
    from_first = jnp.dot(first_hot, returned, preferred_element_type=jnp.float32)
    from_second = jnp.dot(second_hot, returned, preferred_element_type=jnp.float32)
    output = residual + gate_first * from_first + gate_second * from_second
    residue = output - targets.astype(jnp.float32)
    local_loss = jnp.sum(valid_f * jnp.mean(residue * residue, axis=-1))
    loss_sum = lax.psum(local_loss, ("dp", "expert"))
    loss_value = loss_sum / valid_count
    grad_out = total_tokens / valid_count * valid_f[:, None] * residue
    dense_back = (
        lax.all_gather(ln1_gain, ("dp", "expert"), axis=0, tiled=True),
        lax.all_gather(qkv_weight, ("dp", "expert"), axis=0, tiled=True),
        lax.all_gather(out_weight, ("dp", "expert"), axis=0, tiled=True),
        lax.all_gather(ln2_gain, ("dp", "expert"), axis=0, tiled=True),
        lax.all_gather(router_weight, ("dp", "expert"), axis=0, tiled=True),
    )
    expert_back_full = (
        lax.all_gather(expert_in, "dp", axis=1, tiled=True),
        lax.all_gather(expert_out, "dp", axis=1, tiled=True),
    )
    qkv_back = dense_back[1]
    out_back = dense_back[2]
    router_back = dense_back[4]
    weight_in_back = expert_back_full[0][0]
    weight_out_back = expert_back_full[1][0]
    slot_grads = (
        contract_rows(first_hot, (gate_first * grad_out).astype(jnp.bfloat16))
        + contract_rows(second_hot, (gate_second * grad_out).astype(jnp.bfloat16))
    ).astype(jnp.bfloat16)
    expert_grad_rows = lax.all_to_all(
        slot_grads.reshape(experts, capacity, model_width),
        "expert",
        split_axis=0,
        concat_axis=0,
        tiled=True,
    ).reshape(-1, model_width)
    grad_rows, grad_first_weight, grad_second_weight = expert_back(
        arrived, weight_in_back, weight_out_back, expert_grad_rows, hidden_block
    )
    grad_back = lax.all_to_all(
        grad_rows.astype(jnp.bfloat16).reshape(experts, capacity, model_width),
        "expert",
        split_axis=0,
        concat_axis=0,
        tiled=True,
    ).reshape(-1, model_width)
    grad_act_two = jnp.dot(both_hot, grad_back, preferred_element_type=jnp.float32)
    gate_grad = first_pick * jnp.sum(
        grad_out * from_first, axis=-1, keepdims=True
    ) + second_pick * jnp.sum(grad_out * from_second, axis=-1, keepdims=True)
    logit_grad = gate_probs * (gate_grad - jnp.sum(gate_probs * gate_grad, axis=-1, keepdims=True))
    router_f = router_back.astype(jnp.float32)
    grad_act_two = grad_act_two + lax.dot_general(
        logit_grad,
        router_f,
        (((1,), (1,)), ((), ())),
        precision=HIGH,
        preferred_element_type=jnp.float32,
    )
    router_grad = lax.dot_general(
        act_two.astype(jnp.float32),
        logit_grad,
        (((0,), (0,)), ((), ())),
        precision=HIGH,
        preferred_element_type=jnp.float32,
    )
    grad_norm_two, gain_two_grad = layer_norm_back(
        grad_act_two, normed_two, inverse_two, gain_two_f
    )
    grad_resid = grad_out + grad_norm_two
    branch_grad = grad_resid.astype(jnp.bfloat16)
    out_weight_grad = contract_rows(mixed_low, branch_grad)
    grad_mixed = contract_cols(branch_grad, out_back).astype(jnp.bfloat16)
    qkv_grad_low = attention_back(qkv_low, log_total, grad_mixed, IMG_DEV, HEADS)
    qkv_weight_grad = contract_rows(act_one, qkv_grad_low)
    grad_act_one = contract_cols(qkv_grad_low, qkv_back)
    grad_norm_one, gain_one_grad = layer_norm_back(
        grad_act_one, normed_one, inverse_one, gain_one_f
    )
    tokens_grad = grad_resid + grad_norm_one
    dense_grads = (
        lax.psum_scatter(gain_one_grad, ("dp", "expert"), scatter_dimension=0, tiled=True),
        lax.psum_scatter(qkv_weight_grad, ("dp", "expert"), scatter_dimension=0, tiled=True),
        lax.psum_scatter(out_weight_grad, ("dp", "expert"), scatter_dimension=0, tiled=True),
        lax.psum_scatter(gain_two_grad, ("dp", "expert"), scatter_dimension=0, tiled=True),
        lax.psum_scatter(router_grad, ("dp", "expert"), scatter_dimension=0, tiled=True),
    )
    expert_grads = (
        lax.psum_scatter(
            grad_first_weight[None].astype(jnp.bfloat16), "dp", scatter_dimension=1, tiled=True
        ).astype(jnp.float32),
        lax.psum_scatter(
            grad_second_weight[None].astype(jnp.bfloat16), "dp", scatter_dimension=1, tiled=True
        ).astype(jnp.float32),
    )
    first_result = expert_grads[0]
    second_result = expert_grads[1]
    return (
        output.astype(jnp.bfloat16),
        loss_value,
        tokens_grad,
        dense_grads[0],
        dense_grads[1],
        dense_grads[2],
        dense_grads[3],
        dense_grads[4],
        first_result,
        second_result,
    )


F32 = jnp.float32
BF16 = jnp.bfloat16
MB = 2**20


def round_up(value, unit):
    return (value + unit - 1) // unit * unit


def dot(left_side, right_side):
    return jnp.dot(left_side, right_side, preferred_element_type=F32)


def lane_ids(shape):
    return lax.broadcasted_iota(jnp.int32, shape, len(shape) - 1)


def row_ids(shape):
    return lax.broadcasted_iota(jnp.int32, shape, len(shape) - 2)


MESH = pl.DeviceIdType.MESH


def flip(index, bit):
    return index + bit * (1 - 2 * lax.rem(index // bit, 2))


def send(src, dst, sems, slot, device):
    return pltpu.make_async_remote_copy(
        src_ref=src, dst_ref=dst, send_sem=sems[0].at[slot], recv_sem=sems[1].at[slot],
        device_id=device, device_id_type=MESH,
    )


def greet(peers):
    barrier = pltpu.get_barrier_semaphore()
    for peer in peers:
        pl.semaphore_signal(barrier, inc=1, device_id=peer, device_id_type=MESH)
    pl.semaphore_wait(barrier, len(peers))


def place():
    dp_at, ex_at = lax.axis_index("dp"), lax.axis_index("expert")
    near = [None, flip(dp_at, 1), flip(dp_at, 2), flip(flip(dp_at, 1), 2)]
    return dp_at, ex_at, near


def sem_pairs(count):
    return [pltpu.SemaphoreType.DMA((count,)), pltpu.SemaphoreType.DMA((count,))]


def normalize(values):
    centered = values - jnp.mean(values, axis=-1, keepdims=True)
    inverse = lax.rsqrt(jnp.mean(centered * centered, axis=-1, keepdims=True) + EPS)
    return centered * inverse, inverse


def gelu_pair(values):
    size = jnp.abs(values)
    inv = 1.0 / (1.0 + 0.2316419 * size)
    density = 0.3989422804014327 * jnp.exp(-0.5 * values * values)
    series = inv * (
        0.319381530
        + inv * (-0.356563782 + inv * (1.781477937 + inv * (-1.821255978 + inv * 1.330274429)))
    )
    tail = density * series
    cumulative = jnp.where(values >= 0, 1.0 - tail, tail)
    return values * cumulative, cumulative + values * density


def plane_gather(mine, blocks, sems, base, dp_at, ex_at, near):
    half = blocks.shape[1] // 2
    first, second = pl.ds(0, half), pl.ds(half, half)
    own = [
        send(mine, blocks.at[dp_at], sems, base + k - 1, (near[k], ex_at)) for k in (1, 2)
    ]
    passed = [
        send(blocks.at[near[1], first], blocks.at[near[1], first], sems, base + 2, (near[2], ex_at)),
        send(blocks.at[near[2], second], blocks.at[near[2], second], sems, base + 3, (near[1], ex_at)),
    ]
    return own, passed


def group_copies(images, step, buf, dest, tsem, lsem, dp_at, ex_at):
    mate, across = flip(ex_at, 1), flip(ex_at, 2)
    keep = pltpu.make_async_copy(buf.at[step], dest.at[0, step], lsem.at[step])
    to_mate = send(buf.at[step], dest.at[1, step], tsem, step, (dp_at, mate))
    to_chip = send(buf.at[step], dest.at[2, step], tsem, images + step, (dp_at, across))
    onward = send(dest.at[2, step], dest.at[3, step], tsem, 2 * images + step, (dp_at, mate))
    return keep, to_mate, to_chip, onward


def forward_kernel(
    images, real_rows, experts, tok_ref, qkvw_ref, outw_ref, extra_ref, cols_ref, rows_ref, codes_ref, win_ref, wex_ref,
    qkv_ref, probs_ref, mixed_ref, resid_ref, gates_ref, dense_ref, ext_ref,
    act_all, code_all, grow_all, win_all, wex_all, far_in,
    dense, act_buf, grow_buf, d_send, d_recv, t_send, t_recv, r_send, r_recv, w_send, w_recv, local_sem,
):
    step_at = pl.program_id(0)
    dp_at, ex_at, near = place()
    core, floor = lax.rem(ex_at, 2), ex_at // 2
    dsem, tsem, rsem, wsem = (d_send, d_recv), (t_send, t_recv), (r_send, r_recv), (w_send, w_recv)
    group_peers = [(dp_at, flip(ex_at, 1)), (dp_at, flip(ex_at, 2)), (dp_at, flip(flip(ex_at, 1), 2))]
    floors = [floor, flip(floor, 1), flip(floor, 2), flip(flip(floor, 1), 2)]
    columns = [dp_at] + near[1:]

    codes_out = [send(codes_ref, code_all.at[k + 1], rsem, k, group_peers[k]) for k in range(3)]
    grow_out = [send(grow_buf, grow_all.at[k + 1], rsem, 3 + k, group_peers[k]) for k in range(3)]
    keeps = [
        pltpu.make_async_copy(codes_ref, code_all.at[0], local_sem.at[images]),
        pltpu.make_async_copy(win_ref, win_all.at[dp_at], local_sem.at[images + 1]),
        pltpu.make_async_copy(wex_ref, wex_all.at[dp_at], local_sem.at[images + 2]),
    ]
    keep_grow = pltpu.make_async_copy(grow_buf, grow_all.at[0], local_sem.at[images + 3])
    in_own, in_passed = plane_gather(win_ref, win_all, wsem, 0, dp_at, ex_at, near)
    ex_own, ex_passed = plane_gather(wex_ref, wex_all, wsem, 4, dp_at, ex_at, near)
    to_far = send(win_ref, far_in, wsem, 8, (dp_at, flip(ex_at, 4)))
    along_line = [
        send(dense.at[dp_at, floor, core], dense.at[dp_at, floor, core], dsem, k - 1, (dp_at, 2 * floors[k] + core))
        for k in (1, 2, 3)
    ]
    in_plane = [
        [
            send(
                dense.at[dp_at, floors[k], core], dense.at[dp_at, floors[k], core], dsem, 3 + 3 * k + p - 1,
                (near[p], ex_at),
            )
            for p in (1, 2, 3)
        ]
        for k in range(4)
    ]
    to_mate = [
        send(dense.at[columns[p], :, core], dense.at[columns[p], :, core], dsem, 15 + p, group_peers[0])
        for p in range(4)
    ]

    @pl.when(step_at == 0)
    def _():
        for copy in keeps:
            copy.start()
        width = outw_ref.shape[1]
        dense[dp_at, floor, core, :, : 3 * width] = qkvw_ref[...]
        dense[dp_at, floor, core, :, 3 * width : 4 * width] = outw_ref[...]
        dense[dp_at, floor, core, :, 4 * width :] = extra_ref[...]
        greet(
            [(near[k], ex_at) for k in (1, 2, 3)]
            + group_peers
            + [(dp_at, flip(ex_at, 4)), (dp_at, flip(flip(ex_at, 2), 4))]
        )
        for copy in along_line + in_plane[0]:
            copy.start()
        for k in (1, 2, 3):
            along_line[k - 1].wait_recv()
            for copy in in_plane[k]:
                copy.start()
        to_mate[0].start()
        for copy in codes_out:
            copy.start()
        for p in (1, 2, 3):
            for k in range(4):
                in_plane[k][p - 1].wait_recv()
            to_mate[p].start()
        for copy in in_own + ex_own + [to_far]:
            copy.start()
        for copy in to_mate:
            copy.wait_recv()
        full = dense[...].reshape(dense_ref.shape)
        dense_ref[...] = full
        ext_ref[...] = full[:, 4 * width :].astype(F32).T

    inputs = tok_ref[...].astype(F32)
    normed, _ = normalize(inputs)
    width = inputs.shape[1]
    act_one = (normed * ext_ref[experts : experts + 1, :]).astype(BF16)
    qkv = dot(act_one, dense_ref[:, : 3 * width]).astype(BF16)
    qkv_ref[...] = qkv
    rows = inputs.shape[0]
    low_half = lane_ids((1, 128)) < 64
    key_bias = jnp.where(lane_ids((1, rows)) < real_rows, 0.0, -1e30)
    parts = []
    for pair in range(width // 128):
        lanes = slice(128 * pair, 128 * (pair + 1))
        queries = qkv[:, lanes]
        key_rows = qkv[:, width + 128 * pair : width + 128 * (pair + 1)]
        values = qkv[:, 2 * width + 128 * pair : 2 * width + 128 * (pair + 1)]
        outs = []
        for side in range(2):
            mask = low_half if side == 0 else jnp.logical_not(low_half)
            masked = jnp.where(mask, queries, jnp.zeros_like(queries))
            scores = contract_cols(masked, key_rows) * 0.125 + key_bias
            exped = jnp.exp(scores - jnp.max(scores, axis=-1, keepdims=True))
            probs = (exped * (1.0 / jnp.sum(exped, axis=-1, keepdims=True))).astype(BF16)
            probs_ref[2 * pair + side] = probs
            outs.append(dot(probs, values))
        parts.append(jnp.where(low_half, outs[0], outs[1]).astype(BF16))
    mixed = jnp.concatenate(parts, axis=1)
    mixed_ref[...] = mixed
    resid = inputs + dot(mixed, dense_ref[:, 3 * width : 4 * width])
    resid_ref[...] = resid
    normed_two, _ = normalize(resid)
    act_two = (normed_two * ext_ref[experts + 1 : experts + 2, :]).astype(BF16)
    act_buf[step_at] = act_two
    lanes = lane_ids((1, 128))
    logits = jnp.where(lanes < experts, dot(act_two, dense_ref[:, 4 * width :]), -1e30)
    exped = jnp.exp(logits - jnp.max(logits, axis=-1, keepdims=True))
    gates = exped / jnp.sum(exped, axis=-1, keepdims=True)
    cols = cols_ref[...]
    first = jnp.sum(jnp.where(lanes == cols[:, 2:3], gates, 0.0), axis=-1, keepdims=True)
    second = jnp.sum(jnp.where(lanes == cols[:, 3:4], gates, 0.0), axis=-1, keepdims=True)
    gates_ref[...] = jnp.where(lanes == experts, first, jnp.where(lanes == experts + 1, second, gates))
    logits_t = contract_cols(ext_ref[0:16, :].astype(BF16), act_two)[:experts]
    exped_t = jnp.exp(logits_t - jnp.max(logits_t, axis=0, keepdims=True))
    gates_t = exped_t / jnp.sum(exped_t, axis=0, keepdims=True)
    ids_t = row_ids(gates_t.shape)
    first_t = jnp.sum(jnp.where(ids_t == rows_ref[2:3, :], gates_t, 0.0), axis=0, keepdims=True)
    second_t = jnp.sum(jnp.where(ids_t == rows_ref[3:4, :], gates_t, 0.0), axis=0, keepdims=True)
    grow_buf[step_at] = jnp.where(row_ids((8, rows)) == 0, first_t, second_t)

    for step in range(images):
        keep, mate_copy, chip_copy, _ = group_copies(images, step, act_buf, act_all, tsem, local_sem, dp_at, ex_at)

        @pl.when(step_at == step)
        def _():
            keep.start()
            mate_copy.start()
            chip_copy.start()

    def pass_on(step):
        _, _, chip_copy, onward = group_copies(images, step, act_buf, act_all, tsem, local_sem, dp_at, ex_at)
        chip_copy.wait_recv()
        onward.start()

    for step in range(images - 2):

        @pl.when(step_at == step + 2)
        def _():
            pass_on(step)

    @pl.when(step_at == images - 2)
    def _():
        in_own[0].wait_recv()
        in_passed[0].start()
        in_own[1].wait_recv()
        in_passed[1].start()

    @pl.when(step_at == images - 1)
    def _():
        keep_grow.start()
        for copy in grow_out:
            copy.start()
        ex_own[0].wait_recv()
        ex_passed[0].start()
        ex_own[1].wait_recv()
        ex_passed[1].start()
        for step in (images - 2, images - 1):
            pass_on(step)
        for step in range(images):
            keep, mate_copy, chip_copy, onward = group_copies(
                images, step, act_buf, act_all, tsem, local_sem, dp_at, ex_at
            )
            keep.wait()
            mate_copy.wait()
            chip_copy.wait_send()
            onward.wait()
        keep_grow.wait()
        for copy in keeps:
            copy.wait()
        for copy in codes_out + grow_out + in_passed + ex_passed + [to_far]:
            copy.wait()
        for copy in along_line + to_mate + in_own + ex_own + [c for line in in_plane for c in line]:
            copy.wait_send()


def hot_rows(codes, start, count):
    slots = row_ids((count, codes.shape[1])) + start
    return (slots == codes[0:1, :]) | (slots == codes[1:2, :])


def return_copies(buf, back, q, half, sems, local, dp_at, ex_at):
    peers = [None, (dp_at, flip(ex_at, 1)), (dp_at, flip(ex_at, 2)), (dp_at, flip(flip(ex_at, 1), 2))]
    copies = []
    for k in (2 * half, 2 * half + 1):
        if k == 0:
            copies.append(pltpu.make_async_copy(buf.at[q, 0], back.at[q, 0], local.at[q]))
        else:
            copies.append(send(buf.at[q, k], back.at[q, k], sems, 4 * q + k, peers[k]))
    return copies


def expert_forward_kernel(
    cap, group, act_ref, codes_ref, win_own, wex_own, win_far, wex_mine,
    rows_out_ref, hidden_ref, slope_ref, back_ref, win_other, wex_other,
    win_buf, wex_buf, out_buf, y_send, y_recv, w_send, w_recv, local_sem,
):
    which, half_step = pl.program_id(0), pl.program_id(1)
    half = 1 - half_step
    dp_at, ex_at, near = place()
    ysem, wsem = (y_send, y_recv), (w_send, w_recv)
    keep_in = pltpu.make_async_copy(win_far, win_other.at[dp_at], local_sem.at[2])
    loads = [
        pltpu.make_async_copy(win_own, win_buf.at[0], local_sem.at[3]),
        pltpu.make_async_copy(wex_own, wex_buf.at[0], local_sem.at[4]),
        pltpu.make_async_copy(win_other, win_buf.at[1], local_sem.at[5]),
        pltpu.make_async_copy(wex_other, wex_buf.at[1], local_sem.at[6]),
    ]
    in_own, in_passed = plane_gather(win_far, win_other, wsem, 0, dp_at, ex_at, near)
    ex_own, ex_passed = plane_gather(wex_other.at[dp_at], wex_other, wsem, 4, dp_at, ex_at, near)
    to_far = send(wex_mine, wex_other.at[dp_at], wsem, 8, (dp_at, flip(ex_at, 4)))

    def at(q, step):
        return pl.when((which == q) & (half_step == step))

    @at(0, 0)
    def _():
        keep_in.start()
        loads[0].start()
        loads[1].start()
        greet(
            [(near[k], ex_at) for k in (1, 2)]
            + [(dp_at, flip(ex_at, 1)), (dp_at, flip(ex_at, 2)), (dp_at, flip(flip(ex_at, 1), 2)), (dp_at, flip(ex_at, 4))]
        )
        to_far.start()
        keep_in.wait()
        for copy in in_own:
            copy.start()
        loads[0].wait()
        loads[1].wait()

    @at(1, 0)
    def _():
        for copy in in_passed:
            copy.wait_recv()
        loads[2].start()
        loads[2].wait()

    blocks, images = act_ref.shape[0], act_ref.shape[1]
    parts, width, hidden_width = win_buf.shape[1], act_ref.shape[3], win_buf.shape[3]
    pieces = []
    for block in range(blocks):
        start = (which * group + half * blocks + block) * cap
        total = None
        for image in range(images):
            hot = jnp.where(hot_rows(codes_ref[block, image], start, cap), 1.0, 0.0).astype(BF16)
            term = dot(hot, act_ref[block, image])
            total = term if total is None else total + term
        pieces.append(total.astype(BF16))
    rows_in = jnp.concatenate(pieces, axis=0)
    rows_out_ref[...] = rows_in.reshape(rows_out_ref.shape)
    step = hidden_width // parts
    for part in range(parts):
        cut = slice(part * step, (part + 1) * step)
        act, slope = gelu_pair(dot(rows_in, win_buf[which, :, :, cut].reshape(width, step)))
        hidden_ref[:, :, cut] = act.astype(BF16).reshape(blocks, cap, step)
        slope_ref[:, :, cut] = slope.astype(BF16).reshape(blocks, cap, step)

    @at(1, 0)
    def _():
        for own, passed in zip(ex_own, ex_passed):
            own.wait_recv()
            passed.start()
        for copy in ex_passed:
            copy.wait_recv()
        loads[3].start()
        loads[3].wait()

    result = None
    for part in range(parts):
        cut = slice(part * step, (part + 1) * step)
        term = dot(hidden_ref[:, :, cut].reshape(blocks * cap, step), wex_buf[which, part])
        result = term if result is None else result + term
    out_buf[which, pl.ds(half * blocks, blocks)] = result.astype(BF16).reshape(blocks, cap, width)

    for q in range(2):
        for step_at in range(2):

            @at(q, step_at)
            def _():
                for copy in return_copies(out_buf, back_ref, q, 1 - step_at, ysem, local_sem, dp_at, ex_at):
                    copy.start()

    @at(0, 0)
    def _():
        in_own[0].wait_recv()
        in_passed[0].start()
        in_own[1].wait_recv()
        in_passed[1].start()

    @at(0, 1)
    def _():
        to_far.wait_recv()
        for copy in ex_own:
            copy.start()

    @at(1, 1)
    def _():
        for q in range(2):
            for step_at in range(2):
                for copy in return_copies(out_buf, back_ref, q, 1 - step_at, ysem, local_sem, dp_at, ex_at):
                    copy.wait()
        for copy in in_own + in_passed + ex_own + ex_passed + [to_far]:
            copy.wait_send()


def hot_cols(codes, count):
    return lane_ids((codes.shape[0], count)) == codes


def combine_back_kernel(
    images, cap, group, total_tokens, shard, experts, ext_ref, resid_ref, came_ref, cols_ref, gates_ref, target_ref,
    valid_ref, codes_ref, grow_ref, rows_ref, hidden_ref, slope_ref, win_own, wex_own, win_other, wex_other,
    out_ref, dout_ref, dlogit_ref, loss_ref, back_ref, gin_ref, gex_ref, got_in, got_ex,
    dlow, win_buf, wex_buf, acc_in, acc_out, low_in, low_ex, out_buf,
    t_send, t_recv, y_send, y_recv, w_send, w_recv, local_sem,
):
    step_at = pl.program_id(0)
    dp_at, ex_at, near = place()
    mate, across = (dp_at, flip(ex_at, 1)), (dp_at, flip(ex_at, 2))
    tsem, ysem, wsem = (t_send, t_recv), (y_send, y_recv), (w_send, w_recv)
    at_expert = jnp.maximum(step_at - images, 0)
    which, half = 1 - at_expert // 2, lax.rem((at_expert + 1) // 2, 2)
    order = [(1, 0), (1, 1), (0, 1), (0, 0)]
    loads = [
        pltpu.make_async_copy(win_own, win_buf.at[0], local_sem.at[3]),
        pltpu.make_async_copy(wex_own, wex_buf.at[0], local_sem.at[4]),
        pltpu.make_async_copy(win_other, win_buf.at[1], local_sem.at[5]),
        pltpu.make_async_copy(wex_other, wex_buf.at[1], local_sem.at[6]),
    ]
    stores = [
        pltpu.make_async_copy(low_in.at[0], gin_ref.at[0], local_sem.at[7]),
        pltpu.make_async_copy(low_ex.at[0], gex_ref.at[0], local_sem.at[8]),
        pltpu.make_async_copy(low_in.at[1], gin_ref.at[1], local_sem.at[9]),
        pltpu.make_async_copy(low_ex.at[1], gex_ref.at[1], local_sem.at[10]),
    ]
    spread = []
    for t, (grad, got, first) in enumerate(((low_in, got_in, 1), (low_ex, got_ex, 2))):
        for s, owner in enumerate((near[first], near[3])):
            spread.append(send(grad.at[1, owner], got.at[s], wsem, 2 * t + s, (near[first], ex_at)))

    def to_mate(step):
        return send(dlow.at[0, step], dlow.at[1, step], tsem, step, mate)

    def to_chip(step):
        return send(dlow.at[0, step], dlow.at[2, step], tsem, images + step, across)

    def onward(step):
        return send(dlow.at[2, step], dlow.at[3, step], tsem, 2 * images + step, mate)

    def returns(step):
        q, side = order[step]
        return return_copies(out_buf, back_ref, q, side, ysem, local_sem, dp_at, ex_at)

    @pl.when(step_at == 0)
    def _():
        for copy in loads:
            copy.start()
        greet(
            [(near[k], ex_at) for k in (1, 2)] + [mate, across, (dp_at, flip(flip(ex_at, 1), 2))]
        )

    @pl.when(step_at < images)
    def _():
        count = came_ref.shape[0]
        cols = cols_ref[...]
        rows = cols.shape[0]
        hot = jnp.concatenate(
            [
                jnp.where(hot_cols(cols[:, 0:1], count), 1.0, 0.0).astype(BF16),
                jnp.where(hot_cols(cols[:, 1:2], count), 1.0, 0.0).astype(BF16),
            ],
            axis=0,
        )
        both = dot(hot, came_ref[...])
        from_first, from_second = both[:rows], both[rows:]
        gates = gates_ref[...]
        first, second = gates[:, experts : experts + 1], gates[:, experts + 1 : experts + 2]
        output = resid_ref[...] + first * from_first + second * from_second
        out_ref[...] = output.astype(BF16)
        residue = output - target_ref[...].astype(F32)
        valid = valid_ref[...]
        square = jnp.mean(residue * residue, axis=-1, keepdims=True) * valid[:, 0:1]

        @pl.when(step_at == 0)
        def _():
            loss_ref[...] = jnp.zeros_like(loss_ref)

        counts = jnp.sum(ext_ref[experts + 2 : experts + 4, :], axis=-1, keepdims=True)
        count_all = (counts[0:1] * 128.0 + counts[1:2]) / shard
        loss_ref[...] += jnp.sum(square) / count_all
        dout = (total_tokens / count_all * valid[:, 0:1]) * residue
        dout_ref[...] = dout
        dlow[0, step_at] = dout.astype(BF16)
        lanes = lane_ids((1, 128))
        grad = jnp.where(
            lanes == cols[:, 2:3], jnp.sum(dout * from_first, axis=-1, keepdims=True), 0.0
        ) + jnp.where(lanes == cols[:, 3:4], jnp.sum(dout * from_second, axis=-1, keepdims=True), 0.0)
        real = jnp.where(lanes < experts, gates, 0.0)
        dlogit_ref[...] = real * (grad - jnp.sum(real * grad, axis=-1, keepdims=True))

    for step in range(images):

        @pl.when(step_at == step)
        def _():
            to_chip(step).start()
            to_mate(step).start()
            if step >= 3:
                to_chip(step - 3).wait_recv()
                onward(step - 3).start()

    @pl.when(step_at == images)
    def _():
        for copy in loads:
            copy.wait()
        for step in range(images):
            to_mate(step).wait_recv()

    @pl.when(step_at == images + 1)
    def _():
        for step in range(images - 3, images):
            to_chip(step).wait_recv()
            onward(step).start()
        for step in range(images):
            onward(step).wait_recv()

    @pl.when(step_at >= images)
    def _():
        blocks = group // 2
        parts, width, hidden_width = win_buf.shape[1], dlow.shape[3], win_buf.shape[3]
        pieces = []
        for block in range(blocks):
            start = (which * group + half * blocks + block) * cap
            total = None
            slot_gate = None
            for image in range(images):
                codes = codes_ref[half * blocks + block, image]
                slots = row_ids((cap, codes.shape[1])) + start
                is_first = slots == codes[0:1, :]
                is_second = slots == codes[1:2, :]
                hot = jnp.where(is_first | is_second, 1.0, 0.0).astype(BF16)
                term = dot(hot, dlow[half * blocks + block, image])
                gain = grow_ref[half * blocks + block, image]
                picked = jnp.where(is_first, gain[0:1, :], jnp.where(is_second, gain[1:2, :], 0.0))
                picked = jnp.sum(picked, axis=-1, keepdims=True)
                total = term if total is None else total + term
                slot_gate = picked if slot_gate is None else slot_gate + picked
            pieces.append((total * slot_gate).astype(BF16))
        grads = jnp.concatenate(pieces, axis=0)
        grads_t = grads.T
        rows_in_t = rows_ref[...].reshape(blocks * cap, -1).T
        step = hidden_width // parts
        result = None
        for offset in range(0, hidden_width, step):
            cut = slice(offset, offset + step)
            hidden = hidden_ref[:, :, cut].reshape(blocks * cap, step)
            slope = slope_ref[:, :, cut].reshape(blocks * cap, step).astype(F32)
            dpre = (contract_cols(grads, wex_buf[which, offset // step]) * slope).astype(BF16)
            gin = dot(rows_in_t, dpre)
            gout = dot(grads_t, hidden)
            term = contract_cols(dpre, win_buf[which, :, :, cut].reshape(width, step))
            result = term if result is None else result + term

            @pl.when(lax.rem(at_expert, 2) == 0)
            def _():
                acc_in[:, cut] = gin
                acc_out[:, cut] = gout

            @pl.when(lax.rem(at_expert, 2) == 1)
            def _():
                total_in = (acc_in[:, cut] + gin).astype(BF16)
                low_in[which, :, :, cut] = total_in.reshape(parts, width // parts, step)
                low_ex[which, offset // step] = (acc_out[:, cut] + gout).astype(BF16)

        out_buf[which, pl.ds(half * blocks, blocks)] = result.astype(BF16).reshape(blocks, cap, width)

    for step in range(4):

        @pl.when(step_at == images + step)
        def _():
            for copy in returns(step):
                copy.start()
            if step == 1:
                for copy in spread + stores[2:]:
                    copy.start()

    @pl.when(step_at == images + 3)
    def _():
        for copy in stores[:2]:
            copy.start()
        for step in range(4):
            for copy in returns(step):
                copy.wait()
        for copy in spread + stores:
            copy.wait()
        for step in range(images):
            to_mate(step).wait_send()
            to_chip(step).wait_send()
            onward(step).wait_send()


def back_kernel(
    images, experts, tok_ref, dense_w, ext_ref, cols_ref, back_ref, dlogit_ref, resid_ref,
    dout_ref, qkv_ref, probs_ref, mixed_ref, loss_ref, gin_ref, gex_ref, got_in_ref, got_ex_ref,
    tgrad_ref, dense_ref, misc_ref, gin_out, gex_out,
    acc, acc_misc, part_in, part_ex, got_in, got_ex, sum_in, sum_ex, more_in, more_ex, far_in, far_ex, came_in, came_ex,
    low, mate, low_mate, plane, low_plane, line, misc_got, local_sem, w_send, w_recv, d_send, d_recv, m_send, m_recv,
):
    step_at = pl.program_id(0)
    dp_at, ex_at, near = place()
    core, floor = lax.rem(ex_at, 2), ex_at // 2
    wsem, dsem, msem = (w_send, w_recv), (d_send, d_recv), (m_send, m_recv)
    tensors = [
        (gin_ref, part_in, got_in, sum_in, more_in, far_in, came_in, gin_out, 1, 2),
        (gex_ref, part_ex, got_ex, sum_ex, more_ex, far_ex, came_ex, gex_out, 2, 1),
    ]

    def local_copies():
        copies = []
        for t, (grad, part, _, _, _, _, _, _, _, second) in enumerate(tensors):
            for q in range(2):
                for s in range(2):
                    owner = dp_at if s == 0 else near[second]
                    copies.append(
                        pltpu.make_async_copy(grad.at[q, owner], part.at[q, s], local_sem.at[4 * t + 2 * q + s])
                    )
        copies.append(pltpu.make_async_copy(got_in_ref, got_in.at[1], local_sem.at[8]))
        copies.append(pltpu.make_async_copy(got_ex_ref, got_ex.at[1], local_sem.at[9]))
        return copies

    def first_round(q):
        copies = []
        for t, (grad, _, got, _, _, _, _, _, first, _) in enumerate(tensors):
            for s in range(2):
                owner = near[first] if s == 0 else near[3]
                copies.append(
                    send(grad.at[q, owner], got.at[q, s], wsem, 8 * q + 4 * t + s, (near[first], ex_at))
                )
        return copies

    def second_round(q):
        return [
            send(passed.at[q], more.at[q], wsem, 8 * q + 4 * t + 2, (near[second], ex_at))
            for t, (_, _, _, passed, more, _, _, _, _, second) in enumerate(tensors)
        ]

    def far_round():
        return [
            send(far, came, wsem, 4 * t + 3, (dp_at, flip(ex_at, 4)))
            for t, (_, _, _, _, _, far, came, _, _, _) in enumerate(tensors)
        ]

    def add_first(q):
        for _, part, got, passed, _, _, _, _, _, _ in tensors:
            passed[q] = (part[q, 1].astype(F32) + got[q, 1].astype(F32)).astype(BF16)
        for copy in second_round(q):
            copy.start()

    def total_of(tensor, q):
        _, part, got, _, more, _, _, _, _, _ = tensor
        return part[q, 0].astype(F32) + got[q, 0].astype(F32) + more[q].astype(F32)

    @pl.when(step_at == 0)
    def _():
        for copy in local_copies():
            copy.start()
        greet(
            [(near[k], ex_at) for k in (1, 2, 3)]
            + [(dp_at, flip(ex_at, bit)) for bit in (1, 2, 4)]
            + [(dp_at, flip(flip(ex_at, 2), 4))]
        )
        for copy in local_copies():
            copy.wait()
        add_first(1)

    count = back_ref.shape[0]
    cols = cols_ref[...]
    hot = jnp.where(hot_cols(cols[:, 0:1], count) | hot_cols(cols[:, 1:2], count), 1.0, 0.0)
    dlogits = dlogit_ref[...]
    dact = dot(hot.astype(BF16), back_ref[...])
    dlogits_high = dlogits.astype(BF16)
    router_t = ext_ref[...].astype(BF16)
    dlogits_low = (dlogits - dlogits_high.astype(F32)).astype(BF16)
    dact = dact + dot(dlogits_high, router_t) + dot(dlogits_low, router_t)

    resid = resid_ref[...]
    normed_two, inverse_two = normalize(resid)
    gain_two = ext_ref[experts + 1 : experts + 2, :]
    act_two = (normed_two * gain_two).astype(BF16)
    grouter = contract_rows(dlogits_high, act_two) + contract_rows(dlogits_low, act_two)

    def norm_back(grad, normed, inverse, gain):
        scaled = grad * gain
        gain_grad = jnp.sum(grad * normed, axis=0, keepdims=True)
        inner = (
            scaled
            - jnp.mean(scaled, axis=-1, keepdims=True)
            - normed * jnp.mean(scaled * normed, axis=-1, keepdims=True)
        )
        return inverse * inner, gain_grad

    grad_two, ggain_two = norm_back(dact, normed_two, inverse_two, gain_two)
    dresid = dout_ref[...] + grad_two
    branch = dresid.astype(BF16)
    mixed = mixed_ref[...]
    gout = contract_rows(mixed, branch)
    width = branch.shape[1]
    dmixed = contract_cols(branch, dense_w[:, 3 * width : 4 * width]).astype(BF16)
    qkv = qkv_ref[...]
    low_half = lane_ids((1, 128)) < 64
    dqs, dks, dvs = [], [], []
    for pair in range(width // 128):
        cut = slice(128 * pair, 128 * (pair + 1))
        queries = qkv[:, cut]
        key_rows = qkv[:, width + 128 * pair : width + 128 * (pair + 1)]
        values = qkv[:, 2 * width + 128 * pair : 2 * width + 128 * (pair + 1)]
        dmix = dmixed[:, cut]
        dq = []
        dk = dv = None
        for side in range(2):
            mask = low_half if side == 0 else jnp.logical_not(low_half)
            dmask = jnp.where(mask, dmix, jnp.zeros_like(dmix))
            qmask = jnp.where(mask, queries, jnp.zeros_like(queries))
            probs_low = probs_ref[2 * pair + side]
            probs = probs_low.astype(F32)
            dprobs = contract_cols(dmask, values)
            dscore = probs * (dprobs - jnp.sum(probs * dprobs, axis=-1, keepdims=True))
            dscore = dscore.astype(BF16)
            dq.append(dot(dscore, key_rows))
            dk_term = contract_rows(dscore, qmask)
            dv_term = contract_rows(probs_low, dmask)
            dk = dk_term if dk is None else dk + dk_term
            dv = dv_term if dv is None else dv + dv_term
        dqs.append((jnp.where(low_half, dq[0], dq[1]) * 0.125).astype(BF16))
        dks.append((dk * 0.125).astype(BF16))
        dvs.append(dv.astype(BF16))
    dqkv = jnp.concatenate(dqs + dks + dvs, axis=1)
    inputs = tok_ref[...].astype(F32)
    normed_one, inverse_one = normalize(inputs)
    gain_one = ext_ref[experts : experts + 1, :]
    act_one = (normed_one * gain_one).astype(BF16)
    gqkv = contract_rows(act_one, dqkv)
    dact_one = contract_cols(dqkv, dense_w[:, : 3 * width])
    grad_one, ggain_one = norm_back(dact_one, normed_one, inverse_one, gain_one)
    tgrad_ref[...] = dresid + grad_one
    ids = row_ids((8, width))
    gmisc = jnp.concatenate(
        [grouter[:8], jnp.where(ids == 0, ggain_one, jnp.where(ids == 1, ggain_two, 0.0))], axis=0
    )

    @pl.when(step_at == 0)
    def _():
        acc[:, : 3 * width] = gqkv
        acc[:, 3 * width :] = gout
        loss_row = jnp.where(row_ids((8, 128)) == 2, loss_ref[...], 0.0)
        acc_misc[...] = gmisc + jnp.concatenate(
            [jnp.zeros((8, width), F32), jnp.concatenate([loss_row] * (width // 128), axis=1)], axis=0
        )

    @pl.when(step_at > 0)
    def _():
        acc[:, : 3 * width] += gqkv
        acc[:, 3 * width :] += gout
        acc_misc[...] += gmisc

    @pl.when(step_at == 1)
    def _():
        for copy in second_round(1):
            copy.wait_recv()
        for tensor in tensors:
            tensor[5][...] = total_of(tensor, 1).astype(BF16)
        for copy in far_round() + first_round(0):
            copy.start()

    @pl.when(step_at == images - 1)
    def _():
        lines, shard = low.shape[1], low.shape[3]
        low[...] = acc[...].astype(BF16).reshape(low.shape)
        other = lax.rem(core + 1, 2)
        to_mate = send(low.at[:, :, other], mate, dsem, 0, (dp_at, flip(ex_at, 1)))
        to_mate.start()
        misc_peers = [
            (dp_at, flip(ex_at, 1)), (near[1], ex_at), (near[2], ex_at), (dp_at, flip(ex_at, 2)), (dp_at, flip(ex_at, 4)),
        ]
        misc = [send(acc_misc.at[...] if k == 0 else misc_got.at[5 + k - 1], misc_got.at[k], msem, k, misc_peers[k]) for k in range(5)]
        misc[0].start()

        def misc_step(k):
            misc[k].wait_recv()
            before = acc_misc[...] if k == 0 else misc_got[5 + k - 1]
            misc_got[5 + k] = before + misc_got[k]
            if k < 4:
                misc[k + 1].start()

        for copy in first_round(0):
            copy.wait_recv()
        add_first(0)
        to_mate.wait_recv()
        low_mate[...] = (low[:, :, core].astype(F32) + mate[...].astype(F32)).astype(BF16)
        to_plane = [send(low_mate.at[near[k]], plane.at[k - 1], dsem, k, (near[k], ex_at)) for k in (1, 2, 3)]
        for copy in to_plane:
            copy.start()
        misc_step(0)
        misc_step(1)
        misc_step(2)
        for copy in to_plane:
            copy.wait_recv()
        summed = low_mate[dp_at].astype(F32)
        for k in range(3):
            summed = summed + plane[k].astype(F32)
        low_plane[...] = summed.astype(BF16)
        floors = [flip(floor, 1), flip(floor, 2), flip(flip(floor, 1), 2)]
        to_line = [
            send(low_plane.at[floors[k]], line.at[k], dsem, 4 + k, (dp_at, 2 * floors[k] + core)) for k in range(3)
        ]
        for copy in to_line:
            copy.start()
        misc_step(3)
        misc_step(4)
        misc_ref[...] = misc_got[9]
        for copy in to_line:
            copy.wait_recv()
        result = low_plane[floor].astype(F32)
        for k in range(3):
            result = result + line[k].astype(F32)
        dense_ref[...] = result

        for copy in second_round(0):
            copy.wait_recv()
        for copy in far_round():
            copy.wait_recv()
        for tensor in tensors:
            tensor[7][...] = total_of(tensor, 0) + tensor[6][...].astype(F32)
        for copy in [to_mate] + misc + to_plane + to_line + first_round(0):
            copy.wait_send()
        for copy in second_round(0) + second_round(1) + far_round():
            copy.wait_send()


def shape(dims, kind):
    return jax.ShapeDtypeStruct(dims, kind)


def whole(dims):
    return pl.BlockSpec(dims, lambda *_: (0,) * len(dims))


def per_image(*dims):
    return pl.BlockSpec((None,) + dims, lambda i: (i,) + (0,) * len(dims))


def params():
    return pltpu.CompilerParams(vmem_limit_bytes=56 * MB)


def fast_shards(
    tokens, targets, valid_mask, routes, slot_ids, ln1_gain, qkv_weight, out_weight, ln2_gain,
    router_weight, expert_in, expert_out,
):
    axes = ("dp", "expert")
    tok_rows, width = tokens.shape
    experts = lax.axis_size("expert")
    group = experts // 2
    dp = lax.axis_size("dp")
    total_tokens = tok_rows * dp * experts
    hidden_width = expert_in.shape[2]
    capacity = (5 * tok_rows // 2 // experts + 7) // 8 * 8
    cap = round_up(capacity, 16)
    images = IMG_DEV
    real_rows = tok_rows // images
    rows = round_up(real_rows, 16)
    me = lax.axis_index("expert")

    def pad_rows(array, value=0):
        array = array.reshape(images, real_rows, -1)
        return jnp.pad(array, ((0, 0), (0, rows - real_rows), (0, 0)), constant_values=value)

    valid_f = valid_mask.astype(F32)
    my_count = jnp.sum(valid_f)
    count_high = jnp.floor(my_count / 128.0)
    count_low = my_count - 128.0 * count_high
    shard = qkv_weight.shape[0]
    small = jnp.concatenate(
        [
            router_weight,
            ln1_gain[:, None],
            ln2_gain[:, None],
            jnp.broadcast_to(count_high.astype(BF16), (shard, 1)),
            jnp.broadcast_to(count_low.astype(BF16), (shard, 1)),
        ],
        axis=1,
    )
    extra = jnp.pad(small, ((0, 0), (0, 128 - experts - 4)))
    floors = experts // 2
    in_part, ex_part = (width // dp, hidden_width), (hidden_width // dp, width)
    any_space = pl.BlockSpec(memory_space=pl.ANY)

    code = jnp.where(slot_ids < capacity, (routes ^ me) * cap + slot_ids, -1)
    cols = pad_rows(jnp.concatenate([code, routes], axis=1), -1)
    row_codes = jnp.pad(cols.transpose(0, 2, 1), ((0, 0), (0, 4), (0, 0)))
    cols = jnp.pad(cols, ((0, 0), (0, 0), (0, 4)))
    tok_p = pad_rows(tokens)
    target_p = pad_rows(targets)
    valid_p = pad_rows(jnp.broadcast_to(valid_f[:, None], (tok_rows, 8)))

    gate_lanes = 128
    dense_lanes = 4 * width + 128
    (
        qkv_p, probs, mixed, resid, gates, dense_full, ext, act_all, code_all, grow_all, win_own, wex_own, win_far,
    ) = pl.pallas_call(
        lambda *refs: forward_kernel(images, real_rows, experts, *refs),
        grid=(images,),
        in_specs=[
            per_image(rows, width), whole((shard, 3 * width)), whole((shard, width)), whole((shard, 128)),
            per_image(rows, 8), per_image(8, rows), whole((images, 8, rows)), whole(in_part), whole(ex_part),
        ],
        out_specs=[
            per_image(rows, 3 * width), per_image(HEADS, rows, rows), per_image(rows, width),
            per_image(rows, width), per_image(rows, gate_lanes), whole((width, dense_lanes)), whole((128, width)),
            *[any_space] * 6,
        ],
        out_shape=[
            shape((images, rows, 3 * width), BF16), shape((images, HEADS, rows, rows), BF16),
            shape((images, rows, width), BF16), shape((images, rows, width), F32),
            shape((images, rows, gate_lanes), F32), shape((width, dense_lanes), BF16), shape((128, width), F32),
            shape((group, images, rows, width), BF16), shape((group, images, 8, rows), jnp.int32),
            shape((group, images, 8, rows), F32), shape((dp, *in_part), BF16), shape((dp, *ex_part), BF16),
            shape(in_part, BF16),
        ],
        scratch_shapes=[
            pltpu.VMEM((dp, floors, 2, shard, dense_lanes), BF16), pltpu.VMEM((images, rows, width), BF16),
            pltpu.VMEM((images, 8, rows), F32),
            *sem_pairs(19), *sem_pairs(3 * images), *sem_pairs(6), *sem_pairs(9),
            pltpu.SemaphoreType.DMA((images + 4,)),
        ],
        compiler_params=pltpu.CompilerParams(
            vmem_limit_bytes=56 * MB, collective_id=2, has_side_effects=True
        ),
        cost_estimate=pl.CostEstimate(flops=int(5e9), bytes_accessed=int(2e7), transcendentals=0),
        name="attention_forward",
    )(tok_p, qkv_weight, out_weight, extra, cols, row_codes, row_codes, expert_in[0], expert_out[0])

    half_blocks = group // 2
    def by_half(*dims):
        return pl.BlockSpec((half_blocks,) + dims, lambda q, h: (1 - h,) + (0,) * len(dims))

    def by_both(*dims):
        return pl.BlockSpec((None, half_blocks) + dims, lambda q, h: (q, 1 - h) + (0,) * len(dims))

    rows_in, hidden, slope, returned, win_other, wex_other = pl.pallas_call(
        lambda *refs: expert_forward_kernel(cap, group, *refs),
        grid=(2, 2),
        in_specs=[
            by_half(images, rows, width), by_half(images, 8, rows), any_space, any_space, whole(in_part), whole(ex_part),
        ],
        out_specs=[by_both(cap, width), by_both(cap, hidden_width), by_both(cap, hidden_width), *[any_space] * 3],
        out_shape=[
            shape((2, group, cap, width), BF16), shape((2, group, cap, hidden_width), BF16),
            shape((2, group, cap, hidden_width), BF16), shape((2, group, cap, width), BF16),
            shape((dp, *in_part), BF16), shape((dp, *ex_part), BF16),
        ],
        scratch_shapes=[
            pltpu.VMEM((2, dp, *in_part), BF16), pltpu.VMEM((2, dp, *ex_part), BF16),
            pltpu.VMEM((2, group, cap, width), BF16), *sem_pairs(8), *sem_pairs(9), pltpu.SemaphoreType.DMA((7,)),
        ],
        compiler_params=pltpu.CompilerParams(
            vmem_limit_bytes=58 * MB, collective_id=3, has_side_effects=True
        ),
        cost_estimate=pl.CostEstimate(flops=int(14e9), bytes_accessed=int(4e7), transcendentals=0),
        name="expert_forward",
    )(act_all, code_all, win_own, wex_own, win_far, expert_out[0])
    returned = returned.reshape(2 * group * cap, width)

    flip_part = (width, hidden_width // dp)
    last = images - 1

    def early(*dims):
        return pl.BlockSpec((None,) + dims, lambda i: (jnp.minimum(i, last),) + (0,) * len(dims))

    def late(*dims):
        def index(i):
            step = jnp.maximum(i - images, 0)
            return (1 - step // 2, lax.rem((step + 1) // 2, 2)) + (0,) * len(dims)

        return pl.BlockSpec((None, half_blocks) + dims, index)

    def once(dims):
        return pl.BlockSpec(dims, lambda i: (0,) * len(dims), pipeline_mode=pl.Buffered(1))

    block_out, dout, dlogits, loss_part, drows, gin, gout_t, got_in, got_ex = pl.pallas_call(
        lambda *refs: combine_back_kernel(images, cap, group, total_tokens, shard, experts, *refs),
        grid=(images + 4,),
        in_specs=[
            once((16, width)), early(rows, width), once((2 * group * cap, width)), early(rows, 8),
            early(rows, gate_lanes), early(rows, width), early(rows, 8), once((group, images, 8, rows)),
            once((group, images, 8, rows)), late(cap, width), late(cap, hidden_width), late(cap, hidden_width),
            *[any_space] * 4,
        ],
        out_specs=[
            early(rows, width), early(rows, width), early(rows, gate_lanes), whole((8, 128)), *[any_space] * 5,
        ],
        out_shape=[
            shape((images, rows, width), BF16), shape((images, rows, width), F32),
            shape((images, rows, gate_lanes), F32), shape((8, 128), F32),
            shape((2, group, cap, width), BF16), shape((2, dp, *in_part), BF16), shape((2, dp, *flip_part), BF16),
            shape((2, *in_part), BF16), shape((2, *flip_part), BF16),
        ],
        scratch_shapes=[
            pltpu.VMEM((group, images, rows, width), BF16),
            pltpu.VMEM((2, dp, *in_part), BF16), pltpu.VMEM((2, dp, *ex_part), BF16),
            pltpu.VMEM((width, hidden_width), F32), pltpu.VMEM((width, hidden_width), F32),
            pltpu.VMEM((2, dp, *in_part), BF16), pltpu.VMEM((2, dp, *flip_part), BF16),
            pltpu.VMEM((2, group, cap, width), BF16), *sem_pairs(3 * images), *sem_pairs(8), *sem_pairs(4),
            pltpu.SemaphoreType.DMA((11,)),
        ],
        compiler_params=pltpu.CompilerParams(
            vmem_limit_bytes=62 * MB, collective_id=5, has_side_effects=True
        ),
        cost_estimate=pl.CostEstimate(flops=int(24e9), bytes_accessed=int(4e7), transcendentals=0),
        name="combine_expert_backward",
    )(
        ext, resid, returned, cols, gates, target_p, valid_p, code_all, grow_all, rows_in, hidden, slope,
        win_own, wex_own, win_other, wex_other,
    )
    grad_back = drows.reshape(2 * group * cap, width)

    def vmem(*dims):
        return pltpu.VMEM(dims, BF16)

    tgrad, dense_grad, misc, gin_own, gex_own = pl.pallas_call(
        lambda *refs: back_kernel(images, experts, *refs),
        grid=(images,),
        in_specs=[
            per_image(rows, width), whole((width, dense_lanes)), whole((128, width)), per_image(rows, 8),
            whole((2 * group * cap, width)), per_image(rows, gate_lanes), per_image(rows, width), per_image(rows, width),
            per_image(rows, 3 * width), per_image(HEADS, rows, rows), per_image(rows, width), whole((8, 128)),
            *[any_space] * 4,
        ],
        out_specs=[
            per_image(rows, width), whole((shard, 4 * width)), whole((16, width)), whole(in_part), whole(flip_part),
        ],
        out_shape=[
            shape((images, rows, width), F32), shape((shard, 4 * width), F32), shape((16, width), F32),
            shape(in_part, F32), shape(flip_part, F32),
        ],
        scratch_shapes=[
            pltpu.VMEM((width, 4 * width), F32), pltpu.VMEM((16, width), F32),
            vmem(2, 2, *in_part), vmem(2, 2, *flip_part), vmem(2, 2, *in_part), vmem(2, 2, *flip_part),
            vmem(2, *in_part), vmem(2, *flip_part), vmem(2, *in_part), vmem(2, *flip_part),
            vmem(*in_part), vmem(*flip_part), vmem(*in_part), vmem(*flip_part),
            vmem(dp, floors, 2, shard, 4 * width), vmem(dp, floors, shard, 4 * width), vmem(dp, floors, shard, 4 * width),
            vmem(3, floors, shard, 4 * width), vmem(floors, shard, 4 * width), vmem(3, shard, 4 * width),
            pltpu.VMEM((10, 16, width), F32), pltpu.SemaphoreType.DMA((10,)),
            *sem_pairs(16), *sem_pairs(8), *sem_pairs(5),
        ],
        compiler_params=pltpu.CompilerParams(
            vmem_limit_bytes=60 * MB, collective_id=1, has_side_effects=True
        ),
        cost_estimate=pl.CostEstimate(flops=int(10e9), bytes_accessed=int(3e7), transcendentals=0),
        name="attention_backward",
    )(
        tok_p, dense_full, ext, cols, grad_back, dlogits, resid, dout, qkv_p, probs, mixed,
        loss_part, gin, gout_t, got_in, got_ex,
    )
    flat = lax.axis_index("dp") * experts + me
    mine = lax.dynamic_slice_in_dim(misc, flat * shard, shard, axis=1)
    loss_value = misc[10, 0]

    def unpad(array):
        return array[:, :real_rows].reshape(tok_rows, width)

    return (
        unpad(block_out),
        loss_value,
        unpad(tgrad),
        mine[8],
        dense_grad[:, : 3 * width],
        dense_grad[:, 3 * width :],
        mine[9],
        mine[:experts].T,
        gin_own[None],
        gex_own.T[None],
    )


def solution(mesh):
    in_specs = (
        P(("dp", "expert"), None),
        P(("dp", "expert"), None),
        P(("dp", "expert")),
        P(("dp", "expert"), None),
        P(("dp", "expert"), None),
        P(("dp", "expert")),
        P(("dp", "expert"), None),
        P(("dp", "expert"), None),
        P(("dp", "expert")),
        P(("dp", "expert"), None),
        P("expert", "dp", None),
        P("expert", "dp", None),
    )
    out_specs = (
        P(("dp", "expert"), None),
        P(),
        P(("dp", "expert"), None),
        P(("dp", "expert")),
        P(("dp", "expert"), None),
        P(("dp", "expert"), None),
        P(("dp", "expert")),
        P(("dp", "expert"), None),
        P("expert", "dp", None),
        P("expert", "dp", None),
    )
    halves = mesh.shape["expert"] == 8 and mesh.shape["dp"] == 4
    body = fast_shards if halves else shards
    return jax.shard_map(body, mesh=mesh, in_specs=in_specs, out_specs=out_specs, check_vma=False)
```

```python
import jax
import jax.numpy as jnp
from jax import lax
from jax.experimental import pallas as pl
from jax.experimental.pallas import tpu as pltpu
from jax.sharding import PartitionSpec as P

HEADS = 8
IMG_DEV = 5


HIGH = lax.Precision.HIGHEST
EPS = 1e-06


def layer_norm(values, scale_gain):
    row_mean = jnp.mean(values, axis=-1, keepdims=True)
    centered = values - row_mean
    variance = jnp.mean(centered * centered, axis=-1, keepdims=True)
    inverse = lax.rsqrt(variance + EPS)
    normed = centered * inverse
    return (normed * scale_gain, normed, inverse)


def layer_norm_back(grad_in, normed, inverse, scale_gain):
    scaled = grad_in * scale_gain
    gain_grad = jnp.sum(grad_in * normed, axis=0)
    inner_term = (
        scaled
        - jnp.mean(scaled, axis=-1, keepdims=True)
        - normed * jnp.mean(scaled * normed, axis=-1, keepdims=True)
    )
    return (inverse * inner_term, gain_grad)


def contract_rows(left_side, right_side):
    return lax.dot_general(
        left_side, right_side, (((0,), (0,)), ((), ())), preferred_element_type=jnp.float32
    )


def contract_cols(left_side, right_side):
    return lax.dot_general(
        left_side, right_side, (((1,), (1,)), ((), ())), preferred_element_type=jnp.float32
    )


def exact_gelu(values):
    return jax.nn.gelu(values, approximate=False)


def split_heads(qkv_low, images, head_count):
    row_count, triple_width = qkv_low.shape
    head_dim = triple_width // (3 * head_count)
    pieces = qkv_low.reshape(images, row_count // images, 3, head_count, head_dim)
    return (pieces[:, :, 0], pieces[:, :, 1], pieces[:, :, 2], head_dim ** (-0.5))


def attention_forward(qkv_low, images, head_count):
    queries, key_rows, values, score_scale = split_heads(qkv_low, images, head_count)
    scores = (
        jnp.einsum("ilhd,imhd->ihlm", queries, key_rows, preferred_element_type=jnp.float32)
        * score_scale
    )
    row_max = jnp.max(scores, axis=-1, keepdims=True)
    exp_scores = jnp.exp(scores - row_max)
    row_sum = jnp.sum(exp_scores, axis=-1, keepdims=True)
    weights_low = (exp_scores / row_sum).astype(jnp.bfloat16)
    log_total = row_max + jnp.log(row_sum)
    mixed_rows = jnp.einsum(
        "ihlm,imhd->ilhd", weights_low, values, preferred_element_type=jnp.float32
    )
    return (mixed_rows.reshape(qkv_low.shape[0], -1).astype(jnp.bfloat16), log_total)


def attention_back(qkv_low, log_total, grad_mixed, images, head_count):
    queries, key_rows, values, score_scale = split_heads(qkv_low, images, head_count)
    scores = (
        jnp.einsum("ilhd,imhd->ihlm", queries, key_rows, preferred_element_type=jnp.float32)
        * score_scale
    )
    weights_full = jnp.exp(scores - log_total)
    weights_low = weights_full.astype(jnp.bfloat16)
    grad_heads = grad_mixed.reshape(queries.shape)
    grad_weights = jnp.einsum(
        "ilhd,imhd->ihlm", grad_heads, values, preferred_element_type=jnp.float32
    )
    grad_values = jnp.einsum(
        "ihlm,ilhd->imhd", weights_low, grad_heads, preferred_element_type=jnp.float32
    )
    grad_scores = weights_full * (
        grad_weights - jnp.sum(weights_full * grad_weights, axis=-1, keepdims=True)
    )
    grad_low = grad_scores.astype(jnp.bfloat16)
    grad_queries = (
        jnp.einsum("ihlm,imhd->ilhd", grad_low, key_rows, preferred_element_type=jnp.float32)
        * score_scale
    )
    grad_keys = (
        jnp.einsum("ihlm,ilhd->imhd", grad_low, queries, preferred_element_type=jnp.float32)
        * score_scale
    )
    stacked = jnp.stack([grad_queries, grad_keys, grad_values], axis=2)
    return stacked.reshape(qkv_low.shape).astype(jnp.bfloat16)


def expert_forward(rows_in, weight_in, weight_out, block_size):
    result = jnp.zeros((rows_in.shape[0], weight_out.shape[1]), jnp.float32)
    for offset in range(0, weight_in.shape[1], block_size):
        pre_act = jnp.dot(
            rows_in, weight_in[:, offset : offset + block_size], preferred_element_type=jnp.float32
        )
        hidden = exact_gelu(pre_act).astype(jnp.bfloat16)
        result = result + jnp.dot(
            hidden, weight_out[offset : offset + block_size], preferred_element_type=jnp.float32
        )
    return result


def expert_back(rows_in, weight_in, weight_out, grad_rows_out, block_size):
    grad_rows = jnp.zeros(rows_in.shape, jnp.float32)
    grads_first = []
    grads_second = []
    for offset in range(0, weight_in.shape[1], block_size):
        slice_in = weight_in[:, offset : offset + block_size]
        slice_out = weight_out[offset : offset + block_size]
        pre_act = jnp.dot(rows_in, slice_in, preferred_element_type=jnp.float32)
        hidden, gelu_back = jax.vjp(exact_gelu, pre_act)
        grads_second.append(contract_rows(hidden.astype(jnp.bfloat16), grad_rows_out))
        grad_hidden = contract_cols(grad_rows_out, slice_out)
        grad_pre = gelu_back(grad_hidden)[0].astype(jnp.bfloat16)
        grads_first.append(contract_rows(rows_in, grad_pre))
        grad_rows = grad_rows + contract_cols(grad_pre, slice_in)
    return (grad_rows, jnp.concatenate(grads_first, axis=1), jnp.concatenate(grads_second, axis=0))


def shards(
    tokens,
    targets,
    valid_mask,
    routes,
    slot_ids,
    ln1_gain,
    qkv_weight,
    out_weight,
    ln2_gain,
    router_weight,
    expert_in,
    expert_out,
):
    tok_rows, model_width = tokens.shape
    experts = lax.axis_size("expert")
    total_tokens = tok_rows * lax.axis_size("dp") * experts
    capacity = (5 * tok_rows // 2 // experts + 7) // 8 * 8
    dense_full = (
        lax.all_gather(ln1_gain, ("dp", "expert"), axis=0, tiled=True),
        lax.all_gather(qkv_weight, ("dp", "expert"), axis=0, tiled=True),
        lax.all_gather(out_weight, ("dp", "expert"), axis=0, tiled=True),
        lax.all_gather(ln2_gain, ("dp", "expert"), axis=0, tiled=True),
        lax.all_gather(router_weight, ("dp", "expert"), axis=0, tiled=True),
    )
    gain_one, qkv_full, out_full, gain_two, router_full = dense_full
    expert_full = (
        lax.all_gather(expert_in, "dp", axis=1, tiled=True),
        lax.all_gather(expert_out, "dp", axis=1, tiled=True),
    )
    weight_in = expert_full[0][0]
    weight_out = expert_full[1][0]
    valid_f = valid_mask.astype(jnp.float32)
    valid_count = lax.psum(jnp.sum(valid_f), ("dp", "expert"))
    inputs_f = tokens.astype(jnp.float32)
    gain_one_f = gain_one.astype(jnp.float32)
    gain_two_f = gain_two.astype(jnp.float32)
    norm_one, normed_one, inverse_one = layer_norm(inputs_f, gain_one_f)
    act_one = norm_one.astype(jnp.bfloat16)
    qkv_low = jnp.dot(act_one, qkv_full, preferred_element_type=jnp.float32).astype(jnp.bfloat16)
    mixed_low, log_total = attention_forward(qkv_low, IMG_DEV, HEADS)
    residual = inputs_f + jnp.dot(mixed_low, out_full, preferred_element_type=jnp.float32)
    norm_two, normed_two, inverse_two = layer_norm(residual, gain_two_f)
    act_two = norm_two.astype(jnp.bfloat16)
    gate_probs = jax.nn.softmax(
        jnp.dot(act_two, router_full, preferred_element_type=jnp.float32), axis=-1
    )
    expert_ids = lax.broadcasted_iota(jnp.int32, (1, experts), 1)
    first_pick = (routes[:, 0:1] == expert_ids).astype(jnp.float32)
    second_pick = (routes[:, 1:2] == expert_ids).astype(jnp.float32)
    gate_first = jnp.sum(gate_probs * first_pick, axis=-1, keepdims=True)
    gate_second = jnp.sum(gate_probs * second_pick, axis=-1, keepdims=True)
    target_slot = jnp.where(slot_ids < capacity, routes * capacity + slot_ids, -1)
    slot_columns = lax.broadcasted_iota(jnp.int32, (1, experts * capacity), 1)
    first_hot = (target_slot[:, 0:1] == slot_columns).astype(jnp.bfloat16)
    second_hot = (target_slot[:, 1:2] == slot_columns).astype(jnp.bfloat16)
    both_hot = first_hot + second_hot
    outgoing = contract_rows(both_hot, act_two).astype(jnp.bfloat16)
    arrived = lax.all_to_all(
        outgoing.reshape(experts, capacity, model_width),
        "expert",
        split_axis=0,
        concat_axis=0,
        tiled=True,
    ).reshape(-1, model_width)
    hidden_block = min(512, weight_in.shape[1])
    produced = expert_forward(arrived, weight_in, weight_out, hidden_block).astype(jnp.bfloat16)
    returned = lax.all_to_all(
        produced.reshape(experts, capacity, model_width),
        "expert",
        split_axis=0,
        concat_axis=0,
        tiled=True,
    ).reshape(-1, model_width)
    from_first = jnp.dot(first_hot, returned, preferred_element_type=jnp.float32)
    from_second = jnp.dot(second_hot, returned, preferred_element_type=jnp.float32)
    output = residual + gate_first * from_first + gate_second * from_second
    residue = output - targets.astype(jnp.float32)
    local_loss = jnp.sum(valid_f * jnp.mean(residue * residue, axis=-1))
    loss_sum = lax.psum(local_loss, ("dp", "expert"))
    loss_value = loss_sum / valid_count
    grad_out = total_tokens / valid_count * valid_f[:, None] * residue
    dense_back = (
        lax.all_gather(ln1_gain, ("dp", "expert"), axis=0, tiled=True),
        lax.all_gather(qkv_weight, ("dp", "expert"), axis=0, tiled=True),
        lax.all_gather(out_weight, ("dp", "expert"), axis=0, tiled=True),
        lax.all_gather(ln2_gain, ("dp", "expert"), axis=0, tiled=True),
        lax.all_gather(router_weight, ("dp", "expert"), axis=0, tiled=True),
    )
    expert_back_full = (
        lax.all_gather(expert_in, "dp", axis=1, tiled=True),
        lax.all_gather(expert_out, "dp", axis=1, tiled=True),
    )
    qkv_back = dense_back[1]
    out_back = dense_back[2]
    router_back = dense_back[4]
    weight_in_back = expert_back_full[0][0]
    weight_out_back = expert_back_full[1][0]
    slot_grads = (
        contract_rows(first_hot, (gate_first * grad_out).astype(jnp.bfloat16))
        + contract_rows(second_hot, (gate_second * grad_out).astype(jnp.bfloat16))
    ).astype(jnp.bfloat16)
    expert_grad_rows = lax.all_to_all(
        slot_grads.reshape(experts, capacity, model_width),
        "expert",
        split_axis=0,
        concat_axis=0,
        tiled=True,
    ).reshape(-1, model_width)
    grad_rows, grad_first_weight, grad_second_weight = expert_back(
        arrived, weight_in_back, weight_out_back, expert_grad_rows, hidden_block
    )
    grad_back = lax.all_to_all(
        grad_rows.astype(jnp.bfloat16).reshape(experts, capacity, model_width),
        "expert",
        split_axis=0,
        concat_axis=0,
        tiled=True,
    ).reshape(-1, model_width)
    grad_act_two = jnp.dot(both_hot, grad_back, preferred_element_type=jnp.float32)
    gate_grad = first_pick * jnp.sum(
        grad_out * from_first, axis=-1, keepdims=True
    ) + second_pick * jnp.sum(grad_out * from_second, axis=-1, keepdims=True)
    logit_grad = gate_probs * (gate_grad - jnp.sum(gate_probs * gate_grad, axis=-1, keepdims=True))
    router_f = router_back.astype(jnp.float32)
    grad_act_two = grad_act_two + lax.dot_general(
        logit_grad,
        router_f,
        (((1,), (1,)), ((), ())),
        precision=HIGH,
        preferred_element_type=jnp.float32,
    )
    router_grad = lax.dot_general(
        act_two.astype(jnp.float32),
        logit_grad,
        (((0,), (0,)), ((), ())),
        precision=HIGH,
        preferred_element_type=jnp.float32,
    )
    grad_norm_two, gain_two_grad = layer_norm_back(
        grad_act_two, normed_two, inverse_two, gain_two_f
    )
    grad_resid = grad_out + grad_norm_two
    branch_grad = grad_resid.astype(jnp.bfloat16)
    out_weight_grad = contract_rows(mixed_low, branch_grad)
    grad_mixed = contract_cols(branch_grad, out_back).astype(jnp.bfloat16)
    qkv_grad_low = attention_back(qkv_low, log_total, grad_mixed, IMG_DEV, HEADS)
    qkv_weight_grad = contract_rows(act_one, qkv_grad_low)
    grad_act_one = contract_cols(qkv_grad_low, qkv_back)
    grad_norm_one, gain_one_grad = layer_norm_back(
        grad_act_one, normed_one, inverse_one, gain_one_f
    )
    tokens_grad = grad_resid + grad_norm_one
    dense_grads = (
        lax.psum_scatter(gain_one_grad, ("dp", "expert"), scatter_dimension=0, tiled=True),
        lax.psum_scatter(qkv_weight_grad, ("dp", "expert"), scatter_dimension=0, tiled=True),
        lax.psum_scatter(out_weight_grad, ("dp", "expert"), scatter_dimension=0, tiled=True),
        lax.psum_scatter(gain_two_grad, ("dp", "expert"), scatter_dimension=0, tiled=True),
        lax.psum_scatter(router_grad, ("dp", "expert"), scatter_dimension=0, tiled=True),
    )
    expert_grads = (
        lax.psum_scatter(
            grad_first_weight[None].astype(jnp.bfloat16), "dp", scatter_dimension=1, tiled=True
        ).astype(jnp.float32),
        lax.psum_scatter(
            grad_second_weight[None].astype(jnp.bfloat16), "dp", scatter_dimension=1, tiled=True
        ).astype(jnp.float32),
    )
    first_result = expert_grads[0]
    second_result = expert_grads[1]
    return (
        output.astype(jnp.bfloat16),
        loss_value,
        tokens_grad,
        dense_grads[0],
        dense_grads[1],
        dense_grads[2],
        dense_grads[3],
        dense_grads[4],
        first_result,
        second_result,
    )


F32 = jnp.float32
BF16 = jnp.bfloat16
MB = 2**20


def round_up(value, unit):
    return (value + unit - 1) // unit * unit


def dot(left_side, right_side):
    return jnp.dot(left_side, right_side, preferred_element_type=F32)


def lane_ids(shape):
    return lax.broadcasted_iota(jnp.int32, shape, len(shape) - 1)


def row_ids(shape):
    return lax.broadcasted_iota(jnp.int32, shape, len(shape) - 2)


MESH = pl.DeviceIdType.MESH


def flip(index, bit):
    return index + bit * (1 - 2 * lax.rem(index // bit, 2))


def send(src, dst, sems, slot, device):
    return pltpu.make_async_remote_copy(
        src_ref=src, dst_ref=dst, send_sem=sems[0].at[slot], recv_sem=sems[1].at[slot],
        device_id=device, device_id_type=MESH,
    )


def greet(peers):
    barrier = pltpu.get_barrier_semaphore()
    for peer in peers:
        pl.semaphore_signal(barrier, inc=1, device_id=peer, device_id_type=MESH)
    pl.semaphore_wait(barrier, len(peers))


def place():
    dp_at, ex_at = lax.axis_index("dp"), lax.axis_index("expert")
    near = [None, flip(dp_at, 1), flip(dp_at, 2), flip(flip(dp_at, 1), 2)]
    return dp_at, ex_at, near


def sem_pairs(count):
    return [pltpu.SemaphoreType.DMA((count,)), pltpu.SemaphoreType.DMA((count,))]


def normalize(values):
    centered = values - jnp.mean(values, axis=-1, keepdims=True)
    inverse = lax.rsqrt(jnp.mean(centered * centered, axis=-1, keepdims=True) + EPS)
    return centered * inverse, inverse


def gelu_pair(values):
    size = jnp.abs(values)
    inv = 1.0 / (1.0 + 0.2316419 * size)
    density = 0.3989422804014327 * jnp.exp(-0.5 * values * values)
    series = inv * (
        0.319381530
        + inv * (-0.356563782 + inv * (1.781477937 + inv * (-1.821255978 + inv * 1.330274429)))
    )
    tail = density * series
    cumulative = jnp.where(values >= 0, 1.0 - tail, tail)
    return values * cumulative, cumulative + values * density


def plane_gather(mine, blocks, q, sems, base, dp_at, ex_at, near):
    half = blocks.shape[2] // 2
    first, second = pl.ds(0, half), pl.ds(half, half)
    own = [send(mine, blocks.at[q, dp_at], sems, base + k - 1, (near[k], ex_at)) for k in (1, 2)]
    passed = [
        send(blocks.at[q, near[1], first], blocks.at[q, near[1], first], sems, base + 2, (near[2], ex_at)),
        send(blocks.at[q, near[2], second], blocks.at[q, near[2], second], sems, base + 3, (near[1], ex_at)),
    ]
    return own, passed


def hot_rows(codes, start, count):
    slots = row_ids((count, codes.shape[1])) + start
    return (slots == codes[0:1, :]) | (slots == codes[1:2, :])


def return_copies(buf, back, q, half, sems, local, dp_at, ex_at):
    peers = [None, (dp_at, flip(ex_at, 1)), (dp_at, flip(ex_at, 2)), (dp_at, flip(flip(ex_at, 1), 2))]
    copies = []
    for k in (2 * half, 2 * half + 1):
        if k == 0:
            copies.append(pltpu.make_async_copy(buf.at[q, 0], back.at[q, 0], local.at[q]))
        else:
            copies.append(send(buf.at[q, k], back.at[q, k], sems, 4 * q + k, peers[k]))
    return copies


def front_kernel(
    images, real_rows, experts, cap, group,
    tok_ref, qkvw_ref, outw_ref, extra_ref, cols_ref, rows_ref, codes_ref, win_ref, wex_ref,
    qkv_ref, probs_ref, mixed_ref, resid_ref, gates_ref, dense_ref, ext_ref, rows_out_ref, hidden_ref, slope_ref,
    back_ref, code_out, grow_out, win_out, wex_out,
    dense, act, code_buf, grow_buf, win_buf, wex_buf, out_buf, kept,
    d_send, d_recv, t_send, t_recv, r_send, r_recv, w_send, w_recv, y_send, y_recv, local_sem,
):
    step_at = pl.program_id(0)
    dp_at, ex_at, near = place()
    core, floor = lax.rem(ex_at, 2), ex_at // 2
    dsem, tsem, rsem, wsem, ysem = (d_send, d_recv), (t_send, t_recv), (r_send, r_recv), (w_send, w_recv), (y_send, y_recv)
    mate, across, beyond = (dp_at, flip(ex_at, 1)), (dp_at, flip(ex_at, 2)), (dp_at, flip(flip(ex_at, 1), 2))
    far = (dp_at, flip(ex_at, 4))
    group_peers = [mate, across, beyond]
    floors = [floor, flip(floor, 1), flip(floor, 2), flip(flip(floor, 1), 2)]
    columns = [dp_at] + near[1:]
    at_expert = jnp.maximum(step_at - images, 0)
    which, half = at_expert // 2, lax.rem((at_expert + 1) // 2, 2)
    order = [(0, 0), (0, 1), (1, 1), (1, 0)]

    codes_sent = [send(codes_ref, code_buf.at[k + 1], rsem, k, group_peers[k]) for k in range(3)]
    grow_sent = [send(grow_buf.at[0], grow_buf.at[k + 1], rsem, 3 + k, group_peers[k]) for k in range(3)]
    stores = [
        pltpu.make_async_copy(code_buf, code_out, local_sem.at[2]),
        pltpu.make_async_copy(grow_buf, grow_out, local_sem.at[3]),
        pltpu.make_async_copy(win_buf, win_out, local_sem.at[4]),
        pltpu.make_async_copy(wex_buf, wex_out, local_sem.at[5]),
    ]
    in_own, in_passed = plane_gather(win_ref, win_buf, 0, wsem, 0, dp_at, ex_at, near)
    ex_own, ex_passed = plane_gather(wex_ref, wex_buf, 0, wsem, 4, dp_at, ex_at, near)
    in_far, in_far_passed = plane_gather(win_buf.at[1, dp_at], win_buf, 1, wsem, 8, dp_at, ex_at, near)
    ex_far, ex_far_passed = plane_gather(wex_buf.at[1, dp_at], wex_buf, 1, wsem, 12, dp_at, ex_at, near)
    to_far = [
        send(win_ref, win_buf.at[1, dp_at], wsem, 16, far),
        send(wex_ref, wex_buf.at[1, dp_at], wsem, 17, far),
    ]
    along_line = [
        send(dense.at[dp_at, floor, core], dense.at[dp_at, floor, core], dsem, k - 1, (dp_at, 2 * floors[k] + core))
        for k in (1, 2, 3)
    ]
    in_plane = [
        [
            send(
                dense.at[dp_at, floors[k], core], dense.at[dp_at, floors[k], core], dsem, 3 + 3 * k + p - 1,
                (near[p], ex_at),
            )
            for p in (1, 2, 3)
        ]
        for k in range(4)
    ]
    dense_mate = [
        send(dense.at[columns[p], :, core], dense.at[columns[p], :, core], dsem, 15 + p, mate) for p in range(4)
    ]

    def to_mate(step):
        return send(act.at[0, step], act.at[1, step], tsem, step, mate)

    def to_chip(step):
        return send(act.at[0, step], act.at[2, step], tsem, images + step, across)

    def onward(step):
        return send(act.at[2, step], act.at[3, step], tsem, 2 * images + step, mate)

    def returns(step):
        q, side = order[step]
        return return_copies(out_buf, back_ref, q, side, ysem, local_sem, dp_at, ex_at)

    def pass_on(own, passed):
        for first, second in zip(own, passed):
            first.wait_recv()
            second.start()

    @pl.when(step_at == 0)
    def _():
        width = outw_ref.shape[1]
        dense[dp_at, floor, core, :, : 3 * width] = qkvw_ref[...]
        dense[dp_at, floor, core, :, 3 * width : 4 * width] = outw_ref[...]
        dense[dp_at, floor, core, :, 4 * width :] = extra_ref[...]
        code_buf[0] = codes_ref[...]
        greet([(near[k], ex_at) for k in (1, 2, 3)] + group_peers + [far, (dp_at, flip(flip(ex_at, 2), 4))])
        for copy in along_line + in_plane[0]:
            copy.start()
        win_buf[0, dp_at] = win_ref[...]
        wex_buf[0, dp_at] = wex_ref[...]
        for k in (1, 2, 3):
            along_line[k - 1].wait_recv()
            for copy in in_plane[k]:
                copy.start()
        dense_mate[0].start()
        for copy in to_far + codes_sent:
            copy.start()
        for p in (1, 2, 3):
            for k in range(4):
                in_plane[k][p - 1].wait_recv()
            dense_mate[p].start()
        for copy in in_own + ex_own:
            copy.start()
        for copy in dense_mate:
            copy.wait_recv()
        full = dense[...].reshape(dense_ref.shape)
        dense_ref[...] = full
        ext_ref[...] = full[:, 4 * width :].astype(F32).T

    @pl.when(step_at < images)
    def _():
        inputs = tok_ref[...].astype(F32)
        normed, _ = normalize(inputs)
        width = inputs.shape[1]
        act_one = (normed * ext_ref[experts : experts + 1, :]).astype(BF16)
        qkv = dot(act_one, dense_ref[:, : 3 * width]).astype(BF16)
        qkv_ref[...] = qkv
        rows = inputs.shape[0]
        low_half = lane_ids((1, 128)) < 64
        key_bias = jnp.where(lane_ids((1, rows)) < real_rows, 0.0, -1e30)
        parts = []
        for pair in range(width // 128):
            lanes = slice(128 * pair, 128 * (pair + 1))
            queries = qkv[:, lanes]
            key_rows = qkv[:, width + 128 * pair : width + 128 * (pair + 1)]
            values = qkv[:, 2 * width + 128 * pair : 2 * width + 128 * (pair + 1)]
            outs = []
            for side in range(2):
                mask = low_half if side == 0 else jnp.logical_not(low_half)
                masked = jnp.where(mask, queries, jnp.zeros_like(queries))
                scores = contract_cols(masked, key_rows) * 0.125 + key_bias
                exped = jnp.exp(scores - jnp.max(scores, axis=-1, keepdims=True))
                probs = (exped * (1.0 / jnp.sum(exped, axis=-1, keepdims=True))).astype(BF16)
                probs_ref[2 * pair + side] = probs
                outs.append(dot(probs, values))
            parts.append(jnp.where(low_half, outs[0], outs[1]).astype(BF16))
        mixed = jnp.concatenate(parts, axis=1)
        mixed_ref[...] = mixed
        resid = inputs + dot(mixed, dense_ref[:, 3 * width : 4 * width])
        resid_ref[...] = resid
        normed_two, _ = normalize(resid)
        act_two = (normed_two * ext_ref[experts + 1 : experts + 2, :]).astype(BF16)
        act[0, step_at] = act_two
        lanes = lane_ids((1, 128))
        logits = jnp.where(lanes < experts, dot(act_two, dense_ref[:, 4 * width :]), -1e30)
        exped = jnp.exp(logits - jnp.max(logits, axis=-1, keepdims=True))
        gates = exped / jnp.sum(exped, axis=-1, keepdims=True)
        cols = cols_ref[...]
        first = jnp.sum(jnp.where(lanes == cols[:, 2:3], gates, 0.0), axis=-1, keepdims=True)
        second = jnp.sum(jnp.where(lanes == cols[:, 3:4], gates, 0.0), axis=-1, keepdims=True)
        gates_ref[...] = jnp.where(lanes == experts, first, jnp.where(lanes == experts + 1, second, gates))
        logits_t = contract_cols(ext_ref[0:16, :].astype(BF16), act_two)[:experts]
        exped_t = jnp.exp(logits_t - jnp.max(logits_t, axis=0, keepdims=True))
        gates_t = exped_t / jnp.sum(exped_t, axis=0, keepdims=True)
        ids_t = row_ids(gates_t.shape)
        first_t = jnp.sum(jnp.where(ids_t == rows_ref[2:3, :], gates_t, 0.0), axis=0, keepdims=True)
        second_t = jnp.sum(jnp.where(ids_t == rows_ref[3:4, :], gates_t, 0.0), axis=0, keepdims=True)
        grow_buf[0, step_at] = jnp.where(row_ids((8, rows)) == 0, first_t, second_t)

    for step in range(images):

        @pl.when(step_at == step)
        def _():
            to_chip(step).start()
            to_mate(step).start()
            if step >= 3:
                to_chip(step - 3).wait_recv()
                onward(step - 3).start()

    @pl.when(step_at == images - 2)
    def _():
        pass_on(in_own, in_passed)

    @pl.when(step_at == images - 1)
    def _():
        for copy in grow_sent:
            copy.start()

    @pl.when(step_at == images)
    def _():
        pass_on(ex_own, ex_passed)
        to_far[0].wait_recv()
        for copy in in_far:
            copy.start()
        for copy in in_passed + codes_sent:
            copy.wait_recv()
        for step in range(images):
            to_mate(step).wait_recv()

    @pl.when(step_at == images + 1)
    def _():
        for step in range(images - 3, images):
            to_chip(step).wait_recv()
            onward(step).start()
        for step in range(images):
            onward(step).wait_recv()

    @pl.when(step_at == images + 2)
    def _():
        for copy in in_far_passed:
            copy.wait_recv()

    blocks = group // 2
    parts, width, hidden_width = win_buf.shape[1], act.shape[3], win_buf.shape[3]
    step_width = hidden_width // parts

    @pl.when(step_at >= images)
    def _():
        pieces = []
        for block in range(blocks):
            start = (which * group + half * blocks + block) * cap
            total = None
            for image in range(images):
                hot = hot_rows(code_buf[half * blocks + block, image], start, cap)
                term = dot(jnp.where(hot, 1.0, 0.0).astype(BF16), act[half * blocks + block, image])
                total = term if total is None else total + term
            pieces.append(total.astype(BF16))
        rows_in = jnp.concatenate(pieces, axis=0)
        rows_out_ref[...] = rows_in.reshape(rows_out_ref.shape)
        for part in range(parts):
            if part == 1:

                @pl.when(step_at == images + 1)
                def _():
                    pass_on(in_far, in_far_passed)
                    to_far[1].wait_recv()
                    for copy in ex_far:
                        copy.start()

            cut = slice(part * step_width, (part + 1) * step_width)
            hidden, slope = gelu_pair(dot(rows_in, win_buf[which, :, :, cut].reshape(width, step_width)))
            hidden_ref[:, :, cut] = hidden.astype(BF16).reshape(blocks, cap, step_width)
            slope_ref[:, :, cut] = slope.astype(BF16).reshape(blocks, cap, step_width)

    def second_product(source, q, side):
        result = None
        for part in range(parts):
            cut = slice(part * step_width, (part + 1) * step_width)
            term = dot(source[:, :, cut].reshape(blocks * cap, step_width), wex_buf[q, part])
            result = term if result is None else result + term
        out_buf[q, pl.ds(side * blocks, blocks)] = result.astype(BF16).reshape(blocks, cap, width)

    @pl.when(step_at == images)
    def _():
        for copy in ex_passed:
            copy.wait_recv()

    @pl.when(step_at == images + 2)
    def _():
        kept[...] = hidden_ref[...]

    @pl.when(step_at == images + 3)
    def _():
        pass_on(ex_far, ex_far_passed)
        for copy in grow_sent:
            copy.wait_recv()
        for copy in ex_far_passed:
            copy.wait_recv()
        for copy in stores:
            copy.start()
        second_product(kept, 1, 1)
        for copy in returns(2):
            copy.start()

    @pl.when((step_at >= images) & (step_at != images + 2))
    def _():
        second_product(hidden_ref, which, half)

    for step in (0, 1, 3):

        @pl.when(step_at == images + step)
        def _():
            for copy in returns(step):
                copy.start()

    @pl.when(step_at == images + 3)
    def _():
        for step in range(4):
            for copy in returns(step):
                copy.wait()
        for copy in stores:
            copy.wait()
        for step in range(images):
            to_mate(step).wait_send()
            to_chip(step).wait_send()
            onward(step).wait_send()
        for copy in along_line + dense_mate + codes_sent + grow_sent + to_far + [c for line in in_plane for c in line]:
            copy.wait_send()
        for own, passed in ((in_own, in_passed), (ex_own, ex_passed), (in_far, in_far_passed), (ex_far, ex_far_passed)):
            for copy in own + passed:
                copy.wait_send()


def hot_cols(codes, count):
    return lane_ids((codes.shape[0], count)) == codes


def combine_back_kernel(
    images, cap, group, total_tokens, shard, experts, ext_ref, resid_ref, came_ref, cols_ref, gates_ref, target_ref,
    valid_ref, codes_ref, grow_ref, rows_ref, hidden_ref, slope_ref, win_all, wex_all,
    out_ref, dout_ref, dlogit_ref, loss_ref, back_ref, gin_ref, gex_ref, far_in, far_ex,
    dlow, win_buf, wex_buf, acc_in, acc_out, low_in, low_ex, out_buf,
    got_in, got_ex, sum_in, sum_ex, more_in, more_ex,
    t_send, t_recv, y_send, y_recv, w_send, w_recv, local_sem,
):
    step_at = pl.program_id(0)
    dp_at, ex_at, near = place()
    mate, across = (dp_at, flip(ex_at, 1)), (dp_at, flip(ex_at, 2))
    tsem, ysem, wsem = (t_send, t_recv), (y_send, y_recv), (w_send, w_recv)
    at_expert = jnp.maximum(step_at - images, 0)
    which, half = 1 - at_expert // 2, lax.rem((at_expert + 1) // 2, 2)
    order = [(1, 0), (1, 1), (0, 1), (0, 0)]
    loads = [
        pltpu.make_async_copy(win_all, win_buf, local_sem.at[3]),
        pltpu.make_async_copy(wex_all, wex_buf, local_sem.at[4]),
    ]
    stores = [
        pltpu.make_async_copy(low_in.at[0], gin_ref, local_sem.at[7]),
        pltpu.make_async_copy(low_ex.at[0], gex_ref, local_sem.at[8]),
    ]
    tensors = [(low_in, got_in, sum_in, more_in, far_in, 1, 2), (low_ex, got_ex, sum_ex, more_ex, far_ex, 2, 1)]
    spread, second_round = [], []
    for t, (grad, got, passed, more, _, first, second) in enumerate(tensors):
        for s, owner in enumerate((near[first], near[3])):
            spread.append(send(grad.at[1, owner], got.at[s], wsem, 3 * t + s, (near[first], ex_at)))
        second_round.append(send(passed, more, wsem, 3 * t + 2, (near[second], ex_at)))

    def to_mate(step):
        return send(dlow.at[0, step], dlow.at[1, step], tsem, step, mate)

    def to_chip(step):
        return send(dlow.at[0, step], dlow.at[2, step], tsem, images + step, across)

    def onward(step):
        return send(dlow.at[2, step], dlow.at[3, step], tsem, 2 * images + step, mate)

    def returns(step):
        q, side = order[step]
        return return_copies(out_buf, back_ref, q, side, ysem, local_sem, dp_at, ex_at)

    @pl.when(step_at == 0)
    def _():
        for copy in loads:
            copy.start()
        greet(
            [(near[k], ex_at) for k in (1, 2)] + [mate, across, (dp_at, flip(flip(ex_at, 1), 2))]
        )

    @pl.when(step_at < images)
    def _():
        count = came_ref.shape[0]
        cols = cols_ref[...]
        rows = cols.shape[0]
        hot = jnp.concatenate(
            [
                jnp.where(hot_cols(cols[:, 0:1], count), 1.0, 0.0).astype(BF16),
                jnp.where(hot_cols(cols[:, 1:2], count), 1.0, 0.0).astype(BF16),
            ],
            axis=0,
        )
        both = dot(hot, came_ref[...])
        from_first, from_second = both[:rows], both[rows:]
        gates = gates_ref[...]
        first, second = gates[:, experts : experts + 1], gates[:, experts + 1 : experts + 2]
        output = resid_ref[...] + first * from_first + second * from_second
        out_ref[...] = output.astype(BF16)
        residue = output - target_ref[...].astype(F32)
        valid = valid_ref[...]
        square = jnp.mean(residue * residue, axis=-1, keepdims=True) * valid[:, 0:1]

        @pl.when(step_at == 0)
        def _():
            loss_ref[...] = jnp.zeros_like(loss_ref)

        counts = jnp.sum(ext_ref[experts + 2 : experts + 4, :], axis=-1, keepdims=True)
        count_all = (counts[0:1] * 128.0 + counts[1:2]) / shard
        loss_ref[...] += jnp.sum(square) / count_all
        dout = (total_tokens / count_all * valid[:, 0:1]) * residue
        dout_ref[...] = dout
        dlow[0, step_at] = dout.astype(BF16)
        lanes = lane_ids((1, 128))
        grad = jnp.where(
            lanes == cols[:, 2:3], jnp.sum(dout * from_first, axis=-1, keepdims=True), 0.0
        ) + jnp.where(lanes == cols[:, 3:4], jnp.sum(dout * from_second, axis=-1, keepdims=True), 0.0)
        real = jnp.where(lanes < experts, gates, 0.0)
        dlogit_ref[...] = real * (grad - jnp.sum(real * grad, axis=-1, keepdims=True))

    for step in range(images):

        @pl.when(step_at == step)
        def _():
            to_chip(step).start()
            to_mate(step).start()
            if step >= 3:
                to_chip(step - 3).wait_recv()
                onward(step - 3).start()

    @pl.when(step_at == images)
    def _():
        for copy in loads:
            copy.wait()
        for step in range(images):
            to_mate(step).wait_recv()

    @pl.when(step_at == images + 1)
    def _():
        for step in range(images - 3, images):
            to_chip(step).wait_recv()
            onward(step).start()
        for step in range(images):
            onward(step).wait_recv()

    @pl.when(step_at >= images)
    def _():
        blocks = group // 2
        parts, width, hidden_width = win_buf.shape[1], dlow.shape[3], win_buf.shape[3]
        pieces = []
        for block in range(blocks):
            start = (which * group + half * blocks + block) * cap
            total = None
            slot_gate = None
            for image in range(images):
                codes = codes_ref[half * blocks + block, image]
                slots = row_ids((cap, codes.shape[1])) + start
                is_first = slots == codes[0:1, :]
                is_second = slots == codes[1:2, :]
                hot = jnp.where(is_first | is_second, 1.0, 0.0).astype(BF16)
                term = dot(hot, dlow[half * blocks + block, image])
                gain = grow_ref[half * blocks + block, image]
                picked = jnp.where(is_first, gain[0:1, :], jnp.where(is_second, gain[1:2, :], 0.0))
                picked = jnp.sum(picked, axis=-1, keepdims=True)
                total = term if total is None else total + term
                slot_gate = picked if slot_gate is None else slot_gate + picked
            pieces.append((total * slot_gate).astype(BF16))
        grads = jnp.concatenate(pieces, axis=0)
        grads_t = grads.T
        rows_in_t = rows_ref[...].reshape(blocks * cap, -1).T
        step = hidden_width // parts
        result = None
        for offset in range(0, hidden_width, step):
            cut = slice(offset, offset + step)
            hidden = hidden_ref[:, :, cut].reshape(blocks * cap, step)
            slope = slope_ref[:, :, cut].reshape(blocks * cap, step).astype(F32)
            dpre = (contract_cols(grads, wex_buf[which, offset // step]) * slope).astype(BF16)
            gin = dot(rows_in_t, dpre)
            gout = dot(grads_t, hidden)
            term = contract_cols(dpre, win_buf[which, :, :, cut].reshape(width, step))
            result = term if result is None else result + term

            @pl.when(lax.rem(at_expert, 2) == 0)
            def _():
                acc_in[:, cut] = gin
                acc_out[:, cut] = gout

            @pl.when(lax.rem(at_expert, 2) == 1)
            def _():
                total_in = (acc_in[:, cut] + gin).astype(BF16)
                low_in[which, :, :, cut] = total_in.reshape(parts, width // parts, step)
                low_ex[which, offset // step] = (acc_out[:, cut] + gout).astype(BF16)

        out_buf[which, pl.ds(half * blocks, blocks)] = result.astype(BF16).reshape(blocks, cap, width)

    for step in range(4):

        @pl.when(step_at == images + step)
        def _():
            for copy in returns(step):
                copy.start()
            if step == 1:
                for copy in spread:
                    copy.start()

    @pl.when(step_at == images + 3)
    def _():
        for copy in stores:
            copy.start()
        for copy in spread:
            copy.wait_recv()
        for grad, got, passed, _, _, _, second in tensors:
            passed[...] = (grad[1, near[second]].astype(F32) + got[1].astype(F32)).astype(BF16)
        for copy in second_round:
            copy.start()
        for step in range(4):
            for copy in returns(step):
                copy.wait()
        for copy in second_round:
            copy.wait_recv()
        for grad, got, _, more, far, _, _ in tensors:
            far[...] = (grad[1, dp_at].astype(F32) + got[0].astype(F32) + more[...].astype(F32)).astype(BF16)
        for copy in stores:
            copy.wait()
        for copy in spread + second_round:
            copy.wait_send()
        for step in range(images):
            to_mate(step).wait_send()
            to_chip(step).wait_send()
            onward(step).wait_send()


def back_kernel(
    images, experts, tok_ref, dense_w, ext_ref, cols_ref, back_ref, dlogit_ref, resid_ref,
    dout_ref, qkv_ref, probs_ref, mixed_ref, loss_ref, gin_ref, gex_ref, far_in, far_ex,
    tgrad_ref, dense_ref, misc_ref, gin_out, gex_out,
    acc, acc_misc, part_in, part_ex, got_in, got_ex, sum_in, sum_ex, more_in, more_ex, came_in, came_ex,
    low, mate, low_mate, plane, low_plane, line, misc_got, local_sem, w_send, w_recv, d_send, d_recv, m_send, m_recv,
):
    step_at = pl.program_id(0)
    dp_at, ex_at, near = place()
    core, floor = lax.rem(ex_at, 2), ex_at // 2
    wsem, dsem, msem = (w_send, w_recv), (d_send, d_recv), (m_send, m_recv)
    tensors = [
        (gin_ref, part_in, got_in, sum_in, more_in, far_in, came_in, gin_out, 1, 2),
        (gex_ref, part_ex, got_ex, sum_ex, more_ex, far_ex, came_ex, gex_out, 2, 1),
    ]
    local_copies, first_round, second_round, far_round = [], [], [], []
    for t, (grad, part, got, passed, more, far, came, _, first, second) in enumerate(tensors):
        for s in range(2):
            mine = dp_at if s == 0 else near[second]
            theirs = near[first] if s == 0 else near[3]
            local_copies.append(pltpu.make_async_copy(grad.at[mine], part.at[s], local_sem.at[2 * t + s]))
            first_round.append(send(grad.at[theirs], got.at[s], wsem, 4 * t + s, (near[first], ex_at)))
        second_round.append(send(passed, more, wsem, 4 * t + 2, (near[second], ex_at)))
        far_round.append(send(far, came, wsem, 4 * t + 3, (dp_at, flip(ex_at, 4))))

    @pl.when(step_at == 0)
    def _():
        for copy in local_copies:
            copy.start()
        greet(
            [(near[k], ex_at) for k in (1, 2, 3)]
            + [(dp_at, flip(ex_at, bit)) for bit in (1, 2, 4)]
            + [(dp_at, flip(flip(ex_at, 2), 4))]
        )
        for copy in first_round + far_round:
            copy.start()

    count = back_ref.shape[0]
    cols = cols_ref[...]
    hot = jnp.where(hot_cols(cols[:, 0:1], count) | hot_cols(cols[:, 1:2], count), 1.0, 0.0)
    dlogits = dlogit_ref[...]
    dact = dot(hot.astype(BF16), back_ref[...])
    dlogits_high = dlogits.astype(BF16)
    router_t = ext_ref[...].astype(BF16)
    dlogits_low = (dlogits - dlogits_high.astype(F32)).astype(BF16)
    dact = dact + dot(dlogits_high, router_t) + dot(dlogits_low, router_t)

    resid = resid_ref[...]
    normed_two, inverse_two = normalize(resid)
    gain_two = ext_ref[experts + 1 : experts + 2, :]
    act_two = (normed_two * gain_two).astype(BF16)
    grouter = contract_rows(dlogits_high, act_two) + contract_rows(dlogits_low, act_two)

    def norm_back(grad, normed, inverse, gain):
        scaled = grad * gain
        gain_grad = jnp.sum(grad * normed, axis=0, keepdims=True)
        inner = (
            scaled
            - jnp.mean(scaled, axis=-1, keepdims=True)
            - normed * jnp.mean(scaled * normed, axis=-1, keepdims=True)
        )
        return inverse * inner, gain_grad

    grad_two, ggain_two = norm_back(dact, normed_two, inverse_two, gain_two)
    dresid = dout_ref[...] + grad_two
    branch = dresid.astype(BF16)
    mixed = mixed_ref[...]
    gout = contract_rows(mixed, branch)
    width = branch.shape[1]
    dmixed = contract_cols(branch, dense_w[:, 3 * width : 4 * width]).astype(BF16)
    qkv = qkv_ref[...]
    low_half = lane_ids((1, 128)) < 64
    dqs, dks, dvs = [], [], []
    for pair in range(width // 128):
        cut = slice(128 * pair, 128 * (pair + 1))
        queries = qkv[:, cut]
        key_rows = qkv[:, width + 128 * pair : width + 128 * (pair + 1)]
        values = qkv[:, 2 * width + 128 * pair : 2 * width + 128 * (pair + 1)]
        dmix = dmixed[:, cut]
        dq = []
        dk = dv = None
        for side in range(2):
            mask = low_half if side == 0 else jnp.logical_not(low_half)
            dmask = jnp.where(mask, dmix, jnp.zeros_like(dmix))
            qmask = jnp.where(mask, queries, jnp.zeros_like(queries))
            probs_low = probs_ref[2 * pair + side]
            probs = probs_low.astype(F32)
            dprobs = contract_cols(dmask, values)
            dscore = probs * (dprobs - jnp.sum(probs * dprobs, axis=-1, keepdims=True))
            dscore = dscore.astype(BF16)
            dq.append(dot(dscore, key_rows))
            dk_term = contract_rows(dscore, qmask)
            dv_term = contract_rows(probs_low, dmask)
            dk = dk_term if dk is None else dk + dk_term
            dv = dv_term if dv is None else dv + dv_term
        dqs.append((jnp.where(low_half, dq[0], dq[1]) * 0.125).astype(BF16))
        dks.append((dk * 0.125).astype(BF16))
        dvs.append(dv.astype(BF16))
    dqkv = jnp.concatenate(dqs + dks + dvs, axis=1)
    inputs = tok_ref[...].astype(F32)
    normed_one, inverse_one = normalize(inputs)
    gain_one = ext_ref[experts : experts + 1, :]
    act_one = (normed_one * gain_one).astype(BF16)
    gqkv = contract_rows(act_one, dqkv)
    dact_one = contract_cols(dqkv, dense_w[:, : 3 * width])
    grad_one, ggain_one = norm_back(dact_one, normed_one, inverse_one, gain_one)
    tgrad_ref[...] = dresid + grad_one
    ids = row_ids((8, width))
    gmisc = jnp.concatenate(
        [grouter[:8], jnp.where(ids == 0, ggain_one, jnp.where(ids == 1, ggain_two, 0.0))], axis=0
    )

    @pl.when(step_at == 0)
    def _():
        acc[:, : 3 * width] = gqkv
        acc[:, 3 * width :] = gout
        loss_row = jnp.where(row_ids((8, 128)) == 2, loss_ref[...], 0.0)
        acc_misc[...] = gmisc + jnp.concatenate(
            [jnp.zeros((8, width), F32), jnp.concatenate([loss_row] * (width // 128), axis=1)], axis=0
        )

    @pl.when(step_at > 0)
    def _():
        acc[:, : 3 * width] += gqkv
        acc[:, 3 * width :] += gout
        acc_misc[...] += gmisc

    @pl.when(step_at == images - 2)
    def _():
        for copy in local_copies:
            copy.wait()
        for copy in first_round:
            copy.wait_recv()
        for _, part, got, passed, _, _, _, _, _, _ in tensors:
            passed[...] = (part[1].astype(F32) + got[1].astype(F32)).astype(BF16)
        for copy in second_round:
            copy.start()

    @pl.when(step_at == images - 1)
    def _():
        lines, shard = low.shape[1], low.shape[3]
        low[...] = acc[...].astype(BF16).reshape(low.shape)
        other = lax.rem(core + 1, 2)
        to_mate = send(low.at[:, :, other], mate, dsem, 0, (dp_at, flip(ex_at, 1)))
        to_mate.start()
        misc_peers = [
            (dp_at, flip(ex_at, 1)), (near[1], ex_at), (near[2], ex_at), (dp_at, flip(ex_at, 2)), (dp_at, flip(ex_at, 4)),
        ]
        misc = [send(acc_misc.at[...] if k == 0 else misc_got.at[5 + k - 1], misc_got.at[k], msem, k, misc_peers[k]) for k in range(5)]
        misc[0].start()

        def misc_step(k):
            misc[k].wait_recv()
            before = acc_misc[...] if k == 0 else misc_got[5 + k - 1]
            misc_got[5 + k] = before + misc_got[k]
            if k < 4:
                misc[k + 1].start()

        to_mate.wait_recv()
        low_mate[...] = (low[:, :, core].astype(F32) + mate[...].astype(F32)).astype(BF16)
        to_plane = [send(low_mate.at[near[k]], plane.at[k - 1], dsem, k, (near[k], ex_at)) for k in (1, 2, 3)]
        for copy in to_plane:
            copy.start()
        misc_step(0)
        misc_step(1)
        misc_step(2)
        for copy in to_plane:
            copy.wait_recv()
        summed = low_mate[dp_at].astype(F32)
        for k in range(3):
            summed = summed + plane[k].astype(F32)
        low_plane[...] = summed.astype(BF16)
        floors = [flip(floor, 1), flip(floor, 2), flip(flip(floor, 1), 2)]
        to_line = [
            send(low_plane.at[floors[k]], line.at[k], dsem, 4 + k, (dp_at, 2 * floors[k] + core)) for k in range(3)
        ]
        for copy in to_line:
            copy.start()
        misc_step(3)
        misc_step(4)
        misc_ref[...] = misc_got[9]
        for copy in to_line:
            copy.wait_recv()
        result = low_plane[floor].astype(F32)
        for k in range(3):
            result = result + line[k].astype(F32)
        dense_ref[...] = result

        for copy in second_round + far_round:
            copy.wait_recv()
        for _, part, got, _, more, _, came, out, _, _ in tensors:
            out[...] = (
                part[0].astype(F32) + got[0].astype(F32) + more[...].astype(F32) + came[...].astype(F32)
            )
        for copy in [to_mate] + misc + to_plane + to_line + first_round + second_round + far_round:
            copy.wait_send()


def shape(dims, kind):
    return jax.ShapeDtypeStruct(dims, kind)


def whole(dims):
    return pl.BlockSpec(dims, lambda *_: (0,) * len(dims))


def per_image(*dims):
    return pl.BlockSpec((None,) + dims, lambda i: (i,) + (0,) * len(dims))


def params():
    return pltpu.CompilerParams(vmem_limit_bytes=56 * MB)


def fast_shards(
    tokens, targets, valid_mask, routes, slot_ids, ln1_gain, qkv_weight, out_weight, ln2_gain,
    router_weight, expert_in, expert_out,
):
    axes = ("dp", "expert")
    tok_rows, width = tokens.shape
    experts = lax.axis_size("expert")
    group = experts // 2
    dp = lax.axis_size("dp")
    total_tokens = tok_rows * dp * experts
    hidden_width = expert_in.shape[2]
    capacity = (5 * tok_rows // 2 // experts + 7) // 8 * 8
    cap = round_up(capacity, 16)
    images = IMG_DEV
    real_rows = tok_rows // images
    rows = round_up(real_rows, 16)
    me = lax.axis_index("expert")

    def pad_rows(array, value=0):
        array = array.reshape(images, real_rows, -1)
        return jnp.pad(array, ((0, 0), (0, rows - real_rows), (0, 0)), constant_values=value)

    valid_f = valid_mask.astype(F32)
    my_count = jnp.sum(valid_f)
    count_high = jnp.floor(my_count / 128.0)
    count_low = my_count - 128.0 * count_high
    shard = qkv_weight.shape[0]
    small = jnp.concatenate(
        [
            router_weight,
            ln1_gain[:, None],
            ln2_gain[:, None],
            jnp.broadcast_to(count_high.astype(BF16), (shard, 1)),
            jnp.broadcast_to(count_low.astype(BF16), (shard, 1)),
        ],
        axis=1,
    )
    extra = jnp.pad(small, ((0, 0), (0, 128 - experts - 4)))
    floors = experts // 2
    in_part, ex_part = (width // dp, hidden_width), (hidden_width // dp, width)
    any_space = pl.BlockSpec(memory_space=pl.ANY)

    code = jnp.where(slot_ids < capacity, (routes ^ me) * cap + slot_ids, -1)
    cols = pad_rows(jnp.concatenate([code, routes], axis=1), -1)
    row_codes = jnp.pad(cols.transpose(0, 2, 1), ((0, 0), (0, 4), (0, 0)))
    cols = jnp.pad(cols, ((0, 0), (0, 0), (0, 4)))
    tok_p = pad_rows(tokens)
    target_p = pad_rows(targets)
    valid_p = pad_rows(jnp.broadcast_to(valid_f[:, None], (tok_rows, 8)))

    gate_lanes = 128
    dense_lanes = 4 * width + 128
    half_blocks = group // 2
    last = images - 1

    def early(*dims):
        return pl.BlockSpec((None,) + dims, lambda i: (jnp.minimum(i, last),) + (0,) * len(dims))

    def late(far_first, *dims):
        def index(i):
            step = jnp.maximum(i - images, 0)
            which = 1 - step // 2 if far_first else step // 2
            return (which, lax.rem((step + 1) // 2, 2)) + (0,) * len(dims)

        return pl.BlockSpec((None, half_blocks) + dims, index)

    def once(dims):
        return pl.BlockSpec(dims, lambda i: (0,) * len(dims), pipeline_mode=pl.Buffered(1))

    (
        qkv_p, probs, mixed, resid, gates, dense_full, ext, rows_in, hidden, slope, returned, code_all, grow_all,
        win_all, wex_all,
    ) = pl.pallas_call(
        lambda *refs: front_kernel(images, real_rows, experts, cap, group, *refs),
        grid=(images + 4,),
        in_specs=[
            early(rows, width), once((shard, 3 * width)), once((shard, width)), once((shard, 128)),
            early(rows, 8), early(8, rows), once((images, 8, rows)), once(in_part), once(ex_part),
        ],
        out_specs=[
            early(rows, 3 * width), early(HEADS, rows, rows), early(rows, width), early(rows, width),
            early(rows, gate_lanes), whole((width, dense_lanes)), whole((128, width)),
            late(False, cap, width), late(False, cap, hidden_width), late(False, cap, hidden_width),
            *[any_space] * 5,
        ],
        out_shape=[
            shape((images, rows, 3 * width), BF16), shape((images, HEADS, rows, rows), BF16),
            shape((images, rows, width), BF16), shape((images, rows, width), F32),
            shape((images, rows, gate_lanes), F32), shape((width, dense_lanes), BF16), shape((128, width), F32),
            shape((2, group, cap, width), BF16), shape((2, group, cap, hidden_width), BF16),
            shape((2, group, cap, hidden_width), BF16), shape((2, group, cap, width), BF16),
            shape((group, images, 8, rows), jnp.int32), shape((group, images, 8, rows), F32),
            shape((2, dp, *in_part), BF16), shape((2, dp, *ex_part), BF16),
        ],
        scratch_shapes=[
            pltpu.VMEM((dp, floors, 2, shard, dense_lanes), BF16), pltpu.VMEM((group, images, rows, width), BF16),
            pltpu.VMEM((group, images, 8, rows), jnp.int32), pltpu.VMEM((group, images, 8, rows), F32),
            pltpu.VMEM((2, dp, *in_part), BF16), pltpu.VMEM((2, dp, *ex_part), BF16),
            pltpu.VMEM((2, group, cap, width), BF16), pltpu.VMEM((half_blocks, cap, hidden_width), BF16),
            *sem_pairs(19), *sem_pairs(3 * images), *sem_pairs(6), *sem_pairs(18), *sem_pairs(8),
            pltpu.SemaphoreType.DMA((6,)),
        ],
        compiler_params=pltpu.CompilerParams(
            vmem_limit_bytes=60 * MB, collective_id=2, has_side_effects=True
        ),
        cost_estimate=pl.CostEstimate(flops=int(20e9), bytes_accessed=int(6e7), transcendentals=0),
        name="attention_expert_forward",
    )(tok_p, qkv_weight, out_weight, extra, cols, row_codes, row_codes, expert_in[0], expert_out[0])
    returned = returned.reshape(2 * group * cap, width)

    flip_part = (width, hidden_width // dp)
    block_out, dout, dlogits, loss_part, drows, gin, gout_t, far_in, far_ex = pl.pallas_call(
        lambda *refs: combine_back_kernel(images, cap, group, total_tokens, shard, experts, *refs),
        grid=(images + 4,),
        in_specs=[
            once((16, width)), early(rows, width), once((2 * group * cap, width)), early(rows, 8),
            early(rows, gate_lanes), early(rows, width), early(rows, 8), once((group, images, 8, rows)),
            once((group, images, 8, rows)), late(True, cap, width), late(True, cap, hidden_width),
            late(True, cap, hidden_width), any_space, any_space,
        ],
        out_specs=[
            early(rows, width), early(rows, width), early(rows, gate_lanes), whole((8, 128)), *[any_space] * 3,
            once(in_part), once(flip_part),
        ],
        out_shape=[
            shape((images, rows, width), BF16), shape((images, rows, width), F32),
            shape((images, rows, gate_lanes), F32), shape((8, 128), F32),
            shape((2, group, cap, width), BF16), shape((dp, *in_part), BF16), shape((dp, *flip_part), BF16),
            shape(in_part, BF16), shape(flip_part, BF16),
        ],
        scratch_shapes=[
            pltpu.VMEM((group, images, rows, width), BF16),
            pltpu.VMEM((2, dp, *in_part), BF16), pltpu.VMEM((2, dp, *ex_part), BF16),
            pltpu.VMEM((width, hidden_width), F32), pltpu.VMEM((width, hidden_width), F32),
            pltpu.VMEM((2, dp, *in_part), BF16), pltpu.VMEM((2, dp, *flip_part), BF16),
            pltpu.VMEM((2, group, cap, width), BF16),
            *[pltpu.VMEM(dims, BF16) for dims in ((2, *in_part), (2, *flip_part), in_part, flip_part, in_part, flip_part)],
            *sem_pairs(3 * images), *sem_pairs(8), *sem_pairs(6), pltpu.SemaphoreType.DMA((9,)),
        ],
        compiler_params=pltpu.CompilerParams(
            vmem_limit_bytes=62 * MB, collective_id=5, has_side_effects=True
        ),
        cost_estimate=pl.CostEstimate(flops=int(24e9), bytes_accessed=int(4e7), transcendentals=0),
        name="combine_expert_backward",
    )(
        ext, resid, returned, cols, gates, target_p, valid_p, code_all, grow_all, rows_in, hidden, slope,
        win_all, wex_all,
    )
    grad_back = drows.reshape(2 * group * cap, width)

    def vmem(*dims):
        return pltpu.VMEM(dims, BF16)

    tgrad, dense_grad, misc, gin_own, gex_own = pl.pallas_call(
        lambda *refs: back_kernel(images, experts, *refs),
        grid=(images,),
        in_specs=[
            per_image(rows, width), whole((width, dense_lanes)), whole((128, width)), per_image(rows, 8),
            whole((2 * group * cap, width)), per_image(rows, gate_lanes), per_image(rows, width), per_image(rows, width),
            per_image(rows, 3 * width), per_image(HEADS, rows, rows), per_image(rows, width), whole((8, 128)),
            *[any_space] * 4,
        ],
        out_specs=[
            per_image(rows, width), whole((shard, 4 * width)), whole((16, width)), whole(in_part), whole(flip_part),
        ],
        out_shape=[
            shape((images, rows, width), F32), shape((shard, 4 * width), F32), shape((16, width), F32),
            shape(in_part, F32), shape(flip_part, F32),
        ],
        scratch_shapes=[
            pltpu.VMEM((width, 4 * width), F32), pltpu.VMEM((16, width), F32),
            vmem(2, *in_part), vmem(2, *flip_part), vmem(2, *in_part), vmem(2, *flip_part),
            vmem(*in_part), vmem(*flip_part), vmem(*in_part), vmem(*flip_part), vmem(*in_part), vmem(*flip_part),
            vmem(dp, floors, 2, shard, 4 * width), vmem(dp, floors, shard, 4 * width), vmem(dp, floors, shard, 4 * width),
            vmem(3, floors, shard, 4 * width), vmem(floors, shard, 4 * width), vmem(3, shard, 4 * width),
            pltpu.VMEM((10, 16, width), F32), pltpu.SemaphoreType.DMA((4,)),
            *sem_pairs(8), *sem_pairs(8), *sem_pairs(5),
        ],
        compiler_params=pltpu.CompilerParams(
            vmem_limit_bytes=60 * MB, collective_id=1, has_side_effects=True
        ),
        cost_estimate=pl.CostEstimate(flops=int(10e9), bytes_accessed=int(3e7), transcendentals=0),
        name="attention_backward",
    )(
        tok_p, dense_full, ext, cols, grad_back, dlogits, resid, dout, qkv_p, probs, mixed,
        loss_part, gin, gout_t, far_in, far_ex,
    )
    flat = lax.axis_index("dp") * experts + me
    mine = lax.dynamic_slice_in_dim(misc, flat * shard, shard, axis=1)
    loss_value = misc[10, 0]

    def unpad(array):
        return array[:, :real_rows].reshape(tok_rows, width)

    return (
        unpad(block_out),
        loss_value,
        unpad(tgrad),
        mine[8],
        dense_grad[:, : 3 * width],
        dense_grad[:, 3 * width :],
        mine[9],
        mine[:experts].T,
        gin_own[None],
        gex_own.T[None],
    )


def solution(mesh):
    in_specs = (
        P(("dp", "expert"), None),
        P(("dp", "expert"), None),
        P(("dp", "expert")),
        P(("dp", "expert"), None),
        P(("dp", "expert"), None),
        P(("dp", "expert")),
        P(("dp", "expert"), None),
        P(("dp", "expert"), None),
        P(("dp", "expert")),
        P(("dp", "expert"), None),
        P("expert", "dp", None),
        P("expert", "dp", None),
    )
    out_specs = (
        P(("dp", "expert"), None),
        P(),
        P(("dp", "expert"), None),
        P(("dp", "expert")),
        P(("dp", "expert"), None),
        P(("dp", "expert"), None),
        P(("dp", "expert")),
        P(("dp", "expert"), None),
        P("expert", "dp", None),
        P("expert", "dp", None),
    )
    halves = mesh.shape["expert"] == 8 and mesh.shape["dp"] == 4
    body = fast_shards if halves else shards
    return jax.shard_map(body, mesh=mesh, in_specs=in_specs, out_specs=out_specs, check_vma=False)
```

```python
import jax
import jax.numpy as jnp
from jax import lax
from jax.experimental import pallas as pl
from jax.experimental.pallas import tpu as pltpu
from jax.sharding import PartitionSpec as P

HEADS = 8
IMG_DEV = 5


HIGH = lax.Precision.HIGHEST
EPS = 1e-06


def layer_norm(values, scale_gain):
    row_mean = jnp.mean(values, axis=-1, keepdims=True)
    centered = values - row_mean
    variance = jnp.mean(centered * centered, axis=-1, keepdims=True)
    inverse = lax.rsqrt(variance + EPS)
    normed = centered * inverse
    return (normed * scale_gain, normed, inverse)


def layer_norm_back(grad_in, normed, inverse, scale_gain):
    scaled = grad_in * scale_gain
    gain_grad = jnp.sum(grad_in * normed, axis=0)
    inner_term = (
        scaled
        - jnp.mean(scaled, axis=-1, keepdims=True)
        - normed * jnp.mean(scaled * normed, axis=-1, keepdims=True)
    )
    return (inverse * inner_term, gain_grad)


def contract_rows(left_side, right_side):
    return lax.dot_general(
        left_side, right_side, (((0,), (0,)), ((), ())), preferred_element_type=jnp.float32
    )


def contract_cols(left_side, right_side):
    return lax.dot_general(
        left_side, right_side, (((1,), (1,)), ((), ())), preferred_element_type=jnp.float32
    )


def exact_gelu(values):
    return jax.nn.gelu(values, approximate=False)


def split_heads(qkv_low, images, head_count):
    row_count, triple_width = qkv_low.shape
    head_dim = triple_width // (3 * head_count)
    pieces = qkv_low.reshape(images, row_count // images, 3, head_count, head_dim)
    return (pieces[:, :, 0], pieces[:, :, 1], pieces[:, :, 2], head_dim ** (-0.5))


def attention_forward(qkv_low, images, head_count):
    queries, key_rows, values, score_scale = split_heads(qkv_low, images, head_count)
    scores = (
        jnp.einsum("ilhd,imhd->ihlm", queries, key_rows, preferred_element_type=jnp.float32)
        * score_scale
    )
    row_max = jnp.max(scores, axis=-1, keepdims=True)
    exp_scores = jnp.exp(scores - row_max)
    row_sum = jnp.sum(exp_scores, axis=-1, keepdims=True)
    weights_low = (exp_scores / row_sum).astype(jnp.bfloat16)
    log_total = row_max + jnp.log(row_sum)
    mixed_rows = jnp.einsum(
        "ihlm,imhd->ilhd", weights_low, values, preferred_element_type=jnp.float32
    )
    return (mixed_rows.reshape(qkv_low.shape[0], -1).astype(jnp.bfloat16), log_total)


def attention_back(qkv_low, log_total, grad_mixed, images, head_count):
    queries, key_rows, values, score_scale = split_heads(qkv_low, images, head_count)
    scores = (
        jnp.einsum("ilhd,imhd->ihlm", queries, key_rows, preferred_element_type=jnp.float32)
        * score_scale
    )
    weights_full = jnp.exp(scores - log_total)
    weights_low = weights_full.astype(jnp.bfloat16)
    grad_heads = grad_mixed.reshape(queries.shape)
    grad_weights = jnp.einsum(
        "ilhd,imhd->ihlm", grad_heads, values, preferred_element_type=jnp.float32
    )
    grad_values = jnp.einsum(
        "ihlm,ilhd->imhd", weights_low, grad_heads, preferred_element_type=jnp.float32
    )
    grad_scores = weights_full * (
        grad_weights - jnp.sum(weights_full * grad_weights, axis=-1, keepdims=True)
    )
    grad_low = grad_scores.astype(jnp.bfloat16)
    grad_queries = (
        jnp.einsum("ihlm,imhd->ilhd", grad_low, key_rows, preferred_element_type=jnp.float32)
        * score_scale
    )
    grad_keys = (
        jnp.einsum("ihlm,ilhd->imhd", grad_low, queries, preferred_element_type=jnp.float32)
        * score_scale
    )
    stacked = jnp.stack([grad_queries, grad_keys, grad_values], axis=2)
    return stacked.reshape(qkv_low.shape).astype(jnp.bfloat16)


def expert_forward(rows_in, weight_in, weight_out, block_size):
    result = jnp.zeros((rows_in.shape[0], weight_out.shape[1]), jnp.float32)
    for offset in range(0, weight_in.shape[1], block_size):
        pre_act = jnp.dot(
            rows_in, weight_in[:, offset : offset + block_size], preferred_element_type=jnp.float32
        )
        hidden = exact_gelu(pre_act).astype(jnp.bfloat16)
        result = result + jnp.dot(
            hidden, weight_out[offset : offset + block_size], preferred_element_type=jnp.float32
        )
    return result


def expert_back(rows_in, weight_in, weight_out, grad_rows_out, block_size):
    grad_rows = jnp.zeros(rows_in.shape, jnp.float32)
    grads_first = []
    grads_second = []
    for offset in range(0, weight_in.shape[1], block_size):
        slice_in = weight_in[:, offset : offset + block_size]
        slice_out = weight_out[offset : offset + block_size]
        pre_act = jnp.dot(rows_in, slice_in, preferred_element_type=jnp.float32)
        hidden, gelu_back = jax.vjp(exact_gelu, pre_act)
        grads_second.append(contract_rows(hidden.astype(jnp.bfloat16), grad_rows_out))
        grad_hidden = contract_cols(grad_rows_out, slice_out)
        grad_pre = gelu_back(grad_hidden)[0].astype(jnp.bfloat16)
        grads_first.append(contract_rows(rows_in, grad_pre))
        grad_rows = grad_rows + contract_cols(grad_pre, slice_in)
    return (grad_rows, jnp.concatenate(grads_first, axis=1), jnp.concatenate(grads_second, axis=0))


def shards(
    tokens,
    targets,
    valid_mask,
    routes,
    slot_ids,
    ln1_gain,
    qkv_weight,
    out_weight,
    ln2_gain,
    router_weight,
    expert_in,
    expert_out,
):
    tok_rows, model_width = tokens.shape
    experts = lax.axis_size("expert")
    total_tokens = tok_rows * lax.axis_size("dp") * experts
    capacity = (5 * tok_rows // 2 // experts + 7) // 8 * 8
    dense_full = (
        lax.all_gather(ln1_gain, ("dp", "expert"), axis=0, tiled=True),
        lax.all_gather(qkv_weight, ("dp", "expert"), axis=0, tiled=True),
        lax.all_gather(out_weight, ("dp", "expert"), axis=0, tiled=True),
        lax.all_gather(ln2_gain, ("dp", "expert"), axis=0, tiled=True),
        lax.all_gather(router_weight, ("dp", "expert"), axis=0, tiled=True),
    )
    gain_one, qkv_full, out_full, gain_two, router_full = dense_full
    expert_full = (
        lax.all_gather(expert_in, "dp", axis=1, tiled=True),
        lax.all_gather(expert_out, "dp", axis=1, tiled=True),
    )
    weight_in = expert_full[0][0]
    weight_out = expert_full[1][0]
    valid_f = valid_mask.astype(jnp.float32)
    valid_count = lax.psum(jnp.sum(valid_f), ("dp", "expert"))
    inputs_f = tokens.astype(jnp.float32)
    gain_one_f = gain_one.astype(jnp.float32)
    gain_two_f = gain_two.astype(jnp.float32)
    norm_one, normed_one, inverse_one = layer_norm(inputs_f, gain_one_f)
    act_one = norm_one.astype(jnp.bfloat16)
    qkv_low = jnp.dot(act_one, qkv_full, preferred_element_type=jnp.float32).astype(jnp.bfloat16)
    mixed_low, log_total = attention_forward(qkv_low, IMG_DEV, HEADS)
    residual = inputs_f + jnp.dot(mixed_low, out_full, preferred_element_type=jnp.float32)
    norm_two, normed_two, inverse_two = layer_norm(residual, gain_two_f)
    act_two = norm_two.astype(jnp.bfloat16)
    gate_probs = jax.nn.softmax(
        jnp.dot(act_two, router_full, preferred_element_type=jnp.float32), axis=-1
    )
    expert_ids = lax.broadcasted_iota(jnp.int32, (1, experts), 1)
    first_pick = (routes[:, 0:1] == expert_ids).astype(jnp.float32)
    second_pick = (routes[:, 1:2] == expert_ids).astype(jnp.float32)
    gate_first = jnp.sum(gate_probs * first_pick, axis=-1, keepdims=True)
    gate_second = jnp.sum(gate_probs * second_pick, axis=-1, keepdims=True)
    target_slot = jnp.where(slot_ids < capacity, routes * capacity + slot_ids, -1)
    slot_columns = lax.broadcasted_iota(jnp.int32, (1, experts * capacity), 1)
    first_hot = (target_slot[:, 0:1] == slot_columns).astype(jnp.bfloat16)
    second_hot = (target_slot[:, 1:2] == slot_columns).astype(jnp.bfloat16)
    both_hot = first_hot + second_hot
    outgoing = contract_rows(both_hot, act_two).astype(jnp.bfloat16)
    arrived = lax.all_to_all(
        outgoing.reshape(experts, capacity, model_width),
        "expert",
        split_axis=0,
        concat_axis=0,
        tiled=True,
    ).reshape(-1, model_width)
    hidden_block = min(512, weight_in.shape[1])
    produced = expert_forward(arrived, weight_in, weight_out, hidden_block).astype(jnp.bfloat16)
    returned = lax.all_to_all(
        produced.reshape(experts, capacity, model_width),
        "expert",
        split_axis=0,
        concat_axis=0,
        tiled=True,
    ).reshape(-1, model_width)
    from_first = jnp.dot(first_hot, returned, preferred_element_type=jnp.float32)
    from_second = jnp.dot(second_hot, returned, preferred_element_type=jnp.float32)
    output = residual + gate_first * from_first + gate_second * from_second
    residue = output - targets.astype(jnp.float32)
    local_loss = jnp.sum(valid_f * jnp.mean(residue * residue, axis=-1))
    loss_sum = lax.psum(local_loss, ("dp", "expert"))
    loss_value = loss_sum / valid_count
    grad_out = total_tokens / valid_count * valid_f[:, None] * residue
    dense_back = (
        lax.all_gather(ln1_gain, ("dp", "expert"), axis=0, tiled=True),
        lax.all_gather(qkv_weight, ("dp", "expert"), axis=0, tiled=True),
        lax.all_gather(out_weight, ("dp", "expert"), axis=0, tiled=True),
        lax.all_gather(ln2_gain, ("dp", "expert"), axis=0, tiled=True),
        lax.all_gather(router_weight, ("dp", "expert"), axis=0, tiled=True),
    )
    expert_back_full = (
        lax.all_gather(expert_in, "dp", axis=1, tiled=True),
        lax.all_gather(expert_out, "dp", axis=1, tiled=True),
    )
    qkv_back = dense_back[1]
    out_back = dense_back[2]
    router_back = dense_back[4]
    weight_in_back = expert_back_full[0][0]
    weight_out_back = expert_back_full[1][0]
    slot_grads = (
        contract_rows(first_hot, (gate_first * grad_out).astype(jnp.bfloat16))
        + contract_rows(second_hot, (gate_second * grad_out).astype(jnp.bfloat16))
    ).astype(jnp.bfloat16)
    expert_grad_rows = lax.all_to_all(
        slot_grads.reshape(experts, capacity, model_width),
        "expert",
        split_axis=0,
        concat_axis=0,
        tiled=True,
    ).reshape(-1, model_width)
    grad_rows, grad_first_weight, grad_second_weight = expert_back(
        arrived, weight_in_back, weight_out_back, expert_grad_rows, hidden_block
    )
    grad_back = lax.all_to_all(
        grad_rows.astype(jnp.bfloat16).reshape(experts, capacity, model_width),
        "expert",
        split_axis=0,
        concat_axis=0,
        tiled=True,
    ).reshape(-1, model_width)
    grad_act_two = jnp.dot(both_hot, grad_back, preferred_element_type=jnp.float32)
    gate_grad = first_pick * jnp.sum(
        grad_out * from_first, axis=-1, keepdims=True
    ) + second_pick * jnp.sum(grad_out * from_second, axis=-1, keepdims=True)
    logit_grad = gate_probs * (gate_grad - jnp.sum(gate_probs * gate_grad, axis=-1, keepdims=True))
    router_f = router_back.astype(jnp.float32)
    grad_act_two = grad_act_two + lax.dot_general(
        logit_grad,
        router_f,
        (((1,), (1,)), ((), ())),
        precision=HIGH,
        preferred_element_type=jnp.float32,
    )
    router_grad = lax.dot_general(
        act_two.astype(jnp.float32),
        logit_grad,
        (((0,), (0,)), ((), ())),
        precision=HIGH,
        preferred_element_type=jnp.float32,
    )
    grad_norm_two, gain_two_grad = layer_norm_back(
        grad_act_two, normed_two, inverse_two, gain_two_f
    )
    grad_resid = grad_out + grad_norm_two
    branch_grad = grad_resid.astype(jnp.bfloat16)
    out_weight_grad = contract_rows(mixed_low, branch_grad)
    grad_mixed = contract_cols(branch_grad, out_back).astype(jnp.bfloat16)
    qkv_grad_low = attention_back(qkv_low, log_total, grad_mixed, IMG_DEV, HEADS)
    qkv_weight_grad = contract_rows(act_one, qkv_grad_low)
    grad_act_one = contract_cols(qkv_grad_low, qkv_back)
    grad_norm_one, gain_one_grad = layer_norm_back(
        grad_act_one, normed_one, inverse_one, gain_one_f
    )
    tokens_grad = grad_resid + grad_norm_one
    dense_grads = (
        lax.psum_scatter(gain_one_grad, ("dp", "expert"), scatter_dimension=0, tiled=True),
        lax.psum_scatter(qkv_weight_grad, ("dp", "expert"), scatter_dimension=0, tiled=True),
        lax.psum_scatter(out_weight_grad, ("dp", "expert"), scatter_dimension=0, tiled=True),
        lax.psum_scatter(gain_two_grad, ("dp", "expert"), scatter_dimension=0, tiled=True),
        lax.psum_scatter(router_grad, ("dp", "expert"), scatter_dimension=0, tiled=True),
    )
    expert_grads = (
        lax.psum_scatter(
            grad_first_weight[None].astype(jnp.bfloat16), "dp", scatter_dimension=1, tiled=True
        ).astype(jnp.float32),
        lax.psum_scatter(
            grad_second_weight[None].astype(jnp.bfloat16), "dp", scatter_dimension=1, tiled=True
        ).astype(jnp.float32),
    )
    first_result = expert_grads[0]
    second_result = expert_grads[1]
    return (
        output.astype(jnp.bfloat16),
        loss_value,
        tokens_grad,
        dense_grads[0],
        dense_grads[1],
        dense_grads[2],
        dense_grads[3],
        dense_grads[4],
        first_result,
        second_result,
    )


F32 = jnp.float32
BF16 = jnp.bfloat16
MB = 2**20


def round_up(value, unit):
    return (value + unit - 1) // unit * unit


def dot(left_side, right_side):
    return jnp.dot(left_side, right_side, preferred_element_type=F32)


def lane_ids(shape):
    return lax.broadcasted_iota(jnp.int32, shape, len(shape) - 1)


def row_ids(shape):
    return lax.broadcasted_iota(jnp.int32, shape, len(shape) - 2)


MESH = pl.DeviceIdType.MESH


def flip(index, bit):
    return index + bit * (1 - 2 * lax.rem(index // bit, 2))


def send(src, dst, sems, slot, device):
    return pltpu.make_async_remote_copy(
        src_ref=src, dst_ref=dst, send_sem=sems[0].at[slot], recv_sem=sems[1].at[slot],
        device_id=device, device_id_type=MESH,
    )


def greet(peers):
    barrier = pltpu.get_barrier_semaphore()
    for peer in peers:
        pl.semaphore_signal(barrier, inc=1, device_id=peer, device_id_type=MESH)
    pl.semaphore_wait(barrier, len(peers))


def place():
    dp_at, ex_at = lax.axis_index("dp"), lax.axis_index("expert")
    near = [None, flip(dp_at, 1), flip(dp_at, 2), flip(flip(dp_at, 1), 2)]
    return dp_at, ex_at, near


def sem_pairs(count):
    return [pltpu.SemaphoreType.DMA((count,)), pltpu.SemaphoreType.DMA((count,))]


def normalize(values):
    centered = values - jnp.mean(values, axis=-1, keepdims=True)
    inverse = lax.rsqrt(jnp.mean(centered * centered, axis=-1, keepdims=True) + EPS)
    return centered * inverse, inverse


def gelu_pair(values):
    size = jnp.abs(values)
    inv = 1.0 / (1.0 + 0.2316419 * size)
    density = 0.3989422804014327 * jnp.exp(-0.5 * values * values)
    series = inv * (
        0.319381530
        + inv * (-0.356563782 + inv * (1.781477937 + inv * (-1.821255978 + inv * 1.330274429)))
    )
    tail = density * series
    cumulative = jnp.where(values >= 0, 1.0 - tail, tail)
    return values * cumulative, cumulative + values * density


def plane_gather(mine, blocks, q, sems, base, dp_at, ex_at, near):
    half = blocks.shape[2] // 2
    first, second = pl.ds(0, half), pl.ds(half, half)
    own = [send(mine, blocks.at[q, dp_at], sems, base + k - 1, (near[k], ex_at)) for k in (1, 2)]
    passed = [
        send(blocks.at[q, near[1], first], blocks.at[q, near[1], first], sems, base + 2, (near[2], ex_at)),
        send(blocks.at[q, near[2], second], blocks.at[q, near[2], second], sems, base + 3, (near[1], ex_at)),
    ]
    return own, passed


def hot_rows(codes, start, count):
    slots = row_ids((count, codes.shape[1])) + start
    return (slots == codes[0:1, :]) | (slots == codes[1:2, :])


def return_copies(buf, back, q, half, sems, local, dp_at, ex_at):
    peers = [None, (dp_at, flip(ex_at, 1)), (dp_at, flip(ex_at, 2)), (dp_at, flip(flip(ex_at, 1), 2))]
    copies = []
    for k in (2 * half, 2 * half + 1):
        if k == 0:
            copies.append(pltpu.make_async_copy(buf.at[q, 0], back.at[q, 0], local.at[q]))
        else:
            copies.append(send(buf.at[q, k], back.at[q, k], sems, 4 * q + k, peers[k]))
    return copies


def front_kernel(
    images, real_rows, experts, cap, group,
    tok_ref, qkvw_ref, outw_ref, extra_ref, cols_ref, rows_ref, codes_ref, all_cols_ref, win_ref, wex_ref,
    qkv_ref, probs_ref, mixed_ref, resid_ref, gates_ref, dense_ref, ext_ref, rows_out_ref, hidden_ref, slope_ref,
    back_ref, code_out, grow_out, win_out, wex_out,
    dense, act, code_buf, grow_buf, win_buf, wex_buf, out_buf, kept,
    d_send, d_recv, t_send, t_recv, r_send, r_recv, w_send, w_recv, y_send, y_recv, local_sem,
):
    step_at = pl.program_id(0)
    dp_at, ex_at, near = place()
    core, floor = lax.rem(ex_at, 2), ex_at // 2
    dsem, tsem, rsem, wsem, ysem = (d_send, d_recv), (t_send, t_recv), (r_send, r_recv), (w_send, w_recv), (y_send, y_recv)
    mate, across, beyond = (dp_at, flip(ex_at, 1)), (dp_at, flip(ex_at, 2)), (dp_at, flip(flip(ex_at, 1), 2))
    far = (dp_at, flip(ex_at, 4))
    group_peers = [mate, across, beyond]
    floors = [floor, flip(floor, 1), flip(floor, 2), flip(flip(floor, 1), 2)]
    columns = [dp_at] + near[1:]
    at_expert = jnp.maximum(step_at - images, 0)
    which, half = at_expert // 2, lax.rem((at_expert + 1) // 2, 2)
    order = [(0, 0), (0, 1), (1, 1), (1, 0)]

    codes_sent = [send(codes_ref, code_buf.at[k + 1], rsem, k, group_peers[k]) for k in range(3)]
    grow_sent = [send(grow_buf.at[0], grow_buf.at[k + 1], rsem, 3 + k, group_peers[k]) for k in range(3)]
    stores = [
        pltpu.make_async_copy(code_buf, code_out, local_sem.at[2]),
        pltpu.make_async_copy(grow_buf, grow_out, local_sem.at[3]),
        pltpu.make_async_copy(win_buf, win_out, local_sem.at[4]),
        pltpu.make_async_copy(wex_buf, wex_out, local_sem.at[5]),
    ]
    in_own, in_passed = plane_gather(win_ref, win_buf, 0, wsem, 0, dp_at, ex_at, near)
    ex_own, ex_passed = plane_gather(wex_ref, wex_buf, 0, wsem, 4, dp_at, ex_at, near)
    in_far, in_far_passed = plane_gather(win_buf.at[1, dp_at], win_buf, 1, wsem, 8, dp_at, ex_at, near)
    ex_far, ex_far_passed = plane_gather(wex_buf.at[1, dp_at], wex_buf, 1, wsem, 12, dp_at, ex_at, near)
    to_far = [
        send(win_ref, win_buf.at[1, dp_at], wsem, 16, far),
        send(wex_ref, wex_buf.at[1, dp_at], wsem, 17, far),
    ]
    along_line = [
        send(dense.at[dp_at, floor, core], dense.at[dp_at, floor, core], dsem, k - 1, (dp_at, 2 * floors[k] + core))
        for k in (1, 2, 3)
    ]
    in_plane = [
        [
            send(
                dense.at[dp_at, floors[k], core], dense.at[dp_at, floors[k], core], dsem, 3 + 3 * k + p - 1,
                (near[p], ex_at),
            )
            for p in (1, 2, 3)
        ]
        for k in range(4)
    ]
    dense_mate = [
        send(dense.at[columns[p], :, core], dense.at[columns[p], :, core], dsem, 15 + p, mate) for p in range(4)
    ]

    def to_mate(step):
        return send(act.at[0, step], act.at[1, step], tsem, step, mate)

    def to_chip(step):
        return send(act.at[0, step], act.at[2, step], tsem, images + step, across)

    def onward(step):
        return send(act.at[2, step], act.at[3, step], tsem, 2 * images + step, mate)

    def returns(step):
        q, side = order[step]
        return return_copies(out_buf, back_ref, q, side, ysem, local_sem, dp_at, ex_at)

    def pass_on(own, passed):
        for first, second in zip(own, passed):
            first.wait_recv()
            second.start()

    @pl.when(step_at == 0)
    def _():
        width = outw_ref.shape[1]
        dense[dp_at, floor, core, :, : 3 * width] = qkvw_ref[...]
        dense[dp_at, floor, core, :, 3 * width : 4 * width] = outw_ref[...]
        valid = jnp.maximum(all_cols_ref[...], 0).astype(F32)
        per_lane = jnp.sum(jnp.sum(valid, axis=0), axis=0, keepdims=True)
        my_count = jnp.sum(jnp.where(lane_ids((1, 8)) == 4, per_lane, 0.0), axis=-1, keepdims=True)
        count_high = jnp.floor(my_count * (1.0 / 128.0))
        lanes = lane_ids((1, 128))
        counts = jnp.where(lanes == experts + 2, count_high, 0.0) + jnp.where(
            lanes == experts + 3, my_count - 128.0 * count_high, 0.0
        )
        dense[dp_at, floor, core, :, 4 * width :] = (extra_ref[...].astype(F32) + counts).astype(BF16)
        code_buf[0] = codes_ref[...]
        greet([(near[k], ex_at) for k in (1, 2, 3)] + group_peers + [far, (dp_at, flip(flip(ex_at, 2), 4))])
        for copy in along_line + in_plane[0]:
            copy.start()
        win_buf[0, dp_at] = win_ref[...]
        wex_buf[0, dp_at] = wex_ref[...]
        for k in (1, 2, 3):
            along_line[k - 1].wait_recv()
            for copy in in_plane[k]:
                copy.start()
        dense_mate[0].start()
        for copy in to_far + codes_sent:
            copy.start()
        for p in (1, 2, 3):
            for k in range(4):
                in_plane[k][p - 1].wait_recv()
            dense_mate[p].start()
        for copy in in_own + ex_own:
            copy.start()
        for copy in dense_mate:
            copy.wait_recv()
        full = dense[...].reshape(dense_ref.shape)
        dense_ref[...] = full
        ext_ref[...] = full[:, 4 * width :].astype(F32).T

    @pl.when(step_at < images)
    def _():
        inputs = tok_ref[...].astype(F32)
        normed, _ = normalize(inputs)
        width = inputs.shape[1]
        act_one = (normed * ext_ref[experts : experts + 1, :]).astype(BF16)
        qkv = dot(act_one, dense_ref[:, : 3 * width]).astype(BF16)
        qkv_ref[...] = qkv
        rows = inputs.shape[0]
        low_half = lane_ids((1, 128)) < 64
        key_bias = jnp.where(lane_ids((1, rows)) < real_rows, 0.0, -1e30)
        parts = []
        for pair in range(width // 128):
            lanes = slice(128 * pair, 128 * (pair + 1))
            queries = qkv[:, lanes]
            key_rows = qkv[:, width + 128 * pair : width + 128 * (pair + 1)]
            values = qkv[:, 2 * width + 128 * pair : 2 * width + 128 * (pair + 1)]
            outs = []
            for side in range(2):
                mask = low_half if side == 0 else jnp.logical_not(low_half)
                masked = jnp.where(mask, queries, jnp.zeros_like(queries))
                scores = contract_cols(masked, key_rows) * 0.125 + key_bias
                exped = jnp.exp(scores - jnp.max(scores, axis=-1, keepdims=True))
                probs = (exped * (1.0 / jnp.sum(exped, axis=-1, keepdims=True))).astype(BF16)
                probs_ref[2 * pair + side] = probs
                outs.append(dot(probs, values))
            parts.append(jnp.where(low_half, outs[0], outs[1]).astype(BF16))
        mixed = jnp.concatenate(parts, axis=1)
        mixed_ref[...] = mixed
        resid = inputs + dot(mixed, dense_ref[:, 3 * width : 4 * width])
        resid_ref[...] = resid
        normed_two, _ = normalize(resid)
        act_two = (normed_two * ext_ref[experts + 1 : experts + 2, :]).astype(BF16)
        act[0, step_at] = act_two
        lanes = lane_ids((1, 128))
        logits = jnp.where(lanes < experts, dot(act_two, dense_ref[:, 4 * width :]), -1e30)
        exped = jnp.exp(logits - jnp.max(logits, axis=-1, keepdims=True))
        gates = exped / jnp.sum(exped, axis=-1, keepdims=True)
        cols = cols_ref[...]
        first = jnp.sum(jnp.where(lanes == cols[:, 2:3], gates, 0.0), axis=-1, keepdims=True)
        second = jnp.sum(jnp.where(lanes == cols[:, 3:4], gates, 0.0), axis=-1, keepdims=True)
        gates_ref[...] = jnp.where(lanes == experts, first, jnp.where(lanes == experts + 1, second, gates))
        logits_t = contract_cols(ext_ref[0:16, :].astype(BF16), act_two)[:experts]
        exped_t = jnp.exp(logits_t - jnp.max(logits_t, axis=0, keepdims=True))
        gates_t = exped_t / jnp.sum(exped_t, axis=0, keepdims=True)
        ids_t = row_ids(gates_t.shape)
        first_t = jnp.sum(jnp.where(ids_t == rows_ref[2:3, :], gates_t, 0.0), axis=0, keepdims=True)
        second_t = jnp.sum(jnp.where(ids_t == rows_ref[3:4, :], gates_t, 0.0), axis=0, keepdims=True)
        grow_buf[0, step_at] = jnp.where(row_ids((8, rows)) == 0, first_t, second_t)

    for step in range(images):

        @pl.when(step_at == step)
        def _():
            to_chip(step).start()
            to_mate(step).start()
            if step >= 3:
                to_chip(step - 3).wait_recv()
                onward(step - 3).start()

    @pl.when(step_at == images - 2)
    def _():
        pass_on(in_own, in_passed)

    @pl.when(step_at == images - 1)
    def _():
        for copy in grow_sent:
            copy.start()

    @pl.when(step_at == images)
    def _():
        pass_on(ex_own, ex_passed)
        to_far[0].wait_recv()
        for copy in in_far:
            copy.start()
        for copy in in_passed + codes_sent:
            copy.wait_recv()
        for step in range(images):
            to_mate(step).wait_recv()

    @pl.when(step_at == images + 1)
    def _():
        for step in range(images - 3, images):
            to_chip(step).wait_recv()
            onward(step).start()
        for step in range(images):
            onward(step).wait_recv()

    @pl.when(step_at == images + 2)
    def _():
        for copy in in_far_passed:
            copy.wait_recv()

    blocks = group // 2
    parts, width, hidden_width = win_buf.shape[1], act.shape[3], win_buf.shape[3]
    step_width = hidden_width // parts

    @pl.when(step_at >= images)
    def _():
        pieces = []
        for block in range(blocks):
            start = (which * group + half * blocks + block) * cap
            total = None
            for image in range(images):
                hot = hot_rows(code_buf[half * blocks + block, image], start, cap)
                term = dot(jnp.where(hot, 1.0, 0.0).astype(BF16), act[half * blocks + block, image])
                total = term if total is None else total + term
            pieces.append(total.astype(BF16))
        rows_in = jnp.concatenate(pieces, axis=0)
        rows_out_ref[...] = rows_in.reshape(rows_out_ref.shape)
        for part in range(parts):
            if part == 1:

                @pl.when(step_at == images + 1)
                def _():
                    pass_on(in_far, in_far_passed)
                    to_far[1].wait_recv()
                    for copy in ex_far:
                        copy.start()

            cut = slice(part * step_width, (part + 1) * step_width)
            hidden, slope = gelu_pair(dot(rows_in, win_buf[which, :, :, cut].reshape(width, step_width)))
            hidden_ref[:, :, cut] = hidden.astype(BF16).reshape(blocks, cap, step_width)
            slope_ref[:, :, cut] = slope.astype(BF16).reshape(blocks, cap, step_width)

    def second_product(source, q, side):
        result = None
        for part in range(parts):
            cut = slice(part * step_width, (part + 1) * step_width)
            term = dot(source[:, :, cut].reshape(blocks * cap, step_width), wex_buf[q, part])
            result = term if result is None else result + term
        out_buf[q, pl.ds(side * blocks, blocks)] = result.astype(BF16).reshape(blocks, cap, width)

    @pl.when(step_at == images)
    def _():
        for copy in ex_passed:
            copy.wait_recv()

    @pl.when(step_at == images + 2)
    def _():
        kept[...] = hidden_ref[...]

    @pl.when(step_at == images + 3)
    def _():
        pass_on(ex_far, ex_far_passed)
        for copy in grow_sent:
            copy.wait_recv()
        for copy in ex_far_passed:
            copy.wait_recv()
        for copy in stores:
            copy.start()
        second_product(kept, 1, 1)
        for copy in returns(2):
            copy.start()

    @pl.when((step_at >= images) & (step_at != images + 2))
    def _():
        second_product(hidden_ref, which, half)

    for step in (0, 1, 3):

        @pl.when(step_at == images + step)
        def _():
            for copy in returns(step):
                copy.start()

    @pl.when(step_at == images + 3)
    def _():
        for step in range(4):
            for copy in returns(step):
                copy.wait()
        for copy in stores:
            copy.wait()
        for step in range(images):
            to_mate(step).wait_send()
            to_chip(step).wait_send()
            onward(step).wait_send()
        for copy in along_line + dense_mate + codes_sent + grow_sent + to_far + [c for line in in_plane for c in line]:
            copy.wait_send()
        for own, passed in ((in_own, in_passed), (ex_own, ex_passed), (in_far, in_far_passed), (ex_far, ex_far_passed)):
            for copy in own + passed:
                copy.wait_send()


def hot_cols(codes, count):
    return lane_ids((codes.shape[0], count)) == codes


def combine_back_kernel(
    images, cap, group, total_tokens, shard, experts, ext_ref, resid_ref, came_ref, cols_ref, gates_ref, target_ref,
    codes_ref, grow_ref, rows_ref, hidden_ref, slope_ref, win_all, wex_all,
    out_ref, dout_ref, dlogit_ref, loss_ref, back_ref, gin_ref, gex_ref, far_in, far_ex,
    dlow, win_buf, wex_buf, acc_in, acc_out, low_in, low_ex, out_buf,
    got_in, got_ex, sum_in, sum_ex, more_in, more_ex,
    t_send, t_recv, y_send, y_recv, w_send, w_recv, local_sem,
):
    step_at = pl.program_id(0)
    dp_at, ex_at, near = place()
    mate, across = (dp_at, flip(ex_at, 1)), (dp_at, flip(ex_at, 2))
    tsem, ysem, wsem = (t_send, t_recv), (y_send, y_recv), (w_send, w_recv)
    at_expert = jnp.maximum(step_at - images, 0)
    which, half = 1 - at_expert // 2, lax.rem((at_expert + 1) // 2, 2)
    order = [(1, 0), (1, 1), (0, 1), (0, 0)]
    loads = [
        pltpu.make_async_copy(win_all, win_buf, local_sem.at[3]),
        pltpu.make_async_copy(wex_all, wex_buf, local_sem.at[4]),
    ]
    stores = [
        pltpu.make_async_copy(low_in.at[0], gin_ref, local_sem.at[7]),
        pltpu.make_async_copy(low_ex.at[0], gex_ref, local_sem.at[8]),
    ]
    tensors = [(low_in, got_in, sum_in, more_in, far_in, 1, 2), (low_ex, got_ex, sum_ex, more_ex, far_ex, 2, 1)]
    spread, second_round = [], []
    for t, (grad, got, passed, more, _, first, second) in enumerate(tensors):
        for s, owner in enumerate((near[first], near[3])):
            spread.append(send(grad.at[1, owner], got.at[s], wsem, 3 * t + s, (near[first], ex_at)))
        second_round.append(send(passed, more, wsem, 3 * t + 2, (near[second], ex_at)))

    def to_mate(step):
        return send(dlow.at[0, step], dlow.at[1, step], tsem, step, mate)

    def to_chip(step):
        return send(dlow.at[0, step], dlow.at[2, step], tsem, images + step, across)

    def onward(step):
        return send(dlow.at[2, step], dlow.at[3, step], tsem, 2 * images + step, mate)

    def returns(step):
        q, side = order[step]
        return return_copies(out_buf, back_ref, q, side, ysem, local_sem, dp_at, ex_at)

    @pl.when(step_at == 0)
    def _():
        for copy in loads:
            copy.start()
        greet(
            [(near[k], ex_at) for k in (1, 2)] + [mate, across, (dp_at, flip(flip(ex_at, 1), 2))]
        )

    @pl.when(step_at < images)
    def _():
        count = came_ref.shape[0]
        cols = cols_ref[...]
        rows = cols.shape[0]
        hot = jnp.concatenate(
            [
                jnp.where(hot_cols(cols[:, 0:1], count), 1.0, 0.0).astype(BF16),
                jnp.where(hot_cols(cols[:, 1:2], count), 1.0, 0.0).astype(BF16),
            ],
            axis=0,
        )
        both = dot(hot, came_ref[...])
        from_first, from_second = both[:rows], both[rows:]
        gates = gates_ref[...]
        first, second = gates[:, experts : experts + 1], gates[:, experts + 1 : experts + 2]
        output = resid_ref[...] + first * from_first + second * from_second
        out_ref[...] = output.astype(BF16)
        residue = output - target_ref[...].astype(F32)
        valid = jnp.maximum(cols[:, 4:5], 0).astype(F32)
        square = jnp.mean(residue * residue, axis=-1, keepdims=True) * valid

        @pl.when(step_at == 0)
        def _():
            loss_ref[...] = jnp.zeros_like(loss_ref)

        counts = jnp.sum(ext_ref[experts + 2 : experts + 4, :], axis=-1, keepdims=True)
        count_all = (counts[0:1] * 128.0 + counts[1:2]) / shard
        loss_ref[...] += jnp.sum(square) / count_all
        dout = (total_tokens / count_all * valid) * residue
        dout_ref[...] = dout
        dlow[0, step_at] = dout.astype(BF16)
        lanes = lane_ids((1, 128))
        grad = jnp.where(
            lanes == cols[:, 2:3], jnp.sum(dout * from_first, axis=-1, keepdims=True), 0.0
        ) + jnp.where(lanes == cols[:, 3:4], jnp.sum(dout * from_second, axis=-1, keepdims=True), 0.0)
        real = jnp.where(lanes < experts, gates, 0.0)
        dlogit_ref[...] = real * (grad - jnp.sum(real * grad, axis=-1, keepdims=True))

    for step in range(images):

        @pl.when(step_at == step)
        def _():
            to_chip(step).start()
            to_mate(step).start()
            if step >= 3:
                to_chip(step - 3).wait_recv()
                onward(step - 3).start()

    @pl.when(step_at == images)
    def _():
        for copy in loads:
            copy.wait()
        for step in range(images):
            to_mate(step).wait_recv()

    @pl.when(step_at == images + 1)
    def _():
        for step in range(images - 3, images):
            to_chip(step).wait_recv()
            onward(step).start()
        for step in range(images):
            onward(step).wait_recv()

    @pl.when(step_at >= images)
    def _():
        blocks = group // 2
        parts, width, hidden_width = win_buf.shape[1], dlow.shape[3], win_buf.shape[3]
        pieces = []
        for block in range(blocks):
            start = (which * group + half * blocks + block) * cap
            total = None
            slot_gate = None
            for image in range(images):
                codes = codes_ref[half * blocks + block, image]
                slots = row_ids((cap, codes.shape[1])) + start
                is_first = slots == codes[0:1, :]
                is_second = slots == codes[1:2, :]
                hot = jnp.where(is_first | is_second, 1.0, 0.0).astype(BF16)
                term = dot(hot, dlow[half * blocks + block, image])
                gain = grow_ref[half * blocks + block, image]
                picked = jnp.where(is_first, gain[0:1, :], jnp.where(is_second, gain[1:2, :], 0.0))
                picked = jnp.sum(picked, axis=-1, keepdims=True)
                total = term if total is None else total + term
                slot_gate = picked if slot_gate is None else slot_gate + picked
            pieces.append((total * slot_gate).astype(BF16))
        grads = jnp.concatenate(pieces, axis=0)
        grads_t = grads.T
        rows_in_t = rows_ref[...].reshape(blocks * cap, -1).T
        step = hidden_width // parts
        result = None
        for offset in range(0, hidden_width, step):
            cut = slice(offset, offset + step)
            hidden = hidden_ref[:, :, cut].reshape(blocks * cap, step)
            slope = slope_ref[:, :, cut].reshape(blocks * cap, step).astype(F32)
            dpre = (contract_cols(grads, wex_buf[which, offset // step]) * slope).astype(BF16)
            gin = dot(rows_in_t, dpre)
            gout = dot(grads_t, hidden)
            term = contract_cols(dpre, win_buf[which, :, :, cut].reshape(width, step))
            result = term if result is None else result + term

            @pl.when(lax.rem(at_expert, 2) == 0)
            def _():
                acc_in[:, cut] = gin
                acc_out[:, cut] = gout

            @pl.when(lax.rem(at_expert, 2) == 1)
            def _():
                total_in = (acc_in[:, cut] + gin).astype(BF16)
                low_in[which, :, :, cut] = total_in.reshape(parts, width // parts, step)
                low_ex[which, offset // step] = (acc_out[:, cut] + gout).astype(BF16)

        out_buf[which, pl.ds(half * blocks, blocks)] = result.astype(BF16).reshape(blocks, cap, width)

    for step in range(4):

        @pl.when(step_at == images + step)
        def _():
            for copy in returns(step):
                copy.start()
            if step == 1:
                for copy in spread:
                    copy.start()

    @pl.when(step_at == images + 3)
    def _():
        for copy in stores:
            copy.start()
        for copy in spread:
            copy.wait_recv()
        for grad, got, passed, _, _, _, second in tensors:
            passed[...] = (grad[1, near[second]].astype(F32) + got[1].astype(F32)).astype(BF16)
        for copy in second_round:
            copy.start()
        for step in range(4):
            for copy in returns(step):
                copy.wait()
        for copy in second_round:
            copy.wait_recv()
        for grad, got, _, more, far, _, _ in tensors:
            far[...] = (grad[1, dp_at].astype(F32) + got[0].astype(F32) + more[...].astype(F32)).astype(BF16)
        for copy in stores:
            copy.wait()
        for copy in spread + second_round:
            copy.wait_send()
        for step in range(images):
            to_mate(step).wait_send()
            to_chip(step).wait_send()
            onward(step).wait_send()


def back_kernel(
    images, real_rows, experts, tok_ref, dense_w, ext_ref, cols_ref, back_ref, dlogit_ref, resid_ref,
    dout_ref, qkv_ref, probs_ref, mixed_ref, loss_ref, gin_ref, gex_ref, far_in, far_ex,
    tgrad_ref, dense_ref, misc_ref, gin_out, gex_out,
    acc, acc_misc, part_in, part_ex, got_in, got_ex, sum_in, sum_ex, more_in, more_ex, came_in, came_ex,
    low, mate, low_mate, plane, low_plane, line, misc_got, misc_t, local_sem, w_send, w_recv, d_send, d_recv, m_send, m_recv,
):
    step_at = pl.program_id(0)
    dp_at, ex_at, near = place()
    core, floor = lax.rem(ex_at, 2), ex_at // 2
    wsem, dsem, msem = (w_send, w_recv), (d_send, d_recv), (m_send, m_recv)
    tensors = [
        (gin_ref, part_in, got_in, sum_in, more_in, far_in, came_in, gin_out, 1, 2),
        (gex_ref, part_ex, got_ex, sum_ex, more_ex, far_ex, came_ex, gex_out, 2, 1),
    ]
    local_copies, first_round, second_round, far_round = [], [], [], []
    for t, (grad, part, got, passed, more, far, came, _, first, second) in enumerate(tensors):
        for s in range(2):
            mine = dp_at if s == 0 else near[second]
            theirs = near[first] if s == 0 else near[3]
            local_copies.append(pltpu.make_async_copy(grad.at[mine], part.at[s], local_sem.at[2 * t + s]))
            first_round.append(send(grad.at[theirs], got.at[s], wsem, 4 * t + s, (near[first], ex_at)))
        second_round.append(send(passed, more, wsem, 4 * t + 2, (near[second], ex_at)))
        far_round.append(send(far, came, wsem, 4 * t + 3, (dp_at, flip(ex_at, 4))))

    @pl.when(step_at == 0)
    def _():
        for copy in local_copies:
            copy.start()
        greet(
            [(near[k], ex_at) for k in (1, 2, 3)]
            + [(dp_at, flip(ex_at, bit)) for bit in (1, 2, 4)]
            + [(dp_at, flip(flip(ex_at, 2), 4))]
        )
        for copy in first_round + far_round:
            copy.start()

    count = back_ref.shape[0]
    cols = cols_ref[...]
    hot = jnp.where(hot_cols(cols[:, 0:1], count) | hot_cols(cols[:, 1:2], count), 1.0, 0.0)
    dlogits = dlogit_ref[...]
    dact = dot(hot.astype(BF16), back_ref[...])
    dlogits_high = dlogits.astype(BF16)
    router_t = ext_ref[...].astype(BF16)
    dlogits_low = (dlogits - dlogits_high.astype(F32)).astype(BF16)
    dact = dact + dot(dlogits_high, router_t) + dot(dlogits_low, router_t)

    resid = resid_ref[...]
    normed_two, inverse_two = normalize(resid)
    gain_two = ext_ref[experts + 1 : experts + 2, :]
    act_two = (normed_two * gain_two).astype(BF16)
    grouter = contract_rows(dlogits_high, act_two) + contract_rows(dlogits_low, act_two)

    def norm_back(grad, normed, inverse, gain):
        scaled = grad * gain
        gain_grad = jnp.sum(grad * normed, axis=0, keepdims=True)
        inner = (
            scaled
            - jnp.mean(scaled, axis=-1, keepdims=True)
            - normed * jnp.mean(scaled * normed, axis=-1, keepdims=True)
        )
        return inverse * inner, gain_grad

    grad_two, ggain_two = norm_back(dact, normed_two, inverse_two, gain_two)
    dresid = dout_ref[...] + grad_two
    branch = dresid.astype(BF16)
    mixed = mixed_ref[...]
    gout = contract_rows(mixed, branch)
    width = branch.shape[1]
    dmixed = contract_cols(branch, dense_w[:, 3 * width : 4 * width]).astype(BF16)
    qkv = qkv_ref[...]
    low_half = lane_ids((1, 128)) < 64
    dqs, dks, dvs = [], [], []
    for pair in range(width // 128):
        cut = slice(128 * pair, 128 * (pair + 1))
        queries = qkv[:, cut]
        key_rows = qkv[:, width + 128 * pair : width + 128 * (pair + 1)]
        values = qkv[:, 2 * width + 128 * pair : 2 * width + 128 * (pair + 1)]
        dmix = dmixed[:, cut]
        dq = []
        dk = dv = None
        for side in range(2):
            mask = low_half if side == 0 else jnp.logical_not(low_half)
            dmask = jnp.where(mask, dmix, jnp.zeros_like(dmix))
            qmask = jnp.where(mask, queries, jnp.zeros_like(queries))
            probs_low = probs_ref[2 * pair + side]
            probs = probs_low.astype(F32)
            dprobs = contract_cols(dmask, values)
            dscore = probs * (dprobs - jnp.sum(probs * dprobs, axis=-1, keepdims=True))
            dscore = dscore.astype(BF16)
            dq.append(dot(dscore, key_rows))
            dk_term = contract_rows(dscore, qmask)
            dv_term = contract_rows(probs_low, dmask)
            dk = dk_term if dk is None else dk + dk_term
            dv = dv_term if dv is None else dv + dv_term
        dqs.append((jnp.where(low_half, dq[0], dq[1]) * 0.125).astype(BF16))
        dks.append((dk * 0.125).astype(BF16))
        dvs.append(dv.astype(BF16))
    dqkv = jnp.concatenate(dqs + dks + dvs, axis=1)
    inputs = tok_ref[...].astype(F32)
    normed_one, inverse_one = normalize(inputs)
    gain_one = ext_ref[experts : experts + 1, :]
    act_one = (normed_one * gain_one).astype(BF16)
    gqkv = contract_rows(act_one, dqkv)
    dact_one = contract_cols(dqkv, dense_w[:, : 3 * width])
    grad_one, ggain_one = norm_back(dact_one, normed_one, inverse_one, gain_one)
    tgrad = dresid + grad_one
    for image in range(images):

        @pl.when(step_at == image)
        def _():
            tgrad_ref[image * real_rows : (image + 1) * real_rows, :] = tgrad[:real_rows]

    ids = row_ids((8, width))
    gmisc = jnp.concatenate(
        [grouter[:8], jnp.where(ids == 0, ggain_one, jnp.where(ids == 1, ggain_two, 0.0))], axis=0
    )

    @pl.when(step_at == 0)
    def _():
        acc[:, : 3 * width] = gqkv
        acc[:, 3 * width :] = gout
        loss_row = jnp.where(row_ids((8, 128)) == 2, loss_ref[...], 0.0)
        acc_misc[...] = gmisc + jnp.concatenate(
            [jnp.zeros((8, width), F32), jnp.concatenate([loss_row] * (width // 128), axis=1)], axis=0
        )

    @pl.when(step_at > 0)
    def _():
        acc[:, : 3 * width] += gqkv
        acc[:, 3 * width :] += gout
        acc_misc[...] += gmisc

    @pl.when(step_at == images - 2)
    def _():
        for copy in local_copies:
            copy.wait()
        for copy in first_round:
            copy.wait_recv()
        for _, part, got, passed, _, _, _, _, _, _ in tensors:
            passed[...] = (part[1].astype(F32) + got[1].astype(F32)).astype(BF16)
        for copy in second_round:
            copy.start()

    @pl.when(step_at == images - 1)
    def _():
        lines, shard = low.shape[1], low.shape[3]
        low[...] = acc[...].astype(BF16).reshape(low.shape)
        other = lax.rem(core + 1, 2)
        to_mate = send(low.at[:, :, other], mate, dsem, 0, (dp_at, flip(ex_at, 1)))
        to_mate.start()
        misc_peers = [
            (dp_at, flip(ex_at, 1)), (near[1], ex_at), (near[2], ex_at), (dp_at, flip(ex_at, 2)), (dp_at, flip(ex_at, 4)),
        ]
        misc = [send(acc_misc.at[...] if k == 0 else misc_got.at[5 + k - 1], misc_got.at[k], msem, k, misc_peers[k]) for k in range(5)]
        misc[0].start()

        def misc_step(k):
            misc[k].wait_recv()
            before = acc_misc[...] if k == 0 else misc_got[5 + k - 1]
            misc_got[5 + k] = before + misc_got[k]
            if k < 4:
                misc[k + 1].start()

        to_mate.wait_recv()
        low_mate[...] = (low[:, :, core].astype(F32) + mate[...].astype(F32)).astype(BF16)
        to_plane = [send(low_mate.at[near[k]], plane.at[k - 1], dsem, k, (near[k], ex_at)) for k in (1, 2, 3)]
        for copy in to_plane:
            copy.start()
        misc_step(0)
        misc_step(1)
        misc_step(2)
        for copy in to_plane:
            copy.wait_recv()
        summed = low_mate[dp_at].astype(F32)
        for k in range(3):
            summed = summed + plane[k].astype(F32)
        low_plane[...] = summed.astype(BF16)
        floors = [flip(floor, 1), flip(floor, 2), flip(flip(floor, 1), 2)]
        to_line = [
            send(low_plane.at[floors[k]], line.at[k], dsem, 4 + k, (dp_at, 2 * floors[k] + core)) for k in range(3)
        ]
        for copy in to_line:
            copy.start()
        misc_step(3)
        misc_step(4)
        flat = (dp_at * (2 * low.shape[1]) + ex_at) * shard
        rows_t = jnp.concatenate([misc_got[9], jnp.zeros((112, misc_got.shape[2]), F32)], axis=0).T
        misc_t[...] = rows_t
        misc_ref[...] = misc_t[pl.ds(pl.multiple_of(flat, shard), shard), :]
        for copy in to_line:
            copy.wait_recv()
        result = low_plane[floor].astype(F32)
        for k in range(3):
            result = result + line[k].astype(F32)
        dense_ref[...] = result

        for copy in second_round + far_round:
            copy.wait_recv()
        for _, part, got, _, more, _, came, out, _, _ in tensors:
            out[...] = (
                part[0].astype(F32) + got[0].astype(F32) + more[...].astype(F32) + came[...].astype(F32)
            )
        for copy in [to_mate] + misc + to_plane + to_line + first_round + second_round + far_round:
            copy.wait_send()


def prepare_kernel(
    images, capacity, cap, tok_ref, target_ref, routes_ref, slots_ref, valid_ref, router_ref, gain_one_ref, gain_two_ref,
    tok_out, target_out, cols_out, rows_out, extra_out,
    wide, line,
):
    total, width = tok_ref.shape
    real_rows, rows = total // images, tok_out.shape[1]
    for source, out in ((tok_ref, tok_out), (target_ref, target_out)):
        wide[:total, :] = source[...].astype(F32)
        for image in range(images):
            piece = wide[image * real_rows : image * real_rows + rows, :]
            piece = jnp.where(row_ids((rows, 1)) < real_rows, piece, 0.0)
            out[image] = piece.astype(BF16)
    me = lax.axis_index("expert")
    routes, slots = routes_ref[...], slots_ref[...]
    code = jnp.where(slots < capacity, jnp.bitwise_xor(routes, me) * cap + slots, -1)
    line[0:2, :total] = code.astype(F32)
    line[2:4, :total] = routes.astype(F32)
    line[4:5, :total] = valid_ref[...].astype(F32)
    lanes = line.shape[1]
    packed = line[...]
    for image in range(images):
        piece = packed[:, image * real_rows : image * real_rows + rows]
        keep = (lane_ids((8, rows)) < real_rows) & (row_ids((8, rows)) < 5)
        piece = jnp.where(keep, piece, -1.0)
        rows_out[image] = piece.astype(jnp.int32)
        square = jnp.concatenate(
            [
                jnp.concatenate([piece, jnp.full((8, round_up(rows, 128) - rows), -1.0, F32)], axis=1),
                jnp.full((120, round_up(rows, 128)), -1.0, F32),
            ],
            axis=0,
        )
        cols_out[image] = square.T[:rows, :8].astype(jnp.int32)
    experts, shard = router_ref.shape
    tall = jnp.concatenate(
        [
            router_ref[...].astype(F32), gain_one_ref[...].astype(F32), gain_two_ref[...].astype(F32),
            jnp.zeros((126 - experts, shard), F32),
        ],
        axis=0,
    )
    tall = jnp.concatenate([tall, jnp.zeros((128, 128 - shard), F32)], axis=1)
    extra_out[...] = tall.T[:shard].astype(BF16)


def finish_kernel(
    real_rows, experts, padded_ref, tgrad_in, dense_ref, misc_ref, gin_in, gex_in,
    out_ref, loss_ref, tgrad_ref, gain_one_ref, gqkv_ref, gout_ref, gain_two_ref, grouter_ref, gin_ref, gex_ref,
    joined,
):
    images, width = padded_ref.shape[0], padded_ref.shape[2]
    for image in range(images):
        joined[image * real_rows : (image + 1) * real_rows, :] = padded_ref[image].astype(F32)[:real_rows]
    out_ref[...] = joined[: images * real_rows, :].astype(BF16)
    tgrad_ref[...] = tgrad_in[...]
    gqkv_ref[...] = dense_ref[:, : 3 * width]
    gout_ref[...] = dense_ref[:, 3 * width :]
    own = misc_ref[...]
    shard = own.shape[0]
    turned = jnp.concatenate([own, jnp.zeros((128 - shard, 128), F32)], axis=0).T
    gain_one_ref[...] = turned[8:9, :shard]
    gain_two_ref[...] = turned[9:10, :shard]
    grouter_ref[...] = own[:, :experts]
    loss_ref[...] = own[0:1, 10:11]
    gin_ref[...] = gin_in[...]
    gex_ref[...] = gex_in[...].T


def shape(dims, kind):
    return jax.ShapeDtypeStruct(dims, kind)


def whole(dims):
    return pl.BlockSpec(dims, lambda *_: (0,) * len(dims))


def per_image(*dims):
    return pl.BlockSpec((None,) + dims, lambda i: (i,) + (0,) * len(dims))


def params():
    return pltpu.CompilerParams(vmem_limit_bytes=56 * MB)


def fast_shards(
    tokens, targets, valid_mask, routes, slot_ids, ln1_gain, qkv_weight, out_weight, ln2_gain,
    router_weight, expert_in, expert_out,
):
    axes = ("dp", "expert")
    tok_rows, width = tokens.shape
    experts = lax.axis_size("expert")
    group = experts // 2
    dp = lax.axis_size("dp")
    total_tokens = tok_rows * dp * experts
    hidden_width = expert_in.shape[2]
    capacity = (5 * tok_rows // 2 // experts + 7) // 8 * 8
    cap = round_up(capacity, 16)
    images = IMG_DEV
    real_rows = tok_rows // images
    rows = round_up(real_rows, 16)
    shard = qkv_weight.shape[0]
    tok_p, target_p, cols, row_codes, extra = pl.pallas_call(
        lambda *refs: prepare_kernel(images, capacity, cap, *refs),
        out_shape=[
            shape((images, rows, width), BF16), shape((images, rows, width), BF16), shape((images, rows, 8), jnp.int32),
            shape((images, 8, rows), jnp.int32), shape((shard, 128), BF16),
        ],
        scratch_shapes=[
            pltpu.VMEM((round_up(tok_rows + rows - real_rows, 8), width), F32),
            pltpu.VMEM((8, round_up(tok_rows + rows - real_rows, 128)), F32),
        ],
        compiler_params=params(),
        name="prepare",
    )(
        tokens, targets, routes.T, slot_ids.T, valid_mask[None], router_weight.T, ln1_gain[None], ln2_gain[None],
    )
    floors = experts // 2
    in_part, ex_part = (width // dp, hidden_width), (hidden_width // dp, width)
    any_space = pl.BlockSpec(memory_space=pl.ANY)

    gate_lanes = 128
    dense_lanes = 4 * width + 128
    half_blocks = group // 2
    last = images - 1

    def early(*dims):
        return pl.BlockSpec((None,) + dims, lambda i: (jnp.minimum(i, last),) + (0,) * len(dims))

    def late(far_first, *dims):
        def index(i):
            step = jnp.maximum(i - images, 0)
            which = 1 - step // 2 if far_first else step // 2
            return (which, lax.rem((step + 1) // 2, 2)) + (0,) * len(dims)

        return pl.BlockSpec((None, half_blocks) + dims, index)

    def once(dims):
        return pl.BlockSpec(dims, lambda i: (0,) * len(dims), pipeline_mode=pl.Buffered(1))

    (
        qkv_p, probs, mixed, resid, gates, dense_full, ext, rows_in, hidden, slope, returned, code_all, grow_all,
        win_all, wex_all,
    ) = pl.pallas_call(
        lambda *refs: front_kernel(images, real_rows, experts, cap, group, *refs),
        grid=(images + 4,),
        in_specs=[
            early(rows, width), once((shard, 3 * width)), once((shard, width)), once((shard, 128)),
            early(rows, 8), early(8, rows), once((images, 8, rows)), once((images, rows, 8)), once(in_part), once(ex_part),
        ],
        out_specs=[
            early(rows, 3 * width), early(HEADS, rows, rows), early(rows, width), early(rows, width),
            early(rows, gate_lanes), whole((width, dense_lanes)), whole((128, width)),
            late(False, cap, width), late(False, cap, hidden_width), late(False, cap, hidden_width),
            *[any_space] * 5,
        ],
        out_shape=[
            shape((images, rows, 3 * width), BF16), shape((images, HEADS, rows, rows), BF16),
            shape((images, rows, width), BF16), shape((images, rows, width), F32),
            shape((images, rows, gate_lanes), F32), shape((width, dense_lanes), BF16), shape((128, width), F32),
            shape((2, group, cap, width), BF16), shape((2, group, cap, hidden_width), BF16),
            shape((2, group, cap, hidden_width), BF16), shape((2, group, cap, width), BF16),
            shape((group, images, 8, rows), jnp.int32), shape((group, images, 8, rows), F32),
            shape((2, dp, *in_part), BF16), shape((2, dp, *ex_part), BF16),
        ],
        scratch_shapes=[
            pltpu.VMEM((dp, floors, 2, shard, dense_lanes), BF16), pltpu.VMEM((group, images, rows, width), BF16),
            pltpu.VMEM((group, images, 8, rows), jnp.int32), pltpu.VMEM((group, images, 8, rows), F32),
            pltpu.VMEM((2, dp, *in_part), BF16), pltpu.VMEM((2, dp, *ex_part), BF16),
            pltpu.VMEM((2, group, cap, width), BF16), pltpu.VMEM((half_blocks, cap, hidden_width), BF16),
            *sem_pairs(19), *sem_pairs(3 * images), *sem_pairs(6), *sem_pairs(18), *sem_pairs(8),
            pltpu.SemaphoreType.DMA((6,)),
        ],
        compiler_params=pltpu.CompilerParams(
            vmem_limit_bytes=60 * MB, collective_id=2, has_side_effects=True
        ),
        cost_estimate=pl.CostEstimate(flops=int(20e9), bytes_accessed=int(6e7), transcendentals=0),
        name="attention_expert_forward",
    )(tok_p, qkv_weight, out_weight, extra, cols, row_codes, row_codes, cols, expert_in[0], expert_out[0])
    returned = returned.reshape(2 * group * cap, width)

    flip_part = (width, hidden_width // dp)
    block_out, dout, dlogits, loss_part, drows, gin, gout_t, far_in, far_ex = pl.pallas_call(
        lambda *refs: combine_back_kernel(images, cap, group, total_tokens, shard, experts, *refs),
        grid=(images + 4,),
        in_specs=[
            once((16, width)), early(rows, width), once((2 * group * cap, width)), early(rows, 8),
            early(rows, gate_lanes), early(rows, width), once((group, images, 8, rows)),
            once((group, images, 8, rows)), late(True, cap, width), late(True, cap, hidden_width),
            late(True, cap, hidden_width), any_space, any_space,
        ],
        out_specs=[
            early(rows, width), early(rows, width), early(rows, gate_lanes), whole((8, 128)), *[any_space] * 3,
            once(in_part), once(flip_part),
        ],
        out_shape=[
            shape((images, rows, width), BF16), shape((images, rows, width), F32),
            shape((images, rows, gate_lanes), F32), shape((8, 128), F32),
            shape((2, group, cap, width), BF16), shape((dp, *in_part), BF16), shape((dp, *flip_part), BF16),
            shape(in_part, BF16), shape(flip_part, BF16),
        ],
        scratch_shapes=[
            pltpu.VMEM((group, images, rows, width), BF16),
            pltpu.VMEM((2, dp, *in_part), BF16), pltpu.VMEM((2, dp, *ex_part), BF16),
            pltpu.VMEM((width, hidden_width), F32), pltpu.VMEM((width, hidden_width), F32),
            pltpu.VMEM((2, dp, *in_part), BF16), pltpu.VMEM((2, dp, *flip_part), BF16),
            pltpu.VMEM((2, group, cap, width), BF16),
            *[pltpu.VMEM(dims, BF16) for dims in ((2, *in_part), (2, *flip_part), in_part, flip_part, in_part, flip_part)],
            *sem_pairs(3 * images), *sem_pairs(8), *sem_pairs(6), pltpu.SemaphoreType.DMA((9,)),
        ],
        compiler_params=pltpu.CompilerParams(
            vmem_limit_bytes=62 * MB, collective_id=5, has_side_effects=True
        ),
        cost_estimate=pl.CostEstimate(flops=int(24e9), bytes_accessed=int(4e7), transcendentals=0),
        name="combine_expert_backward",
    )(
        ext, resid, returned, cols, gates, target_p, code_all, grow_all, rows_in, hidden, slope,
        win_all, wex_all,
    )
    grad_back = drows.reshape(2 * group * cap, width)

    def vmem(*dims):
        return pltpu.VMEM(dims, BF16)

    tgrad, dense_grad, misc, gin_own, gex_own = pl.pallas_call(
        lambda *refs: back_kernel(images, real_rows, experts, *refs),
        grid=(images,),
        in_specs=[
            per_image(rows, width), whole((width, dense_lanes)), whole((128, width)), per_image(rows, 8),
            whole((2 * group * cap, width)), per_image(rows, gate_lanes), per_image(rows, width), per_image(rows, width),
            per_image(rows, 3 * width), per_image(HEADS, rows, rows), per_image(rows, width), whole((8, 128)),
            *[any_space] * 4,
        ],
        out_specs=[
            once((tok_rows, width)), whole((shard, 4 * width)), whole((shard, 128)), whole(in_part), whole(flip_part),
        ],
        out_shape=[
            shape((tok_rows, width), F32), shape((shard, 4 * width), F32), shape((shard, 128), F32),
            shape(in_part, F32), shape(flip_part, F32),
        ],
        scratch_shapes=[
            pltpu.VMEM((width, 4 * width), F32), pltpu.VMEM((16, width), F32),
            vmem(2, *in_part), vmem(2, *flip_part), vmem(2, *in_part), vmem(2, *flip_part),
            vmem(*in_part), vmem(*flip_part), vmem(*in_part), vmem(*flip_part), vmem(*in_part), vmem(*flip_part),
            vmem(dp, floors, 2, shard, 4 * width), vmem(dp, floors, shard, 4 * width), vmem(dp, floors, shard, 4 * width),
            vmem(3, floors, shard, 4 * width), vmem(floors, shard, 4 * width), vmem(3, shard, 4 * width),
            pltpu.VMEM((10, 16, width), F32), pltpu.VMEM((width, 128), F32),
            pltpu.SemaphoreType.DMA((4,)),
            *sem_pairs(8), *sem_pairs(8), *sem_pairs(5),
        ],
        compiler_params=pltpu.CompilerParams(
            vmem_limit_bytes=60 * MB, collective_id=1, has_side_effects=True
        ),
        cost_estimate=pl.CostEstimate(flops=int(10e9), bytes_accessed=int(3e7), transcendentals=0),
        name="attention_backward",
    )(
        tok_p, dense_full, ext, cols, grad_back, dlogits, resid, dout, qkv_p, probs, mixed,
        loss_part, gin, gout_t, far_in, far_ex,
    )
    out, loss, tokens_grad, gain_one_grad, qkv_grad, out_grad, gain_two_grad, router_grad, in_grad, ex_grad = pl.pallas_call(
        lambda *refs: finish_kernel(real_rows, experts, *refs),
        out_shape=[
            shape((tok_rows, width), BF16), shape((1, 1), F32), shape((tok_rows, width), F32), shape((1, shard), F32),
            shape((shard, 3 * width), F32), shape((shard, width), F32), shape((1, shard), F32),
            shape((shard, experts), F32), shape(in_part, F32), shape(ex_part, F32),
        ],
        scratch_shapes=[pltpu.VMEM((round_up(tok_rows, 8), width), F32)],
        compiler_params=params(),
        name="finish",
    )(block_out, tgrad, dense_grad, misc, gin_own, gex_own)
    return (
        out,
        loss.reshape(()),
        tokens_grad,
        gain_one_grad.reshape(shard),
        qkv_grad,
        out_grad,
        gain_two_grad.reshape(shard),
        router_grad,
        in_grad[None],
        ex_grad[None],
    )


def solution(mesh):
    in_specs = (
        P(("dp", "expert"), None),
        P(("dp", "expert"), None),
        P(("dp", "expert")),
        P(("dp", "expert"), None),
        P(("dp", "expert"), None),
        P(("dp", "expert")),
        P(("dp", "expert"), None),
        P(("dp", "expert"), None),
        P(("dp", "expert")),
        P(("dp", "expert"), None),
        P("expert", "dp", None),
        P("expert", "dp", None),
    )
    out_specs = (
        P(("dp", "expert"), None),
        P(),
        P(("dp", "expert"), None),
        P(("dp", "expert")),
        P(("dp", "expert"), None),
        P(("dp", "expert"), None),
        P(("dp", "expert")),
        P(("dp", "expert"), None),
        P("expert", "dp", None),
        P("expert", "dp", None),
    )
    halves = mesh.shape["expert"] == 8 and mesh.shape["dp"] == 4
    body = fast_shards if halves else shards
    return jax.shard_map(body, mesh=mesh, in_specs=in_specs, out_specs=out_specs, check_vma=False)
```

```python
import jax
import jax.numpy as jnp
from jax import lax
from jax.experimental import pallas as pl
from jax.experimental.pallas import tpu as pltpu
from jax.sharding import PartitionSpec as P

HEADS = 8
IMG_DEV = 5


HIGH = lax.Precision.HIGHEST
EPS = 1e-06


def layer_norm(values, scale_gain):
    row_mean = jnp.mean(values, axis=-1, keepdims=True)
    centered = values - row_mean
    variance = jnp.mean(centered * centered, axis=-1, keepdims=True)
    inverse = lax.rsqrt(variance + EPS)
    normed = centered * inverse
    return (normed * scale_gain, normed, inverse)


def layer_norm_back(grad_in, normed, inverse, scale_gain):
    scaled = grad_in * scale_gain
    gain_grad = jnp.sum(grad_in * normed, axis=0)
    inner_term = (
        scaled
        - jnp.mean(scaled, axis=-1, keepdims=True)
        - normed * jnp.mean(scaled * normed, axis=-1, keepdims=True)
    )
    return (inverse * inner_term, gain_grad)


def contract_rows(left_side, right_side):
    return lax.dot_general(
        left_side, right_side, (((0,), (0,)), ((), ())), preferred_element_type=jnp.float32
    )


def contract_cols(left_side, right_side):
    return lax.dot_general(
        left_side, right_side, (((1,), (1,)), ((), ())), preferred_element_type=jnp.float32
    )


def exact_gelu(values):
    return jax.nn.gelu(values, approximate=False)


def split_heads(qkv_low, images, head_count):
    row_count, triple_width = qkv_low.shape
    head_dim = triple_width // (3 * head_count)
    pieces = qkv_low.reshape(images, row_count // images, 3, head_count, head_dim)
    return (pieces[:, :, 0], pieces[:, :, 1], pieces[:, :, 2], head_dim ** (-0.5))


def attention_forward(qkv_low, images, head_count):
    queries, key_rows, values, score_scale = split_heads(qkv_low, images, head_count)
    scores = (
        jnp.einsum("ilhd,imhd->ihlm", queries, key_rows, preferred_element_type=jnp.float32)
        * score_scale
    )
    row_max = jnp.max(scores, axis=-1, keepdims=True)
    exp_scores = jnp.exp(scores - row_max)
    row_sum = jnp.sum(exp_scores, axis=-1, keepdims=True)
    weights_low = (exp_scores / row_sum).astype(jnp.bfloat16)
    log_total = row_max + jnp.log(row_sum)
    mixed_rows = jnp.einsum(
        "ihlm,imhd->ilhd", weights_low, values, preferred_element_type=jnp.float32
    )
    return (mixed_rows.reshape(qkv_low.shape[0], -1).astype(jnp.bfloat16), log_total)


def attention_back(qkv_low, log_total, grad_mixed, images, head_count):
    queries, key_rows, values, score_scale = split_heads(qkv_low, images, head_count)
    scores = (
        jnp.einsum("ilhd,imhd->ihlm", queries, key_rows, preferred_element_type=jnp.float32)
        * score_scale
    )
    weights_full = jnp.exp(scores - log_total)
    weights_low = weights_full.astype(jnp.bfloat16)
    grad_heads = grad_mixed.reshape(queries.shape)
    grad_weights = jnp.einsum(
        "ilhd,imhd->ihlm", grad_heads, values, preferred_element_type=jnp.float32
    )
    grad_values = jnp.einsum(
        "ihlm,ilhd->imhd", weights_low, grad_heads, preferred_element_type=jnp.float32
    )
    grad_scores = weights_full * (
        grad_weights - jnp.sum(weights_full * grad_weights, axis=-1, keepdims=True)
    )
    grad_low = grad_scores.astype(jnp.bfloat16)
    grad_queries = (
        jnp.einsum("ihlm,imhd->ilhd", grad_low, key_rows, preferred_element_type=jnp.float32)
        * score_scale
    )
    grad_keys = (
        jnp.einsum("ihlm,ilhd->imhd", grad_low, queries, preferred_element_type=jnp.float32)
        * score_scale
    )
    stacked = jnp.stack([grad_queries, grad_keys, grad_values], axis=2)
    return stacked.reshape(qkv_low.shape).astype(jnp.bfloat16)


def expert_forward(rows_in, weight_in, weight_out, block_size):
    result = jnp.zeros((rows_in.shape[0], weight_out.shape[1]), jnp.float32)
    for offset in range(0, weight_in.shape[1], block_size):
        pre_act = jnp.dot(
            rows_in, weight_in[:, offset : offset + block_size], preferred_element_type=jnp.float32
        )
        hidden = exact_gelu(pre_act).astype(jnp.bfloat16)
        result = result + jnp.dot(
            hidden, weight_out[offset : offset + block_size], preferred_element_type=jnp.float32
        )
    return result


def expert_back(rows_in, weight_in, weight_out, grad_rows_out, block_size):
    grad_rows = jnp.zeros(rows_in.shape, jnp.float32)
    grads_first = []
    grads_second = []
    for offset in range(0, weight_in.shape[1], block_size):
        slice_in = weight_in[:, offset : offset + block_size]
        slice_out = weight_out[offset : offset + block_size]
        pre_act = jnp.dot(rows_in, slice_in, preferred_element_type=jnp.float32)
        hidden, gelu_back = jax.vjp(exact_gelu, pre_act)
        grads_second.append(contract_rows(hidden.astype(jnp.bfloat16), grad_rows_out))
        grad_hidden = contract_cols(grad_rows_out, slice_out)
        grad_pre = gelu_back(grad_hidden)[0].astype(jnp.bfloat16)
        grads_first.append(contract_rows(rows_in, grad_pre))
        grad_rows = grad_rows + contract_cols(grad_pre, slice_in)
    return (grad_rows, jnp.concatenate(grads_first, axis=1), jnp.concatenate(grads_second, axis=0))


def shards(
    tokens,
    targets,
    valid_mask,
    routes,
    slot_ids,
    ln1_gain,
    qkv_weight,
    out_weight,
    ln2_gain,
    router_weight,
    expert_in,
    expert_out,
):
    tok_rows, model_width = tokens.shape
    experts = lax.axis_size("expert")
    total_tokens = tok_rows * lax.axis_size("dp") * experts
    capacity = (5 * tok_rows // 2 // experts + 7) // 8 * 8
    dense_full = (
        lax.all_gather(ln1_gain, ("dp", "expert"), axis=0, tiled=True),
        lax.all_gather(qkv_weight, ("dp", "expert"), axis=0, tiled=True),
        lax.all_gather(out_weight, ("dp", "expert"), axis=0, tiled=True),
        lax.all_gather(ln2_gain, ("dp", "expert"), axis=0, tiled=True),
        lax.all_gather(router_weight, ("dp", "expert"), axis=0, tiled=True),
    )
    gain_one, qkv_full, out_full, gain_two, router_full = dense_full
    expert_full = (
        lax.all_gather(expert_in, "dp", axis=1, tiled=True),
        lax.all_gather(expert_out, "dp", axis=1, tiled=True),
    )
    weight_in = expert_full[0][0]
    weight_out = expert_full[1][0]
    valid_f = valid_mask.astype(jnp.float32)
    valid_count = lax.psum(jnp.sum(valid_f), ("dp", "expert"))
    inputs_f = tokens.astype(jnp.float32)
    gain_one_f = gain_one.astype(jnp.float32)
    gain_two_f = gain_two.astype(jnp.float32)
    norm_one, normed_one, inverse_one = layer_norm(inputs_f, gain_one_f)
    act_one = norm_one.astype(jnp.bfloat16)
    qkv_low = jnp.dot(act_one, qkv_full, preferred_element_type=jnp.float32).astype(jnp.bfloat16)
    mixed_low, log_total = attention_forward(qkv_low, IMG_DEV, HEADS)
    residual = inputs_f + jnp.dot(mixed_low, out_full, preferred_element_type=jnp.float32)
    norm_two, normed_two, inverse_two = layer_norm(residual, gain_two_f)
    act_two = norm_two.astype(jnp.bfloat16)
    gate_probs = jax.nn.softmax(
        jnp.dot(act_two, router_full, preferred_element_type=jnp.float32), axis=-1
    )
    expert_ids = lax.broadcasted_iota(jnp.int32, (1, experts), 1)
    first_pick = (routes[:, 0:1] == expert_ids).astype(jnp.float32)
    second_pick = (routes[:, 1:2] == expert_ids).astype(jnp.float32)
    gate_first = jnp.sum(gate_probs * first_pick, axis=-1, keepdims=True)
    gate_second = jnp.sum(gate_probs * second_pick, axis=-1, keepdims=True)
    target_slot = jnp.where(slot_ids < capacity, routes * capacity + slot_ids, -1)
    slot_columns = lax.broadcasted_iota(jnp.int32, (1, experts * capacity), 1)
    first_hot = (target_slot[:, 0:1] == slot_columns).astype(jnp.bfloat16)
    second_hot = (target_slot[:, 1:2] == slot_columns).astype(jnp.bfloat16)
    both_hot = first_hot + second_hot
    outgoing = contract_rows(both_hot, act_two).astype(jnp.bfloat16)
    arrived = lax.all_to_all(
        outgoing.reshape(experts, capacity, model_width),
        "expert",
        split_axis=0,
        concat_axis=0,
        tiled=True,
    ).reshape(-1, model_width)
    hidden_block = min(512, weight_in.shape[1])
    produced = expert_forward(arrived, weight_in, weight_out, hidden_block).astype(jnp.bfloat16)
    returned = lax.all_to_all(
        produced.reshape(experts, capacity, model_width),
        "expert",
        split_axis=0,
        concat_axis=0,
        tiled=True,
    ).reshape(-1, model_width)
    from_first = jnp.dot(first_hot, returned, preferred_element_type=jnp.float32)
    from_second = jnp.dot(second_hot, returned, preferred_element_type=jnp.float32)
    output = residual + gate_first * from_first + gate_second * from_second
    residue = output - targets.astype(jnp.float32)
    local_loss = jnp.sum(valid_f * jnp.mean(residue * residue, axis=-1))
    loss_sum = lax.psum(local_loss, ("dp", "expert"))
    loss_value = loss_sum / valid_count
    grad_out = total_tokens / valid_count * valid_f[:, None] * residue
    dense_back = (
        lax.all_gather(ln1_gain, ("dp", "expert"), axis=0, tiled=True),
        lax.all_gather(qkv_weight, ("dp", "expert"), axis=0, tiled=True),
        lax.all_gather(out_weight, ("dp", "expert"), axis=0, tiled=True),
        lax.all_gather(ln2_gain, ("dp", "expert"), axis=0, tiled=True),
        lax.all_gather(router_weight, ("dp", "expert"), axis=0, tiled=True),
    )
    expert_back_full = (
        lax.all_gather(expert_in, "dp", axis=1, tiled=True),
        lax.all_gather(expert_out, "dp", axis=1, tiled=True),
    )
    qkv_back = dense_back[1]
    out_back = dense_back[2]
    router_back = dense_back[4]
    weight_in_back = expert_back_full[0][0]
    weight_out_back = expert_back_full[1][0]
    slot_grads = (
        contract_rows(first_hot, (gate_first * grad_out).astype(jnp.bfloat16))
        + contract_rows(second_hot, (gate_second * grad_out).astype(jnp.bfloat16))
    ).astype(jnp.bfloat16)
    expert_grad_rows = lax.all_to_all(
        slot_grads.reshape(experts, capacity, model_width),
        "expert",
        split_axis=0,
        concat_axis=0,
        tiled=True,
    ).reshape(-1, model_width)
    grad_rows, grad_first_weight, grad_second_weight = expert_back(
        arrived, weight_in_back, weight_out_back, expert_grad_rows, hidden_block
    )
    grad_back = lax.all_to_all(
        grad_rows.astype(jnp.bfloat16).reshape(experts, capacity, model_width),
        "expert",
        split_axis=0,
        concat_axis=0,
        tiled=True,
    ).reshape(-1, model_width)
    grad_act_two = jnp.dot(both_hot, grad_back, preferred_element_type=jnp.float32)
    gate_grad = first_pick * jnp.sum(
        grad_out * from_first, axis=-1, keepdims=True
    ) + second_pick * jnp.sum(grad_out * from_second, axis=-1, keepdims=True)
    logit_grad = gate_probs * (gate_grad - jnp.sum(gate_probs * gate_grad, axis=-1, keepdims=True))
    router_f = router_back.astype(jnp.float32)
    grad_act_two = grad_act_two + lax.dot_general(
        logit_grad,
        router_f,
        (((1,), (1,)), ((), ())),
        precision=HIGH,
        preferred_element_type=jnp.float32,
    )
    router_grad = lax.dot_general(
        act_two.astype(jnp.float32),
        logit_grad,
        (((0,), (0,)), ((), ())),
        precision=HIGH,
        preferred_element_type=jnp.float32,
    )
    grad_norm_two, gain_two_grad = layer_norm_back(
        grad_act_two, normed_two, inverse_two, gain_two_f
    )
    grad_resid = grad_out + grad_norm_two
    branch_grad = grad_resid.astype(jnp.bfloat16)
    out_weight_grad = contract_rows(mixed_low, branch_grad)
    grad_mixed = contract_cols(branch_grad, out_back).astype(jnp.bfloat16)
    qkv_grad_low = attention_back(qkv_low, log_total, grad_mixed, IMG_DEV, HEADS)
    qkv_weight_grad = contract_rows(act_one, qkv_grad_low)
    grad_act_one = contract_cols(qkv_grad_low, qkv_back)
    grad_norm_one, gain_one_grad = layer_norm_back(
        grad_act_one, normed_one, inverse_one, gain_one_f
    )
    tokens_grad = grad_resid + grad_norm_one
    dense_grads = (
        lax.psum_scatter(gain_one_grad, ("dp", "expert"), scatter_dimension=0, tiled=True),
        lax.psum_scatter(qkv_weight_grad, ("dp", "expert"), scatter_dimension=0, tiled=True),
        lax.psum_scatter(out_weight_grad, ("dp", "expert"), scatter_dimension=0, tiled=True),
        lax.psum_scatter(gain_two_grad, ("dp", "expert"), scatter_dimension=0, tiled=True),
        lax.psum_scatter(router_grad, ("dp", "expert"), scatter_dimension=0, tiled=True),
    )
    expert_grads = (
        lax.psum_scatter(
            grad_first_weight[None].astype(jnp.bfloat16), "dp", scatter_dimension=1, tiled=True
        ).astype(jnp.float32),
        lax.psum_scatter(
            grad_second_weight[None].astype(jnp.bfloat16), "dp", scatter_dimension=1, tiled=True
        ).astype(jnp.float32),
    )
    first_result = expert_grads[0]
    second_result = expert_grads[1]
    return (
        output.astype(jnp.bfloat16),
        loss_value,
        tokens_grad,
        dense_grads[0],
        dense_grads[1],
        dense_grads[2],
        dense_grads[3],
        dense_grads[4],
        first_result,
        second_result,
    )


F32 = jnp.float32
BF16 = jnp.bfloat16
MB = 2**20


def round_up(value, unit):
    return (value + unit - 1) // unit * unit


def dot(left_side, right_side):
    return jnp.dot(left_side, right_side, preferred_element_type=F32)


def lane_ids(shape):
    return lax.broadcasted_iota(jnp.int32, shape, len(shape) - 1)


def row_ids(shape):
    return lax.broadcasted_iota(jnp.int32, shape, len(shape) - 2)


MESH = pl.DeviceIdType.MESH


def flip(index, bit):
    return index + bit * (1 - 2 * lax.rem(index // bit, 2))


def send(src, dst, sems, slot, device):
    return pltpu.make_async_remote_copy(
        src_ref=src, dst_ref=dst, send_sem=sems[0].at[slot], recv_sem=sems[1].at[slot],
        device_id=device, device_id_type=MESH,
    )


def greet(peers):
    barrier = pltpu.get_barrier_semaphore()
    for peer in peers:
        pl.semaphore_signal(barrier, inc=1, device_id=peer, device_id_type=MESH)
    pl.semaphore_wait(barrier, len(peers))


def place():
    dp_at, ex_at = lax.axis_index("dp"), lax.axis_index("expert")
    near = [None, flip(dp_at, 1), flip(dp_at, 2), flip(flip(dp_at, 1), 2)]
    return dp_at, ex_at, near


def sem_pairs(count):
    return [pltpu.SemaphoreType.DMA((count,)), pltpu.SemaphoreType.DMA((count,))]


def normalize(values):
    centered = values - jnp.mean(values, axis=-1, keepdims=True)
    inverse = lax.rsqrt(jnp.mean(centered * centered, axis=-1, keepdims=True) + EPS)
    return centered * inverse, inverse


def gelu_pair(values):
    size = jnp.abs(values)
    inv = 1.0 / (1.0 + 0.2316419 * size)
    density = 0.3989422804014327 * jnp.exp(-0.5 * values * values)
    series = inv * (
        0.319381530
        + inv * (-0.356563782 + inv * (1.781477937 + inv * (-1.821255978 + inv * 1.330274429)))
    )
    tail = density * series
    cumulative = jnp.where(values >= 0, 1.0 - tail, tail)
    return values * cumulative, cumulative + values * density


def plane_gather(mine, blocks, q, sems, base, dp_at, ex_at, near):
    half = blocks.shape[2] // 2
    first, second = pl.ds(0, half), pl.ds(half, half)
    own = [send(mine, blocks.at[q, dp_at], sems, base + k - 1, (near[k], ex_at)) for k in (1, 2)]
    passed = [
        send(blocks.at[q, near[1], first], blocks.at[q, near[1], first], sems, base + 2, (near[2], ex_at)),
        send(blocks.at[q, near[2], second], blocks.at[q, near[2], second], sems, base + 3, (near[1], ex_at)),
    ]
    return own, passed


def hot_rows(codes, start, count):
    slots = row_ids((count, codes.shape[1])) + start
    return (slots == codes[0:1, :]) | (slots == codes[1:2, :])


def return_copies(buf, back, q, half, sems, local, dp_at, ex_at):
    peers = [None, (dp_at, flip(ex_at, 1)), (dp_at, flip(ex_at, 2)), (dp_at, flip(flip(ex_at, 1), 2))]
    copies = []
    for k in (2 * half, 2 * half + 1):
        if k == 0:
            copies.append(pltpu.make_async_copy(buf.at[q, 0], back.at[q, 0], local.at[q]))
        else:
            copies.append(send(buf.at[q, k], back.at[q, k], sems, 4 * q + k, peers[k]))
    return copies


def front_kernel(
    images, real_rows, experts, cap, group,
    tok_ref, qkvw_ref, outw_ref, extra_ref, cols_ref, rows_ref, codes_ref, all_cols_ref, win_ref, wex_ref,
    qkv_ref, probs_ref, mixed_ref, resid_ref, gates_ref, dense_ref, ext_ref, rows_out_ref, hidden_ref, slope_ref,
    back_ref, code_out, grow_out, win_out, wex_out,
    dense, act, code_buf, grow_buf, win_buf, wex_buf, out_buf, kept,
    d_send, d_recv, t_send, t_recv, r_send, r_recv, w_send, w_recv, y_send, y_recv, local_sem,
):
    step_at = pl.program_id(0)
    dp_at, ex_at, near = place()
    core, floor = lax.rem(ex_at, 2), ex_at // 2
    dsem, tsem, rsem, wsem, ysem = (d_send, d_recv), (t_send, t_recv), (r_send, r_recv), (w_send, w_recv), (y_send, y_recv)
    mate, across, beyond = (dp_at, flip(ex_at, 1)), (dp_at, flip(ex_at, 2)), (dp_at, flip(flip(ex_at, 1), 2))
    far = (dp_at, flip(ex_at, 4))
    group_peers = [mate, across, beyond]
    floors = [floor, flip(floor, 1), flip(floor, 2), flip(flip(floor, 1), 2)]
    columns = [dp_at] + near[1:]
    at_expert = jnp.maximum(step_at - images, 0)
    which, half = at_expert // 2, lax.rem((at_expert + 1) // 2, 2)
    order = [(0, 0), (0, 1), (1, 1), (1, 0)]

    codes_sent = [send(codes_ref, code_buf.at[k + 1], rsem, k, group_peers[k]) for k in range(3)]
    grow_sent = [send(grow_buf.at[0], grow_buf.at[k + 1], rsem, 3 + k, group_peers[k]) for k in range(3)]
    stores = [
        pltpu.make_async_copy(code_buf, code_out, local_sem.at[2]),
        pltpu.make_async_copy(grow_buf, grow_out, local_sem.at[3]),
        pltpu.make_async_copy(win_buf, win_out, local_sem.at[4]),
        pltpu.make_async_copy(wex_buf, wex_out, local_sem.at[5]),
    ]
    in_own, in_passed = plane_gather(win_ref, win_buf, 0, wsem, 0, dp_at, ex_at, near)
    ex_own, ex_passed = plane_gather(wex_ref, wex_buf, 0, wsem, 4, dp_at, ex_at, near)
    in_far, in_far_passed = plane_gather(win_buf.at[1, dp_at], win_buf, 1, wsem, 8, dp_at, ex_at, near)
    ex_far, ex_far_passed = plane_gather(wex_buf.at[1, dp_at], wex_buf, 1, wsem, 12, dp_at, ex_at, near)
    to_far = [
        send(win_ref, win_buf.at[1, dp_at], wsem, 16, far),
        send(wex_ref, wex_buf.at[1, dp_at], wsem, 17, far),
    ]
    along_line = [
        send(dense.at[dp_at, floor, core], dense.at[dp_at, floor, core], dsem, k - 1, (dp_at, 2 * floors[k] + core))
        for k in (1, 2, 3)
    ]
    in_plane = [
        [
            send(
                dense.at[dp_at, floors[k], core], dense.at[dp_at, floors[k], core], dsem, 3 + 3 * k + p - 1,
                (near[p], ex_at),
            )
            for p in (1, 2, 3)
        ]
        for k in range(4)
    ]
    dense_mate = [
        send(dense.at[columns[p], :, core], dense.at[columns[p], :, core], dsem, 15 + p, mate) for p in range(4)
    ]

    def to_mate(step):
        return send(act.at[0, step], act.at[1, step], tsem, step, mate)

    def to_chip(step):
        return send(act.at[0, step], act.at[2, step], tsem, images + step, across)

    def onward(step):
        return send(act.at[2, step], act.at[3, step], tsem, 2 * images + step, mate)

    def returns(step):
        q, side = order[step]
        return return_copies(out_buf, back_ref, q, side, ysem, local_sem, dp_at, ex_at)

    def pass_on(own, passed):
        for first, second in zip(own, passed):
            first.wait_recv()
            second.start()

    @pl.when(step_at == 0)
    def _():
        width = outw_ref.shape[1]
        dense[dp_at, floor, core, :, : 3 * width] = qkvw_ref[...]
        dense[dp_at, floor, core, :, 3 * width : 4 * width] = outw_ref[...]
        valid = jnp.maximum(all_cols_ref[...], 0).astype(F32)
        per_lane = jnp.sum(jnp.sum(valid, axis=0), axis=0, keepdims=True)
        my_count = jnp.sum(jnp.where(lane_ids((1, 8)) == 4, per_lane, 0.0), axis=-1, keepdims=True)
        count_high = jnp.floor(my_count * (1.0 / 128.0))
        lanes = lane_ids((1, 128))
        counts = jnp.where(lanes == experts + 2, count_high, 0.0) + jnp.where(
            lanes == experts + 3, my_count - 128.0 * count_high, 0.0
        )
        dense[dp_at, floor, core, :, 4 * width :] = (extra_ref[...].astype(F32) + counts).astype(BF16)
        code_buf[0] = codes_ref[...]
        greet([(near[k], ex_at) for k in (1, 2, 3)] + group_peers + [far, (dp_at, flip(flip(ex_at, 2), 4))])
        for copy in along_line + in_plane[0]:
            copy.start()
        win_buf[0, dp_at] = win_ref[...]
        wex_buf[0, dp_at] = wex_ref[...]
        for k in (1, 2, 3):
            along_line[k - 1].wait_recv()
            for copy in in_plane[k]:
                copy.start()
        dense_mate[0].start()
        for copy in to_far + codes_sent:
            copy.start()
        for p in (1, 2, 3):
            for k in range(4):
                in_plane[k][p - 1].wait_recv()
            dense_mate[p].start()
        for copy in in_own + ex_own:
            copy.start()
        for copy in dense_mate:
            copy.wait_recv()
        full = dense[...].reshape(dense_ref.shape)
        dense_ref[...] = full
        ext_ref[...] = full[:, 4 * width :].astype(F32).T

    @pl.when(step_at < images)
    def _():
        inputs = tok_ref[...].astype(F32)
        normed, _ = normalize(inputs)
        width = inputs.shape[1]
        act_one = (normed * ext_ref[experts : experts + 1, :]).astype(BF16)
        qkv = dot(act_one, dense_ref[:, : 3 * width]).astype(BF16)
        qkv_ref[...] = qkv
        rows = inputs.shape[0]
        low_half = lane_ids((1, 128)) < 64
        key_bias = jnp.where(lane_ids((1, rows)) < real_rows, 0.0, -1e30)
        parts = []
        for pair in range(width // 128):
            lanes = slice(128 * pair, 128 * (pair + 1))
            queries = qkv[:, lanes]
            key_rows = qkv[:, width + 128 * pair : width + 128 * (pair + 1)]
            values = qkv[:, 2 * width + 128 * pair : 2 * width + 128 * (pair + 1)]
            outs = []
            for side in range(2):
                mask = low_half if side == 0 else jnp.logical_not(low_half)
                masked = jnp.where(mask, queries, jnp.zeros_like(queries))
                scores = contract_cols(masked, key_rows) * 0.125 + key_bias
                exped = jnp.exp(scores - jnp.max(scores, axis=-1, keepdims=True))
                probs = (exped * (1.0 / jnp.sum(exped, axis=-1, keepdims=True))).astype(BF16)
                probs_ref[2 * pair + side] = probs
                outs.append(dot(probs, values))
            parts.append(jnp.where(low_half, outs[0], outs[1]).astype(BF16))
        mixed = jnp.concatenate(parts, axis=1)
        mixed_ref[...] = mixed
        resid = inputs + dot(mixed, dense_ref[:, 3 * width : 4 * width])
        resid_ref[...] = resid
        normed_two, _ = normalize(resid)
        act_two = (normed_two * ext_ref[experts + 1 : experts + 2, :]).astype(BF16)
        act[0, step_at] = act_two
        lanes = lane_ids((1, 128))
        logits = jnp.where(lanes < experts, dot(act_two, dense_ref[:, 4 * width :]), -1e30)
        exped = jnp.exp(logits - jnp.max(logits, axis=-1, keepdims=True))
        gates = exped / jnp.sum(exped, axis=-1, keepdims=True)
        cols = cols_ref[...]
        first = jnp.sum(jnp.where(lanes == cols[:, 2:3], gates, 0.0), axis=-1, keepdims=True)
        second = jnp.sum(jnp.where(lanes == cols[:, 3:4], gates, 0.0), axis=-1, keepdims=True)
        gates_ref[...] = jnp.where(lanes == experts, first, jnp.where(lanes == experts + 1, second, gates))
        logits_t = contract_cols(ext_ref[0:16, :].astype(BF16), act_two)[:experts]
        exped_t = jnp.exp(logits_t - jnp.max(logits_t, axis=0, keepdims=True))
        gates_t = exped_t / jnp.sum(exped_t, axis=0, keepdims=True)
        ids_t = row_ids(gates_t.shape)
        first_t = jnp.sum(jnp.where(ids_t == rows_ref[2:3, :], gates_t, 0.0), axis=0, keepdims=True)
        second_t = jnp.sum(jnp.where(ids_t == rows_ref[3:4, :], gates_t, 0.0), axis=0, keepdims=True)
        grow_buf[0, step_at] = jnp.where(row_ids((8, rows)) == 0, first_t, second_t)

    for step in range(images):

        @pl.when(step_at == step)
        def _():
            to_chip(step).start()
            to_mate(step).start()
            if step >= 3:
                to_chip(step - 3).wait_recv()
                onward(step - 3).start()

    @pl.when(step_at == images - 2)
    def _():
        pass_on(in_own, in_passed)

    @pl.when(step_at == images - 1)
    def _():
        for copy in grow_sent:
            copy.start()

    @pl.when(step_at == images)
    def _():
        pass_on(ex_own, ex_passed)
        to_far[0].wait_recv()
        for copy in in_far:
            copy.start()
        for copy in in_passed + codes_sent:
            copy.wait_recv()
        for step in range(images):
            to_mate(step).wait_recv()

    @pl.when(step_at == images + 1)
    def _():
        for step in range(images - 3, images):
            to_chip(step).wait_recv()
            onward(step).start()
        for step in range(images):
            onward(step).wait_recv()

    @pl.when(step_at == images + 2)
    def _():
        for copy in in_far_passed:
            copy.wait_recv()

    blocks = group // 2
    parts, width, hidden_width = win_buf.shape[1], act.shape[3], win_buf.shape[3]
    step_width = hidden_width // parts

    @pl.when(step_at >= images)
    def _():
        pieces = []
        for block in range(blocks):
            start = (which * group + half * blocks + block) * cap
            total = None
            for image in range(images):
                hot = hot_rows(code_buf[half * blocks + block, image], start, cap)
                term = dot(jnp.where(hot, 1.0, 0.0).astype(BF16), act[half * blocks + block, image])
                total = term if total is None else total + term
            pieces.append(total.astype(BF16))
        rows_in = jnp.concatenate(pieces, axis=0)
        rows_out_ref[...] = rows_in.reshape(rows_out_ref.shape)
        for part in range(parts):
            if part == 1:

                @pl.when(step_at == images + 1)
                def _():
                    pass_on(in_far, in_far_passed)
                    to_far[1].wait_recv()
                    for copy in ex_far:
                        copy.start()

            cut = slice(part * step_width, (part + 1) * step_width)
            hidden, slope = gelu_pair(dot(rows_in, win_buf[which, :, :, cut].reshape(width, step_width)))
            hidden_ref[:, :, cut] = hidden.astype(BF16).reshape(blocks, cap, step_width)
            slope_ref[:, :, cut] = slope.astype(BF16).reshape(blocks, cap, step_width)

    def second_product(source, q, side):
        result = None
        for part in range(parts):
            cut = slice(part * step_width, (part + 1) * step_width)
            term = dot(source[:, :, cut].reshape(blocks * cap, step_width), wex_buf[q, part])
            result = term if result is None else result + term
        out_buf[q, pl.ds(side * blocks, blocks)] = result.astype(BF16).reshape(blocks, cap, width)

    @pl.when(step_at == images)
    def _():
        for copy in ex_passed:
            copy.wait_recv()

    @pl.when(step_at == images + 2)
    def _():
        kept[...] = hidden_ref[...]

    @pl.when(step_at == images + 3)
    def _():
        pass_on(ex_far, ex_far_passed)
        for copy in grow_sent:
            copy.wait_recv()
        for copy in ex_far_passed:
            copy.wait_recv()
        for copy in stores:
            copy.start()
        second_product(kept, 1, 1)
        for copy in returns(2):
            copy.start()

    @pl.when((step_at >= images) & (step_at != images + 2))
    def _():
        second_product(hidden_ref, which, half)

    for step in (0, 1, 3):

        @pl.when(step_at == images + step)
        def _():
            for copy in returns(step):
                copy.start()

    @pl.when(step_at == images + 3)
    def _():
        for step in range(4):
            for copy in returns(step):
                copy.wait()
        for copy in stores:
            copy.wait()
        for step in range(images):
            to_mate(step).wait_send()
            to_chip(step).wait_send()
            onward(step).wait_send()
        for copy in along_line + dense_mate + codes_sent + grow_sent + to_far + [c for line in in_plane for c in line]:
            copy.wait_send()
        for own, passed in ((in_own, in_passed), (ex_own, ex_passed), (in_far, in_far_passed), (ex_far, ex_far_passed)):
            for copy in own + passed:
                copy.wait_send()


def hot_cols(codes, count):
    return lane_ids((codes.shape[0], count)) == codes


def combine_back_kernel(
    images, cap, group, total_tokens, shard, experts, ext_ref, resid_ref, came_ref, cols_ref, gates_ref, target_ref,
    codes_ref, grow_ref, rows_ref, hidden_ref, slope_ref, win_all, wex_all,
    out_ref, dout_ref, dlogit_ref, loss_ref, back_ref, gin_ref, gex_ref, far_in, far_ex,
    dlow, win_buf, wex_buf, acc_in, acc_out, low_in, low_ex, out_buf,
    got_in, got_ex, sum_in, sum_ex, more_in, more_ex,
    t_send, t_recv, y_send, y_recv, w_send, w_recv, local_sem,
):
    step_at = pl.program_id(0)
    dp_at, ex_at, near = place()
    mate, across = (dp_at, flip(ex_at, 1)), (dp_at, flip(ex_at, 2))
    tsem, ysem, wsem = (t_send, t_recv), (y_send, y_recv), (w_send, w_recv)
    at_expert = jnp.maximum(step_at - images, 0)
    which, half = 1 - at_expert // 2, lax.rem((at_expert + 1) // 2, 2)
    order = [(1, 0), (1, 1), (0, 1), (0, 0)]
    loads = [
        pltpu.make_async_copy(win_all, win_buf, local_sem.at[3]),
        pltpu.make_async_copy(wex_all, wex_buf, local_sem.at[4]),
    ]
    stores = [
        pltpu.make_async_copy(low_in.at[0], gin_ref, local_sem.at[7]),
        pltpu.make_async_copy(low_ex.at[0], gex_ref, local_sem.at[8]),
    ]
    tensors = [(low_in, got_in, sum_in, more_in, far_in, 1, 2), (low_ex, got_ex, sum_ex, more_ex, far_ex, 2, 1)]
    parts, width, hidden_width = win_buf.shape[1], dlow.shape[3], win_buf.shape[3]
    step_width = hidden_width // parts
    spread_in, spread_ex = [], []
    for s, owner in enumerate((near[1], near[3])):
        for part in range(parts):
            cut = slice(part * step_width, (part + 1) * step_width)
            spread_in.append(
                send(low_in.at[1, owner, :, cut], got_in.at[s, :, cut], wsem, 4 + parts * s + part, (near[1], ex_at))
            )
    for s, owner in enumerate((near[2], near[3])):
        spread_ex.append(send(low_ex.at[1, owner], got_ex.at[s], wsem, s, (near[2], ex_at)))
    spread = spread_in + spread_ex
    second_round = [
        send(passed, more, wsem, 2 + t, (near[second], ex_at))
        for t, (_, _, passed, more, _, _, second) in enumerate(tensors)
    ]

    def to_mate(step):
        return send(dlow.at[0, step], dlow.at[1, step], tsem, step, mate)

    def to_chip(step):
        return send(dlow.at[0, step], dlow.at[2, step], tsem, images + step, across)

    def onward(step):
        return send(dlow.at[2, step], dlow.at[3, step], tsem, 2 * images + step, mate)

    def returns(step):
        q, side = order[step]
        return return_copies(out_buf, back_ref, q, side, ysem, local_sem, dp_at, ex_at)

    @pl.when(step_at == 0)
    def _():
        for copy in loads:
            copy.start()
        greet(
            [(near[k], ex_at) for k in (1, 2)] + [mate, across, (dp_at, flip(flip(ex_at, 1), 2))]
        )

    @pl.when(step_at < images)
    def _():
        count = came_ref.shape[0]
        cols = cols_ref[...]
        rows = cols.shape[0]
        hot = jnp.concatenate(
            [
                jnp.where(hot_cols(cols[:, 0:1], count), 1.0, 0.0).astype(BF16),
                jnp.where(hot_cols(cols[:, 1:2], count), 1.0, 0.0).astype(BF16),
            ],
            axis=0,
        )
        both = dot(hot, came_ref[...])
        from_first, from_second = both[:rows], both[rows:]
        gates = gates_ref[...]
        first, second = gates[:, experts : experts + 1], gates[:, experts + 1 : experts + 2]
        output = resid_ref[...] + first * from_first + second * from_second
        out_ref[...] = output.astype(BF16)
        residue = output - target_ref[...].astype(F32)
        valid = jnp.maximum(cols[:, 4:5], 0).astype(F32)
        square = jnp.mean(residue * residue, axis=-1, keepdims=True) * valid

        @pl.when(step_at == 0)
        def _():
            loss_ref[...] = jnp.zeros_like(loss_ref)

        counts = jnp.sum(ext_ref[experts + 2 : experts + 4, :], axis=-1, keepdims=True)
        count_all = (counts[0:1] * 128.0 + counts[1:2]) / shard
        loss_ref[...] += jnp.sum(square) / count_all
        dout = (total_tokens / count_all * valid) * residue
        dout_ref[...] = dout
        dlow[0, step_at] = dout.astype(BF16)
        lanes = lane_ids((1, 128))
        grad = jnp.where(
            lanes == cols[:, 2:3], jnp.sum(dout * from_first, axis=-1, keepdims=True), 0.0
        ) + jnp.where(lanes == cols[:, 3:4], jnp.sum(dout * from_second, axis=-1, keepdims=True), 0.0)
        real = jnp.where(lanes < experts, gates, 0.0)
        dlogit_ref[...] = real * (grad - jnp.sum(real * grad, axis=-1, keepdims=True))

    for step in range(images):

        @pl.when(step_at == step)
        def _():
            to_chip(step).start()
            to_mate(step).start()
            if step >= 3:
                to_chip(step - 3).wait_recv()
                onward(step - 3).start()

    @pl.when(step_at == images)
    def _():
        for copy in loads:
            copy.wait()
        for step in range(images):
            to_mate(step).wait_recv()

    @pl.when(step_at == images + 1)
    def _():
        for step in range(images - 3, images):
            to_chip(step).wait_recv()
            onward(step).start()
        for step in range(images):
            onward(step).wait_recv()

    @pl.when(step_at >= images)
    def _():
        blocks = group // 2
        parts, width, hidden_width = win_buf.shape[1], dlow.shape[3], win_buf.shape[3]
        pieces = []
        for block in range(blocks):
            start = (which * group + half * blocks + block) * cap
            total = None
            slot_gate = None
            for image in range(images):
                codes = codes_ref[half * blocks + block, image]
                slots = row_ids((cap, codes.shape[1])) + start
                is_first = slots == codes[0:1, :]
                is_second = slots == codes[1:2, :]
                hot = jnp.where(is_first | is_second, 1.0, 0.0).astype(BF16)
                term = dot(hot, dlow[half * blocks + block, image])
                gain = grow_ref[half * blocks + block, image]
                picked = jnp.where(is_first, gain[0:1, :], jnp.where(is_second, gain[1:2, :], 0.0))
                picked = jnp.sum(picked, axis=-1, keepdims=True)
                total = term if total is None else total + term
                slot_gate = picked if slot_gate is None else slot_gate + picked
            pieces.append((total * slot_gate).astype(BF16))
        grads = jnp.concatenate(pieces, axis=0)
        grads_t = grads.T
        rows_in_t = rows_ref[...].reshape(blocks * cap, -1).T
        step = hidden_width // parts
        result = None
        for offset in range(0, hidden_width, step):
            cut = slice(offset, offset + step)
            hidden = hidden_ref[:, :, cut].reshape(blocks * cap, step)
            slope = slope_ref[:, :, cut].reshape(blocks * cap, step).astype(F32)
            dpre = (contract_cols(grads, wex_buf[which, offset // step]) * slope).astype(BF16)
            gin = dot(rows_in_t, dpre)
            gout = dot(grads_t, hidden)
            term = contract_cols(dpre, win_buf[which, :, :, cut].reshape(width, step))
            result = term if result is None else result + term

            @pl.when(lax.rem(at_expert, 2) == 0)
            def _():
                acc_in[:, cut] = gin
                acc_out[:, cut] = gout

            @pl.when(lax.rem(at_expert, 2) == 1)
            def _():
                total_in = (acc_in[:, cut] + gin).astype(BF16)
                low_in[which, :, :, cut] = total_in.reshape(parts, width // parts, step)
                low_ex[which, offset // step] = (acc_out[:, cut] + gout).astype(BF16)

            part = offset // step

            @pl.when(at_expert == 1)
            def _():
                for s in range(2):
                    spread_in[parts * s + part].start()

            for s, owner in enumerate((near[2], near[3])):

                @pl.when((at_expert == 1) & (owner == part))
                def _():
                    spread_ex[s].start()

        out_buf[which, pl.ds(half * blocks, blocks)] = result.astype(BF16).reshape(blocks, cap, width)

    for step in range(4):

        @pl.when(step_at == images + step)
        def _():
            for copy in returns(step):
                copy.start()

    @pl.when(step_at == images + 3)
    def _():
        for copy in stores:
            copy.start()
        for copy in spread:
            copy.wait_recv()
        for grad, got, passed, _, _, _, second in tensors:
            passed[...] = (grad[1, near[second]].astype(F32) + got[1].astype(F32)).astype(BF16)
        for copy in second_round:
            copy.start()
        for step in range(4):
            for copy in returns(step):
                copy.wait()
        for copy in second_round:
            copy.wait_recv()
        for grad, got, _, more, far, _, _ in tensors:
            far[...] = (grad[1, dp_at].astype(F32) + got[0].astype(F32) + more[...].astype(F32)).astype(BF16)
        for copy in stores:
            copy.wait()
        for copy in spread + second_round:
            copy.wait_send()
        for step in range(images):
            to_mate(step).wait_send()
            to_chip(step).wait_send()
            onward(step).wait_send()


def back_kernel(
    images, real_rows, experts, tok_ref, dense_w, ext_ref, cols_ref, back_ref, dlogit_ref, resid_ref,
    dout_ref, qkv_ref, probs_ref, mixed_ref, loss_ref, gin_ref, gex_ref, far_in, far_ex,
    tgrad_ref, dense_ref, misc_ref, gin_out, gex_out,
    acc, acc_misc, part_in, part_ex, got_in, got_ex, sum_in, sum_ex, more_in, more_ex, came_in, came_ex,
    low, mate, low_mate, plane, low_plane, line, misc_got, misc_t, local_sem, w_send, w_recv, d_send, d_recv, m_send, m_recv,
):
    step_at = pl.program_id(0)
    dp_at, ex_at, near = place()
    core, floor = lax.rem(ex_at, 2), ex_at // 2
    wsem, dsem, msem = (w_send, w_recv), (d_send, d_recv), (m_send, m_recv)
    tensors = [
        (gin_ref, part_in, got_in, sum_in, more_in, far_in, came_in, gin_out, 1, 2),
        (gex_ref, part_ex, got_ex, sum_ex, more_ex, far_ex, came_ex, gex_out, 2, 1),
    ]
    local_copies, first_round, second_round, far_round = [], [], [], []
    for t, (grad, part, got, passed, more, far, came, _, first, second) in enumerate(tensors):
        for s in range(2):
            mine = dp_at if s == 0 else near[second]
            theirs = near[first] if s == 0 else near[3]
            local_copies.append(pltpu.make_async_copy(grad.at[mine], part.at[s], local_sem.at[2 * t + s]))
            first_round.append(send(grad.at[theirs], got.at[s], wsem, 4 * t + s, (near[first], ex_at)))
        second_round.append(send(passed, more, wsem, 4 * t + 2, (near[second], ex_at)))
        far_round.append(send(far, came, wsem, 4 * t + 3, (dp_at, flip(ex_at, 4))))

    @pl.when(step_at == 0)
    def _():
        for copy in local_copies:
            copy.start()
        greet(
            [(near[k], ex_at) for k in (1, 2, 3)]
            + [(dp_at, flip(ex_at, bit)) for bit in (1, 2, 4)]
            + [(dp_at, flip(flip(ex_at, 2), 4))]
        )
        for copy in first_round + far_round:
            copy.start()

    count = back_ref.shape[0]
    cols = cols_ref[...]
    hot = jnp.where(hot_cols(cols[:, 0:1], count) | hot_cols(cols[:, 1:2], count), 1.0, 0.0)
    dlogits = dlogit_ref[...]
    dact = dot(hot.astype(BF16), back_ref[...])
    dlogits_high = dlogits.astype(BF16)
    router_t = ext_ref[...].astype(BF16)
    dlogits_low = (dlogits - dlogits_high.astype(F32)).astype(BF16)
    dact = dact + dot(dlogits_high, router_t) + dot(dlogits_low, router_t)

    resid = resid_ref[...]
    normed_two, inverse_two = normalize(resid)
    gain_two = ext_ref[experts + 1 : experts + 2, :]
    act_two = (normed_two * gain_two).astype(BF16)
    grouter = contract_rows(dlogits_high, act_two) + contract_rows(dlogits_low, act_two)

    def norm_back(grad, normed, inverse, gain):
        scaled = grad * gain
        gain_grad = jnp.sum(grad * normed, axis=0, keepdims=True)
        inner = (
            scaled
            - jnp.mean(scaled, axis=-1, keepdims=True)
            - normed * jnp.mean(scaled * normed, axis=-1, keepdims=True)
        )
        return inverse * inner, gain_grad

    grad_two, ggain_two = norm_back(dact, normed_two, inverse_two, gain_two)
    dresid = dout_ref[...] + grad_two
    branch = dresid.astype(BF16)
    mixed = mixed_ref[...]
    gout = contract_rows(mixed, branch)
    width = branch.shape[1]
    dmixed = contract_cols(branch, dense_w[:, 3 * width : 4 * width]).astype(BF16)
    qkv = qkv_ref[...]
    low_half = lane_ids((1, 128)) < 64
    dqs, dks, dvs = [], [], []
    for pair in range(width // 128):
        cut = slice(128 * pair, 128 * (pair + 1))
        queries = qkv[:, cut]
        key_rows = qkv[:, width + 128 * pair : width + 128 * (pair + 1)]
        values = qkv[:, 2 * width + 128 * pair : 2 * width + 128 * (pair + 1)]
        dmix = dmixed[:, cut]
        dq = []
        dk = dv = None
        for side in range(2):
            mask = low_half if side == 0 else jnp.logical_not(low_half)
            dmask = jnp.where(mask, dmix, jnp.zeros_like(dmix))
            qmask = jnp.where(mask, queries, jnp.zeros_like(queries))
            probs_low = probs_ref[2 * pair + side]
            probs = probs_low.astype(F32)
            dprobs = contract_cols(dmask, values)
            dscore = probs * (dprobs - jnp.sum(probs * dprobs, axis=-1, keepdims=True))
            dscore = dscore.astype(BF16)
            dq.append(dot(dscore, key_rows))
            dk_term = contract_rows(dscore, qmask)
            dv_term = contract_rows(probs_low, dmask)
            dk = dk_term if dk is None else dk + dk_term
            dv = dv_term if dv is None else dv + dv_term
        dqs.append((jnp.where(low_half, dq[0], dq[1]) * 0.125).astype(BF16))
        dks.append((dk * 0.125).astype(BF16))
        dvs.append(dv.astype(BF16))
    dqkv = jnp.concatenate(dqs + dks + dvs, axis=1)
    inputs = tok_ref[...].astype(F32)
    normed_one, inverse_one = normalize(inputs)
    gain_one = ext_ref[experts : experts + 1, :]
    act_one = (normed_one * gain_one).astype(BF16)
    gqkv = contract_rows(act_one, dqkv)
    dact_one = contract_cols(dqkv, dense_w[:, : 3 * width])
    grad_one, ggain_one = norm_back(dact_one, normed_one, inverse_one, gain_one)
    tgrad = dresid + grad_one
    for image in range(images):

        @pl.when(step_at == image)
        def _():
            tgrad_ref[image * real_rows : (image + 1) * real_rows, :] = tgrad[:real_rows]

    ids = row_ids((8, width))
    gmisc = jnp.concatenate(
        [grouter[:8], jnp.where(ids == 0, ggain_one, jnp.where(ids == 1, ggain_two, 0.0))], axis=0
    )

    @pl.when(step_at == 0)
    def _():
        acc[:, : 3 * width] = gqkv
        acc[:, 3 * width :] = gout
        loss_row = jnp.where(row_ids((8, 128)) == 2, loss_ref[...], 0.0)
        acc_misc[...] = gmisc + jnp.concatenate(
            [jnp.zeros((8, width), F32), jnp.concatenate([loss_row] * (width // 128), axis=1)], axis=0
        )

    @pl.when(step_at > 0)
    def _():
        acc[:, : 3 * width] += gqkv
        acc[:, 3 * width :] += gout
        acc_misc[...] += gmisc

    @pl.when(step_at == images - 2)
    def _():
        for copy in local_copies:
            copy.wait()
        for copy in first_round:
            copy.wait_recv()
        for _, part, got, passed, _, _, _, _, _, _ in tensors:
            passed[...] = (part[1].astype(F32) + got[1].astype(F32)).astype(BF16)
        for copy in second_round:
            copy.start()

    @pl.when(step_at == images - 1)
    def _():
        lines, shard = low.shape[1], low.shape[3]
        low[...] = acc[...].astype(BF16).reshape(low.shape)
        other = lax.rem(core + 1, 2)
        to_mate = send(low.at[:, :, other], mate, dsem, 0, (dp_at, flip(ex_at, 1)))
        to_mate.start()
        misc_peers = [
            (dp_at, flip(ex_at, 1)), (near[1], ex_at), (near[2], ex_at), (dp_at, flip(ex_at, 2)), (dp_at, flip(ex_at, 4)),
        ]
        misc = [send(acc_misc.at[...] if k == 0 else misc_got.at[5 + k - 1], misc_got.at[k], msem, k, misc_peers[k]) for k in range(5)]
        misc[0].start()

        def misc_step(k):
            misc[k].wait_recv()
            before = acc_misc[...] if k == 0 else misc_got[5 + k - 1]
            misc_got[5 + k] = before + misc_got[k]
            if k < 4:
                misc[k + 1].start()

        to_mate.wait_recv()
        low_mate[...] = (low[:, :, core].astype(F32) + mate[...].astype(F32)).astype(BF16)
        to_plane = [send(low_mate.at[near[k]], plane.at[k - 1], dsem, k, (near[k], ex_at)) for k in (1, 2, 3)]
        for copy in to_plane:
            copy.start()
        misc_step(0)
        misc_step(1)
        misc_step(2)
        for copy in to_plane:
            copy.wait_recv()
        summed = low_mate[dp_at].astype(F32)
        for k in range(3):
            summed = summed + plane[k].astype(F32)
        low_plane[...] = summed.astype(BF16)
        floors = [flip(floor, 1), flip(floor, 2), flip(flip(floor, 1), 2)]
        to_line = [
            send(low_plane.at[floors[k]], line.at[k], dsem, 4 + k, (dp_at, 2 * floors[k] + core)) for k in range(3)
        ]
        for copy in to_line:
            copy.start()
        misc_step(3)
        misc_step(4)
        flat = (dp_at * (2 * low.shape[1]) + ex_at) * shard
        rows_t = jnp.concatenate([misc_got[9], jnp.zeros((112, misc_got.shape[2]), F32)], axis=0).T
        misc_t[...] = rows_t
        misc_ref[...] = misc_t[pl.ds(pl.multiple_of(flat, shard), shard), :]
        for copy in to_line:
            copy.wait_recv()
        result = low_plane[floor].astype(F32)
        for k in range(3):
            result = result + line[k].astype(F32)
        dense_ref[...] = result

        for copy in second_round + far_round:
            copy.wait_recv()
        for _, part, got, _, more, _, came, out, _, _ in tensors:
            out[...] = (
                part[0].astype(F32) + got[0].astype(F32) + more[...].astype(F32) + came[...].astype(F32)
            )
        for copy in [to_mate] + misc + to_plane + to_line + first_round + second_round + far_round:
            copy.wait_send()


def prepare_kernel(
    images, capacity, cap, tok_ref, target_ref, routes_ref, slots_ref, valid_ref, router_ref, gain_one_ref, gain_two_ref,
    tok_out, target_out, cols_out, rows_out, extra_out,
    wide, line,
):
    total, width = tok_ref.shape
    real_rows, rows = total // images, tok_out.shape[1]
    for source, out in ((tok_ref, tok_out), (target_ref, target_out)):
        wide[:total, :] = source[...].astype(F32)
        for image in range(images):
            piece = wide[image * real_rows : image * real_rows + rows, :]
            piece = jnp.where(row_ids((rows, 1)) < real_rows, piece, 0.0)
            out[image] = piece.astype(BF16)
    me = lax.axis_index("expert")
    routes, slots = routes_ref[...], slots_ref[...]
    code = jnp.where(slots < capacity, jnp.bitwise_xor(routes, me) * cap + slots, -1)
    line[0:2, :total] = code.astype(F32)
    line[2:4, :total] = routes.astype(F32)
    line[4:5, :total] = valid_ref[...].astype(F32)
    lanes = line.shape[1]
    packed = line[...]
    for image in range(images):
        piece = packed[:, image * real_rows : image * real_rows + rows]
        keep = (lane_ids((8, rows)) < real_rows) & (row_ids((8, rows)) < 5)
        piece = jnp.where(keep, piece, -1.0)
        rows_out[image] = piece.astype(jnp.int32)
        square = jnp.concatenate(
            [
                jnp.concatenate([piece, jnp.full((8, round_up(rows, 128) - rows), -1.0, F32)], axis=1),
                jnp.full((120, round_up(rows, 128)), -1.0, F32),
            ],
            axis=0,
        )
        cols_out[image] = square.T[:rows, :8].astype(jnp.int32)
    experts, shard = router_ref.shape
    tall = jnp.concatenate(
        [
            router_ref[...].astype(F32), gain_one_ref[...].astype(F32), gain_two_ref[...].astype(F32),
            jnp.zeros((126 - experts, shard), F32),
        ],
        axis=0,
    )
    tall = jnp.concatenate([tall, jnp.zeros((128, 128 - shard), F32)], axis=1)
    extra_out[...] = tall.T[:shard].astype(BF16)


def finish_kernel(
    real_rows, experts, padded_ref, tgrad_in, dense_ref, misc_ref, gin_in, gex_in,
    out_ref, loss_ref, tgrad_ref, gain_one_ref, gqkv_ref, gout_ref, gain_two_ref, grouter_ref, gin_ref, gex_ref,
    joined,
):
    images, width = padded_ref.shape[0], padded_ref.shape[2]
    for image in range(images):
        joined[image * real_rows : (image + 1) * real_rows, :] = padded_ref[image].astype(F32)[:real_rows]
    out_ref[...] = joined[: images * real_rows, :].astype(BF16)
    tgrad_ref[...] = tgrad_in[...]
    gqkv_ref[...] = dense_ref[:, : 3 * width]
    gout_ref[...] = dense_ref[:, 3 * width :]
    own = misc_ref[...]
    shard = own.shape[0]
    turned = jnp.concatenate([own, jnp.zeros((128 - shard, 128), F32)], axis=0).T
    gain_one_ref[...] = turned[8:9, :shard]
    gain_two_ref[...] = turned[9:10, :shard]
    grouter_ref[...] = turned[:experts, :shard]
    loss_ref[...] = own[0:1, 10:11]
    gin_ref[...] = gin_in[...]
    gex_ref[...] = gex_in[...].T


def shape(dims, kind):
    return jax.ShapeDtypeStruct(dims, kind)


def whole(dims):
    return pl.BlockSpec(dims, lambda *_: (0,) * len(dims))


def per_image(*dims):
    return pl.BlockSpec((None,) + dims, lambda i: (i,) + (0,) * len(dims))


def params():
    return pltpu.CompilerParams(vmem_limit_bytes=56 * MB)


def fast_shards(
    tokens, targets, valid_mask, routes, slot_ids, ln1_gain, qkv_weight, out_weight, ln2_gain,
    router_weight, expert_in, expert_out,
):
    axes = ("dp", "expert")
    tok_rows, width = tokens.shape
    experts = lax.axis_size("expert")
    group = experts // 2
    dp = lax.axis_size("dp")
    total_tokens = tok_rows * dp * experts
    hidden_width = expert_in.shape[2]
    capacity = (5 * tok_rows // 2 // experts + 7) // 8 * 8
    cap = round_up(capacity, 16)
    images = IMG_DEV
    real_rows = tok_rows // images
    rows = round_up(real_rows, 16)
    shard = qkv_weight.shape[0]
    tok_p, target_p, cols, row_codes, extra = pl.pallas_call(
        lambda *refs: prepare_kernel(images, capacity, cap, *refs),
        out_shape=[
            shape((images, rows, width), BF16), shape((images, rows, width), BF16), shape((images, rows, 8), jnp.int32),
            shape((images, 8, rows), jnp.int32), shape((shard, 128), BF16),
        ],
        scratch_shapes=[
            pltpu.VMEM((round_up(tok_rows + rows - real_rows, 8), width), F32),
            pltpu.VMEM((8, round_up(tok_rows + rows - real_rows, 128)), F32),
        ],
        compiler_params=params(),
        name="prepare",
    )(
        tokens, targets, routes.T, slot_ids.T, valid_mask[None], router_weight.T, ln1_gain[None], ln2_gain[None],
    )
    floors = experts // 2
    in_part, ex_part = (width // dp, hidden_width), (hidden_width // dp, width)
    any_space = pl.BlockSpec(memory_space=pl.ANY)

    gate_lanes = 128
    dense_lanes = 4 * width + 128
    half_blocks = group // 2
    last = images - 1

    def early(*dims):
        return pl.BlockSpec((None,) + dims, lambda i: (jnp.minimum(i, last),) + (0,) * len(dims))

    def late(far_first, *dims):
        def index(i):
            step = jnp.maximum(i - images, 0)
            which = 1 - step // 2 if far_first else step // 2
            return (which, lax.rem((step + 1) // 2, 2)) + (0,) * len(dims)

        return pl.BlockSpec((None, half_blocks) + dims, index)

    def once(dims):
        return pl.BlockSpec(dims, lambda i: (0,) * len(dims), pipeline_mode=pl.Buffered(1))

    (
        qkv_p, probs, mixed, resid, gates, dense_full, ext, rows_in, hidden, slope, returned, code_all, grow_all,
        win_all, wex_all,
    ) = pl.pallas_call(
        lambda *refs: front_kernel(images, real_rows, experts, cap, group, *refs),
        grid=(images + 4,),
        in_specs=[
            early(rows, width), once((shard, 3 * width)), once((shard, width)), once((shard, 128)),
            early(rows, 8), early(8, rows), once((images, 8, rows)), once((images, rows, 8)), once(in_part), once(ex_part),
        ],
        out_specs=[
            early(rows, 3 * width), early(HEADS, rows, rows), early(rows, width), early(rows, width),
            early(rows, gate_lanes), whole((width, dense_lanes)), whole((128, width)),
            late(False, cap, width), late(False, cap, hidden_width), late(False, cap, hidden_width),
            *[any_space] * 5,
        ],
        out_shape=[
            shape((images, rows, 3 * width), BF16), shape((images, HEADS, rows, rows), BF16),
            shape((images, rows, width), BF16), shape((images, rows, width), F32),
            shape((images, rows, gate_lanes), F32), shape((width, dense_lanes), BF16), shape((128, width), F32),
            shape((2, group, cap, width), BF16), shape((2, group, cap, hidden_width), BF16),
            shape((2, group, cap, hidden_width), BF16), shape((2, group, cap, width), BF16),
            shape((group, images, 8, rows), jnp.int32), shape((group, images, 8, rows), F32),
            shape((2, dp, *in_part), BF16), shape((2, dp, *ex_part), BF16),
        ],
        scratch_shapes=[
            pltpu.VMEM((dp, floors, 2, shard, dense_lanes), BF16), pltpu.VMEM((group, images, rows, width), BF16),
            pltpu.VMEM((group, images, 8, rows), jnp.int32), pltpu.VMEM((group, images, 8, rows), F32),
            pltpu.VMEM((2, dp, *in_part), BF16), pltpu.VMEM((2, dp, *ex_part), BF16),
            pltpu.VMEM((2, group, cap, width), BF16), pltpu.VMEM((half_blocks, cap, hidden_width), BF16),
            *sem_pairs(19), *sem_pairs(3 * images), *sem_pairs(6), *sem_pairs(18), *sem_pairs(8),
            pltpu.SemaphoreType.DMA((6,)),
        ],
        compiler_params=pltpu.CompilerParams(
            vmem_limit_bytes=60 * MB, collective_id=2, has_side_effects=True
        ),
        cost_estimate=pl.CostEstimate(flops=int(20e9), bytes_accessed=int(6e7), transcendentals=0),
        name="attention_expert_forward",
    )(tok_p, qkv_weight, out_weight, extra, cols, row_codes, row_codes, cols, expert_in[0], expert_out[0])
    returned = returned.reshape(2 * group * cap, width)

    flip_part = (width, hidden_width // dp)
    block_out, dout, dlogits, loss_part, drows, gin, gout_t, far_in, far_ex = pl.pallas_call(
        lambda *refs: combine_back_kernel(images, cap, group, total_tokens, shard, experts, *refs),
        grid=(images + 4,),
        in_specs=[
            once((16, width)), early(rows, width), once((2 * group * cap, width)), early(rows, 8),
            early(rows, gate_lanes), early(rows, width), once((group, images, 8, rows)),
            once((group, images, 8, rows)), late(True, cap, width), late(True, cap, hidden_width),
            late(True, cap, hidden_width), any_space, any_space,
        ],
        out_specs=[
            early(rows, width), early(rows, width), early(rows, gate_lanes), whole((8, 128)), *[any_space] * 3,
            once(in_part), once(flip_part),
        ],
        out_shape=[
            shape((images, rows, width), BF16), shape((images, rows, width), F32),
            shape((images, rows, gate_lanes), F32), shape((8, 128), F32),
            shape((2, group, cap, width), BF16), shape((dp, *in_part), BF16), shape((dp, *flip_part), BF16),
            shape(in_part, BF16), shape(flip_part, BF16),
        ],
        scratch_shapes=[
            pltpu.VMEM((group, images, rows, width), BF16),
            pltpu.VMEM((2, dp, *in_part), BF16), pltpu.VMEM((2, dp, *ex_part), BF16),
            pltpu.VMEM((width, hidden_width), F32), pltpu.VMEM((width, hidden_width), F32),
            pltpu.VMEM((2, dp, *in_part), BF16), pltpu.VMEM((2, dp, *flip_part), BF16),
            pltpu.VMEM((2, group, cap, width), BF16),
            *[pltpu.VMEM(dims, BF16) for dims in ((2, *in_part), (2, *flip_part), in_part, flip_part, in_part, flip_part)],
            *sem_pairs(3 * images), *sem_pairs(8), *sem_pairs(4 + 2 * dp), pltpu.SemaphoreType.DMA((9,)),
        ],
        compiler_params=pltpu.CompilerParams(
            vmem_limit_bytes=62 * MB, collective_id=5, has_side_effects=True
        ),
        cost_estimate=pl.CostEstimate(flops=int(24e9), bytes_accessed=int(4e7), transcendentals=0),
        name="combine_expert_backward",
    )(
        ext, resid, returned, cols, gates, target_p, code_all, grow_all, rows_in, hidden, slope,
        win_all, wex_all,
    )
    grad_back = drows.reshape(2 * group * cap, width)

    def vmem(*dims):
        return pltpu.VMEM(dims, BF16)

    tgrad, dense_grad, misc, gin_own, gex_own = pl.pallas_call(
        lambda *refs: back_kernel(images, real_rows, experts, *refs),
        grid=(images,),
        in_specs=[
            per_image(rows, width), whole((width, dense_lanes)), whole((128, width)), per_image(rows, 8),
            whole((2 * group * cap, width)), per_image(rows, gate_lanes), per_image(rows, width), per_image(rows, width),
            per_image(rows, 3 * width), per_image(HEADS, rows, rows), per_image(rows, width), whole((8, 128)),
            *[any_space] * 4,
        ],
        out_specs=[
            once((tok_rows, width)), whole((shard, 4 * width)), whole((shard, 128)), whole(in_part), whole(flip_part),
        ],
        out_shape=[
            shape((tok_rows, width), F32), shape((shard, 4 * width), F32), shape((shard, 128), F32),
            shape(in_part, F32), shape(flip_part, F32),
        ],
        scratch_shapes=[
            pltpu.VMEM((width, 4 * width), F32), pltpu.VMEM((16, width), F32),
            vmem(2, *in_part), vmem(2, *flip_part), vmem(2, *in_part), vmem(2, *flip_part),
            vmem(*in_part), vmem(*flip_part), vmem(*in_part), vmem(*flip_part), vmem(*in_part), vmem(*flip_part),
            vmem(dp, floors, 2, shard, 4 * width), vmem(dp, floors, shard, 4 * width), vmem(dp, floors, shard, 4 * width),
            vmem(3, floors, shard, 4 * width), vmem(floors, shard, 4 * width), vmem(3, shard, 4 * width),
            pltpu.VMEM((10, 16, width), F32), pltpu.VMEM((width, 128), F32),
            pltpu.SemaphoreType.DMA((4,)),
            *sem_pairs(8), *sem_pairs(8), *sem_pairs(5),
        ],
        compiler_params=pltpu.CompilerParams(
            vmem_limit_bytes=60 * MB, collective_id=1, has_side_effects=True
        ),
        cost_estimate=pl.CostEstimate(flops=int(10e9), bytes_accessed=int(3e7), transcendentals=0),
        name="attention_backward",
    )(
        tok_p, dense_full, ext, cols, grad_back, dlogits, resid, dout, qkv_p, probs, mixed,
        loss_part, gin, gout_t, far_in, far_ex,
    )
    out, loss, tokens_grad, gain_one_grad, qkv_grad, out_grad, gain_two_grad, router_grad, in_grad, ex_grad = pl.pallas_call(
        lambda *refs: finish_kernel(real_rows, experts, *refs),
        out_shape=[
            shape((tok_rows, width), BF16), shape((1, 1), F32), shape((tok_rows, width), F32), shape((1, shard), F32),
            shape((shard, 3 * width), F32), shape((shard, width), F32), shape((1, shard), F32),
            shape((experts, shard), F32), shape(in_part, F32), shape(ex_part, F32),
        ],
        scratch_shapes=[pltpu.VMEM((round_up(tok_rows, 8), width), F32)],
        compiler_params=params(),
        name="finish",
    )(block_out, tgrad, dense_grad, misc, gin_own, gex_own)
    return (
        out,
        loss.reshape(()),
        tokens_grad,
        gain_one_grad.reshape(shard),
        qkv_grad,
        out_grad,
        gain_two_grad.reshape(shard),
        router_grad.T,
        in_grad[None],
        ex_grad[None],
    )


def solution(mesh):
    in_specs = (
        P(("dp", "expert"), None),
        P(("dp", "expert"), None),
        P(("dp", "expert")),
        P(("dp", "expert"), None),
        P(("dp", "expert"), None),
        P(("dp", "expert")),
        P(("dp", "expert"), None),
        P(("dp", "expert"), None),
        P(("dp", "expert")),
        P(("dp", "expert"), None),
        P("expert", "dp", None),
        P("expert", "dp", None),
    )
    out_specs = (
        P(("dp", "expert"), None),
        P(),
        P(("dp", "expert"), None),
        P(("dp", "expert")),
        P(("dp", "expert"), None),
        P(("dp", "expert"), None),
        P(("dp", "expert")),
        P(("dp", "expert"), None),
        P("expert", "dp", None),
        P("expert", "dp", None),
    )
    halves = mesh.shape["expert"] == 8 and mesh.shape["dp"] == 4
    body = fast_shards if halves else shards
    return jax.shard_map(body, mesh=mesh, in_specs=in_specs, out_specs=out_specs, check_vma=False)
```

```python
import jax
import jax.numpy as jnp
from jax import lax
from jax.experimental import pallas as pl
from jax.experimental.pallas import tpu as pltpu
from jax.sharding import PartitionSpec as P

HEADS = 8
IMG_DEV = 5


HIGH = lax.Precision.HIGHEST
EPS = 1e-06


def layer_norm(values, scale_gain):
    row_mean = jnp.mean(values, axis=-1, keepdims=True)
    centered = values - row_mean
    variance = jnp.mean(centered * centered, axis=-1, keepdims=True)
    inverse = lax.rsqrt(variance + EPS)
    normed = centered * inverse
    return (normed * scale_gain, normed, inverse)


def layer_norm_back(grad_in, normed, inverse, scale_gain):
    scaled = grad_in * scale_gain
    gain_grad = jnp.sum(grad_in * normed, axis=0)
    inner_term = (
        scaled
        - jnp.mean(scaled, axis=-1, keepdims=True)
        - normed * jnp.mean(scaled * normed, axis=-1, keepdims=True)
    )
    return (inverse * inner_term, gain_grad)


def contract_rows(left_side, right_side):
    return lax.dot_general(
        left_side, right_side, (((0,), (0,)), ((), ())), preferred_element_type=jnp.float32
    )


def contract_cols(left_side, right_side):
    return lax.dot_general(
        left_side, right_side, (((1,), (1,)), ((), ())), preferred_element_type=jnp.float32
    )


def exact_gelu(values):
    return jax.nn.gelu(values, approximate=False)


def split_heads(qkv_low, images, head_count):
    row_count, triple_width = qkv_low.shape
    head_dim = triple_width // (3 * head_count)
    pieces = qkv_low.reshape(images, row_count // images, 3, head_count, head_dim)
    return (pieces[:, :, 0], pieces[:, :, 1], pieces[:, :, 2], head_dim ** (-0.5))


def attention_forward(qkv_low, images, head_count):
    queries, key_rows, values, score_scale = split_heads(qkv_low, images, head_count)
    scores = (
        jnp.einsum("ilhd,imhd->ihlm", queries, key_rows, preferred_element_type=jnp.float32)
        * score_scale
    )
    row_max = jnp.max(scores, axis=-1, keepdims=True)
    exp_scores = jnp.exp(scores - row_max)
    row_sum = jnp.sum(exp_scores, axis=-1, keepdims=True)
    weights_low = (exp_scores / row_sum).astype(jnp.bfloat16)
    log_total = row_max + jnp.log(row_sum)
    mixed_rows = jnp.einsum(
        "ihlm,imhd->ilhd", weights_low, values, preferred_element_type=jnp.float32
    )
    return (mixed_rows.reshape(qkv_low.shape[0], -1).astype(jnp.bfloat16), log_total)


def attention_back(qkv_low, log_total, grad_mixed, images, head_count):
    queries, key_rows, values, score_scale = split_heads(qkv_low, images, head_count)
    scores = (
        jnp.einsum("ilhd,imhd->ihlm", queries, key_rows, preferred_element_type=jnp.float32)
        * score_scale
    )
    weights_full = jnp.exp(scores - log_total)
    weights_low = weights_full.astype(jnp.bfloat16)
    grad_heads = grad_mixed.reshape(queries.shape)
    grad_weights = jnp.einsum(
        "ilhd,imhd->ihlm", grad_heads, values, preferred_element_type=jnp.float32
    )
    grad_values = jnp.einsum(
        "ihlm,ilhd->imhd", weights_low, grad_heads, preferred_element_type=jnp.float32
    )
    grad_scores = weights_full * (
        grad_weights - jnp.sum(weights_full * grad_weights, axis=-1, keepdims=True)
    )
    grad_low = grad_scores.astype(jnp.bfloat16)
    grad_queries = (
        jnp.einsum("ihlm,imhd->ilhd", grad_low, key_rows, preferred_element_type=jnp.float32)
        * score_scale
    )
    grad_keys = (
        jnp.einsum("ihlm,ilhd->imhd", grad_low, queries, preferred_element_type=jnp.float32)
        * score_scale
    )
    stacked = jnp.stack([grad_queries, grad_keys, grad_values], axis=2)
    return stacked.reshape(qkv_low.shape).astype(jnp.bfloat16)


def expert_forward(rows_in, weight_in, weight_out, block_size):
    result = jnp.zeros((rows_in.shape[0], weight_out.shape[1]), jnp.float32)
    for offset in range(0, weight_in.shape[1], block_size):
        pre_act = jnp.dot(
            rows_in, weight_in[:, offset : offset + block_size], preferred_element_type=jnp.float32
        )
        hidden = exact_gelu(pre_act).astype(jnp.bfloat16)
        result = result + jnp.dot(
            hidden, weight_out[offset : offset + block_size], preferred_element_type=jnp.float32
        )
    return result


def expert_back(rows_in, weight_in, weight_out, grad_rows_out, block_size):
    grad_rows = jnp.zeros(rows_in.shape, jnp.float32)
    grads_first = []
    grads_second = []
    for offset in range(0, weight_in.shape[1], block_size):
        slice_in = weight_in[:, offset : offset + block_size]
        slice_out = weight_out[offset : offset + block_size]
        pre_act = jnp.dot(rows_in, slice_in, preferred_element_type=jnp.float32)
        hidden, gelu_back = jax.vjp(exact_gelu, pre_act)
        grads_second.append(contract_rows(hidden.astype(jnp.bfloat16), grad_rows_out))
        grad_hidden = contract_cols(grad_rows_out, slice_out)
        grad_pre = gelu_back(grad_hidden)[0].astype(jnp.bfloat16)
        grads_first.append(contract_rows(rows_in, grad_pre))
        grad_rows = grad_rows + contract_cols(grad_pre, slice_in)
    return (grad_rows, jnp.concatenate(grads_first, axis=1), jnp.concatenate(grads_second, axis=0))


def shards(
    tokens,
    targets,
    valid_mask,
    routes,
    slot_ids,
    ln1_gain,
    qkv_weight,
    out_weight,
    ln2_gain,
    router_weight,
    expert_in,
    expert_out,
):
    tok_rows, model_width = tokens.shape
    experts = lax.axis_size("expert")
    total_tokens = tok_rows * lax.axis_size("dp") * experts
    capacity = (5 * tok_rows // 2 // experts + 7) // 8 * 8
    dense_full = (
        lax.all_gather(ln1_gain, ("dp", "expert"), axis=0, tiled=True),
        lax.all_gather(qkv_weight, ("dp", "expert"), axis=0, tiled=True),
        lax.all_gather(out_weight, ("dp", "expert"), axis=0, tiled=True),
        lax.all_gather(ln2_gain, ("dp", "expert"), axis=0, tiled=True),
        lax.all_gather(router_weight, ("dp", "expert"), axis=0, tiled=True),
    )
    gain_one, qkv_full, out_full, gain_two, router_full = dense_full
    expert_full = (
        lax.all_gather(expert_in, "dp", axis=1, tiled=True),
        lax.all_gather(expert_out, "dp", axis=1, tiled=True),
    )
    weight_in = expert_full[0][0]
    weight_out = expert_full[1][0]
    valid_f = valid_mask.astype(jnp.float32)
    valid_count = lax.psum(jnp.sum(valid_f), ("dp", "expert"))
    inputs_f = tokens.astype(jnp.float32)
    gain_one_f = gain_one.astype(jnp.float32)
    gain_two_f = gain_two.astype(jnp.float32)
    norm_one, normed_one, inverse_one = layer_norm(inputs_f, gain_one_f)
    act_one = norm_one.astype(jnp.bfloat16)
    qkv_low = jnp.dot(act_one, qkv_full, preferred_element_type=jnp.float32).astype(jnp.bfloat16)
    mixed_low, log_total = attention_forward(qkv_low, IMG_DEV, HEADS)
    residual = inputs_f + jnp.dot(mixed_low, out_full, preferred_element_type=jnp.float32)
    norm_two, normed_two, inverse_two = layer_norm(residual, gain_two_f)
    act_two = norm_two.astype(jnp.bfloat16)
    gate_probs = jax.nn.softmax(
        jnp.dot(act_two, router_full, preferred_element_type=jnp.float32), axis=-1
    )
    expert_ids = lax.broadcasted_iota(jnp.int32, (1, experts), 1)
    first_pick = (routes[:, 0:1] == expert_ids).astype(jnp.float32)
    second_pick = (routes[:, 1:2] == expert_ids).astype(jnp.float32)
    gate_first = jnp.sum(gate_probs * first_pick, axis=-1, keepdims=True)
    gate_second = jnp.sum(gate_probs * second_pick, axis=-1, keepdims=True)
    target_slot = jnp.where(slot_ids < capacity, routes * capacity + slot_ids, -1)
    slot_columns = lax.broadcasted_iota(jnp.int32, (1, experts * capacity), 1)
    first_hot = (target_slot[:, 0:1] == slot_columns).astype(jnp.bfloat16)
    second_hot = (target_slot[:, 1:2] == slot_columns).astype(jnp.bfloat16)
    both_hot = first_hot + second_hot
    outgoing = contract_rows(both_hot, act_two).astype(jnp.bfloat16)
    arrived = lax.all_to_all(
        outgoing.reshape(experts, capacity, model_width),
        "expert",
        split_axis=0,
        concat_axis=0,
        tiled=True,
    ).reshape(-1, model_width)
    hidden_block = min(512, weight_in.shape[1])
    produced = expert_forward(arrived, weight_in, weight_out, hidden_block).astype(jnp.bfloat16)
    returned = lax.all_to_all(
        produced.reshape(experts, capacity, model_width),
        "expert",
        split_axis=0,
        concat_axis=0,
        tiled=True,
    ).reshape(-1, model_width)
    from_first = jnp.dot(first_hot, returned, preferred_element_type=jnp.float32)
    from_second = jnp.dot(second_hot, returned, preferred_element_type=jnp.float32)
    output = residual + gate_first * from_first + gate_second * from_second
    residue = output - targets.astype(jnp.float32)
    local_loss = jnp.sum(valid_f * jnp.mean(residue * residue, axis=-1))
    loss_sum = lax.psum(local_loss, ("dp", "expert"))
    loss_value = loss_sum / valid_count
    grad_out = total_tokens / valid_count * valid_f[:, None] * residue
    dense_back = (
        lax.all_gather(ln1_gain, ("dp", "expert"), axis=0, tiled=True),
        lax.all_gather(qkv_weight, ("dp", "expert"), axis=0, tiled=True),
        lax.all_gather(out_weight, ("dp", "expert"), axis=0, tiled=True),
        lax.all_gather(ln2_gain, ("dp", "expert"), axis=0, tiled=True),
        lax.all_gather(router_weight, ("dp", "expert"), axis=0, tiled=True),
    )
    expert_back_full = (
        lax.all_gather(expert_in, "dp", axis=1, tiled=True),
        lax.all_gather(expert_out, "dp", axis=1, tiled=True),
    )
    qkv_back = dense_back[1]
    out_back = dense_back[2]
    router_back = dense_back[4]
    weight_in_back = expert_back_full[0][0]
    weight_out_back = expert_back_full[1][0]
    slot_grads = (
        contract_rows(first_hot, (gate_first * grad_out).astype(jnp.bfloat16))
        + contract_rows(second_hot, (gate_second * grad_out).astype(jnp.bfloat16))
    ).astype(jnp.bfloat16)
    expert_grad_rows = lax.all_to_all(
        slot_grads.reshape(experts, capacity, model_width),
        "expert",
        split_axis=0,
        concat_axis=0,
        tiled=True,
    ).reshape(-1, model_width)
    grad_rows, grad_first_weight, grad_second_weight = expert_back(
        arrived, weight_in_back, weight_out_back, expert_grad_rows, hidden_block
    )
    grad_back = lax.all_to_all(
        grad_rows.astype(jnp.bfloat16).reshape(experts, capacity, model_width),
        "expert",
        split_axis=0,
        concat_axis=0,
        tiled=True,
    ).reshape(-1, model_width)
    grad_act_two = jnp.dot(both_hot, grad_back, preferred_element_type=jnp.float32)
    gate_grad = first_pick * jnp.sum(
        grad_out * from_first, axis=-1, keepdims=True
    ) + second_pick * jnp.sum(grad_out * from_second, axis=-1, keepdims=True)
    logit_grad = gate_probs * (gate_grad - jnp.sum(gate_probs * gate_grad, axis=-1, keepdims=True))
    router_f = router_back.astype(jnp.float32)
    grad_act_two = grad_act_two + lax.dot_general(
        logit_grad,
        router_f,
        (((1,), (1,)), ((), ())),
        precision=HIGH,
        preferred_element_type=jnp.float32,
    )
    router_grad = lax.dot_general(
        act_two.astype(jnp.float32),
        logit_grad,
        (((0,), (0,)), ((), ())),
        precision=HIGH,
        preferred_element_type=jnp.float32,
    )
    grad_norm_two, gain_two_grad = layer_norm_back(
        grad_act_two, normed_two, inverse_two, gain_two_f
    )
    grad_resid = grad_out + grad_norm_two
    branch_grad = grad_resid.astype(jnp.bfloat16)
    out_weight_grad = contract_rows(mixed_low, branch_grad)
    grad_mixed = contract_cols(branch_grad, out_back).astype(jnp.bfloat16)
    qkv_grad_low = attention_back(qkv_low, log_total, grad_mixed, IMG_DEV, HEADS)
    qkv_weight_grad = contract_rows(act_one, qkv_grad_low)
    grad_act_one = contract_cols(qkv_grad_low, qkv_back)
    grad_norm_one, gain_one_grad = layer_norm_back(
        grad_act_one, normed_one, inverse_one, gain_one_f
    )
    tokens_grad = grad_resid + grad_norm_one
    dense_grads = (
        lax.psum_scatter(gain_one_grad, ("dp", "expert"), scatter_dimension=0, tiled=True),
        lax.psum_scatter(qkv_weight_grad, ("dp", "expert"), scatter_dimension=0, tiled=True),
        lax.psum_scatter(out_weight_grad, ("dp", "expert"), scatter_dimension=0, tiled=True),
        lax.psum_scatter(gain_two_grad, ("dp", "expert"), scatter_dimension=0, tiled=True),
        lax.psum_scatter(router_grad, ("dp", "expert"), scatter_dimension=0, tiled=True),
    )
    expert_grads = (
        lax.psum_scatter(
            grad_first_weight[None].astype(jnp.bfloat16), "dp", scatter_dimension=1, tiled=True
        ).astype(jnp.float32),
        lax.psum_scatter(
            grad_second_weight[None].astype(jnp.bfloat16), "dp", scatter_dimension=1, tiled=True
        ).astype(jnp.float32),
    )
    first_result = expert_grads[0]
    second_result = expert_grads[1]
    return (
        output.astype(jnp.bfloat16),
        loss_value,
        tokens_grad,
        dense_grads[0],
        dense_grads[1],
        dense_grads[2],
        dense_grads[3],
        dense_grads[4],
        first_result,
        second_result,
    )


F32 = jnp.float32
BF16 = jnp.bfloat16
MB = 2**20


def round_up(value, unit):
    return (value + unit - 1) // unit * unit


def dot(left_side, right_side):
    return jnp.dot(left_side, right_side, preferred_element_type=F32)


def lane_ids(shape):
    return lax.broadcasted_iota(jnp.int32, shape, len(shape) - 1)


def row_ids(shape):
    return lax.broadcasted_iota(jnp.int32, shape, len(shape) - 2)


MESH = pl.DeviceIdType.MESH


def flip(index, bit):
    return index + bit * (1 - 2 * lax.rem(index // bit, 2))


def send(src, dst, sems, slot, device):
    return pltpu.make_async_remote_copy(
        src_ref=src, dst_ref=dst, send_sem=sems[0].at[slot], recv_sem=sems[1].at[slot],
        device_id=device, device_id_type=MESH,
    )


def greet(peers):
    barrier = pltpu.get_barrier_semaphore()
    for peer in peers:
        pl.semaphore_signal(barrier, inc=1, device_id=peer, device_id_type=MESH)
    pl.semaphore_wait(barrier, len(peers))


def place():
    dp_at, ex_at = lax.axis_index("dp"), lax.axis_index("expert")
    near = [None, flip(dp_at, 1), flip(dp_at, 2), flip(flip(dp_at, 1), 2)]
    return dp_at, ex_at, near


def sem_pairs(count):
    return [pltpu.SemaphoreType.DMA((count,)), pltpu.SemaphoreType.DMA((count,))]


def normalize(values):
    centered = values - jnp.mean(values, axis=-1, keepdims=True)
    inverse = lax.rsqrt(jnp.mean(centered * centered, axis=-1, keepdims=True) + EPS)
    return centered * inverse, inverse


def gelu_pair(values):
    size = jnp.abs(values)
    inv = 1.0 / (1.0 + 0.2316419 * size)
    density = 0.3989422804014327 * jnp.exp(-0.5 * values * values)
    series = inv * (
        0.319381530
        + inv * (-0.356563782 + inv * (1.781477937 + inv * (-1.821255978 + inv * 1.330274429)))
    )
    tail = density * series
    cumulative = jnp.where(values >= 0, 1.0 - tail, tail)
    return values * cumulative, cumulative + values * density


def plane_gather(mine, blocks, q, sems, base, dp_at, ex_at, near):
    half = blocks.shape[2] // 2
    first, second = pl.ds(0, half), pl.ds(half, half)
    own = [send(mine, blocks.at[q, dp_at], sems, base + k - 1, (near[k], ex_at)) for k in (1, 2)]
    passed = [
        send(blocks.at[q, near[1], first], blocks.at[q, near[1], first], sems, base + 2, (near[2], ex_at)),
        send(blocks.at[q, near[2], second], blocks.at[q, near[2], second], sems, base + 3, (near[1], ex_at)),
    ]
    return own, passed


def hot_rows(codes, start, count):
    slots = row_ids((count, codes.shape[1])) + start
    return (slots == codes[0:1, :]) | (slots == codes[1:2, :])


def return_copies(buf, back, q, half, sems, local, dp_at, ex_at):
    peers = [None, (dp_at, flip(ex_at, 1)), (dp_at, flip(ex_at, 2)), (dp_at, flip(flip(ex_at, 1), 2))]
    copies = []
    for k in (2 * half, 2 * half + 1):
        if k == 0:
            copies.append(pltpu.make_async_copy(buf.at[q, 0], back.at[q, 0], local.at[q]))
        else:
            copies.append(send(buf.at[q, k], back.at[q, k], sems, 4 * q + k, peers[k]))
    return copies


def front_kernel(
    images, real_rows, experts, cap, group,
    tok_ref, qkvw_ref, outw_ref, extra_ref, cols_ref, rows_ref, codes_ref, all_cols_ref, win_ref, wex_ref,
    qkv_ref, probs_ref, mixed_ref, resid_ref, gates_ref, dense_ref, ext_ref, rows_out_ref, hidden_ref, slope_ref,
    back_ref, code_out, grow_out, win_out, wex_out,
    dense, act, code_buf, grow_buf, win_buf, wex_buf, out_buf, kept,
    d_send, d_recv, t_send, t_recv, r_send, r_recv, w_send, w_recv, y_send, y_recv, local_sem,
):
    step_at = pl.program_id(0)
    dp_at, ex_at, near = place()
    core, floor = lax.rem(ex_at, 2), ex_at // 2
    dsem, tsem, rsem, wsem, ysem = (d_send, d_recv), (t_send, t_recv), (r_send, r_recv), (w_send, w_recv), (y_send, y_recv)
    mate, across, beyond = (dp_at, flip(ex_at, 1)), (dp_at, flip(ex_at, 2)), (dp_at, flip(flip(ex_at, 1), 2))
    far = (dp_at, flip(ex_at, 4))
    group_peers = [mate, across, beyond]
    floors = [floor, flip(floor, 1), flip(floor, 2), flip(flip(floor, 1), 2)]
    columns = [dp_at] + near[1:]
    at_expert = jnp.maximum(step_at - images, 0)
    which, half = at_expert // 2, lax.rem((at_expert + 1) // 2, 2)
    order = [(0, 0), (0, 1), (1, 1), (1, 0)]

    codes_sent = [send(codes_ref, code_buf.at[k + 1], rsem, k, group_peers[k]) for k in range(3)]
    grow_sent = [send(grow_buf.at[0], grow_buf.at[k + 1], rsem, 3 + k, group_peers[k]) for k in range(3)]
    stores = [
        pltpu.make_async_copy(code_buf, code_out, local_sem.at[2]),
        pltpu.make_async_copy(grow_buf, grow_out, local_sem.at[3]),
        pltpu.make_async_copy(win_buf, win_out, local_sem.at[4]),
        pltpu.make_async_copy(wex_buf, wex_out, local_sem.at[5]),
    ]
    in_own, in_passed = plane_gather(win_ref, win_buf, 0, wsem, 0, dp_at, ex_at, near)
    ex_own, ex_passed = plane_gather(wex_ref, wex_buf, 0, wsem, 4, dp_at, ex_at, near)
    in_far, in_far_passed = plane_gather(win_buf.at[1, dp_at], win_buf, 1, wsem, 8, dp_at, ex_at, near)
    ex_far, ex_far_passed = plane_gather(wex_buf.at[1, dp_at], wex_buf, 1, wsem, 12, dp_at, ex_at, near)
    to_far = [
        send(win_ref, win_buf.at[1, dp_at], wsem, 16, far),
        send(wex_ref, wex_buf.at[1, dp_at], wsem, 17, far),
    ]
    along_line = [
        send(dense.at[dp_at, floor, core], dense.at[dp_at, floor, core], dsem, k - 1, (dp_at, 2 * floors[k] + core))
        for k in (1, 2, 3)
    ]
    in_plane = [
        [
            send(
                dense.at[dp_at, floors[k], core], dense.at[dp_at, floors[k], core], dsem, 3 + 3 * k + p - 1,
                (near[p], ex_at),
            )
            for p in (1, 2, 3)
        ]
        for k in range(4)
    ]
    dense_mate = [
        send(dense.at[columns[p], :, core], dense.at[columns[p], :, core], dsem, 15 + p, mate) for p in range(4)
    ]

    def to_mate(step):
        return send(act.at[0, step], act.at[1, step], tsem, step, mate)

    def to_chip(step):
        return send(act.at[0, step], act.at[2, step], tsem, images + step, across)

    def onward(step):
        return send(act.at[2, step], act.at[3, step], tsem, 2 * images + step, mate)

    def returns(step):
        q, side = order[step]
        return return_copies(out_buf, back_ref, q, side, ysem, local_sem, dp_at, ex_at)

    def pass_on(own, passed):
        for first, second in zip(own, passed):
            first.wait_recv()
            second.start()

    @pl.when(step_at == 0)
    def _():
        width = outw_ref.shape[1]
        dense[dp_at, floor, core, :, : 3 * width] = qkvw_ref[...]
        dense[dp_at, floor, core, :, 3 * width : 4 * width] = outw_ref[...]
        valid = jnp.maximum(all_cols_ref[...], 0).astype(F32)
        per_lane = jnp.sum(jnp.sum(valid, axis=0), axis=0, keepdims=True)
        my_count = jnp.sum(jnp.where(lane_ids((1, 8)) == 4, per_lane, 0.0), axis=-1, keepdims=True)
        count_high = jnp.floor(my_count * (1.0 / 128.0))
        lanes = lane_ids((1, 128))
        counts = jnp.where(lanes == experts + 2, count_high, 0.0) + jnp.where(
            lanes == experts + 3, my_count - 128.0 * count_high, 0.0
        )
        dense[dp_at, floor, core, :, 4 * width :] = (extra_ref[...].astype(F32) + counts).astype(BF16)
        code_buf[0] = codes_ref[...]
        greet([(near[k], ex_at) for k in (1, 2, 3)] + group_peers + [far, (dp_at, flip(flip(ex_at, 2), 4))])
        for copy in along_line + in_plane[0]:
            copy.start()
        win_buf[0, dp_at] = win_ref[...]
        wex_buf[0, dp_at] = wex_ref[...]
        for k in (1, 2, 3):
            along_line[k - 1].wait_recv()
            for copy in in_plane[k]:
                copy.start()
        dense_mate[0].start()
        for copy in to_far + codes_sent:
            copy.start()
        for p in (1, 2, 3):
            for k in range(4):
                in_plane[k][p - 1].wait_recv()
            dense_mate[p].start()
        for copy in in_own + ex_own:
            copy.start()
        for copy in dense_mate:
            copy.wait_recv()
        full = dense[...].reshape(dense_ref.shape)
        dense_ref[...] = full
        ext_ref[...] = full[:, 4 * width :].astype(F32).T

    @pl.when(step_at < images)
    def _():
        inputs = tok_ref[...].astype(F32)
        normed, _ = normalize(inputs)
        width = inputs.shape[1]
        act_one = (normed * ext_ref[experts : experts + 1, :]).astype(BF16)
        qkv = dot(act_one, dense_ref[:, : 3 * width]).astype(BF16)
        qkv_ref[...] = qkv
        rows = inputs.shape[0]
        low_half = lane_ids((1, 128)) < 64
        key_bias = jnp.where(lane_ids((1, rows)) < real_rows, 0.0, -1e30)
        parts = []
        for pair in range(width // 128):
            lanes = slice(128 * pair, 128 * (pair + 1))
            queries = qkv[:, lanes]
            key_rows = qkv[:, width + 128 * pair : width + 128 * (pair + 1)]
            values = qkv[:, 2 * width + 128 * pair : 2 * width + 128 * (pair + 1)]
            outs = []
            for side in range(2):
                mask = low_half if side == 0 else jnp.logical_not(low_half)
                masked = jnp.where(mask, queries, jnp.zeros_like(queries))
                scores = contract_cols(masked, key_rows) * 0.125 + key_bias
                exped = jnp.exp(scores - jnp.max(scores, axis=-1, keepdims=True))
                probs = (exped * (1.0 / jnp.sum(exped, axis=-1, keepdims=True))).astype(BF16)
                probs_ref[2 * pair + side] = probs
                outs.append(dot(probs, values))
            parts.append(jnp.where(low_half, outs[0], outs[1]).astype(BF16))
        mixed = jnp.concatenate(parts, axis=1)
        mixed_ref[...] = mixed
        resid = inputs + dot(mixed, dense_ref[:, 3 * width : 4 * width])
        resid_ref[...] = resid
        normed_two, _ = normalize(resid)
        act_two = (normed_two * ext_ref[experts + 1 : experts + 2, :]).astype(BF16)
        act[0, step_at] = act_two
        lanes = lane_ids((1, 128))
        logits = jnp.where(lanes < experts, dot(act_two, dense_ref[:, 4 * width :]), -1e30)
        exped = jnp.exp(logits - jnp.max(logits, axis=-1, keepdims=True))
        gates = exped / jnp.sum(exped, axis=-1, keepdims=True)
        cols = cols_ref[...]
        first = jnp.sum(jnp.where(lanes == cols[:, 2:3], gates, 0.0), axis=-1, keepdims=True)
        second = jnp.sum(jnp.where(lanes == cols[:, 3:4], gates, 0.0), axis=-1, keepdims=True)
        gates_ref[...] = jnp.where(lanes == experts, first, jnp.where(lanes == experts + 1, second, gates))
        logits_t = contract_cols(ext_ref[0:16, :].astype(BF16), act_two)[:experts]
        exped_t = jnp.exp(logits_t - jnp.max(logits_t, axis=0, keepdims=True))
        gates_t = exped_t / jnp.sum(exped_t, axis=0, keepdims=True)
        ids_t = row_ids(gates_t.shape)
        first_t = jnp.sum(jnp.where(ids_t == rows_ref[2:3, :], gates_t, 0.0), axis=0, keepdims=True)
        second_t = jnp.sum(jnp.where(ids_t == rows_ref[3:4, :], gates_t, 0.0), axis=0, keepdims=True)
        grow_buf[0, step_at] = jnp.where(row_ids((8, rows)) == 0, first_t, second_t)

    for step in range(images):

        @pl.when(step_at == step)
        def _():
            to_chip(step).start()
            to_mate(step).start()
            if step >= 3:
                to_chip(step - 3).wait_recv()
                onward(step - 3).start()

    @pl.when(step_at == images - 2)
    def _():
        pass_on(in_own, in_passed)

    @pl.when(step_at == images - 1)
    def _():
        for copy in grow_sent:
            copy.start()

    @pl.when(step_at == images)
    def _():
        pass_on(ex_own, ex_passed)
        to_far[0].wait_recv()
        for copy in in_far:
            copy.start()
        for copy in in_passed + codes_sent:
            copy.wait_recv()
        for step in range(images):
            to_mate(step).wait_recv()

    @pl.when(step_at == images + 1)
    def _():
        for step in range(images - 3, images):
            to_chip(step).wait_recv()
            onward(step).start()
        for step in range(images):
            onward(step).wait_recv()

    @pl.when(step_at == images + 2)
    def _():
        for copy in in_far_passed:
            copy.wait_recv()

    blocks = group // 2
    parts, width, hidden_width = win_buf.shape[1], act.shape[3], win_buf.shape[3]
    step_width = hidden_width // parts

    @pl.when(step_at >= images)
    def _():
        pieces = []
        for block in range(blocks):
            start = (which * group + half * blocks + block) * cap
            total = None
            for image in range(images):
                hot = hot_rows(code_buf[half * blocks + block, image], start, cap)
                term = dot(jnp.where(hot, 1.0, 0.0).astype(BF16), act[half * blocks + block, image])
                total = term if total is None else total + term
            pieces.append(total.astype(BF16))
        rows_in = jnp.concatenate(pieces, axis=0)
        rows_out_ref[...] = rows_in.reshape(rows_out_ref.shape)
        for part in range(parts):
            if part == 1:

                @pl.when(step_at == images + 1)
                def _():
                    pass_on(in_far, in_far_passed)
                    to_far[1].wait_recv()
                    for copy in ex_far:
                        copy.start()

            cut = slice(part * step_width, (part + 1) * step_width)
            hidden, slope = gelu_pair(dot(rows_in, win_buf[which, :, :, cut].reshape(width, step_width)))
            hidden_ref[:, :, cut] = hidden.astype(BF16).reshape(blocks, cap, step_width)
            slope_ref[:, :, cut] = slope.astype(BF16).reshape(blocks, cap, step_width)

    def second_product(source, q, side):
        result = None
        for part in range(parts):
            cut = slice(part * step_width, (part + 1) * step_width)
            term = dot(source[:, :, cut].reshape(blocks * cap, step_width), wex_buf[q, part])
            result = term if result is None else result + term
        out_buf[q, pl.ds(side * blocks, blocks)] = result.astype(BF16).reshape(blocks, cap, width)

    @pl.when(step_at == images)
    def _():
        for copy in ex_passed:
            copy.wait_recv()

    @pl.when(step_at == images + 2)
    def _():
        kept[...] = hidden_ref[...]

    @pl.when(step_at == images + 3)
    def _():
        pass_on(ex_far, ex_far_passed)
        for copy in grow_sent:
            copy.wait_recv()
        for copy in ex_far_passed:
            copy.wait_recv()
        for block, copy in reversed(list(enumerate(returns(2)))):
            result = None
            for part in range(parts):
                cut = slice(part * step_width, (part + 1) * step_width)
                term = dot(kept[block, :, cut], wex_buf[1, part])
                result = term if result is None else result + term
            out_buf[1, blocks + block] = result.astype(BF16)
            copy.start()
        for copy in stores:
            copy.start()

    @pl.when((step_at >= images) & (step_at != images + 2))
    def _():
        second_product(hidden_ref, which, half)

    for step in (0, 1, 3):

        @pl.when(step_at == images + step)
        def _():
            for copy in returns(step):
                copy.start()

    @pl.when(step_at == images + 3)
    def _():
        for step in range(4):
            for copy in returns(step):
                copy.wait()
        for copy in stores:
            copy.wait()
        for step in range(images):
            to_mate(step).wait_send()
            to_chip(step).wait_send()
            onward(step).wait_send()
        for copy in along_line + dense_mate + codes_sent + grow_sent + to_far + [c for line in in_plane for c in line]:
            copy.wait_send()
        for own, passed in ((in_own, in_passed), (ex_own, ex_passed), (in_far, in_far_passed), (ex_far, ex_far_passed)):
            for copy in own + passed:
                copy.wait_send()


def hot_cols(codes, count):
    return lane_ids((codes.shape[0], count)) == codes


def combine_back_kernel(
    images, cap, group, total_tokens, shard, experts, ext_ref, resid_ref, came_ref, cols_ref, gates_ref, target_ref,
    codes_ref, grow_ref, rows_ref, hidden_ref, slope_ref, win_all, wex_all,
    out_ref, dout_ref, dlogit_ref, loss_ref, back_ref, gin_ref, gex_ref, far_in, far_ex,
    dlow, win_buf, wex_buf, acc_in, acc_out, low_in, low_ex, out_buf,
    got_in, got_ex, sum_in, sum_ex, more_in, more_ex,
    t_send, t_recv, y_send, y_recv, w_send, w_recv, local_sem,
):
    step_at = pl.program_id(0)
    dp_at, ex_at, near = place()
    mate, across = (dp_at, flip(ex_at, 1)), (dp_at, flip(ex_at, 2))
    tsem, ysem, wsem = (t_send, t_recv), (y_send, y_recv), (w_send, w_recv)
    at_expert = jnp.maximum(step_at - images, 0)
    which, half = 1 - at_expert // 2, lax.rem((at_expert + 1) // 2, 2)
    order = [(1, 0), (1, 1), (0, 1), (0, 0)]
    loads = [
        pltpu.make_async_copy(win_all, win_buf, local_sem.at[3]),
        pltpu.make_async_copy(wex_all, wex_buf, local_sem.at[4]),
    ]
    stores = [
        pltpu.make_async_copy(low_in.at[0], gin_ref, local_sem.at[7]),
        pltpu.make_async_copy(low_ex.at[0], gex_ref, local_sem.at[8]),
    ]
    tensors = [(low_in, got_in, sum_in, more_in, far_in, 1, 2), (low_ex, got_ex, sum_ex, more_ex, far_ex, 2, 1)]
    parts, width, hidden_width = win_buf.shape[1], dlow.shape[3], win_buf.shape[3]
    step_width = hidden_width // parts
    spread_in, spread_ex = [], []
    for s, owner in enumerate((near[1], near[3])):
        for part in range(parts):
            cut = slice(part * step_width, (part + 1) * step_width)
            spread_in.append(
                send(low_in.at[1, owner, :, cut], got_in.at[s, :, cut], wsem, 4 + parts * s + part, (near[1], ex_at))
            )
    for s, owner in enumerate((near[2], near[3])):
        spread_ex.append(send(low_ex.at[1, owner], got_ex.at[s], wsem, s, (near[2], ex_at)))
    spread = spread_in + spread_ex
    second_round = [
        send(passed, more, wsem, 2 + t, (near[second], ex_at))
        for t, (_, _, passed, more, _, _, second) in enumerate(tensors)
    ]

    def to_mate(step):
        return send(dlow.at[0, step], dlow.at[1, step], tsem, step, mate)

    def to_chip(step):
        return send(dlow.at[0, step], dlow.at[2, step], tsem, images + step, across)

    def onward(step):
        return send(dlow.at[2, step], dlow.at[3, step], tsem, 2 * images + step, mate)

    def returns(step):
        q, side = order[step]
        return return_copies(out_buf, back_ref, q, side, ysem, local_sem, dp_at, ex_at)

    @pl.when(step_at == 0)
    def _():
        for copy in loads:
            copy.start()
        greet(
            [(near[k], ex_at) for k in (1, 2)] + [mate, across, (dp_at, flip(flip(ex_at, 1), 2))]
        )

    @pl.when(step_at < images)
    def _():
        count = came_ref.shape[0]
        cols = cols_ref[...]
        rows = cols.shape[0]
        hot = jnp.concatenate(
            [
                jnp.where(hot_cols(cols[:, 0:1], count), 1.0, 0.0).astype(BF16),
                jnp.where(hot_cols(cols[:, 1:2], count), 1.0, 0.0).astype(BF16),
            ],
            axis=0,
        )
        both = dot(hot, came_ref[...])
        from_first, from_second = both[:rows], both[rows:]
        gates = gates_ref[...]
        first, second = gates[:, experts : experts + 1], gates[:, experts + 1 : experts + 2]
        output = resid_ref[...] + first * from_first + second * from_second
        out_ref[...] = output.astype(BF16)
        residue = output - target_ref[...].astype(F32)
        valid = jnp.maximum(cols[:, 4:5], 0).astype(F32)
        square = jnp.mean(residue * residue, axis=-1, keepdims=True) * valid

        @pl.when(step_at == 0)
        def _():
            loss_ref[...] = jnp.zeros_like(loss_ref)

        counts = jnp.sum(ext_ref[experts + 2 : experts + 4, :], axis=-1, keepdims=True)
        count_all = (counts[0:1] * 128.0 + counts[1:2]) / shard
        loss_ref[...] += jnp.sum(square) / count_all
        dout = (total_tokens / count_all * valid) * residue
        dout_ref[...] = dout
        dlow[0, step_at] = dout.astype(BF16)
        lanes = lane_ids((1, 128))
        grad = jnp.where(
            lanes == cols[:, 2:3], jnp.sum(dout * from_first, axis=-1, keepdims=True), 0.0
        ) + jnp.where(lanes == cols[:, 3:4], jnp.sum(dout * from_second, axis=-1, keepdims=True), 0.0)
        real = jnp.where(lanes < experts, gates, 0.0)
        dlogit_ref[...] = real * (grad - jnp.sum(real * grad, axis=-1, keepdims=True))

    for step in range(images):

        @pl.when(step_at == step)
        def _():
            to_chip(step).start()
            to_mate(step).start()
            if step >= 3:
                to_chip(step - 3).wait_recv()
                onward(step - 3).start()

    @pl.when(step_at == images)
    def _():
        for copy in loads:
            copy.wait()
        for step in range(images):
            to_mate(step).wait_recv()

    @pl.when(step_at == images + 1)
    def _():
        for step in range(images - 3, images):
            to_chip(step).wait_recv()
            onward(step).start()
        for step in range(images):
            onward(step).wait_recv()

    @pl.when(step_at >= images)
    def _():
        blocks = group // 2
        parts, width, hidden_width = win_buf.shape[1], dlow.shape[3], win_buf.shape[3]
        pieces = []
        for block in range(blocks):
            start = (which * group + half * blocks + block) * cap
            total = None
            slot_gate = None
            for image in range(images):
                codes = codes_ref[half * blocks + block, image]
                slots = row_ids((cap, codes.shape[1])) + start
                is_first = slots == codes[0:1, :]
                is_second = slots == codes[1:2, :]
                hot = jnp.where(is_first | is_second, 1.0, 0.0).astype(BF16)
                term = dot(hot, dlow[half * blocks + block, image])
                gain = grow_ref[half * blocks + block, image]
                picked = jnp.where(is_first, gain[0:1, :], jnp.where(is_second, gain[1:2, :], 0.0))
                picked = jnp.sum(picked, axis=-1, keepdims=True)
                total = term if total is None else total + term
                slot_gate = picked if slot_gate is None else slot_gate + picked
            pieces.append((total * slot_gate).astype(BF16))
        grads = jnp.concatenate(pieces, axis=0)
        grads_t = grads.T
        rows_in_t = rows_ref[...].reshape(blocks * cap, -1).T
        step = hidden_width // parts
        result = None
        for offset in range(0, hidden_width, step):
            if offset == hidden_width - step:

                @pl.when(at_expert == 3)
                def _():
                    for copy in spread:
                        copy.wait_recv()
                    for grad, got, passed, _, _, _, second in tensors:
                        passed[...] = (grad[1, near[second]].astype(F32) + got[1].astype(F32)).astype(BF16)
                    for copy in second_round:
                        copy.start()

            cut = slice(offset, offset + step)
            hidden = hidden_ref[:, :, cut].reshape(blocks * cap, step)
            slope = slope_ref[:, :, cut].reshape(blocks * cap, step).astype(F32)
            dpre = (contract_cols(grads, wex_buf[which, offset // step]) * slope).astype(BF16)
            gin = dot(rows_in_t, dpre)
            gout = dot(grads_t, hidden)
            term = contract_cols(dpre, win_buf[which, :, :, cut].reshape(width, step))
            result = term if result is None else result + term

            @pl.when(lax.rem(at_expert, 2) == 0)
            def _():
                acc_in[:, cut] = gin
                acc_out[:, cut] = gout

            @pl.when(lax.rem(at_expert, 2) == 1)
            def _():
                total_in = (acc_in[:, cut] + gin).astype(BF16)
                low_in[which, :, :, cut] = total_in.reshape(parts, width // parts, step)
                low_ex[which, offset // step] = (acc_out[:, cut] + gout).astype(BF16)

            part = offset // step

            @pl.when(at_expert == 1)
            def _():
                for s in range(2):
                    spread_in[parts * s + part].start()

            for s, owner in enumerate((near[2], near[3])):

                @pl.when((at_expert == 1) & (owner == part))
                def _():
                    spread_ex[s].start()

        out_buf[which, pl.ds(half * blocks, blocks)] = result.astype(BF16).reshape(blocks, cap, width)

    for step in range(4):

        @pl.when(step_at == images + step)
        def _():
            for copy in returns(step):
                copy.start()

    @pl.when(step_at == images + 3)
    def _():
        for copy in stores:
            copy.start()
        for step in range(4):
            for copy in returns(step):
                copy.wait()
        for copy in second_round:
            copy.wait_recv()
        for grad, got, _, more, far, _, _ in tensors:
            far[...] = (grad[1, dp_at].astype(F32) + got[0].astype(F32) + more[...].astype(F32)).astype(BF16)
        for copy in stores:
            copy.wait()
        for copy in spread + second_round:
            copy.wait_send()
        for step in range(images):
            to_mate(step).wait_send()
            to_chip(step).wait_send()
            onward(step).wait_send()


def back_kernel(
    images, real_rows, experts, tok_ref, dense_w, ext_ref, cols_ref, back_ref, dlogit_ref, resid_ref,
    dout_ref, qkv_ref, probs_ref, mixed_ref, loss_ref, gin_ref, gex_ref, far_in, far_ex,
    tgrad_ref, dense_ref, misc_ref, gin_out, gex_out,
    acc, acc_misc, part_in, part_ex, got_in, got_ex, sum_in, sum_ex, more_in, more_ex, came_in, came_ex,
    low, mate, low_mate, plane, low_plane, line, misc_got, misc_t, local_sem, w_send, w_recv, d_send, d_recv, m_send, m_recv,
):
    step_at = pl.program_id(0)
    dp_at, ex_at, near = place()
    core, floor = lax.rem(ex_at, 2), ex_at // 2
    wsem, dsem, msem = (w_send, w_recv), (d_send, d_recv), (m_send, m_recv)
    tensors = [
        (gin_ref, part_in, got_in, sum_in, more_in, far_in, came_in, gin_out, 1, 2),
        (gex_ref, part_ex, got_ex, sum_ex, more_ex, far_ex, came_ex, gex_out, 2, 1),
    ]
    local_copies, first_round, second_round, far_round = [], [], [], []
    for t, (grad, part, got, passed, more, far, came, _, first, second) in enumerate(tensors):
        for s in range(2):
            mine = dp_at if s == 0 else near[second]
            theirs = near[first] if s == 0 else near[3]
            local_copies.append(pltpu.make_async_copy(grad.at[mine], part.at[s], local_sem.at[2 * t + s]))
            first_round.append(send(grad.at[theirs], got.at[s], wsem, 4 * t + s, (near[first], ex_at)))
        second_round.append(send(passed, more, wsem, 4 * t + 2, (near[second], ex_at)))
        far_round.append(send(far, came, wsem, 4 * t + 3, (dp_at, flip(ex_at, 4))))

    @pl.when(step_at == 0)
    def _():
        for copy in local_copies:
            copy.start()
        greet(
            [(near[k], ex_at) for k in (1, 2, 3)]
            + [(dp_at, flip(ex_at, bit)) for bit in (1, 2, 4)]
            + [(dp_at, flip(flip(ex_at, 2), 4))]
        )
        for copy in first_round + far_round:
            copy.start()

    count = back_ref.shape[0]
    cols = cols_ref[...]
    hot = jnp.where(hot_cols(cols[:, 0:1], count) | hot_cols(cols[:, 1:2], count), 1.0, 0.0)
    dlogits = dlogit_ref[...]
    dact = dot(hot.astype(BF16), back_ref[...])
    dlogits_high = dlogits.astype(BF16)
    router_t = ext_ref[...].astype(BF16)
    dlogits_low = (dlogits - dlogits_high.astype(F32)).astype(BF16)
    dact = dact + dot(dlogits_high, router_t) + dot(dlogits_low, router_t)

    resid = resid_ref[...]
    normed_two, inverse_two = normalize(resid)
    gain_two = ext_ref[experts + 1 : experts + 2, :]
    act_two = (normed_two * gain_two).astype(BF16)
    grouter = contract_rows(dlogits_high, act_two) + contract_rows(dlogits_low, act_two)

    def norm_back(grad, normed, inverse, gain):
        scaled = grad * gain
        gain_grad = jnp.sum(grad * normed, axis=0, keepdims=True)
        inner = (
            scaled
            - jnp.mean(scaled, axis=-1, keepdims=True)
            - normed * jnp.mean(scaled * normed, axis=-1, keepdims=True)
        )
        return inverse * inner, gain_grad

    grad_two, ggain_two = norm_back(dact, normed_two, inverse_two, gain_two)
    dresid = dout_ref[...] + grad_two
    branch = dresid.astype(BF16)
    mixed = mixed_ref[...]
    gout = contract_rows(mixed, branch)
    width = branch.shape[1]
    dmixed = contract_cols(branch, dense_w[:, 3 * width : 4 * width]).astype(BF16)
    qkv = qkv_ref[...]
    low_half = lane_ids((1, 128)) < 64
    dqs, dks, dvs = [], [], []
    for pair in range(width // 128):
        cut = slice(128 * pair, 128 * (pair + 1))
        queries = qkv[:, cut]
        key_rows = qkv[:, width + 128 * pair : width + 128 * (pair + 1)]
        values = qkv[:, 2 * width + 128 * pair : 2 * width + 128 * (pair + 1)]
        dmix = dmixed[:, cut]
        dq = []
        dk = dv = None
        for side in range(2):
            mask = low_half if side == 0 else jnp.logical_not(low_half)
            dmask = jnp.where(mask, dmix, jnp.zeros_like(dmix))
            qmask = jnp.where(mask, queries, jnp.zeros_like(queries))
            probs_low = probs_ref[2 * pair + side]
            probs = probs_low.astype(F32)
            dprobs = contract_cols(dmask, values)
            dscore = probs * (dprobs - jnp.sum(probs * dprobs, axis=-1, keepdims=True))
            dscore = dscore.astype(BF16)
            dq.append(dot(dscore, key_rows))
            dk_term = contract_rows(dscore, qmask)
            dv_term = contract_rows(probs_low, dmask)
            dk = dk_term if dk is None else dk + dk_term
            dv = dv_term if dv is None else dv + dv_term
        dqs.append((jnp.where(low_half, dq[0], dq[1]) * 0.125).astype(BF16))
        dks.append((dk * 0.125).astype(BF16))
        dvs.append(dv.astype(BF16))
    dqkv = jnp.concatenate(dqs + dks + dvs, axis=1)
    inputs = tok_ref[...].astype(F32)
    normed_one, inverse_one = normalize(inputs)
    gain_one = ext_ref[experts : experts + 1, :]
    act_one = (normed_one * gain_one).astype(BF16)
    gqkv = contract_rows(act_one, dqkv)
    dact_one = contract_cols(dqkv, dense_w[:, : 3 * width])
    grad_one, ggain_one = norm_back(dact_one, normed_one, inverse_one, gain_one)
    tgrad = dresid + grad_one
    for image in range(images):

        @pl.when(step_at == image)
        def _():
            tgrad_ref[image * real_rows : (image + 1) * real_rows, :] = tgrad[:real_rows]

    ids = row_ids((8, width))
    gmisc = jnp.concatenate(
        [grouter[:8], jnp.where(ids == 0, ggain_one, jnp.where(ids == 1, ggain_two, 0.0))], axis=0
    )

    @pl.when(step_at == 0)
    def _():
        acc[:, : 3 * width] = gqkv
        acc[:, 3 * width :] = gout
        loss_row = jnp.where(row_ids((8, 128)) == 2, loss_ref[...], 0.0)
        acc_misc[...] = gmisc + jnp.concatenate(
            [jnp.zeros((8, width), F32), jnp.concatenate([loss_row] * (width // 128), axis=1)], axis=0
        )

    @pl.when(step_at > 0)
    def _():
        acc[:, : 3 * width] += gqkv
        acc[:, 3 * width :] += gout
        acc_misc[...] += gmisc

    @pl.when(step_at == images - 2)
    def _():
        for copy in local_copies:
            copy.wait()
        for copy in first_round:
            copy.wait_recv()
        for _, part, got, passed, _, _, _, _, _, _ in tensors:
            passed[...] = (part[1].astype(F32) + got[1].astype(F32)).astype(BF16)
        for copy in second_round:
            copy.start()

    @pl.when(step_at == images - 1)
    def _():
        lines, shard = low.shape[1], low.shape[3]
        low[...] = acc[...].astype(BF16).reshape(low.shape)
        other = lax.rem(core + 1, 2)
        to_mate = send(low.at[:, :, other], mate, dsem, 0, (dp_at, flip(ex_at, 1)))
        to_mate.start()
        misc_peers = [
            (dp_at, flip(ex_at, 1)), (near[1], ex_at), (near[2], ex_at), (dp_at, flip(ex_at, 2)), (dp_at, flip(ex_at, 4)),
        ]
        misc = [send(acc_misc.at[...] if k == 0 else misc_got.at[5 + k - 1], misc_got.at[k], msem, k, misc_peers[k]) for k in range(5)]
        misc[0].start()

        def misc_step(k):
            misc[k].wait_recv()
            before = acc_misc[...] if k == 0 else misc_got[5 + k - 1]
            misc_got[5 + k] = before + misc_got[k]
            if k < 4:
                misc[k + 1].start()

        to_mate.wait_recv()
        low_mate[...] = (low[:, :, core].astype(F32) + mate[...].astype(F32)).astype(BF16)
        to_plane = [send(low_mate.at[near[k]], plane.at[k - 1], dsem, k, (near[k], ex_at)) for k in (1, 2, 3)]
        for copy in to_plane:
            copy.start()
        misc_step(0)
        misc_step(1)
        misc_step(2)
        for copy in to_plane:
            copy.wait_recv()
        summed = low_mate[dp_at].astype(F32)
        for k in range(3):
            summed = summed + plane[k].astype(F32)
        low_plane[...] = summed.astype(BF16)
        floors = [flip(floor, 1), flip(floor, 2), flip(flip(floor, 1), 2)]
        to_line = [
            send(low_plane.at[floors[k]], line.at[k], dsem, 4 + k, (dp_at, 2 * floors[k] + core)) for k in range(3)
        ]
        for copy in to_line:
            copy.start()
        misc_step(3)
        misc_step(4)
        flat = (dp_at * (2 * low.shape[1]) + ex_at) * shard
        rows_t = jnp.concatenate([misc_got[9], jnp.zeros((112, misc_got.shape[2]), F32)], axis=0).T
        misc_t[...] = rows_t
        misc_ref[...] = misc_t[pl.ds(pl.multiple_of(flat, shard), shard), :]
        for copy in to_line:
            copy.wait_recv()
        result = low_plane[floor].astype(F32)
        for k in range(3):
            result = result + line[k].astype(F32)
        dense_ref[...] = result

        for copy in second_round + far_round:
            copy.wait_recv()
        for _, part, got, _, more, _, came, out, _, _ in tensors:
            out[...] = (
                part[0].astype(F32) + got[0].astype(F32) + more[...].astype(F32) + came[...].astype(F32)
            )
        for copy in [to_mate] + misc + to_plane + to_line + first_round + second_round + far_round:
            copy.wait_send()


def prepare_kernel(
    images, capacity, cap, tok_ref, target_ref, routes_ref, slots_ref, valid_ref, router_ref, gain_one_ref, gain_two_ref,
    tok_out, target_out, cols_out, rows_out, extra_out,
    wide, line,
):
    total, width = tok_ref.shape
    real_rows, rows = total // images, tok_out.shape[1]
    for source, out in ((tok_ref, tok_out), (target_ref, target_out)):
        wide[:total, :] = source[...].astype(F32)
        for image in range(images):
            piece = wide[image * real_rows : image * real_rows + rows, :]
            piece = jnp.where(row_ids((rows, 1)) < real_rows, piece, 0.0)
            out[image] = piece.astype(BF16)
    me = lax.axis_index("expert")
    routes, slots = routes_ref[...], slots_ref[...]
    code = jnp.where(slots < capacity, jnp.bitwise_xor(routes, me) * cap + slots, -1)
    line[0:2, :total] = code.astype(F32)
    line[2:4, :total] = routes.astype(F32)
    line[4:5, :total] = valid_ref[...].astype(F32)
    lanes = line.shape[1]
    packed = line[...]
    for image in range(images):
        piece = packed[:, image * real_rows : image * real_rows + rows]
        keep = (lane_ids((8, rows)) < real_rows) & (row_ids((8, rows)) < 5)
        piece = jnp.where(keep, piece, -1.0)
        rows_out[image] = piece.astype(jnp.int32)
        square = jnp.concatenate(
            [
                jnp.concatenate([piece, jnp.full((8, round_up(rows, 128) - rows), -1.0, F32)], axis=1),
                jnp.full((120, round_up(rows, 128)), -1.0, F32),
            ],
            axis=0,
        )
        cols_out[image] = square.T[:rows, :8].astype(jnp.int32)
    experts, shard = router_ref.shape
    tall = jnp.concatenate(
        [
            router_ref[...].astype(F32), gain_one_ref[...].astype(F32), gain_two_ref[...].astype(F32),
            jnp.zeros((126 - experts, shard), F32),
        ],
        axis=0,
    )
    tall = jnp.concatenate([tall, jnp.zeros((128, 128 - shard), F32)], axis=1)
    extra_out[...] = tall.T[:shard].astype(BF16)


def finish_kernel(
    real_rows, experts, padded_ref, tgrad_in, dense_ref, misc_ref, gin_in, gex_in,
    out_ref, loss_ref, tgrad_ref, gain_one_ref, gqkv_ref, gout_ref, gain_two_ref, grouter_ref, gin_ref, gex_ref,
    joined,
):
    images, width = padded_ref.shape[0], padded_ref.shape[2]
    for image in range(images):
        joined[image * real_rows : (image + 1) * real_rows, :] = padded_ref[image].astype(F32)[:real_rows]
    out_ref[...] = joined[: images * real_rows, :].astype(BF16)
    tgrad_ref[...] = tgrad_in[...]
    gqkv_ref[...] = dense_ref[:, : 3 * width]
    gout_ref[...] = dense_ref[:, 3 * width :]
    own = misc_ref[...]
    shard = own.shape[0]
    turned = jnp.concatenate([own, jnp.zeros((128 - shard, 128), F32)], axis=0).T
    gain_one_ref[...] = turned[8:9, :shard]
    gain_two_ref[...] = turned[9:10, :shard]
    grouter_ref[...] = turned[:experts, :shard]
    loss_ref[...] = own[0:1, 10:11]
    gin_ref[...] = gin_in[...]
    gex_ref[...] = gex_in[...].T


def shape(dims, kind):
    return jax.ShapeDtypeStruct(dims, kind)


def whole(dims):
    return pl.BlockSpec(dims, lambda *_: (0,) * len(dims))


def per_image(*dims):
    return pl.BlockSpec((None,) + dims, lambda i: (i,) + (0,) * len(dims))


def params():
    return pltpu.CompilerParams(vmem_limit_bytes=56 * MB)


def fast_shards(
    tokens, targets, valid_mask, routes, slot_ids, ln1_gain, qkv_weight, out_weight, ln2_gain,
    router_weight, expert_in, expert_out,
):
    axes = ("dp", "expert")
    tok_rows, width = tokens.shape
    experts = lax.axis_size("expert")
    group = experts // 2
    dp = lax.axis_size("dp")
    total_tokens = tok_rows * dp * experts
    hidden_width = expert_in.shape[2]
    capacity = (5 * tok_rows // 2 // experts + 7) // 8 * 8
    cap = round_up(capacity, 16)
    images = IMG_DEV
    real_rows = tok_rows // images
    rows = round_up(real_rows, 16)
    shard = qkv_weight.shape[0]
    tok_p, target_p, cols, row_codes, extra = pl.pallas_call(
        lambda *refs: prepare_kernel(images, capacity, cap, *refs),
        out_shape=[
            shape((images, rows, width), BF16), shape((images, rows, width), BF16), shape((images, rows, 8), jnp.int32),
            shape((images, 8, rows), jnp.int32), shape((shard, 128), BF16),
        ],
        scratch_shapes=[
            pltpu.VMEM((round_up(tok_rows + rows - real_rows, 8), width), F32),
            pltpu.VMEM((8, round_up(tok_rows + rows - real_rows, 128)), F32),
        ],
        compiler_params=params(),
        name="prepare",
    )(
        tokens, targets, routes.T, slot_ids.T, valid_mask[None], router_weight.T, ln1_gain[None], ln2_gain[None],
    )
    floors = experts // 2
    in_part, ex_part = (width // dp, hidden_width), (hidden_width // dp, width)
    any_space = pl.BlockSpec(memory_space=pl.ANY)

    gate_lanes = 128
    dense_lanes = 4 * width + 128
    half_blocks = group // 2
    last = images - 1

    def early(*dims):
        return pl.BlockSpec((None,) + dims, lambda i: (jnp.minimum(i, last),) + (0,) * len(dims))

    def late(far_first, *dims):
        def index(i):
            step = jnp.maximum(i - images, 0)
            which = 1 - step // 2 if far_first else step // 2
            return (which, lax.rem((step + 1) // 2, 2)) + (0,) * len(dims)

        return pl.BlockSpec((None, half_blocks) + dims, index)

    def once(dims):
        return pl.BlockSpec(dims, lambda i: (0,) * len(dims), pipeline_mode=pl.Buffered(1))

    (
        qkv_p, probs, mixed, resid, gates, dense_full, ext, rows_in, hidden, slope, returned, code_all, grow_all,
        win_all, wex_all,
    ) = pl.pallas_call(
        lambda *refs: front_kernel(images, real_rows, experts, cap, group, *refs),
        grid=(images + 4,),
        in_specs=[
            early(rows, width), once((shard, 3 * width)), once((shard, width)), once((shard, 128)),
            early(rows, 8), early(8, rows), once((images, 8, rows)), once((images, rows, 8)), once(in_part), once(ex_part),
        ],
        out_specs=[
            early(rows, 3 * width), early(HEADS, rows, rows), early(rows, width), early(rows, width),
            early(rows, gate_lanes), whole((width, dense_lanes)), whole((128, width)),
            late(False, cap, width), late(False, cap, hidden_width), late(False, cap, hidden_width),
            *[any_space] * 5,
        ],
        out_shape=[
            shape((images, rows, 3 * width), BF16), shape((images, HEADS, rows, rows), BF16),
            shape((images, rows, width), BF16), shape((images, rows, width), F32),
            shape((images, rows, gate_lanes), F32), shape((width, dense_lanes), BF16), shape((128, width), F32),
            shape((2, group, cap, width), BF16), shape((2, group, cap, hidden_width), BF16),
            shape((2, group, cap, hidden_width), BF16), shape((2, group, cap, width), BF16),
            shape((group, images, 8, rows), jnp.int32), shape((group, images, 8, rows), F32),
            shape((2, dp, *in_part), BF16), shape((2, dp, *ex_part), BF16),
        ],
        scratch_shapes=[
            pltpu.VMEM((dp, floors, 2, shard, dense_lanes), BF16), pltpu.VMEM((group, images, rows, width), BF16),
            pltpu.VMEM((group, images, 8, rows), jnp.int32), pltpu.VMEM((group, images, 8, rows), F32),
            pltpu.VMEM((2, dp, *in_part), BF16), pltpu.VMEM((2, dp, *ex_part), BF16),
            pltpu.VMEM((2, group, cap, width), BF16), pltpu.VMEM((half_blocks, cap, hidden_width), BF16),
            *sem_pairs(19), *sem_pairs(3 * images), *sem_pairs(6), *sem_pairs(18), *sem_pairs(8),
            pltpu.SemaphoreType.DMA((6,)),
        ],
        compiler_params=pltpu.CompilerParams(
            vmem_limit_bytes=60 * MB, collective_id=2, has_side_effects=True
        ),
        cost_estimate=pl.CostEstimate(flops=int(20e9), bytes_accessed=int(6e7), transcendentals=0),
        name="attention_expert_forward",
    )(tok_p, qkv_weight, out_weight, extra, cols, row_codes, row_codes, cols, expert_in[0], expert_out[0])
    returned = returned.reshape(2 * group * cap, width)

    flip_part = (width, hidden_width // dp)
    block_out, dout, dlogits, loss_part, drows, gin, gout_t, far_in, far_ex = pl.pallas_call(
        lambda *refs: combine_back_kernel(images, cap, group, total_tokens, shard, experts, *refs),
        grid=(images + 4,),
        in_specs=[
            once((16, width)), early(rows, width), once((2 * group * cap, width)), early(rows, 8),
            early(rows, gate_lanes), early(rows, width), once((group, images, 8, rows)),
            once((group, images, 8, rows)), late(True, cap, width), late(True, cap, hidden_width),
            late(True, cap, hidden_width), any_space, any_space,
        ],
        out_specs=[
            early(rows, width), early(rows, width), early(rows, gate_lanes), whole((8, 128)), *[any_space] * 3,
            once(in_part), once(flip_part),
        ],
        out_shape=[
            shape((images, rows, width), BF16), shape((images, rows, width), F32),
            shape((images, rows, gate_lanes), F32), shape((8, 128), F32),
            shape((2, group, cap, width), BF16), shape((dp, *in_part), BF16), shape((dp, *flip_part), BF16),
            shape(in_part, BF16), shape(flip_part, BF16),
        ],
        scratch_shapes=[
            pltpu.VMEM((group, images, rows, width), BF16),
            pltpu.VMEM((2, dp, *in_part), BF16), pltpu.VMEM((2, dp, *ex_part), BF16),
            pltpu.VMEM((width, hidden_width), F32), pltpu.VMEM((width, hidden_width), F32),
            pltpu.VMEM((2, dp, *in_part), BF16), pltpu.VMEM((2, dp, *flip_part), BF16),
            pltpu.VMEM((2, group, cap, width), BF16),
            *[pltpu.VMEM(dims, BF16) for dims in ((2, *in_part), (2, *flip_part), in_part, flip_part, in_part, flip_part)],
            *sem_pairs(3 * images), *sem_pairs(8), *sem_pairs(4 + 2 * dp), pltpu.SemaphoreType.DMA((9,)),
        ],
        compiler_params=pltpu.CompilerParams(
            vmem_limit_bytes=62 * MB, collective_id=5, has_side_effects=True
        ),
        cost_estimate=pl.CostEstimate(flops=int(24e9), bytes_accessed=int(4e7), transcendentals=0),
        name="combine_expert_backward",
    )(
        ext, resid, returned, cols, gates, target_p, code_all, grow_all, rows_in, hidden, slope,
        win_all, wex_all,
    )
    grad_back = drows.reshape(2 * group * cap, width)

    def vmem(*dims):
        return pltpu.VMEM(dims, BF16)

    tgrad, dense_grad, misc, gin_own, gex_own = pl.pallas_call(
        lambda *refs: back_kernel(images, real_rows, experts, *refs),
        grid=(images,),
        in_specs=[
            per_image(rows, width), whole((width, dense_lanes)), whole((128, width)), per_image(rows, 8),
            whole((2 * group * cap, width)), per_image(rows, gate_lanes), per_image(rows, width), per_image(rows, width),
            per_image(rows, 3 * width), per_image(HEADS, rows, rows), per_image(rows, width), whole((8, 128)),
            *[any_space] * 4,
        ],
        out_specs=[
            once((tok_rows, width)), whole((shard, 4 * width)), whole((shard, 128)), whole(in_part), whole(flip_part),
        ],
        out_shape=[
            shape((tok_rows, width), F32), shape((shard, 4 * width), F32), shape((shard, 128), F32),
            shape(in_part, F32), shape(flip_part, F32),
        ],
        scratch_shapes=[
            pltpu.VMEM((width, 4 * width), F32), pltpu.VMEM((16, width), F32),
            vmem(2, *in_part), vmem(2, *flip_part), vmem(2, *in_part), vmem(2, *flip_part),
            vmem(*in_part), vmem(*flip_part), vmem(*in_part), vmem(*flip_part), vmem(*in_part), vmem(*flip_part),
            vmem(dp, floors, 2, shard, 4 * width), vmem(dp, floors, shard, 4 * width), vmem(dp, floors, shard, 4 * width),
            vmem(3, floors, shard, 4 * width), vmem(floors, shard, 4 * width), vmem(3, shard, 4 * width),
            pltpu.VMEM((10, 16, width), F32), pltpu.VMEM((width, 128), F32),
            pltpu.SemaphoreType.DMA((4,)),
            *sem_pairs(8), *sem_pairs(8), *sem_pairs(5),
        ],
        compiler_params=pltpu.CompilerParams(
            vmem_limit_bytes=60 * MB, collective_id=1, has_side_effects=True
        ),
        cost_estimate=pl.CostEstimate(flops=int(10e9), bytes_accessed=int(3e7), transcendentals=0),
        name="attention_backward",
    )(
        tok_p, dense_full, ext, cols, grad_back, dlogits, resid, dout, qkv_p, probs, mixed,
        loss_part, gin, gout_t, far_in, far_ex,
    )
    out, loss, tokens_grad, gain_one_grad, qkv_grad, out_grad, gain_two_grad, router_grad, in_grad, ex_grad = pl.pallas_call(
        lambda *refs: finish_kernel(real_rows, experts, *refs),
        out_shape=[
            shape((tok_rows, width), BF16), shape((1, 1), F32), shape((tok_rows, width), F32), shape((1, shard), F32),
            shape((shard, 3 * width), F32), shape((shard, width), F32), shape((1, shard), F32),
            shape((experts, shard), F32), shape(in_part, F32), shape(ex_part, F32),
        ],
        scratch_shapes=[pltpu.VMEM((round_up(tok_rows, 8), width), F32)],
        compiler_params=params(),
        name="finish",
    )(block_out, tgrad, dense_grad, misc, gin_own, gex_own)
    return (
        out,
        loss.reshape(()),
        tokens_grad,
        gain_one_grad.reshape(shard),
        qkv_grad,
        out_grad,
        gain_two_grad.reshape(shard),
        router_grad.T,
        in_grad[None],
        ex_grad[None],
    )


def solution(mesh):
    in_specs = (
        P(("dp", "expert"), None),
        P(("dp", "expert"), None),
        P(("dp", "expert")),
        P(("dp", "expert"), None),
        P(("dp", "expert"), None),
        P(("dp", "expert")),
        P(("dp", "expert"), None),
        P(("dp", "expert"), None),
        P(("dp", "expert")),
        P(("dp", "expert"), None),
        P("expert", "dp", None),
        P("expert", "dp", None),
    )
    out_specs = (
        P(("dp", "expert"), None),
        P(),
        P(("dp", "expert"), None),
        P(("dp", "expert")),
        P(("dp", "expert"), None),
        P(("dp", "expert"), None),
        P(("dp", "expert")),
        P(("dp", "expert"), None),
        P("expert", "dp", None),
        P("expert", "dp", None),
    )
    halves = mesh.shape["expert"] == 8 and mesh.shape["dp"] == 4
    body = fast_shards if halves else shards
    return jax.shard_map(body, mesh=mesh, in_specs=in_specs, out_specs=out_specs, check_vma=False)
```
